32 devices in a mesh: dp: 16 (over z, x, core), mod: 2 (over y).
Axes of the slice: x: 2, y: 2, z: 4, core: 2. Of those that a mesh axis runs over, the one named last changes fastest.
Arguments:
- tokens: bfloat16 [32, 1024, 1152], P(('dp', 'mod')), may hold values from -6 to 6
- cond: float32 [32, 4, 1152], P(('dp', 'mod')), may hold values from -6 to 6
- segments: int32 [32, 1024], P(('dp', 'mod')), may hold values from 0 to 3, as said below
- coords: int32 [32, 2, 1024], P(('dp', 'mod')), may hold values from 0 to 31, as said below
- w_ada: bfloat16 [1152, 6912], P(None, 'mod'), may hold values from -0.1875 to 0.1875
- w_qkv: bfloat16 [1152, 3456], replicated, may hold values from -0.1875 to 0.1875
- q_gain: float32 [72], replicated, may hold values from 1 to 2
- k_gain: float32 [72], replicated, may hold values from 1 to 2
- w_out: bfloat16 [1152, 1152], replicated, may hold values from -1.5 to 1.5
- w_gate: bfloat16 [1152, 3072], replicated, may hold values from -0.1875 to 0.1875
- w_up: bfloat16 [1152, 3072], replicated, may hold values from -0.1875 to 0.1875
- w_down: bfloat16 [3072, 1152], replicated, may hold values from -0.109375 to 0.109375
- cotangent: bfloat16 [32, 1024, 1152], P(('dp', 'mod')), may hold values from -6 to 6
Outputs:
- output: bfloat16 [32, 1024, 1152], P(('dp', 'mod'))
- grad_tokens: bfloat16 [32, 1024, 1152], P(('dp', 'mod'))
- grad_cond: float32 [32, 4, 1152], P(('dp', 'mod'))
- grad_w_ada: float32 [1152, 6912], P('dp', 'mod')
- grad_w_qkv: float32 [1152, 3456], P(('dp', 'mod'))
- grad_q_gain: float32 [72], replicated
- grad_k_gain: float32 [72], replicated
- grad_w_out: float32 [1152, 1152], P(('dp', 'mod'))
- grad_w_gate: float32 [1152, 3072], P(('dp', 'mod'))
- grad_w_up: float32 [1152, 3072], P(('dp', 'mod'))
- grad_w_down: float32 [3072, 1152], P(('dp', 'mod'))
The draws below stay inside these ranges and needn't reach their ends.
Inputs may be any that keep to these rules, and one draw needn't show every extreme that they name: `segments`: each packed row holds either one item of 1024 tokens, all in slot 0, or four items of 256 tokens in slots 0 to 3 in order; exactly half of the rows are of each kind. `coords`: coordinates of a token's patch on its item's square grid, 32 per side for a whole-row item and 16 for the others; each item's grid may be flipped along either side or transposed.
All inputs are finite; a program needn't handle non-finite values.
Results may differ from the reference program's by a relative error of at most 0.0131.
The reference program's roundings to bfloat16 on the way count: a program that leaves them out, or rounds other values in their place, can miss the bound.
Values may be sent and summed in bfloat16 or wider, within the bound.
No kernel may reach another device: no remote copies, remote signals or barrier semaphores. Data moves between devices by JAX's collectives and lax.ppermute only.
A program may use at most 576 MiB of HBM per device.

```python
import math
import jax
import jax.numpy as jnp
from jax import lax

D = 1152
HEADS = 16
HD = 72
FF = 3072
GRID = 32
SLOTS = 4
ROW = 1024
ROWS = 32


def layout(key):
    kind_key = jax.random.fold_in(key, 101)
    flip_key = jax.random.fold_in(key, 202)
    whole = jax.random.permutation(kind_key, ROWS) % 2 == 1
    position = jnp.arange(ROW)
    quarter = ROW // 4
    small_side = GRID // 2
    segment_ids = jnp.where(whole[:, None], 0, (position // quarter)[None, :]).astype(jnp.int32)
    inner_index = jnp.where(whole[:, None], position[None, :], (position % quarter)[None, :])
    side_len = jnp.where(whole, GRID, small_side)[:, None]
    along_rows = inner_index // side_len
    along_cols = inner_index % side_len
    flip_bits = jax.random.randint(flip_key, (ROWS, SLOTS, 3), 0, 2)
    chosen = (segment_ids[:, :, None] == jnp.arange(SLOTS)[None, None, :]).astype(jnp.int32)
    token_bits = jnp.sum(chosen[:, :, :, None] * flip_bits[:, None, :, :], axis=2)
    along_rows = jnp.where(token_bits[:, :, 0] == 1, side_len - 1 - along_rows, along_rows)
    along_cols = jnp.where(token_bits[:, :, 1] == 1, side_len - 1 - along_cols, along_cols)
    row_coord = jnp.where(token_bits[:, :, 2] == 1, along_cols, along_rows)
    col_coord = jnp.where(token_bits[:, :, 2] == 1, along_rows, along_cols)
    coord_pair = jnp.stack([row_coord, col_coord], axis=1).astype(jnp.int32)
    return (segment_ids, coord_pair)


def draw_segments(key, part):
    return layout(key)[0]


def draw_coords(key, part):
    return layout(key)[1]


def with_spikes(entries, stream_key, source, target, parts, factor):
    owner, partner = [(jnp.arange(entries.shape[axis_at]) // (entries.shape[axis_at] // parts)).reshape([-1 if axis == axis_at else 1 for axis in range(entries.ndim)]) for axis_at in (source, target)]
    chosen = jax.random.permutation(stream_key, parts)[partner]
    strong = (owner == chosen) | (owner == (partner + parts // 2) % parts)
    return jnp.where(strong, factor * entries, entries)


def level_of(rng, extent, pieces, least, top_value):
    factor_of, own = 1.0, jax.random.fold_in(rng, 6)
    for axis_at, shards_of in pieces:
        steps = jnp.exp(jax.random.uniform(jax.random.fold_in(own, axis_at), (shards_of,), jnp.float32, least / len(pieces), top_value / len(pieces)))
        factor_of = factor_of * jnp.repeat(steps, extent[axis_at] // shards_of).reshape([-1 if axis == axis_at else 1 for axis in range(len(extent))])
    return factor_of


def gaussian(stream_key, shape, width, limit, pieces=(), kind=jnp.bfloat16):
    loudness = level_of(stream_key, shape, pieces, -0.22, 0.18) if pieces else 1.0
    values = jax.random.normal(stream_key, shape, jnp.float32) * width * loudness
    return jnp.minimum(jnp.maximum(values, -limit), limit).astype(kind)


def noise_with(stream_key, shape, spread, reach, pieces, heavy, kind=jnp.bfloat16):
    result = spread * jax.random.normal(stream_key, shape, jnp.float32)
    if pieces:
        result = result * level_of(stream_key, shape, pieces, -0.22, 0.18)
    return jnp.clip(with_spikes(result, jax.random.fold_in(stream_key, 3), *heavy), -reach, reach).astype(kind)


def setup_inputs(seed: int = 0) -> dict:
    splits = jax.random.split(jax.random.key(seed), 14)
    return {
        "tokens": noise_with(splits[0], (ROWS, ROW, D), 1.0, 6.0, ((0, 32),), (0, 2, 32, 2.75)),
        "cond": noise_with(splits[1], (ROWS, SLOTS, D), 1.0, 6.0, ((0, 32),), (0, 2, 32, 2.75), jnp.float32),
        "segments": draw_segments(jax.random.fold_in(splits[13], 71), 0),
        "coords": draw_coords(jax.random.fold_in(splits[13], 71), 0),
        "w_ada": gaussian(splits[4], (D, 6 * D), D ** -0.5, 0.1875, ((1, 2),)),
        "w_qkv": gaussian(splits[5], (D, 3 * D), D ** -0.5, 0.1875),
        "q_gain": jnp.clip(jnp.exp(jax.random.uniform(splits[6], (HD,), jnp.float32, math.log(1.0), math.log(2.0))), 1.0, 2.0),
        "k_gain": jnp.clip(jnp.exp(jax.random.uniform(splits[7], (HD,), jnp.float32, math.log(1.0), math.log(2.0))), 1.0, 2.0),
        "w_out": gaussian(splits[8], (D, D), (D // 64) ** -0.5, 1.5),
        "w_gate": gaussian(splits[9], (D, FF), D ** -0.5, 0.1875),
        "w_up": gaussian(splits[10], (D, FF), D ** -0.5, 0.1875),
        "w_down": gaussian(splits[11], (FF, D), FF ** -0.5, 0.109375),
        "cotangent": gaussian(splits[12], (ROWS, ROW, D), 1.0, 6.0, ((0, 32),)),
    }


HIGHEST_PRECISION = lax.Precision.HIGHEST
EPS_NORM = 1e-06
ROPE_BASE = 10000.0
MASKED = -1e+30

@jax.custom_vjp
def low(v):
    return lax.optimization_barrier(v.astype(jnp.bfloat16)).astype(jnp.float32)

@jax.custom_vjp
def low_back(v):
    return v

def low_keep(v):
    return (low(v), None)

def low_pass(kept, grad):
    return (grad,)

def back_keep(v):
    return (v, None)

def back_low(kept, grad):
    return (low(grad),)
low.defvjp(low_keep, low_pass)
low_back.defvjp(back_keep, back_low)

def product(a, b):
    return jnp.dot(a, b, precision=HIGHEST_PRECISION, preferred_element_type=jnp.float32)

def layer_norm(v):
    centred = v - lax.optimization_barrier(jnp.mean(v, axis=-1, keepdims=True))
    variance = lax.optimization_barrier(jnp.mean(centred * centred, axis=-1, keepdims=True))
    return centred * lax.rsqrt(variance + EPS_NORM)

def rms_norm(v, gain):
    return v * lax.rsqrt(lax.optimization_barrier(jnp.mean(v * v, axis=-1, keepdims=True)) + EPS_NORM) * gain

def rope_angles(coord_pair):
    quarter = HD // 4
    freqs = ROPE_BASE ** (-jnp.arange(quarter).astype(jnp.float32) / quarter)
    position = coord_pair.astype(jnp.float32)
    angle = position[:, :, None] * freqs[None, None, :]
    angle = jnp.transpose(angle, (1, 0, 2))[:, None, :, :]
    return (jnp.cos(angle), jnp.sin(angle))

def rotate(vectors, cosine_table, sine_table):
    shaped = vectors.reshape(vectors.shape[0], vectors.shape[1], 2, 2, HD // 4)
    lead = shaped[:, :, :, 0]
    trail = shaped[:, :, :, 1]
    new_lead = lead * cosine_table - trail * sine_table
    new_trail = lead * sine_table + trail * cosine_table
    return jnp.stack([new_lead, new_trail], axis=3).reshape(vectors.shape)

def block_row(x, cond_row, seg_row, coord_row, w_ada, w_qkv, q_gain, k_gain, w_out, w_gate, w_up, w_down):
    activated = low(jax.nn.silu(cond_row))
    modulation = low_back(low(product(activated, w_ada)))
    slot_onehot = (seg_row[:, None] == jnp.arange(SLOTS)[None, :]).astype(jnp.float32)
    per_token = product(slot_onehot, modulation)
    shift_attn, scale_attn, gate_attn, shift_ffn, scale_ffn, gate_ffn = jnp.split(per_token, 6, axis=1)
    mod_attn = low(layer_norm(x) * (1.0 + scale_attn) + shift_attn)
    projected = low_back(product(mod_attn, w_qkv))
    cosine_table, sine_table = rope_angles(coord_row)
    queries = low(rotate(rms_norm(projected[:, :D].reshape(ROW, HEADS, HD), q_gain), cosine_table, sine_table))
    key_vectors = low(rotate(rms_norm(projected[:, D:2 * D].reshape(ROW, HEADS, HD), k_gain), cosine_table, sine_table))
    value_vectors = low(projected[:, 2 * D:].reshape(ROW, HEADS, HD))
    query_block = min(512, ROW)

    def attend(inputs):
        query_part, seg_part = inputs
        scores = low_back(jnp.einsum('qhd,khd->hqk', query_part, key_vectors, precision=HIGHEST_PRECISION) * HD ** (-0.5))
        allowed = (seg_part[:, None] == seg_row[None, :])[None]
        scores = jnp.where(allowed, scores, MASKED)
        attn_probs = low(jax.nn.softmax(scores, axis=-1))
        return jnp.einsum('hqk,khd->qhd', attn_probs, value_vectors, precision=HIGHEST_PRECISION)
    blocks = lax.map(jax.checkpoint(attend), (queries.reshape(ROW // query_block, query_block, HEADS, HD), seg_row.reshape(ROW // query_block, query_block)))
    attended = low_back(low(blocks.reshape(ROW, D)))
    attn = low_back(product(attended, w_out))
    mid = x + gate_attn * attn
    mod_ffn = low(layer_norm(mid) * (1.0 + scale_ffn) + shift_ffn)
    gate_h = low_back(product(mod_ffn, w_gate))
    up_h = low_back(product(mod_ffn, w_up))
    hidden = low(jax.nn.silu(gate_h) * up_h)
    ffn = low_back(product(hidden, w_down))
    return mid + gate_ffn * ffn

def reference(tokens, cond, segments, coords, w_ada, w_qkv, q_gain, k_gain, w_out, w_gate, w_up, w_down, cotangent):

    def forward(x, cond_all, wa, wq, qg, kg, wo, wg, wu, wd):

        def per_row(inputs):
            x_row, cond_row, seg_row, coord_row = inputs
            return block_row(x_row, cond_row, seg_row, coord_row, wa, wq, qg, kg, wo, wg, wu, wd)
        return lax.map(jax.checkpoint(per_row), (x, cond_all, segments, coords))
    block_out, pullback = jax.vjp(forward, tokens.astype(jnp.float32), cond.astype(jnp.float32), w_ada.astype(jnp.float32), w_qkv.astype(jnp.float32), q_gain.astype(jnp.float32), k_gain.astype(jnp.float32), w_out.astype(jnp.float32), w_gate.astype(jnp.float32), w_up.astype(jnp.float32), w_down.astype(jnp.float32))
    gradients = pullback(cotangent.astype(jnp.float32))
    return (block_out.astype(jnp.bfloat16), gradients[0].astype(jnp.bfloat16), gradients[1], gradients[2], gradients[3], gradients[4], gradients[5], gradients[6], gradients[7], gradients[8], gradients[9])
```

```python
import functools

import jax
import jax.numpy as jnp
from jax import lax
from jax.sharding import PartitionSpec as P

HEADS = 16
HD = 72


EPS_NORM = 1e-06
ROPE_BASE = 10000.0
MASKED = -1e30


def layer_norm(v):
    centred = v - jnp.mean(v, axis=-1, keepdims=True)
    variance = jnp.mean(centred * centred, axis=-1, keepdims=True)
    return centred * lax.rsqrt(variance + EPS_NORM)


def modulate(v, shift_part, scale_part):
    return layer_norm(v) * (1.0 + scale_part) + shift_part


def rms_norm(v, gain):
    return v * lax.rsqrt(jnp.mean(v * v, axis=-1, keepdims=True) + EPS_NORM) * gain


def rope_angles(coord_pair):
    quarter = HD // 4
    freqs = ROPE_BASE ** (-jnp.arange(quarter).astype(jnp.float32) / quarter)
    position = coord_pair.astype(jnp.float32)
    angle = position[:, :, None] * freqs[None, None, :]
    angle = jnp.transpose(angle, (1, 0, 2))[:, None, :, :]
    return (jnp.cos(angle), jnp.sin(angle))


def rotate(vectors, cosine_table, sine_table):
    shaped = vectors.reshape(vectors.shape[0], vectors.shape[1], 2, 2, HD // 4)
    lead = shaped[:, :, :, 0]
    trail = shaped[:, :, :, 1]
    new_lead = lead * cosine_table - trail * sine_table
    new_trail = lead * sine_table + trail * cosine_table
    return jnp.stack([new_lead, new_trail], axis=3).reshape(vectors.shape)


def silu_grad(v):
    sigmoid = jax.nn.sigmoid(v)
    return sigmoid * (1.0 + v * (1.0 - sigmoid))


def take_bit(arr, axis, bit):
    return lax.dynamic_index_in_dim(arr, bit, axis=axis, keepdims=False)


def reduce_rows(grad, n_dp, n_mod):
    n_dev = n_dp * n_mod
    bits = n_dp.bit_length() - 1
    position = lax.axis_index("dp")
    arr = grad.reshape((2,) * bits + (n_mod, grad.shape[0] // n_dev, grad.shape[1]))
    order = [0] + ["mod"] + list(range(1, bits))
    axes = list(range(bits - 1, -1, -1)) + ["mod"]
    for step in order:
        axis = axes.index(step)
        if step == "mod":
            mine = lax.axis_index("mod")
            name, pairs = "mod", [(i, i ^ 1) for i in range(n_mod)]
        else:
            mine = lax.shift_right_logical(position, step) & 1
            name, pairs = "dp", [(i, i ^ (1 << step)) for i in range(n_dp)]
        sent = take_bit(arr, axis, 1 - mine).astype(jnp.bfloat16)
        kept = take_bit(arr, axis, mine)
        got = lax.ppermute(sent, name, pairs)
        arr = kept + got.astype(jnp.float32)
        axes.pop(axis)
    return arr


def body(
    n_dp,
    n_mod,
    tokens,
    cond,
    segments,
    coords,
    w_ada,
    w_qkv,
    q_gain,
    k_gain,
    w_out,
    w_gate,
    w_up,
    w_down,
    cotangent,
):
    rows_here, row_len, width = tokens.shape
    slots = cond.shape[1]
    token_count = rows_here * row_len
    half_channels = w_ada.shape[1]
    score_scale = HD ** (-0.5)
    query_block = min(512, row_len)
    block_count = row_len // query_block
    cond_both = lax.all_gather(cond, "mod", axis=0, tiled=True)
    activated = jax.nn.silu(cond_both).astype(jnp.bfloat16).reshape(-1, width)
    mod_half = jnp.dot(activated, w_ada, preferred_element_type=jnp.float32).astype(jnp.bfloat16)
    mod_half = mod_half.reshape(cond_both.shape[0], slots, half_channels)
    modulation = lax.all_to_all(mod_half, "mod", split_axis=0, concat_axis=2, tiled=True)
    slot_onehot = (segments[:, :, None] == jnp.arange(slots)[None, None, :]).astype(jnp.float32)
    per_token = jnp.einsum(
        "rts,rsc->rtc", slot_onehot, modulation.astype(jnp.float32), precision=lax.Precision.HIGHEST
    )
    per_token = per_token.reshape(token_count, 6 * width)
    shift_attn, scale_attn, gate_attn, shift_ffn, scale_ffn, gate_ffn = jnp.split(
        per_token, 6, axis=1
    )
    stream = tokens.reshape(token_count, width).astype(jnp.float32)
    mod_attn, pull_attn_norm = jax.vjp(modulate, stream, shift_attn, scale_attn)
    mod_attn_low = mod_attn.astype(jnp.bfloat16)
    projected = jnp.dot(mod_attn_low, w_qkv, preferred_element_type=jnp.float32)
    cosine_table, sine_table = rope_angles(jnp.transpose(coords, (1, 0, 2)).reshape(2, token_count))

    def prepare(query_raw, key_raw, query_gain, key_gain):
        queries = rotate(
            rms_norm(query_raw.reshape(token_count, HEADS, HD), query_gain),
            cosine_table,
            sine_table,
        )
        key_vectors = rotate(
            rms_norm(key_raw.reshape(token_count, HEADS, HD), key_gain), cosine_table, sine_table
        )
        return (queries, key_vectors)

    (queries, key_vectors), pull_prepare = jax.vjp(
        prepare, projected[:, :width], projected[:, width : 2 * width], q_gain, k_gain
    )
    query_low = queries.astype(jnp.bfloat16)
    key_low = key_vectors.astype(jnp.bfloat16)
    value_low = projected[:, 2 * width :].astype(jnp.bfloat16).reshape(token_count, HEADS, HD)

    def block_scores(row_index, block_index):
        start_row = row_index * row_len + block_index * query_block
        query_part = query_low[start_row : start_row + query_block]
        seg_row = segments[row_index]
        seg_part = seg_row[block_index * query_block : (block_index + 1) * query_block]
        scores = (
            jnp.einsum("qhd,khd->hqk", query_part, key_low, preferred_element_type=jnp.float32)
            * score_scale
        )
        allowed = (seg_part[:, None] == seg_row[None, :])[None]
        return jnp.where(allowed, scores, MASKED)

    attended_parts = []
    log_totals = []
    row_index = 0
    for block_index in range(block_count):
        scores = block_scores(row_index, block_index)
        row_peak = jnp.max(scores, axis=-1, keepdims=True)
        exp_total = jnp.sum(jnp.exp(scores - row_peak), axis=-1, keepdims=True)
        log_total = row_peak + jnp.log(exp_total)
        probs_low = jnp.exp(scores - log_total).astype(jnp.bfloat16)
        attended_parts.append(
            jnp.einsum("hqk,khd->qhd", probs_low, value_low, preferred_element_type=jnp.float32)
        )
        log_totals.append(log_total)
    attended = (
        jnp.concatenate(attended_parts, axis=0).reshape(token_count, width).astype(jnp.bfloat16)
    )
    attn = jnp.dot(attended, w_out, preferred_element_type=jnp.float32)
    mid = stream + gate_attn * attn
    mod_ffn, pull_ffn_norm = jax.vjp(modulate, mid, shift_ffn, scale_ffn)
    mod_ffn_low = mod_ffn.astype(jnp.bfloat16)
    gate_h = jnp.dot(mod_ffn_low, w_gate, preferred_element_type=jnp.float32)
    up_h = jnp.dot(mod_ffn_low, w_up, preferred_element_type=jnp.float32)
    hidden = (jax.nn.silu(gate_h) * up_h).astype(jnp.bfloat16)
    ffn = jnp.dot(hidden, w_down, preferred_element_type=jnp.float32)
    output = (mid + gate_ffn * ffn).astype(jnp.bfloat16).reshape(rows_here, row_len, width)
    incoming = cotangent.reshape(token_count, width).astype(jnp.float32)
    grad_gate_ffn = incoming * ffn
    grad_ffn = (incoming * gate_ffn).astype(jnp.bfloat16)
    grad_w_down = jnp.einsum("nf,nd->fd", hidden, grad_ffn, preferred_element_type=jnp.float32)
    grad_hidden = jnp.einsum("nd,fd->nf", grad_ffn, w_down, preferred_element_type=jnp.float32)
    grad_gate_h = (grad_hidden * up_h * silu_grad(gate_h)).astype(jnp.bfloat16)
    grad_up_h = (grad_hidden * jax.nn.silu(gate_h)).astype(jnp.bfloat16)
    grad_w_gate = jnp.einsum(
        "nd,nf->df", mod_ffn_low, grad_gate_h, preferred_element_type=jnp.float32
    )
    grad_w_up = jnp.einsum("nd,nf->df", mod_ffn_low, grad_up_h, preferred_element_type=jnp.float32)
    grad_mod_ffn = jnp.einsum("nf,df->nd", grad_gate_h, w_gate, preferred_element_type=jnp.float32)
    grad_mod_ffn = grad_mod_ffn + jnp.einsum(
        "nf,df->nd", grad_up_h, w_up, preferred_element_type=jnp.float32
    )
    grad_mid_part, grad_shift_ffn, grad_scale_ffn = pull_ffn_norm(grad_mod_ffn)
    grad_mid = incoming + grad_mid_part
    grad_gate_attn = grad_mid * attn
    grad_attn = (grad_mid * gate_attn).astype(jnp.bfloat16)
    grad_w_out = jnp.einsum("nc,nd->cd", attended, grad_attn, preferred_element_type=jnp.float32)
    grad_attended = jnp.einsum("nd,cd->nc", grad_attn, w_out, preferred_element_type=jnp.float32)
    grad_attended = grad_attended.astype(jnp.bfloat16).reshape(token_count, HEADS, HD)
    grad_query_parts = []
    row_index = 0
    grad_key_row = jnp.zeros((row_len, HEADS, HD), jnp.float32)
    grad_value_row = jnp.zeros((row_len, HEADS, HD), jnp.float32)
    for block_index in range(block_count):
        start_row = row_index * row_len + block_index * query_block
        query_part = query_low[start_row : start_row + query_block]
        grad_out_part = grad_attended[start_row : start_row + query_block]
        scores = block_scores(row_index, block_index)
        attn_probs = jnp.exp(scores - log_totals[row_index * block_count + block_index])
        probs_low = attn_probs.astype(jnp.bfloat16)
        grad_value_row = grad_value_row + jnp.einsum(
            "hqk,qhd->khd", probs_low, grad_out_part, preferred_element_type=jnp.float32
        )
        grad_probs = jnp.einsum(
            "qhd,khd->hqk", grad_out_part, value_low, preferred_element_type=jnp.float32
        )
        dot_term = jnp.sum(attn_probs * grad_probs, axis=-1, keepdims=True)
        grad_scores = (attn_probs * (grad_probs - dot_term)).astype(jnp.bfloat16)
        grad_query_parts.append(
            jnp.einsum("hqk,khd->qhd", grad_scores, key_low, preferred_element_type=jnp.float32)
            * score_scale
        )
        grad_key_row = (
            grad_key_row
            + jnp.einsum(
                "hqk,qhd->khd", grad_scores, query_part, preferred_element_type=jnp.float32
            )
            * score_scale
        )
    grad_queries = jnp.concatenate(grad_query_parts, axis=0)
    grad_values = grad_value_row.reshape(token_count, width)
    grad_query_raw, grad_key_raw, grad_q_gain, grad_k_gain = pull_prepare(
        (grad_queries, grad_key_row)
    )
    grad_projected = jnp.concatenate([grad_query_raw, grad_key_raw, grad_values], axis=1).astype(
        jnp.bfloat16
    )
    grad_w_qkv = jnp.einsum(
        "nd,ne->de", mod_attn_low, grad_projected, preferred_element_type=jnp.float32
    )
    grad_mod_attn = jnp.einsum(
        "ne,de->nd", grad_projected, w_qkv, preferred_element_type=jnp.float32
    )
    grad_stream, grad_shift_attn, grad_scale_attn = pull_attn_norm(grad_mod_attn)
    grad_tokens = (grad_mid + grad_stream).astype(jnp.bfloat16).reshape(rows_here, row_len, width)
    grad_per_token = jnp.concatenate(
        [
            grad_shift_attn,
            grad_scale_attn,
            grad_gate_attn,
            grad_shift_ffn,
            grad_scale_ffn,
            grad_gate_ffn,
        ],
        axis=1,
    )
    grad_per_token = grad_per_token.reshape(rows_here, row_len, 6 * width)
    grad_modulation = jnp.einsum(
        "rts,rtc->rsc", slot_onehot, grad_per_token, precision=lax.Precision.HIGHEST
    ).astype(jnp.bfloat16)
    grad_mod_half = lax.all_to_all(grad_modulation, "mod", split_axis=2, concat_axis=0, tiled=True)
    grad_mod_flat = grad_mod_half.reshape(-1, half_channels)
    all_activated = lax.all_gather(activated, "dp", axis=0, tiled=True)
    rows_ada = width // n_dp
    own_activated = lax.dynamic_slice_in_dim(
        all_activated, lax.axis_index("dp") * rows_ada, rows_ada, axis=1
    )
    all_grad_mod = lax.all_gather(grad_mod_flat, "dp", axis=0, tiled=True)
    grad_w_ada = jnp.einsum(
        "nd,nc->dc", own_activated, all_grad_mod, preferred_element_type=jnp.float32
    )
    grad_activated = jnp.einsum(
        "nc,dc->nd", grad_mod_flat, w_ada, preferred_element_type=jnp.float32
    )
    grad_activated = grad_activated.reshape(cond_both.shape[0], slots, width)
    grad_own = lax.psum_scatter(
        grad_activated.astype(jnp.bfloat16), "mod", scatter_dimension=0, tiled=True
    ).astype(jnp.float32)
    grad_cond = grad_own * silu_grad(cond)
    summed_q_gain, summed_k_gain = lax.psum((grad_q_gain, grad_k_gain), ("dp", "mod"))
    summed_qkv, summed_out, summed_gate, summed_up, summed_down = (
        reduce_rows(grad_w_qkv, n_dp, n_mod),
        reduce_rows(grad_w_out, n_dp, n_mod),
        reduce_rows(grad_w_gate, n_dp, n_mod),
        reduce_rows(grad_w_up, n_dp, n_mod),
        reduce_rows(grad_w_down, n_dp, n_mod),
    )
    return (
        output,
        grad_tokens,
        grad_cond,
        grad_w_ada,
        summed_qkv,
        summed_q_gain,
        summed_k_gain,
        summed_out,
        summed_gate,
        summed_up,
        summed_down,
    )


def solution(mesh):
    in_specs = (
        P(("dp", "mod"), None, None),
        P(("dp", "mod"), None, None),
        P(("dp", "mod"), None),
        P(("dp", "mod"), None, None),
        P(None, "mod"),
        P(),
        P(),
        P(),
        P(),
        P(),
        P(),
        P(),
        P(("dp", "mod"), None, None),
    )
    out_specs = (
        P(("dp", "mod"), None, None),
        P(("dp", "mod"), None, None),
        P(("dp", "mod"), None, None),
        P("dp", "mod"),
        P(("dp", "mod"), None),
        P(),
        P(),
        P(("dp", "mod"), None),
        P(("dp", "mod"), None),
        P(("dp", "mod"), None),
        P(("dp", "mod"), None),
    )
    return jax.shard_map(
        functools.partial(body, mesh.shape['dp'], mesh.shape['mod']), mesh=mesh, in_specs=in_specs, out_specs=out_specs, check_vma=False)
```

```python
import functools

import jax
import jax.numpy as jnp
import numpy as np
from jax import lax
from jax.experimental import pallas as pl
from jax.experimental.pallas import tpu as pltpu
from jax.sharding import PartitionSpec as P

HEADS = 16
HD = 72
GRID = 32
EPS = 1e-06
ROPE_BASE = 10000.0
TB = 256
WIN = 256
SCORE_SCALE = float(HD**-0.5)
SCORE_LOG2 = float(np.log2(np.e) * HD**-0.5)
VMEM = 60 * 2**20
f32 = jnp.float32
bf16 = jnp.bfloat16


def nn(a, b):
    return lax.dot_general(a, b, (((1,), (0,)), ((), ())), preferred_element_type=f32)


def nt(a, b):
    return lax.dot_general(a, b, (((1,), (1,)), ((), ())), preferred_element_type=f32)


def tn(a, b):
    return lax.dot_general(a, b, (((0,), (0,)), ((), ())), preferred_element_type=f32)


def split3(v):
    hi = v.astype(bf16).astype(f32)
    mid = (v - hi).astype(bf16).astype(f32)
    return hi, mid, v - hi - mid


def np_split3(v):
    v = v.astype(np.float32)
    hi = v.astype(jnp.bfloat16).astype(np.float32)
    mid = (v - hi).astype(jnp.bfloat16).astype(np.float32)
    return [part.astype(jnp.bfloat16) for part in (hi, mid, v - hi - mid)]


@functools.lru_cache(None)
def rope_tables(width):
    quarter = HD // 4
    freqs = ROPE_BASE ** (-np.arange(quarter, dtype=np.float64) / quarter)
    lane = np.arange(width) % HD
    group = lane // quarter
    angle = np.arange(GRID)[:, None] * freqs[lane % quarter][None, :]
    cosine, sine = np.cos(angle), np.sin(angle)
    sine = np.where((group % 2 == 0)[None, :], -sine, sine)
    uses_col = (group >= 2)[None, :]
    tables = []
    for table in (cosine, sine):
        whole = np.concatenate(
            [np.where(uses_col, 0.0, table), np.where(uses_col, table, 0.0)], axis=0
        )
        tables.append(np.concatenate(np_split3(whole), axis=0))
    return tables


@functools.lru_cache(None)
def head_tables(width):
    head = np.arange(width) // HD
    gather = np.zeros((width, 128), np.float32)
    for copy in range(3):
        gather[np.arange(width), copy * HEADS + head] = 1.0
    return gather.astype(jnp.bfloat16), gather.T.astype(jnp.bfloat16)


def unit_of(index, n_mod):
    mod = index % n_mod
    dp = index // n_mod
    return (dp % 2) * 2 * n_mod + mod * 2 + (dp // 2) % 2, dp // 4


@functools.lru_cache(None)
def unit_permutation(width, n_dp, n_mod):
    rows = width // (n_dp * n_mod)
    matrix = np.zeros((width, width), np.float32)
    for index in range(n_dp * n_mod):
        unit, rest = unit_of(index, n_mod)
        start = unit * (width // 8) + rest * rows
        matrix[start + np.arange(rows), index * rows + np.arange(rows)] = 1.0
    return matrix.astype(jnp.bfloat16)


def normed(v):
    centred = v - jnp.mean(v, axis=-1, keepdims=True)
    inverse = lax.rsqrt(jnp.mean(centred * centred, axis=-1, keepdims=True) + EPS)
    return centred * inverse, inverse


def norm_back(grad, scale_part, norm, inverse):
    e = grad * (1.0 + scale_part)
    return inverse * (
        e - jnp.mean(e, axis=-1, keepdims=True) - norm * jnp.mean(e * norm, axis=-1, keepdims=True)
    )


def part(mod_ref, slot, index, width):
    return mod_ref[pl.ds(slot, 1), index * width : (index + 1) * width]


def angles(coords_ref, cos_ref, sin_ref):
    value = lax.broadcasted_iota(jnp.int32, (GRID, 1), 0)
    hot = [(value == coords_ref[i : i + 1, :]).astype(f32) for i in range(2)]
    hot = jnp.concatenate(hot * 3, axis=0).astype(bf16)
    return tn(hot, cos_ref[...]), tn(hot, sin_ref[...])


def partner(v):
    width = v.shape[1]
    quarter = HD // 4
    lane = lax.broadcasted_iota(jnp.int32, (1, width), 1)
    leads = (lane // quarter) % 2 == 0
    return jnp.where(leads, pltpu.roll(v, width - quarter, 1), pltpu.roll(v, quarter, 1))


def head_sum(v, gather_ref):
    hi = v.astype(bf16)
    low = (v - hi.astype(f32)).astype(bf16)
    return nn(hi, gather_ref[...]) + nn(low, gather_ref[...])


def head_spread(v, spread_ref):
    hi, mid, low = split3(v)
    lane = lax.broadcasted_iota(jnp.int32, (1, 128), 1)
    chosen = jnp.where(lane < HEADS, hi, jnp.where(lane < 2 * HEADS, mid, low))
    return nn(chosen.astype(bf16), spread_ref[...])


def window(head, width):
    start = jnp.minimum((head * HD) // 128, width // 128 - WIN // 128) * 128
    return pl.multiple_of(start, 128), head * HD - start


def head_lanes(offset):
    lane = lax.broadcasted_iota(jnp.int32, (1, WIN), 1)
    return (lane >= offset) & (lane < offset + HD)


def project_kernel(
    slots, x_ref, mod_ref, w_ref, coords_ref, cos_ref, sin_ref, gain_ref, gather_ref, spread_ref,
    perm_ref, units_ref, raw_ref, inv_ref, q_ref, k_ref, v_ref, kt_ref,
):
    width = x_ref.shape[1]
    slot = slots[pl.program_id(0)]
    norm, _ = normed(x_ref[...].astype(f32))
    low = (norm * (1.0 + part(mod_ref, slot, 1, width)) + part(mod_ref, slot, 0, width)).astype(bf16)
    units_ref[...] = nt(perm_ref[...], low).astype(bf16).reshape(units_ref.shape)
    cosine, sine = angles(coords_ref, cos_ref, sin_ref)
    for index, out_ref in enumerate((q_ref, k_ref)):
        raw = nn(low, w_ref[:, index * width : (index + 1) * width])
        raw_ref[:, index * width : (index + 1) * width] = raw
        inverse = lax.rsqrt(head_sum(raw * raw, gather_ref) * (1.0 / HD) + EPS)
        inv_ref[:, index * 128 : (index + 1) * 128] = inverse
        scaled = raw * head_spread(inverse, spread_ref) * gain_ref[index : index + 1, :]
        turned = scaled * cosine + partner(scaled) * sine
        out_ref[...] = turned.astype(bf16)
        if index == 1:
            kt_ref[...] = turned.T.astype(bf16)
    v_ref[...] = nn(low, w_ref[:, 2 * width :]).astype(bf16)


def attend_kernel(
    slots, x_ref, cot_ref, mod_ref, q_ref, k_ref, v_ref, w_out_ref, perm_ref,
    o_ref, lse_ref, attn_ref, mid_ref, low_ref, gf_ref, att_units_ref, ffn_units_ref, lse_acc,
):
    block = pl.program_id(0)
    width = x_ref.shape[1]
    tokens = k_ref.shape[0]
    lane128 = lax.broadcasted_iota(jnp.int32, (1, 128), 1)
    lane = lax.broadcasted_iota(jnp.int32, (1, WIN), 1)
    o_ref[...] = jnp.zeros_like(o_ref)
    lse_acc[...] = jnp.zeros_like(lse_acc)

    def run(rows):
        def head(h, carry):
            start, offset = window(h, width)
            inside = head_lanes(offset)
            columns = pl.ds(start, WIN)
            query = jnp.where(inside, q_ref[:, columns], 0)
            value = jnp.where(inside, v_ref[rows, columns], 1)
            weight = jnp.exp2(nt(query, k_ref[rows, columns]) * SCORE_LOG2).astype(bf16)
            summed = nn(weight, value)
            free = jnp.where(offset > 0, 0, WIN - 1)
            total = jnp.sum(jnp.where(lane == free, summed, 0.0), axis=1, keepdims=True)
            o_ref[:, columns] += jnp.where(inside, summed * (1.0 / total), 0.0)
            lse_acc[...] += jnp.where(lane128 == h, jnp.log2(total), 0.0)
            return carry

        lax.fori_loop(0, HEADS, head, 0, unroll=2)

    whole = slots[tokens // TB - 1] == slots[0]

    @pl.when(whole)
    def _():
        run(slice(None))

    @pl.when(jnp.logical_not(whole))
    def _():
        run(pl.ds(pl.multiple_of(block * TB, TB), TB))

    lse_ref[...] = lse_acc[...].T
    slot = slots[block]
    attended = o_ref[...].astype(bf16)
    att_units_ref[...] = nt(perm_ref[...], attended).astype(bf16).reshape(att_units_ref.shape)
    attn = nn(attended, w_out_ref[...])
    attn_ref[...] = attn
    mid = x_ref[...].astype(f32) + part(mod_ref, slot, 2, width) * attn
    mid_ref[...] = mid
    norm, _ = normed(mid)
    low = (norm * (1.0 + part(mod_ref, slot, 4, width)) + part(mod_ref, slot, 3, width)).astype(bf16)
    low_ref[...] = low
    ffn_units_ref[...] = nt(perm_ref[...], low).astype(bf16).reshape(ffn_units_ref.shape)
    gf_ref[...] = (cot_ref[...].astype(f32) * part(mod_ref, slot, 5, width)).astype(bf16)


def ffn_kernel(
    x_ref, gf_ref, wg_ref, wu_ref, wd_ref, units_ref, dg_ref, du_ref, ffn_ref, dmod_ref, *, n_mod
):
    first = pl.program_id(0) == 0
    gate = nn(x_ref[...], wg_ref[...])
    up = nn(x_ref[...], wu_ref[...])
    grad_hidden = nt(gf_ref[...], wd_ref[...])
    sigmoid = 1.0 / (1.0 + jnp.exp(-gate))
    silu = gate * sigmoid
    hidden = silu * up
    rows = units_ref.shape[3]
    turned = hidden.T.astype(bf16)
    for index in range(turned.shape[0] // rows):
        unit, rest = unit_of(index, n_mod)
        nxt = unit % 2 if units_ref.shape[1] == 2 else 0
        units_ref[unit // 2, nxt, rest if units_ref.shape[1] == 2 else 0] = turned[
            index * rows : (index + 1) * rows
        ]
    dg = (grad_hidden * up * (sigmoid * (1.0 + gate * (1.0 - sigmoid)))).astype(bf16)
    du = (grad_hidden * silu).astype(bf16)
    dg_ref[...] = dg
    du_ref[...] = du

    @pl.when(first)
    def _():
        ffn_ref[...] = jnp.zeros_like(ffn_ref)
        dmod_ref[...] = jnp.zeros_like(dmod_ref)

    ffn_ref[...] += nn(hidden.astype(bf16), wd_ref[...])
    dmod_ref[...] += nt(dg, wg_ref[...]) + nt(du, wu_ref[...])


def middle_kernel(
    slots, mid_ref, ffn_ref, dmod_ref, cot_ref, attn_ref, o_ref, mod_ref, w_out_ref, gather_ref,
    out_ref, grad_mid_ref, ga_ref, do_ref, dot_ref, sums_ref,
):
    width = mid_ref.shape[1]
    slot = slots[pl.program_id(0)]
    incoming = cot_ref[...].astype(f32)
    mid = mid_ref[...]
    out_ref[...] = (mid + part(mod_ref, slot, 5, width) * ffn_ref[...]).astype(bf16)
    norm, inverse = normed(mid)
    dmod = dmod_ref[...]
    grad_mid = incoming + norm_back(dmod, part(mod_ref, slot, 4, width), norm, inverse)
    grad_mid_ref[...] = grad_mid
    ga = (grad_mid * part(mod_ref, slot, 2, width)).astype(bf16)
    ga_ref[...] = ga
    do = nt(ga, w_out_ref[...]).astype(bf16)
    do_ref[...] = do
    dot_ref[...] = head_sum(do.astype(f32) * o_ref[...], gather_ref).T
    sums_ref[0, 0:1, :] = jnp.sum(grad_mid * attn_ref[...], axis=0, keepdims=True)
    sums_ref[0, 1:2, :] = jnp.sum(dmod, axis=0, keepdims=True)
    sums_ref[0, 2:3, :] = jnp.sum(dmod * norm, axis=0, keepdims=True)
    sums_ref[0, 3:4, :] = jnp.sum(incoming * ffn_ref[...], axis=0, keepdims=True)


def attend_back_kernel(
    slots, q_ref, k_ref, v_ref, do_ref, lse_ref, dot_ref, kt_ref, dqt_ref, dk_ref, dv_ref
):
    h = pl.program_id(0)
    tokens, width = q_ref.shape

    @pl.when(h == 0)
    def _():
        dqt_ref[...] = jnp.zeros_like(dqt_ref)
        dk_ref[...] = jnp.zeros_like(dk_ref)
        dv_ref[...] = jnp.zeros_like(dv_ref)

    start, offset = window(h, width)
    inside = head_lanes(offset)
    columns = pl.ds(start, WIN)
    first_row = pl.multiple_of((h * HD) // 16 * 16, 16)
    row = lax.broadcasted_iota(jnp.int32, (HD + 8, 1), 0) + first_row
    own_rows = (row >= h * HD) & (row < h * HD + HD)

    def step(rows):
        query = q_ref[rows, columns]
        grad_out = do_ref[rows, columns]
        key = jnp.where(inside, k_ref[rows, columns], 0)
        value = jnp.where(inside, v_ref[rows, columns], 0)
        probs = jnp.exp2(nt(key, query) * SCORE_LOG2 - lse_ref[pl.ds(h, 1), rows])
        scores = (probs * (nt(value, grad_out) - dot_ref[pl.ds(h, 1), rows])).astype(bf16)
        dv_ref[rows, columns] += jnp.where(inside, nn(probs.astype(bf16), grad_out), 0.0)
        dk_ref[rows, columns] += jnp.where(inside, nn(scores, query) * SCORE_SCALE, 0.0)
        turned = nn(kt_ref[pl.ds(first_row, HD + 8), rows], scores) * SCORE_SCALE
        dqt_ref[pl.ds(first_row, HD + 8), rows] += jnp.where(own_rows, turned, 0.0)

    whole = slots[tokens // TB - 1] == slots[0]

    @pl.when(whole)
    def _():
        step(slice(None))

    @pl.when(jnp.logical_not(whole))
    def _():
        def block(i, carry):
            step(pl.ds(pl.multiple_of(i * TB, TB), TB))
            return carry

        lax.fori_loop(0, tokens // TB, block, 0)


def project_back_kernel(
    slots, dqt_ref, dk_ref, dv_ref, raw_ref, inv_ref, q_ref, k_ref, x_ref, grad_mid_ref, mod_ref,
    w_ref, coords_ref, cos_ref, sin_ref, gain_ref, gather_ref, spread_ref,
    gp_ref, grad_x_ref, sums_ref, gains_ref,
):
    width = x_ref.shape[1]
    slot = slots[pl.program_id(0)]

    @pl.when(pl.program_id(0) == 0)
    def _():
        gains_ref[...] = jnp.zeros_like(gains_ref)

    cosine, sine = angles(coords_ref, cos_ref, sin_ref)
    for index, low_ref in enumerate((q_ref, k_ref)):
        grad = dqt_ref[...].T if index == 0 else dk_ref[...]
        raw = raw_ref[:, index * width : (index + 1) * width]
        inverse = head_spread(inv_ref[:, index * 128 : (index + 1) * 128], spread_ref)
        mean = head_sum(grad * low_ref[...].astype(f32), gather_ref) * (1.0 / HD)
        norm = raw * inverse
        back = grad * cosine - partner(grad) * sine
        gains_ref[index : index + 1, :] += jnp.sum(back * norm, axis=0, keepdims=True)
        gp_ref[:, index * width : (index + 1) * width] = (
            inverse * (back * gain_ref[index : index + 1, :] - norm * head_spread(mean, spread_ref))
        ).astype(bf16)
    gp_ref[:, 2 * width :] = dv_ref[...].astype(bf16)
    dmod = nt(gp_ref[...], w_ref[...])
    norm, inverse = normed(x_ref[...].astype(f32))
    grad_x = grad_mid_ref[...] + norm_back(dmod, part(mod_ref, slot, 1, width), norm, inverse)
    grad_x_ref[...] = grad_x.astype(bf16)
    sums_ref[0, 0:1, :] = jnp.sum(dmod, axis=0, keepdims=True)
    sums_ref[0, 1:2, :] = jnp.sum(dmod * norm, axis=0, keepdims=True)


def send_kernel(where, units_ref, rhs_ref, out_ref):
    units, rows, _ = units_ref.shape
    result = nn(units_ref[...].reshape(units * rows, -1), rhs_ref[...])
    out_ref[...] = result.astype(bf16).reshape(out_ref.shape)


def keep_kernel(where, units_ref, rhs_ref, got_ref, send_ref, keep_ref, scratch):
    units, rows, _ = units_ref.shape
    result = nn(units_ref[...].reshape(units * rows, -1), rhs_ref[...])
    scratch[...] = result.reshape(scratch.shape)
    for i in range(units // 2):
        away, own = where[2 + i], where[4 + i]
        send_ref[i] = (scratch[away] + got_ref[away].astype(f32)).astype(bf16)
        keep_ref[i] = scratch[own] + got_ref[own].astype(f32)


def fold_kernel(where, keep_ref, got_ref, send_ref, own_ref):
    away, own = where[0], where[1]
    send_ref[...] = (keep_ref[away] + got_ref[away].astype(f32)).astype(bf16)
    own_ref[...] = keep_ref[own] + got_ref[own].astype(f32)


def call(kernel, grid, in_specs, out_specs, out_shape, args, scalars=None, scratch=(), cost=None, name=None):
    cost = cost or (0, 0)
    spec = pltpu.PrefetchScalarGridSpec(
        num_scalar_prefetch=0 if scalars is None else 1,
        grid=grid,
        in_specs=in_specs,
        out_specs=out_specs,
        scratch_shapes=scratch,
    )
    return pl.pallas_call(
        kernel,
        grid_spec=spec,
        out_shape=out_shape,
        compiler_params=pltpu.CompilerParams(vmem_limit_bytes=VMEM),
        cost_estimate=pl.CostEstimate(flops=int(cost[0]), bytes_accessed=int(cost[1]), transcendentals=0),
        name=name,
    )(*(() if scalars is None else (scalars,)), *args)


def shape(dims, dtype):
    return jax.ShapeDtypeStruct(dims, dtype)


def fixed(dims):
    return pl.BlockSpec(dims, lambda *_: (0,) * len(dims), pipeline_mode=pl.Buffered(1))


def rows_of(dims, axis=0):
    return pl.BlockSpec(dims, lambda b, *_: tuple(b if i == axis else 0 for i in range(len(dims))))


class Reducer:
    def __init__(self, n_dp, n_mod):
        self.n_dp, self.n_mod = n_dp, n_mod
        position = lax.axis_index("dp")
        self.core = position & 1
        self.nxt = lax.shift_right_logical(position, 1) & 1
        self.mod = lax.axis_index("mod")
        self.position = position

    def swap(self, arr, bit):
        if bit == "mod":
            return lax.ppermute(arr, "mod", [(i, i ^ 1) for i in range(self.n_mod)])
        return lax.ppermute(arr, "dp", [(i, i ^ (1 << bit)) for i in range(self.n_dp)])

    def start(self, units, rhs, name):
        _, rows, tokens = units.shape
        columns = rhs.shape[1]
        chunk = 384
        half = pl.BlockSpec((4, rows, tokens), lambda j, w: (w[0], 0, 0), pipeline_mode=pl.Buffered(1))
        sent = call(
            send_kernel,
            (columns // chunk,),
            [half, rows_of((tokens, chunk), 1)],
            rows_of((4, rows, chunk), 2),
            shape((4, rows, columns), bf16),
            (units, rhs),
            scalars=jnp.stack([1 - self.core]),
            cost=(8 * rows * tokens * columns, 2 * tokens * (columns + 4 * rows) + 8 * rows * columns),
            name=name + "_send",
        )
        return self.swap(sent, 0)

    def finish(self, units, rhs, got, mod_first, name):
        _, rows, tokens = units.shape
        columns = rhs.shape[1]
        chunk = 384
        if mod_first:
            where = [2 * (1 - self.mod), 2 * (1 - self.mod) + 1, 2 * self.mod, 2 * self.mod + 1]
            second, third, third_bit = "mod", 1, self.nxt
        else:
            where = [1 - self.nxt, 3 - self.nxt, self.nxt, 2 + self.nxt]
            second, third, third_bit = 1, "mod", self.mod
        half = pl.BlockSpec((4, rows, tokens), lambda j, w: (w[0], 0, 0), pipeline_mode=pl.Buffered(1))
        sent, kept = call(
            keep_kernel,
            (columns // chunk,),
            [half, rows_of((tokens, chunk), 1), rows_of((4, rows, chunk), 2)],
            [rows_of((2, rows, chunk), 2), rows_of((2, rows, chunk), 2)],
            [shape((2, rows, columns), bf16), shape((2, rows, columns), f32)],
            (units, rhs, got),
            scalars=jnp.stack([self.core, self.core] + where),
            scratch=[pltpu.VMEM((4, rows, chunk), f32)],
            cost=(8 * rows * tokens * columns, 2 * tokens * (columns + 4 * rows) + 20 * rows * columns),
            name=name + "_keep",
        )
        got = self.swap(sent, second)
        sent, kept = call(
            fold_kernel,
            (columns // chunk,),
            [rows_of((2, rows, chunk), 2), rows_of((2, rows, chunk), 2)],
            [rows_of((rows, chunk), 1), rows_of((rows, chunk), 1)],
            [shape((rows, columns), bf16), shape((rows, columns), f32)],
            (kept, got),
            scalars=jnp.stack([1 - third_bit, third_bit]),
            cost=(0, 18 * rows * columns),
            name=name + "_fold",
        )
        total = kept + self.swap(sent, third).astype(f32)
        bits = self.n_dp.bit_length() - 1
        total = total.reshape((2,) * (bits - 2) + (rows * 4 // self.n_dp, columns))
        for bit in range(2, bits):
            axis = bits - 1 - bit
            mine = lax.shift_right_logical(self.position, bit) & 1
            away = lax.dynamic_index_in_dim(total, 1 - mine, axis=axis, keepdims=False)
            own = lax.dynamic_index_in_dim(total, mine, axis=axis, keepdims=False)
            total = own + self.swap(away.astype(bf16), bit).astype(f32)
        return total


def silu_grad(v):
    sigmoid = jax.nn.sigmoid(v)
    return sigmoid * (1.0 + v * (1.0 - sigmoid))


def pair_order(own, other, mod):
    return jnp.where(mod == 0, jnp.stack([own, other]), jnp.stack([other, own]))


def body(
    n_dp, n_mod, tokens, cond, segments, coords, w_ada, w_qkv, q_gain, k_gain, w_out, w_gate, w_up,
    w_down, cotangent,
):
    _, count, width = tokens.shape
    slots_n = cond.shape[1]
    half = w_ada.shape[1]
    ff = w_gate.shape[1]
    blocks = count // TB
    n_dev = n_dp * n_mod
    reducer = Reducer(n_dp, n_mod)
    mod_index = lax.axis_index("mod")
    x = tokens[0]
    cot = cotangent[0]
    slots = segments[0, ::TB]
    coord = coords[0]
    cos_table, sin_table = (jnp.asarray(t) for t in rope_tables(width))
    gather, spread = (jnp.asarray(t) for t in head_tables(width))
    perm = jnp.asarray(unit_permutation(width, n_dp, n_mod))
    gains = jnp.stack([jnp.tile(q_gain, HEADS), jnp.tile(k_gain, HEADS)])

    cond_both = pair_order(cond[0], reducer.swap(cond[0], "mod"), mod_index)
    activated = jax.nn.silu(cond_both).astype(bf16).reshape(-1, width)
    mod_half = jnp.dot(activated, w_ada, preferred_element_type=f32).astype(bf16)
    mod_half = mod_half.reshape(n_mod, slots_n, half)
    own_half = lax.dynamic_index_in_dim(mod_half, mod_index, 0, keepdims=False)
    other_half = lax.dynamic_index_in_dim(mod_half, 1 - mod_index, 0, keepdims=False)
    pair = pair_order(own_half, reducer.swap(other_half, "mod"), mod_index)
    modulation = jnp.concatenate([pair[0], pair[1]], axis=1).astype(f32)

    token_f32 = shape((count, width), f32)
    token_bf16 = shape((count, width), bf16)
    units = shape((8, width // 8, count), bf16)
    units_spec = rows_of((8, width // 8, TB), 2)
    token_spec = rows_of((TB, width))
    mod_spec = fixed((slots_n, 6 * width))
    square = fixed((width, width))
    table_specs = [fixed(cos_table.shape), fixed(sin_table.shape), fixed((2, width)), fixed(gather.shape), fixed(spread.shape)]
    tables = (cos_table, sin_table, gains, gather, spread)
    lane_rows = shape((128, count), f32)
    macs = count * width * width

    attn_units, raw, inverse, query, key, value, key_t = call(
        project_kernel,
        (blocks,),
        [token_spec, mod_spec, fixed((width, 3 * width)), rows_of((2, TB), 1)] + table_specs + [square],
        [units_spec, rows_of((TB, 2 * width)), rows_of((TB, 256))] + [token_spec] * 3 + [rows_of((width, TB), 1)],
        [units, shape((count, 2 * width), f32), shape((count, 256), f32)] + [token_bf16] * 3
        + [shape((width, count), bf16)],
        (x, modulation, w_qkv, coord) + tables + (perm,),
        scalars=slots,
        cost=(2 * 5 * macs, 40e6),
        name="project",
    )
    attended, lse, attn, mid, ffn_in, grad_ffn, out_units, ffn_units = call(
        attend_kernel,
        (blocks,),
        [token_spec, token_spec, mod_spec, token_spec] + [fixed((count, width))] * 2 + [square, square],
        [token_spec, rows_of((128, TB), 1)] + [token_spec] * 4 + [units_spec] * 2,
        [token_f32, lane_rows, token_f32, token_f32, token_bf16, token_bf16, units, units],
        (x, cot, modulation, query, key, value, w_out, perm),
        scalars=slots,
        scratch=[pltpu.VMEM((TB, 128), f32)],
        cost=(2 * 10 * macs, 40e6),
        name="attend",
    )

    rows_ff = ff // n_dev
    rest = n_dp // 4
    chunk = 384
    group = chunk // rows_ff
    if group >= 8:
        unit_block = pl.BlockSpec((4, 2, group // 8, rows_ff, count), lambda i: (0, 0, i, 0, 0))
    else:
        unit_block = pl.BlockSpec((4, 1, 1, rows_ff, count), lambda i: (0, i % 2, i // 2, 0, 0))
    down_units, grad_gate, grad_up, ffn, grad_mod_ffn = call(
        functools.partial(ffn_kernel, n_mod=n_mod),
        (ff // chunk,),
        [fixed((count, width))] * 2 + [rows_of((width, chunk), 1)] * 2 + [rows_of((chunk, width))],
        [unit_block] + [rows_of((count, chunk), 1)] * 2 + [fixed((count, width))] * 2,
        [shape((4, 2, rest, rows_ff, count), bf16)] + [shape((count, ff), bf16)] * 2 + [token_f32] * 2,
        (ffn_in, grad_ffn, w_gate, w_up, w_down),
        cost=(2 * 6 * count * width * ff, 60e6),
        name="ffn",
    )
    down_units = down_units.reshape(8, rest * rows_ff, count)

    got_gate = reducer.start(ffn_units, grad_gate, "gate")
    got_up = reducer.start(ffn_units, grad_up, "up")
    got_down = reducer.start(down_units, grad_ffn, "down")
    summed_gate = reducer.finish(ffn_units, grad_gate, got_gate, True, "gate")
    summed_up = reducer.finish(ffn_units, grad_up, got_up, False, "up")
    summed_down = reducer.finish(down_units, grad_ffn, got_down, True, "down")

    output, grad_mid, grad_attn, grad_attended, dot_term, sums_b = call(
        middle_kernel,
        (blocks,),
        [token_spec] * 6 + [mod_spec, square, fixed(gather.shape)],
        [token_spec] * 4 + [rows_of((128, TB), 1), rows_of((1, 4, width))],
        [token_bf16, token_f32, token_bf16, token_bf16, lane_rows, shape((blocks, 4, width), f32)],
        (mid, ffn, grad_mod_ffn, cot, attn, attended, modulation, w_out, gather),
        scalars=slots,
        cost=(2 * macs, 40e6),
        name="middle",
    )
    got_out = reducer.start(out_units, grad_attn, "out")
    summed_out = reducer.finish(out_units, grad_attn, got_out, False, "out")

    grad_query_t, grad_key, grad_value = call(
        attend_back_kernel,
        (HEADS,),
        [fixed((count, width))] * 4 + [fixed((128, count))] * 2 + [fixed((width, count))],
        [fixed((width, count))] + [fixed((count, width))] * 2,
        [shape((width, count), f32), token_f32, token_f32],
        (query, key, value, grad_attended, lse, dot_term, key_t),
        scalars=slots,
        cost=(2 * 22 * macs, 40e6),
        name="attend_back",
    )
    grad_projected, grad_tokens, sums_a, gain_sums = call(
        project_back_kernel,
        (blocks,),
        [rows_of((width, TB), 1), token_spec, token_spec, rows_of((TB, 2 * width)), rows_of((TB, 256))]
        + [token_spec] * 4
        + [mod_spec, fixed((width, 3 * width)), rows_of((2, TB), 1)]
        + table_specs,
        [rows_of((TB, 3 * width)), token_spec, rows_of((1, 2, width)), fixed((2, width))],
        [shape((count, 3 * width), bf16), token_bf16, shape((blocks, 2, width), f32), shape((2, width), f32)],
        (grad_query_t, grad_key, grad_value, raw, inverse, query, key, x, grad_mid, modulation, w_qkv, coord)
        + tables,
        scalars=slots,
        cost=(2 * 4 * macs, 50e6),
        name="project_back",
    )
    got_qkv = reducer.start(attn_units, grad_projected, "qkv")
    summed_qkv = reducer.finish(attn_units, grad_projected, got_qkv, True, "qkv")

    sums = jnp.concatenate([sums_a, sums_b], axis=1).reshape(blocks, 6 * width)
    in_slot = slots[None, :, None] == jnp.arange(slots_n)[:, None, None]
    grad_modulation = jnp.sum(jnp.where(in_slot, sums[None], 0.0), axis=1).astype(bf16)
    halves = grad_modulation.reshape(slots_n, n_mod, half)
    own_half = lax.dynamic_index_in_dim(halves, mod_index, 1, keepdims=False)
    other_half = lax.dynamic_index_in_dim(halves, 1 - mod_index, 1, keepdims=False)
    grad_mod_flat = pair_order(own_half, reducer.swap(other_half, "mod"), mod_index).reshape(-1, half)
    all_activated = lax.all_gather(activated, "dp", axis=0, tiled=True)
    rows_ada = width // n_dp
    own_activated = lax.dynamic_slice_in_dim(
        all_activated, lax.axis_index("dp") * rows_ada, rows_ada, axis=1
    )
    all_grad_mod = lax.all_gather(grad_mod_flat, "dp", axis=0, tiled=True)
    grad_w_ada = jnp.einsum("nd,nc->dc", own_activated, all_grad_mod, preferred_element_type=f32)
    grad_activated = jnp.einsum("nc,dc->nd", grad_mod_flat, w_ada, preferred_element_type=f32)
    grad_activated = grad_activated.reshape(n_mod, slots_n, width)
    own_part = lax.dynamic_index_in_dim(grad_activated, mod_index, 0, keepdims=False)
    other_part = lax.dynamic_index_in_dim(grad_activated, 1 - mod_index, 0, keepdims=False)
    grad_own = own_part + reducer.swap(other_part.astype(bf16), "mod").astype(f32)
    grad_cond = grad_own[None] * silu_grad(cond)

    gain_grads = jnp.sum(gain_sums.reshape(2, HEADS, HD), axis=1)
    for bit in [0, "mod"] + list(range(1, n_dp.bit_length() - 1)):
        gain_grads = gain_grads + reducer.swap(gain_grads, bit)
    return (
        output[None],
        grad_tokens[None],
        grad_cond,
        grad_w_ada,
        summed_qkv,
        gain_grads[0],
        gain_grads[1],
        summed_out,
        summed_gate,
        summed_up,
        summed_down,
    )


def solution(mesh):
    rows = ("dp", "mod")
    in_specs = (
        P(rows, None, None),
        P(rows, None, None),
        P(rows, None),
        P(rows, None, None),
        P(None, "mod"),
        P(),
        P(),
        P(),
        P(),
        P(),
        P(),
        P(),
        P(rows, None, None),
    )
    out_specs = (
        P(rows, None, None),
        P(rows, None, None),
        P(rows, None, None),
        P("dp", "mod"),
        P(rows, None),
        P(),
        P(),
        P(rows, None),
        P(rows, None),
        P(rows, None),
        P(rows, None),
    )
    return jax.shard_map(
        functools.partial(body, mesh.shape["dp"], mesh.shape["mod"]),
        mesh=mesh,
        in_specs=in_specs,
        out_specs=out_specs,
        check_vma=False,
    )
```

```python
import functools

import jax
import jax.numpy as jnp
import numpy as np
from jax import lax
from jax.experimental import pallas as pl
from jax.experimental.pallas import tpu as pltpu
from jax.sharding import PartitionSpec as P

HEADS = 16
HD = 72
GRID = 32
EPS = 1e-06
ROPE_BASE = 10000.0
TB = 256
WIN = 256
SCORE_SCALE = float(HD**-0.5)
SCORE_LOG2 = float(np.log2(np.e) * HD**-0.5)
VMEM = 60 * 2**20
f32 = jnp.float32
bf16 = jnp.bfloat16


def nn(a, b):
    return lax.dot_general(a, b, (((1,), (0,)), ((), ())), preferred_element_type=f32)


def nt(a, b):
    return lax.dot_general(a, b, (((1,), (1,)), ((), ())), preferred_element_type=f32)


def tn(a, b):
    return lax.dot_general(a, b, (((0,), (0,)), ((), ())), preferred_element_type=f32)


def split3(v):
    hi = v.astype(bf16).astype(f32)
    mid = (v - hi).astype(bf16).astype(f32)
    return hi, mid, v - hi - mid


def np_split3(v):
    v = v.astype(np.float32)
    hi = v.astype(jnp.bfloat16).astype(np.float32)
    mid = (v - hi).astype(jnp.bfloat16).astype(np.float32)
    return [part.astype(jnp.bfloat16) for part in (hi, mid, v - hi - mid)]


@functools.lru_cache(None)
def rope_tables(width):
    quarter = HD // 4
    freqs = ROPE_BASE ** (-np.arange(quarter, dtype=np.float64) / quarter)
    lane = np.arange(width) % HD
    group = lane // quarter
    angle = np.arange(GRID)[:, None] * freqs[lane % quarter][None, :]
    cosine, sine = np.cos(angle), np.sin(angle)
    sine = np.where((group % 2 == 0)[None, :], -sine, sine)
    uses_col = (group >= 2)[None, :]
    tables = []
    for table in (cosine, sine):
        whole = np.concatenate(
            [np.where(uses_col, 0.0, table), np.where(uses_col, table, 0.0)], axis=0
        )
        tables.append(np.concatenate(np_split3(whole), axis=0))
    return tables


@functools.lru_cache(None)
def head_tables(width):
    head = np.arange(width) // HD
    gather = np.zeros((width, 128), np.float32)
    for copy in range(3):
        gather[np.arange(width), copy * HEADS + head] = 1.0
    return gather.astype(jnp.bfloat16), gather.T.astype(jnp.bfloat16)


def unit_of(index, n_mod):
    mod = index % n_mod
    dp = index // n_mod
    return (dp % 2) * 2 * n_mod + mod * 2 + (dp // 2) % 2, dp // 4


@functools.lru_cache(None)
def unit_permutation(width, n_dp, n_mod):
    rows = width // (n_dp * n_mod)
    matrix = np.zeros((width, width), np.float32)
    for index in range(n_dp * n_mod):
        unit, rest = unit_of(index, n_mod)
        start = unit * (width // 8) + rest * rows
        matrix[start + np.arange(rows), index * rows + np.arange(rows)] = 1.0
    return matrix.astype(jnp.bfloat16)


def normed(v):
    centred = v - jnp.mean(v, axis=-1, keepdims=True)
    inverse = lax.rsqrt(jnp.mean(centred * centred, axis=-1, keepdims=True) + EPS)
    return centred * inverse, inverse


def norm_back(grad, scale_part, norm, inverse):
    e = grad * (1.0 + scale_part)
    return inverse * (
        e - jnp.mean(e, axis=-1, keepdims=True) - norm * jnp.mean(e * norm, axis=-1, keepdims=True)
    )


def part(mod_ref, slot, index, width):
    return mod_ref[pl.ds(slot, 1), index * width : (index + 1) * width]


def angles(coords_ref, cos_ref, sin_ref):
    value = lax.broadcasted_iota(jnp.int32, (GRID, 1), 0)
    hot = [(value == coords_ref[i : i + 1, :]).astype(f32) for i in range(2)]
    hot = jnp.concatenate(hot * 3, axis=0).astype(bf16)
    return tn(hot, cos_ref[...]), tn(hot, sin_ref[...])


def partner(v):
    width = v.shape[1]
    quarter = HD // 4
    lane = lax.broadcasted_iota(jnp.int32, (1, width), 1)
    leads = (lane // quarter) % 2 == 0
    return jnp.where(leads, pltpu.roll(v, width - quarter, 1), pltpu.roll(v, quarter, 1))


def head_sum(v, gather_ref):
    hi = v.astype(bf16)
    low = (v - hi.astype(f32)).astype(bf16)
    return nn(hi, gather_ref[...]) + nn(low, gather_ref[...])


def head_spread(v, spread_ref):
    hi, mid, low = split3(v)
    lane = lax.broadcasted_iota(jnp.int32, (1, 128), 1)
    chosen = jnp.where(lane < HEADS, hi, jnp.where(lane < 2 * HEADS, mid, low))
    return nn(chosen.astype(bf16), spread_ref[...])


def window(head, width):
    start = jnp.minimum((head * HD) // 128, width // 128 - WIN // 128) * 128
    return pl.multiple_of(start, 128), head * HD - start


def head_lanes(offset):
    lane = lax.broadcasted_iota(jnp.int32, (1, WIN), 1)
    return (lane >= offset) & (lane < offset + HD)


def project_kernel(
    slots, x_ref, mod_ref, w_ref, coords_ref, cos_ref, sin_ref, gain_ref, gather_ref, spread_ref,
    perm_ref, units_ref, raw_ref, inv_ref, q_ref, k_ref, v_ref, kt_ref,
):
    width = x_ref.shape[1]
    slot = slots[pl.program_id(0)]
    norm, _ = normed(x_ref[...].astype(f32))
    low = (norm * (1.0 + part(mod_ref, slot, 1, width)) + part(mod_ref, slot, 0, width)).astype(bf16)
    units_ref[...] = nt(perm_ref[...], low).astype(bf16).reshape(units_ref.shape)
    cosine, sine = angles(coords_ref, cos_ref, sin_ref)
    for index, out_ref in enumerate((q_ref, k_ref)):
        raw = nn(low, w_ref[:, index * width : (index + 1) * width])
        raw_ref[:, index * width : (index + 1) * width] = raw
        inverse = lax.rsqrt(head_sum(raw * raw, gather_ref) * (1.0 / HD) + EPS)
        inv_ref[:, index * 128 : (index + 1) * 128] = inverse
        scaled = raw * head_spread(inverse, spread_ref) * gain_ref[index : index + 1, :]
        turned = scaled * cosine + partner(scaled) * sine
        out_ref[...] = turned.astype(bf16)
        if index == 1:
            kt_ref[...] = turned.T.astype(bf16)
    v_ref[...] = nn(low, w_ref[:, 2 * width :]).astype(bf16)


def attend_kernel(
    slots, x_ref, cot_ref, mod_ref, q_ref, k_ref, v_ref, w_out_ref, perm_ref,
    o_ref, lse_ref, attn_ref, mid_ref, low_ref, gf_ref, att_units_ref, ffn_units_ref, lse_acc,
):
    block = pl.program_id(0)
    width = x_ref.shape[1]
    tokens = k_ref.shape[0]
    lane128 = lax.broadcasted_iota(jnp.int32, (1, 128), 1)
    lane = lax.broadcasted_iota(jnp.int32, (1, WIN), 1)
    o_ref[...] = jnp.zeros_like(o_ref)
    lse_acc[...] = jnp.zeros_like(lse_acc)

    def run(rows):
        def head(h, carry):
            start, offset = window(h, width)
            inside = head_lanes(offset)
            columns = pl.ds(start, WIN)
            query = jnp.where(inside, q_ref[:, columns], 0)
            value = jnp.where(inside, v_ref[rows, columns], 1)
            weight = jnp.exp2(nt(query, k_ref[rows, columns]) * SCORE_LOG2).astype(bf16)
            summed = nn(weight, value)
            free = jnp.where(offset > 0, 0, WIN - 1)
            total = jnp.sum(jnp.where(lane == free, summed, 0.0), axis=1, keepdims=True)
            o_ref[:, columns] += jnp.where(inside, summed * (1.0 / total), 0.0)
            lse_acc[...] += jnp.where(lane128 == h, jnp.log2(total), 0.0)
            return carry

        lax.fori_loop(0, HEADS, head, 0, unroll=2)

    whole = slots[tokens // TB - 1] == slots[0]

    @pl.when(whole)
    def _():
        run(slice(None))

    @pl.when(jnp.logical_not(whole))
    def _():
        run(pl.ds(pl.multiple_of(block * TB, TB), TB))

    lse_ref[...] = lse_acc[...].T
    slot = slots[block]
    attended = o_ref[...].astype(bf16)
    att_units_ref[...] = nt(perm_ref[...], attended).astype(bf16).reshape(att_units_ref.shape)
    attn = nn(attended, w_out_ref[...])
    attn_ref[...] = attn
    mid = x_ref[...].astype(f32) + part(mod_ref, slot, 2, width) * attn
    mid_ref[...] = mid
    norm, _ = normed(mid)
    low = (norm * (1.0 + part(mod_ref, slot, 4, width)) + part(mod_ref, slot, 3, width)).astype(bf16)
    low_ref[...] = low
    ffn_units_ref[...] = nt(perm_ref[...], low).astype(bf16).reshape(ffn_units_ref.shape)
    gf_ref[...] = (cot_ref[...].astype(f32) * part(mod_ref, slot, 5, width)).astype(bf16)


def ffn_kernel(
    x_ref, gf_ref, wg_ref, wu_ref, wd_ref, units_ref, dg_ref, du_ref, ffn_ref, dmod_ref, *, n_mod
):
    first = pl.program_id(0) == 0
    gate = nn(x_ref[...], wg_ref[...])
    up = nn(x_ref[...], wu_ref[...])
    grad_hidden = nt(gf_ref[...], wd_ref[...])
    sigmoid = 1.0 / (1.0 + jnp.exp(-gate))
    silu = gate * sigmoid
    hidden = silu * up
    rows = units_ref.shape[3]
    turned = hidden.T.astype(bf16)
    for index in range(turned.shape[0] // rows):
        unit, rest = unit_of(index, n_mod)
        nxt = unit % 2 if units_ref.shape[1] == 2 else 0
        units_ref[unit // 2, nxt, rest if units_ref.shape[1] == 2 else 0] = turned[
            index * rows : (index + 1) * rows
        ]
    dg = (grad_hidden * up * (sigmoid * (1.0 + gate * (1.0 - sigmoid)))).astype(bf16)
    du = (grad_hidden * silu).astype(bf16)
    dg_ref[...] = dg
    du_ref[...] = du

    @pl.when(first)
    def _():
        ffn_ref[...] = jnp.zeros_like(ffn_ref)
        dmod_ref[...] = jnp.zeros_like(dmod_ref)

    ffn_ref[...] += nn(hidden.astype(bf16), wd_ref[...])
    dmod_ref[...] += nt(dg, wg_ref[...]) + nt(du, wu_ref[...])


def middle_kernel(
    slots, mid_ref, ffn_ref, dmod_ref, cot_ref, attn_ref, o_ref, mod_ref, w_out_ref, gather_ref,
    out_ref, grad_mid_ref, ga_ref, do_ref, dot_ref, sums_ref,
):
    width = mid_ref.shape[1]
    slot = slots[pl.program_id(0)]
    incoming = cot_ref[...].astype(f32)
    mid = mid_ref[...]
    out_ref[...] = (mid + part(mod_ref, slot, 5, width) * ffn_ref[...]).astype(bf16)
    norm, inverse = normed(mid)
    dmod = dmod_ref[...]
    grad_mid = incoming + norm_back(dmod, part(mod_ref, slot, 4, width), norm, inverse)
    grad_mid_ref[...] = grad_mid
    ga = (grad_mid * part(mod_ref, slot, 2, width)).astype(bf16)
    ga_ref[...] = ga
    do = nt(ga, w_out_ref[...]).astype(bf16)
    do_ref[...] = do
    dot_ref[...] = head_sum(do.astype(f32) * o_ref[...], gather_ref).T
    sums_ref[0, 0:1, :] = jnp.sum(grad_mid * attn_ref[...], axis=0, keepdims=True)
    sums_ref[0, 1:2, :] = jnp.sum(dmod, axis=0, keepdims=True)
    sums_ref[0, 2:3, :] = jnp.sum(dmod * norm, axis=0, keepdims=True)
    sums_ref[0, 3:4, :] = jnp.sum(incoming * ffn_ref[...], axis=0, keepdims=True)


def attend_back_kernel(
    slots, q_ref, k_ref, v_ref, do_ref, lse_ref, dot_ref, kt_ref, dqt_ref, dk_ref, dv_low_ref, dv_ref
):
    h = pl.program_id(0)
    tokens, width = q_ref.shape

    @pl.when(h == 0)
    def _():
        dqt_ref[...] = jnp.zeros_like(dqt_ref)
        dk_ref[...] = jnp.zeros_like(dk_ref)
        dv_ref[...] = jnp.zeros_like(dv_ref)

    start, offset = window(h, width)
    inside = head_lanes(offset)
    columns = pl.ds(start, WIN)
    first_row = pl.multiple_of((h * HD) // 16 * 16, 16)
    row = lax.broadcasted_iota(jnp.int32, (HD + 8, 1), 0) + first_row
    own_rows = (row >= h * HD) & (row < h * HD + HD)

    def step(rows):
        query = q_ref[rows, columns]
        grad_out = do_ref[rows, columns]
        key = jnp.where(inside, k_ref[rows, columns], 0)
        value = jnp.where(inside, v_ref[rows, columns], 0)
        probs = jnp.exp2(nt(key, query) * SCORE_LOG2 - lse_ref[pl.ds(h, 1), rows])
        scores = (probs * (nt(value, grad_out) - dot_ref[pl.ds(h, 1), rows])).astype(bf16)
        dv_ref[rows, columns] += jnp.where(inside, nn(probs.astype(bf16), grad_out), 0.0)
        dk_ref[rows, columns] += jnp.where(inside, nn(scores, query) * SCORE_SCALE, 0.0)
        turned = nn(kt_ref[pl.ds(first_row, HD + 8), rows], scores) * SCORE_SCALE
        dqt_ref[pl.ds(first_row, HD + 8), rows] += jnp.where(own_rows, turned, 0.0)

    whole = slots[tokens // TB - 1] == slots[0]

    @pl.when(whole)
    def _():
        step(slice(None))

    @pl.when(jnp.logical_not(whole))
    def _():
        def block(i, carry):
            step(pl.ds(pl.multiple_of(i * TB, TB), TB))
            return carry

        lax.fori_loop(0, tokens // TB, block, 0)

    @pl.when(h == HEADS - 1)
    def _():
        dv_low_ref[...] = dv_ref[...].astype(bf16)


def project_back_kernel(
    slots, dqt_ref, dk_ref, dv_ref, raw_ref, inv_ref, q_ref, k_ref, x_ref, grad_mid_ref, mod_ref,
    w_ref, coords_ref, cos_ref, sin_ref, gain_ref, gather_ref, spread_ref,
    gq_ref, gk_ref, grad_x_ref, sums_ref, gains_ref,
):
    width = x_ref.shape[1]
    slot = slots[pl.program_id(0)]

    @pl.when(pl.program_id(0) == 0)
    def _():
        gains_ref[...] = jnp.zeros_like(gains_ref)

    cosine, sine = angles(coords_ref, cos_ref, sin_ref)
    for index, (low_ref, gp_ref) in enumerate(((q_ref, gq_ref), (k_ref, gk_ref))):
        grad = dqt_ref[...].T if index == 0 else dk_ref[...]
        raw = raw_ref[:, index * width : (index + 1) * width]
        inverse = head_spread(inv_ref[:, index * 128 : (index + 1) * 128], spread_ref)
        mean = head_sum(grad * low_ref[...].astype(f32), gather_ref) * (1.0 / HD)
        norm = raw * inverse
        back = grad * cosine - partner(grad) * sine
        gains_ref[index : index + 1, :] += jnp.sum(back * norm, axis=0, keepdims=True)
        gp_ref[...] = (
            inverse * (back * gain_ref[index : index + 1, :] - norm * head_spread(mean, spread_ref))
        ).astype(bf16)
    dmod = nt(gq_ref[...], w_ref[:, :width]) + nt(gk_ref[...], w_ref[:, width : 2 * width])
    dmod = dmod + nt(dv_ref[...], w_ref[:, 2 * width :])
    norm, inverse = normed(x_ref[...].astype(f32))
    grad_x = grad_mid_ref[...] + norm_back(dmod, part(mod_ref, slot, 1, width), norm, inverse)
    grad_x_ref[...] = grad_x.astype(bf16)
    sums_ref[0, 0:1, :] = jnp.sum(dmod, axis=0, keepdims=True)
    sums_ref[0, 1:2, :] = jnp.sum(dmod * norm, axis=0, keepdims=True)


def send_kernel(where, units_ref, rhs_ref, out_ref):
    units, rows, _ = units_ref.shape
    result = nn(units_ref[...].reshape(units * rows, -1), rhs_ref[...])
    out_ref[...] = result.astype(bf16).reshape(out_ref.shape)


def keep_kernel(where, units_ref, rhs_ref, got_ref, send_ref, keep_ref, scratch):
    units, rows, _ = units_ref.shape
    result = nn(units_ref[...].reshape(units * rows, -1), rhs_ref[...])
    scratch[...] = result.reshape(scratch.shape)
    for i in range(units // 2):
        away, own = where[2 + i], where[4 + i]
        send_ref[i] = (scratch[away] + got_ref[away].astype(f32)).astype(bf16)
        keep_ref[i] = scratch[own] + got_ref[own].astype(f32)


def fold_kernel(where, keep_ref, got_ref, send_ref, own_ref):
    away, own = where[0], where[1]
    send_ref[...] = (keep_ref[away] + got_ref[away].astype(f32)).astype(bf16)
    own_ref[...] = keep_ref[own] + got_ref[own].astype(f32)


class Chain:
    def __init__(self):
        self.last = None

    def __call__(
        self, kernel, grid, in_specs, out_specs, out_shape, args, scalars=None, scratch=(), cost=(0, 0), name=None
    ):
        ahead = 0 if scalars is None else 1
        body = kernel
        token = ()
        if self.last is not None:
            token = (self.last,)
            in_specs = [pl.BlockSpec(memory_space=pl.ANY)] + list(in_specs)

            def body(*refs):
                kernel(*refs[:ahead], *refs[ahead + 1 :])

        spec = pltpu.PrefetchScalarGridSpec(
            num_scalar_prefetch=ahead,
            grid=grid,
            in_specs=in_specs,
            out_specs=out_specs,
            scratch_shapes=scratch,
        )
        outs = pl.pallas_call(
            body,
            grid_spec=spec,
            out_shape=out_shape,
            compiler_params=pltpu.CompilerParams(vmem_limit_bytes=VMEM),
            cost_estimate=pl.CostEstimate(flops=int(cost[0]), bytes_accessed=int(cost[1]), transcendentals=0),
            name=name,
        )(*(() if scalars is None else (scalars,)), *token, *args)
        self.last = outs[-1] if isinstance(outs, (list, tuple)) else outs
        return outs


def shape(dims, dtype):
    return jax.ShapeDtypeStruct(dims, dtype)


def fixed(dims):
    return pl.BlockSpec(dims, lambda *_: (0,) * len(dims), pipeline_mode=pl.Buffered(1))


def rows_of(dims, axis=0):
    return pl.BlockSpec(dims, lambda b, *_: tuple(b if i == axis else 0 for i in range(len(dims))))


class Reducer:
    def __init__(self, n_dp, n_mod, call):
        self.n_dp, self.n_mod, self.call = n_dp, n_mod, call
        self.position = lax.axis_index("dp")
        self.core = self.position & 1
        self.nxt = lax.shift_right_logical(self.position, 1) & 1
        self.mod = lax.axis_index("mod")

    def swap(self, arr, bit):
        if bit == "mod":
            return lax.ppermute(arr, "mod", [(i, i ^ 1) for i in range(self.n_mod)])
        return lax.ppermute(arr, "dp", [(i, i ^ (1 << bit)) for i in range(self.n_dp)])

    def stream(self, units, rhs, mod_first, name):
        return Stream(self, units, rhs, mod_first, name)


class Stream:
    def __init__(self, reducer, units, rhs, mod_first, name):
        self.r, self.units, self.rhs, self.mod_first, self.name = reducer, units, rhs, mod_first, name
        _, self.rows, self.tokens = units.shape
        self.columns = rhs.shape[1]
        self.chunk = next(c for c in (1024, 1152) if self.columns % c == 0)
        self.cost = (
            8 * self.rows * self.tokens * self.columns,
            2 * self.tokens * (self.columns + 4 * self.rows) + 8 * self.rows * self.columns,
        )

    def half(self):
        return pl.BlockSpec(
            (4, self.rows, self.tokens), lambda j, w: (w[0], 0, 0), pipeline_mode=pl.Buffered(1)
        )

    def send(self):
        rows, columns, chunk = self.rows, self.columns, self.chunk
        sent = self.r.call(
            send_kernel,
            (columns // chunk,),
            [self.half(), rows_of((self.tokens, chunk), 1)],
            rows_of((4, rows, chunk), 2),
            shape((4, rows, columns), bf16),
            (self.units, self.rhs),
            scalars=jnp.stack([1 - self.r.core]),
            cost=self.cost,
            name=self.name + "_send",
        )
        self.got = self.r.swap(sent, 0)

    def keep(self):
        rows, columns, chunk = self.rows, self.columns, self.chunk
        mod, nxt = self.r.mod, self.r.nxt
        if self.mod_first:
            where = [2 * (1 - mod), 2 * (1 - mod) + 1, 2 * mod, 2 * mod + 1]
        else:
            where = [1 - nxt, 3 - nxt, nxt, 2 + nxt]
        sent, self.kept = self.r.call(
            keep_kernel,
            (columns // chunk,),
            [self.half(), rows_of((self.tokens, chunk), 1), rows_of((4, rows, chunk), 2)],
            [rows_of((2, rows, chunk), 2), rows_of((2, rows, chunk), 2)],
            [shape((2, rows, columns), bf16), shape((2, rows, columns), f32)],
            (self.units, self.rhs, self.got),
            scalars=jnp.stack([self.r.core, self.r.core] + where),
            scratch=[pltpu.VMEM((4, rows, chunk), f32)],
            cost=(self.cost[0], self.cost[1] + 12 * rows * columns),
            name=self.name + "_keep",
        )
        self.got = self.r.swap(sent, "mod" if self.mod_first else 1)

    def fold(self):
        rows, columns, chunk = self.rows, self.columns, self.chunk
        bit = self.r.nxt if self.mod_first else self.r.mod
        sent, self.kept = self.r.call(
            fold_kernel,
            (columns // chunk,),
            [rows_of((2, rows, chunk), 2), rows_of((2, rows, chunk), 2)],
            [rows_of((rows, chunk), 1), rows_of((rows, chunk), 1)],
            [shape((rows, columns), bf16), shape((rows, columns), f32)],
            (self.kept, self.got),
            scalars=jnp.stack([1 - bit, bit]),
            cost=(0, 18 * rows * columns),
            name=self.name + "_fold",
        )
        self.got = self.r.swap(sent, 1 if self.mod_first else "mod")

    def total(self):
        n_dp = self.r.n_dp
        total = self.kept + self.got.astype(f32)
        bits = n_dp.bit_length() - 1
        total = total.reshape((2,) * (bits - 2) + (self.rows * 4 // n_dp, self.columns))
        for bit in range(2, bits):
            axis = bits - 1 - bit
            mine = lax.shift_right_logical(self.r.position, bit) & 1
            away = lax.dynamic_index_in_dim(total, 1 - mine, axis=axis, keepdims=False)
            own = lax.dynamic_index_in_dim(total, mine, axis=axis, keepdims=False)
            total = own + self.r.swap(away.astype(bf16), bit).astype(f32)
        return total


def silu_grad(v):
    sigmoid = jax.nn.sigmoid(v)
    return sigmoid * (1.0 + v * (1.0 - sigmoid))


def pair_order(own, other, mod):
    return jnp.where(mod == 0, jnp.stack([own, other]), jnp.stack([other, own]))


def body(
    n_dp, n_mod, tokens, cond, segments, coords, w_ada, w_qkv, q_gain, k_gain, w_out, w_gate, w_up,
    w_down, cotangent,
):
    _, count, width = tokens.shape
    slots_n = cond.shape[1]
    half = w_ada.shape[1]
    ff = w_gate.shape[1]
    blocks = count // TB
    n_dev = n_dp * n_mod
    call = Chain()
    reducer = Reducer(n_dp, n_mod, call)
    mod_index = lax.axis_index("mod")
    x = tokens[0]
    cot = cotangent[0]
    slots = segments[0, ::TB]
    coord = coords[0]
    cos_table, sin_table = (jnp.asarray(t) for t in rope_tables(width))
    gather, spread = (jnp.asarray(t) for t in head_tables(width))
    perm = jnp.asarray(unit_permutation(width, n_dp, n_mod))
    gains = jnp.stack([jnp.tile(q_gain, HEADS), jnp.tile(k_gain, HEADS)])

    cond_both = pair_order(cond[0], reducer.swap(cond[0], "mod"), mod_index)
    activated = jax.nn.silu(cond_both).astype(bf16).reshape(-1, width)
    mod_half = jnp.dot(activated, w_ada, preferred_element_type=f32).astype(bf16)
    mod_half = mod_half.reshape(n_mod, slots_n, half)
    own_half = lax.dynamic_index_in_dim(mod_half, mod_index, 0, keepdims=False)
    other_half = lax.dynamic_index_in_dim(mod_half, 1 - mod_index, 0, keepdims=False)
    pair = pair_order(own_half, reducer.swap(other_half, "mod"), mod_index)
    modulation = jnp.concatenate([pair[0], pair[1]], axis=1).astype(f32)

    token_f32 = shape((count, width), f32)
    token_bf16 = shape((count, width), bf16)
    units = shape((8, width // 8, count), bf16)
    units_spec = rows_of((8, width // 8, TB), 2)
    token_spec = rows_of((TB, width))
    mod_spec = fixed((slots_n, 6 * width))
    square = fixed((width, width))
    table_specs = [fixed(cos_table.shape), fixed(sin_table.shape), fixed((2, width)), fixed(gather.shape), fixed(spread.shape)]
    tables = (cos_table, sin_table, gains, gather, spread)
    lane_rows = shape((128, count), f32)
    macs = count * width * width

    attn_units, raw, inverse, query, key, value, key_t = call(
        project_kernel,
        (blocks,),
        [token_spec, mod_spec, fixed((width, 3 * width)), rows_of((2, TB), 1)] + table_specs + [square],
        [units_spec, rows_of((TB, 2 * width)), rows_of((TB, 256))] + [token_spec] * 3 + [rows_of((width, TB), 1)],
        [units, shape((count, 2 * width), f32), shape((count, 256), f32)] + [token_bf16] * 3
        + [shape((width, count), bf16)],
        (x, modulation, w_qkv, coord) + tables + (perm,),
        scalars=slots,
        cost=(2 * 5 * macs, 40e6),
        name="project",
    )
    attended, lse, attn, mid, ffn_in, grad_ffn, out_units, ffn_units = call(
        attend_kernel,
        (blocks,),
        [token_spec, token_spec, mod_spec, token_spec] + [fixed((count, width))] * 2 + [square, square],
        [token_spec, rows_of((128, TB), 1)] + [token_spec] * 4 + [units_spec] * 2,
        [token_f32, lane_rows, token_f32, token_f32, token_bf16, token_bf16, units, units],
        (x, cot, modulation, query, key, value, w_out, perm),
        scalars=slots,
        scratch=[pltpu.VMEM((TB, 128), f32)],
        cost=(2 * 10 * macs, 40e6),
        name="attend",
    )

    rows_ff = ff // n_dev
    rest = n_dp // 4
    chunk = 768
    group = chunk // rows_ff
    if group >= 8:
        unit_block = pl.BlockSpec((4, 2, group // 8, rows_ff, count), lambda i: (0, 0, i, 0, 0))
    else:
        unit_block = pl.BlockSpec((4, 1, 1, rows_ff, count), lambda i: (0, i % 2, i // 2, 0, 0))
    down_units, grad_gate, grad_up, ffn, grad_mod_ffn = call(
        functools.partial(ffn_kernel, n_mod=n_mod),
        (ff // chunk,),
        [fixed((count, width))] * 2 + [rows_of((width, chunk), 1)] * 2 + [rows_of((chunk, width))],
        [unit_block] + [rows_of((count, chunk), 1)] * 2 + [fixed((count, width))] * 2,
        [shape((4, 2, rest, rows_ff, count), bf16)] + [shape((count, ff), bf16)] * 2 + [token_f32] * 2,
        (ffn_in, grad_ffn, w_gate, w_up, w_down),
        cost=(2 * 6 * count * width * ff, 60e6),
        name="ffn",
    )
    down_units = down_units.reshape(8, rest * rows_ff, count)

    gate = reducer.stream(ffn_units, grad_gate, True, "gate")
    up = reducer.stream(ffn_units, grad_up, False, "up")
    down = reducer.stream(down_units, grad_ffn, True, "down")
    gate.send()
    up.send()
    down.send()

    output, grad_mid, grad_attn, grad_attended, dot_term, sums_b = call(
        middle_kernel,
        (blocks,),
        [token_spec] * 6 + [mod_spec, square, fixed(gather.shape)],
        [token_spec] * 4 + [rows_of((128, TB), 1), rows_of((1, 4, width))],
        [token_bf16, token_f32, token_bf16, token_bf16, lane_rows, shape((blocks, 4, width), f32)],
        (mid, ffn, grad_mod_ffn, cot, attn, attended, modulation, w_out, gather),
        scalars=slots,
        cost=(2 * macs, 40e6),
        name="middle",
    )
    out = reducer.stream(out_units, grad_attn, False, "out")
    gate.keep()
    up.keep()
    out.send()
    down.keep()
    out.keep()

    grad_query_t, grad_key, grad_value = call(
        attend_back_kernel,
        (HEADS,),
        [fixed((count, width))] * 4 + [fixed((128, count))] * 2 + [fixed((width, count))],
        [fixed((width, count))] + [fixed((count, width))] * 2,
        [shape((width, count), f32), token_f32, token_bf16],
        (query, key, value, grad_attended, lse, dot_term, key_t),
        scratch=[pltpu.VMEM((count, width), f32)],
        scalars=slots,
        cost=(2 * 22 * macs, 40e6),
        name="attend_back",
    )
    v_part = reducer.stream(attn_units, grad_value, True, "v")
    v_part.send()
    gate.fold()
    up.fold()
    v_part.keep()
    out.fold()
    grad_q, grad_k, grad_tokens, sums_a, gain_sums = call(
        project_back_kernel,
        (blocks,),
        [rows_of((width, TB), 1), token_spec, token_spec, rows_of((TB, 2 * width)), rows_of((TB, 256))]
        + [token_spec] * 4
        + [mod_spec, fixed((width, 3 * width)), rows_of((2, TB), 1)]
        + table_specs,
        [token_spec, token_spec, token_spec, rows_of((1, 2, width)), fixed((2, width))],
        [token_bf16, token_bf16, token_bf16, shape((blocks, 2, width), f32), shape((2, width), f32)],
        (grad_query_t, grad_key, grad_value, raw, inverse, query, key, x, grad_mid, modulation, w_qkv, coord)
        + tables,
        scalars=slots,
        cost=(2 * 4 * macs, 50e6),
        name="project_back",
    )
    q_part = reducer.stream(attn_units, grad_q, False, "q")
    k_part = reducer.stream(attn_units, grad_k, True, "k")
    q_part.send()
    k_part.send()
    down.fold()
    v_part.fold()
    q_part.keep()
    k_part.keep()
    q_part.fold()
    k_part.fold()
    summed_qkv = jnp.concatenate([q_part.total(), k_part.total(), v_part.total()], axis=1)

    sums = jnp.concatenate([sums_a, sums_b], axis=1).reshape(blocks, 6 * width)
    in_slot = slots[None, :, None] == jnp.arange(slots_n)[:, None, None]
    grad_modulation = jnp.sum(jnp.where(in_slot, sums[None], 0.0), axis=1).astype(bf16)
    halves = grad_modulation.reshape(slots_n, n_mod, half)
    own_half = lax.dynamic_index_in_dim(halves, mod_index, 1, keepdims=False)
    other_half = lax.dynamic_index_in_dim(halves, 1 - mod_index, 1, keepdims=False)
    grad_mod_flat = pair_order(own_half, reducer.swap(other_half, "mod"), mod_index).reshape(-1, half)
    rows_ada = width // n_dp
    gathered = jnp.concatenate([activated, grad_mod_flat], axis=1)
    for bit in range(n_dp.bit_length() - 1):
        other = reducer.swap(gathered, bit)
        second = (lax.shift_right_logical(reducer.position, bit) & 1) == 1
        gathered = jnp.where(
            second, jnp.concatenate([other, gathered]), jnp.concatenate([gathered, other])
        )
    own_activated = lax.dynamic_slice_in_dim(
        gathered[:, :width], reducer.position * rows_ada, rows_ada, axis=1
    )
    grad_w_ada = jnp.einsum("nd,nc->dc", own_activated, gathered[:, width:], preferred_element_type=f32)
    grad_activated = jnp.einsum("nc,dc->nd", grad_mod_flat, w_ada, preferred_element_type=f32)
    grad_activated = grad_activated.reshape(n_mod, slots_n, width)
    own_part = lax.dynamic_index_in_dim(grad_activated, mod_index, 0, keepdims=False)
    other_part = lax.dynamic_index_in_dim(grad_activated, 1 - mod_index, 0, keepdims=False)
    grad_own = own_part + reducer.swap(other_part.astype(bf16), "mod").astype(f32)
    grad_cond = grad_own[None] * silu_grad(cond)

    gain_grads = jnp.sum(gain_sums.reshape(2, HEADS, HD), axis=1)
    for bit in [0, "mod"] + list(range(1, n_dp.bit_length() - 1)):
        gain_grads = gain_grads + reducer.swap(gain_grads, bit)
    return (
        output[None],
        grad_tokens[None],
        grad_cond,
        grad_w_ada,
        summed_qkv,
        gain_grads[0],
        gain_grads[1],
        out.total(),
        gate.total(),
        up.total(),
        down.total(),
    )


def solution(mesh):
    rows = ("dp", "mod")
    in_specs = (
        P(rows, None, None),
        P(rows, None, None),
        P(rows, None),
        P(rows, None, None),
        P(None, "mod"),
        P(),
        P(),
        P(),
        P(),
        P(),
        P(),
        P(),
        P(rows, None, None),
    )
    out_specs = (
        P(rows, None, None),
        P(rows, None, None),
        P(rows, None, None),
        P("dp", "mod"),
        P(rows, None),
        P(),
        P(),
        P(rows, None),
        P(rows, None),
        P(rows, None),
        P(rows, None),
    )
    return jax.shard_map(
        functools.partial(body, mesh.shape["dp"], mesh.shape["mod"]),
        mesh=mesh,
        in_specs=in_specs,
        out_specs=out_specs,
        check_vma=False,
    )
```

```python
import functools

import jax
import jax.numpy as jnp
import numpy as np
from jax import lax
from jax.experimental import pallas as pl
from jax.experimental.pallas import tpu as pltpu
from jax.sharding import PartitionSpec as P

HEADS = 16
HD = 72
GRID = 32
EPS = 1e-06
ROPE_BASE = 10000.0
TB = 256
WIN = 256
SCORE_SCALE = float(HD**-0.5)
SCORE_LOG2 = float(np.log2(np.e) * HD**-0.5)
VMEM = 60 * 2**20
f32 = jnp.float32
bf16 = jnp.bfloat16


def nn(a, b):
    return lax.dot_general(a, b, (((1,), (0,)), ((), ())), preferred_element_type=f32)


def nt(a, b):
    return lax.dot_general(a, b, (((1,), (1,)), ((), ())), preferred_element_type=f32)


def tn(a, b):
    return lax.dot_general(a, b, (((0,), (0,)), ((), ())), preferred_element_type=f32)


def split3(v):
    hi = v.astype(bf16).astype(f32)
    mid = (v - hi).astype(bf16).astype(f32)
    return hi, mid, v - hi - mid


def np_split3(v):
    v = v.astype(np.float32)
    hi = v.astype(jnp.bfloat16).astype(np.float32)
    mid = (v - hi).astype(jnp.bfloat16).astype(np.float32)
    return [part.astype(jnp.bfloat16) for part in (hi, mid, v - hi - mid)]


@functools.lru_cache(None)
def rope_tables(width):
    quarter = HD // 4
    freqs = ROPE_BASE ** (-np.arange(quarter, dtype=np.float64) / quarter)
    lane = np.arange(width) % HD
    group = lane // quarter
    angle = np.arange(GRID)[:, None] * freqs[lane % quarter][None, :]
    cosine, sine = np.cos(angle), np.sin(angle)
    sine = np.where((group % 2 == 0)[None, :], -sine, sine)
    uses_col = (group >= 2)[None, :]
    tables = []
    for table in (cosine, sine):
        whole = np.concatenate(
            [np.where(uses_col, 0.0, table), np.where(uses_col, table, 0.0)], axis=0
        )
        tables.append(np.concatenate(np_split3(whole), axis=0))
    return tables


@functools.lru_cache(None)
def head_tables(width):
    head = np.arange(width) // HD
    gather = np.zeros((width, 128), np.float32)
    for copy in range(3):
        gather[np.arange(width), copy * HEADS + head] = 1.0
    return gather.astype(jnp.bfloat16), gather.T.astype(jnp.bfloat16)


def unit_of(index, n_mod):
    mod = index % n_mod
    dp = index // n_mod
    return (dp % 2) * 2 * n_mod + mod * 2 + (dp // 2) % 2, dp // 4


def reversed_bits(value, size):
    result = 0
    for bit in range(size.bit_length() - 1):
        result = 2 * result + (value >> bit) % 2
    return result


@functools.lru_cache(None)
def unit_permutation(width, n_dp, n_mod):
    rows = width // (n_dp * n_mod)
    matrix = np.zeros((width, width), np.float32)
    for index in range(n_dp * n_mod):
        unit, rest = unit_of(index, n_mod)
        start = unit * (width // 8) + reversed_bits(rest, n_dp // 4) * rows
        matrix[start + np.arange(rows), index * rows + np.arange(rows)] = 1.0
    return matrix.astype(jnp.bfloat16)


def normed(v):
    centred = v - jnp.mean(v, axis=-1, keepdims=True)
    inverse = lax.rsqrt(jnp.mean(centred * centred, axis=-1, keepdims=True) + EPS)
    return centred * inverse, inverse


def norm_back(grad, scale_part, norm, inverse):
    e = grad * (1.0 + scale_part)
    return inverse * (
        e - jnp.mean(e, axis=-1, keepdims=True) - norm * jnp.mean(e * norm, axis=-1, keepdims=True)
    )


def part(mod_ref, slot, index, width):
    return mod_ref[pl.ds(slot, 1), index * width : (index + 1) * width]


def angles(coords_ref, cos_ref, sin_ref):
    value = lax.broadcasted_iota(jnp.int32, (GRID, 1), 0)
    hot = [(value == coords_ref[i : i + 1, :]).astype(f32) for i in range(2)]
    hot = jnp.concatenate(hot * 3, axis=0).astype(bf16)
    return tn(hot, cos_ref[...]), tn(hot, sin_ref[...])


def partner(v):
    width = v.shape[1]
    quarter = HD // 4
    lane = lax.broadcasted_iota(jnp.int32, (1, width), 1)
    leads = (lane // quarter) % 2 == 0
    return jnp.where(leads, pltpu.roll(v, width - quarter, 1), pltpu.roll(v, quarter, 1))


def head_sum(v, gather_ref):
    hi = v.astype(bf16)
    low = (v - hi.astype(f32)).astype(bf16)
    return nn(hi, gather_ref[...]) + nn(low, gather_ref[...])


def head_spread(v, spread_ref):
    hi, mid, low = split3(v)
    lane = lax.broadcasted_iota(jnp.int32, (1, 128), 1)
    chosen = jnp.where(lane < HEADS, hi, jnp.where(lane < 2 * HEADS, mid, low))
    return nn(chosen.astype(bf16), spread_ref[...])


def window(head, width):
    start = jnp.minimum((head * HD) // 128, width // 128 - WIN // 128) * 128
    return pl.multiple_of(start, 128), head * HD - start


def head_lanes(offset):
    lane = lax.broadcasted_iota(jnp.int32, (1, WIN), 1)
    return (lane >= offset) & (lane < offset + HD)


def product(units_ref, half, rhs, out_ref):
    _, rows, tokens = units_ref.shape
    units = units_ref[pl.ds(4 * half, 4)].reshape(4 * rows, tokens)
    out_ref[...] = nn(units, rhs).astype(bf16).reshape(out_ref.shape)


def halves_out(acc_ref, core, send_ref, own_ref):
    rows = acc_ref.shape[0] // 2
    for half, out_ref in ((1 - core, send_ref), (core, own_ref)):
        start = pl.multiple_of(half * rows, rows)
        out_ref[...] = acc_ref[pl.ds(start, rows)].astype(bf16).reshape(out_ref.shape)


def project_kernel(
    slots, x_ref, mod_ref, w_ref, coords_ref, cos_ref, sin_ref, gain_ref, gather_ref, spread_ref,
    perm_ref, units_ref, raw_ref, inv_ref, q_ref, k_ref, v_ref, kt_ref,
):
    width = x_ref.shape[1]
    slot = slots[pl.program_id(0)]
    norm, _ = normed(x_ref[...].astype(f32))
    low = (norm * (1.0 + part(mod_ref, slot, 1, width)) + part(mod_ref, slot, 0, width)).astype(bf16)
    units_ref[...] = nt(perm_ref[...], low).astype(bf16).reshape(units_ref.shape)
    cosine, sine = angles(coords_ref, cos_ref, sin_ref)
    for index, out_ref in enumerate((q_ref, k_ref)):
        raw = nn(low, w_ref[:, index * width : (index + 1) * width])
        raw_ref[:, index * width : (index + 1) * width] = raw
        inverse = lax.rsqrt(head_sum(raw * raw, gather_ref) * (1.0 / HD) + EPS)
        inv_ref[:, index * 128 : (index + 1) * 128] = inverse
        scaled = raw * head_spread(inverse, spread_ref) * gain_ref[index : index + 1, :]
        turned = scaled * cosine + partner(scaled) * sine
        out_ref[...] = turned.astype(bf16)
        if index == 1:
            kt_ref[...] = turned.T.astype(bf16)
    v_ref[...] = nn(low, w_ref[:, 2 * width :]).astype(bf16)


def attend_kernel(
    slots, x_ref, cot_ref, mod_ref, q_ref, k_ref, v_ref, w_out_ref, perm_ref,
    o_ref, lse_ref, attn_ref, mid_ref, low_ref, gf_ref, att_units_ref, ffn_units_ref, lse_acc,
):
    block = pl.program_id(0)
    width = x_ref.shape[1]
    tokens = k_ref.shape[0]
    lane128 = lax.broadcasted_iota(jnp.int32, (1, 128), 1)
    lane = lax.broadcasted_iota(jnp.int32, (1, WIN), 1)
    o_ref[...] = jnp.zeros_like(o_ref)
    lse_acc[...] = jnp.zeros_like(lse_acc)

    def run(rows):
        def head(h, carry):
            start, offset = window(h, width)
            inside = head_lanes(offset)
            columns = pl.ds(start, WIN)
            query = jnp.where(inside, q_ref[:, columns], 0)
            value = jnp.where(inside, v_ref[rows, columns], 1)
            weight = jnp.exp2(nt(query, k_ref[rows, columns]) * SCORE_LOG2).astype(bf16)
            summed = nn(weight, value)
            free = jnp.where(offset > 0, 0, WIN - 1)
            total = jnp.sum(jnp.where(lane == free, summed, 0.0), axis=1, keepdims=True)
            o_ref[:, columns] += jnp.where(inside, summed * (1.0 / total), 0.0)
            lse_acc[...] += jnp.where(lane128 == h, jnp.log2(total), 0.0)
            return carry

        lax.fori_loop(0, HEADS, head, 0, unroll=2)

    whole = slots[tokens // TB - 1] == slots[0]

    @pl.when(whole)
    def _():
        run(slice(None))

    @pl.when(jnp.logical_not(whole))
    def _():
        run(pl.ds(pl.multiple_of(block * TB, TB), TB))

    lse_ref[...] = lse_acc[...].T
    slot = slots[block]
    attended = o_ref[...].astype(bf16)
    att_units_ref[...] = nt(perm_ref[...], attended).astype(bf16).reshape(att_units_ref.shape)
    attn = nn(attended, w_out_ref[...])
    attn_ref[...] = attn
    mid = x_ref[...].astype(f32) + part(mod_ref, slot, 2, width) * attn
    mid_ref[...] = mid
    norm, _ = normed(mid)
    low = (norm * (1.0 + part(mod_ref, slot, 4, width)) + part(mod_ref, slot, 3, width)).astype(bf16)
    low_ref[...] = low
    ffn_units_ref[...] = nt(perm_ref[...], low).astype(bf16).reshape(ffn_units_ref.shape)
    gf_ref[...] = (cot_ref[...].astype(f32) * part(mod_ref, slot, 5, width)).astype(bf16)


def ffn_kernel(
    bits, x_ref, gf_ref, units_ref, wg_ref, wu_ref, wd_ref,
    gate_send_ref, gate_own_ref, up_send_ref, up_own_ref, down_send_ref, down_own_ref, ffn_ref, dmod_ref,
    turned_ref, *, n_mod, rows_ff,
):
    core = bits[0]
    gate = nn(x_ref[...], wg_ref[...])
    up = nn(x_ref[...], wu_ref[...])
    grad_hidden = nt(gf_ref[...], wd_ref[...])
    sigmoid = 1.0 / (1.0 + jnp.exp(-gate))
    silu = gate * sigmoid
    hidden = (silu * up).astype(bf16)
    turned = hidden.T
    for index in range(turned.shape[0] // rows_ff):
        unit, rest = unit_of(index, n_mod)
        turned_ref[unit, rest * rows_ff : (rest + 1) * rows_ff] = turned[
            index * rows_ff : (index + 1) * rows_ff
        ]
    dg = (grad_hidden * up * (sigmoid * (1.0 + gate * (1.0 - sigmoid)))).astype(bf16)
    du = (grad_hidden * silu).astype(bf16)

    @pl.when(pl.program_id(0) == 0)
    def _():
        ffn_ref[...] = jnp.zeros_like(ffn_ref)
        dmod_ref[...] = jnp.zeros_like(dmod_ref)

    ffn_ref[...] += nn(hidden, wd_ref[...])
    dmod_ref[...] += nt(dg, wg_ref[...]) + nt(du, wu_ref[...])
    product(units_ref, 1 - core, dg, gate_send_ref)
    product(units_ref, 1 - core, du, up_send_ref)
    product(turned_ref, 1 - core, gf_ref[...], down_send_ref)
    product(units_ref, core, dg, gate_own_ref)
    product(units_ref, core, du, up_own_ref)
    product(turned_ref, core, gf_ref[...], down_own_ref)


def middle_kernel(
    slots, mid_ref, ffn_ref, dmod_ref, cot_ref, attn_ref, o_ref, units_ref, mod_ref, w_out_ref, gather_ref,
    out_ref, grad_mid_ref, do_ref, dot_ref, sums_ref, send_ref, own_ref, acc_ref,
):
    width = mid_ref.shape[1]
    block = pl.program_id(0)
    slot = slots[block]
    incoming = cot_ref[...].astype(f32)
    mid = mid_ref[...]
    out_ref[...] = (mid + part(mod_ref, slot, 5, width) * ffn_ref[...]).astype(bf16)
    norm, inverse = normed(mid)
    dmod = dmod_ref[...]
    grad_mid = incoming + norm_back(dmod, part(mod_ref, slot, 4, width), norm, inverse)
    grad_mid_ref[...] = grad_mid
    ga = (grad_mid * part(mod_ref, slot, 2, width)).astype(bf16)
    grow = nn(units_ref[...].reshape(width, TB), ga)

    @pl.when(block == 0)
    def _():
        acc_ref[...] = grow

    @pl.when(block > 0)
    def _():
        acc_ref[...] += grow

    @pl.when(block == pl.num_programs(0) - 1)
    def _():
        halves_out(acc_ref, slots[pl.num_programs(0)], send_ref, own_ref)

    do = nt(ga, w_out_ref[...]).astype(bf16)
    do_ref[...] = do
    dot_ref[...] = head_sum(do.astype(f32) * o_ref[...], gather_ref).T
    sums_ref[0, 0:1, :] = jnp.sum(grad_mid * attn_ref[...], axis=0, keepdims=True)
    sums_ref[0, 1:2, :] = jnp.sum(dmod, axis=0, keepdims=True)
    sums_ref[0, 2:3, :] = jnp.sum(dmod * norm, axis=0, keepdims=True)
    sums_ref[0, 3:4, :] = jnp.sum(incoming * ffn_ref[...], axis=0, keepdims=True)


def attend_back_kernel(
    slots, q_ref, k_ref, v_ref, do_ref, lse_ref, dot_ref, kt_ref, dqt_ref, dk_ref, dv_low_ref, dv_ref
):
    h = pl.program_id(0)
    tokens, width = q_ref.shape

    @pl.when(h == 0)
    def _():
        dqt_ref[...] = jnp.zeros_like(dqt_ref)
        dk_ref[...] = jnp.zeros_like(dk_ref)
        dv_ref[...] = jnp.zeros_like(dv_ref)

    start, offset = window(h, width)
    inside = head_lanes(offset)
    columns = pl.ds(start, WIN)
    first_row = pl.multiple_of((h * HD) // 16 * 16, 16)
    row = lax.broadcasted_iota(jnp.int32, (HD + 8, 1), 0) + first_row
    own_rows = (row >= h * HD) & (row < h * HD + HD)

    def step(rows):
        query = q_ref[rows, columns]
        grad_out = do_ref[rows, columns]
        key = jnp.where(inside, k_ref[rows, columns], 0)
        value = jnp.where(inside, v_ref[rows, columns], 0)
        probs = jnp.exp2(nt(key, query) * SCORE_LOG2 - lse_ref[pl.ds(h, 1), rows])
        scores = (probs * (nt(value, grad_out) - dot_ref[pl.ds(h, 1), rows])).astype(bf16)
        dv_ref[rows, columns] += jnp.where(inside, nn(probs.astype(bf16), grad_out), 0.0)
        dk_ref[rows, columns] += jnp.where(inside, nn(scores, query) * SCORE_SCALE, 0.0)
        turned = nn(kt_ref[pl.ds(first_row, HD + 8), rows], scores) * SCORE_SCALE
        dqt_ref[pl.ds(first_row, HD + 8), rows] += jnp.where(own_rows, turned, 0.0)

    whole = slots[tokens // TB - 1] == slots[0]

    @pl.when(whole)
    def _():
        step(slice(None))

    @pl.when(jnp.logical_not(whole))
    def _():
        def block(i, carry):
            step(pl.ds(pl.multiple_of(i * TB, TB), TB))
            return carry

        lax.fori_loop(0, tokens // TB, block, 0)

    @pl.when(h == HEADS - 1)
    def _():
        dv_low_ref[...] = dv_ref[...].astype(bf16)


def project_back_kernel(
    slots, dqt_ref, dk_ref, dv_ref, raw_ref, inv_ref, q_ref, k_ref, x_ref, grad_mid_ref, units_ref, mod_ref,
    w_ref, coords_ref, cos_ref, sin_ref, gain_ref, gather_ref, spread_ref,
    grad_x_ref, sums_ref, gains_ref, q_send_ref, q_own_ref, k_send_ref, k_own_ref, accq_ref, acck_ref,
):
    width = x_ref.shape[1]
    block = pl.program_id(0)
    slot = slots[block]

    @pl.when(block == 0)
    def _():
        gains_ref[...] = jnp.zeros_like(gains_ref)
        accq_ref[...] = jnp.zeros_like(accq_ref)
        acck_ref[...] = jnp.zeros_like(acck_ref)

    dmod = nt(dv_ref[...], w_ref[:, 2 * width :])

    cosine, sine = angles(coords_ref, cos_ref, sin_ref)
    for index, (low_ref, acc_ref) in enumerate(((q_ref, accq_ref), (k_ref, acck_ref))):
        grad = dqt_ref[...].T if index == 0 else dk_ref[...]
        raw = raw_ref[:, index * width : (index + 1) * width]
        inverse = head_spread(inv_ref[:, index * 128 : (index + 1) * 128], spread_ref)
        mean = head_sum(grad * low_ref[...].astype(f32), gather_ref) * (1.0 / HD)
        norm = raw * inverse
        back = grad * cosine - partner(grad) * sine
        gains_ref[index : index + 1, :] += jnp.sum(back * norm, axis=0, keepdims=True)
        grad_raw = (
            inverse * (back * gain_ref[index : index + 1, :] - norm * head_spread(mean, spread_ref))
        ).astype(bf16)
        acc_ref[...] += nn(units_ref[...].reshape(width, TB), grad_raw)
        dmod = dmod + nt(grad_raw, w_ref[:, index * width : (index + 1) * width])

    @pl.when(block == pl.num_programs(0) - 1)
    def _():
        halves_out(accq_ref, slots[pl.num_programs(0)], q_send_ref, q_own_ref)
        halves_out(acck_ref, slots[pl.num_programs(0)], k_send_ref, k_own_ref)

    norm, inverse = normed(x_ref[...].astype(f32))
    grad_x = grad_mid_ref[...] + norm_back(dmod, part(mod_ref, slot, 1, width), norm, inverse)
    grad_x_ref[...] = grad_x.astype(bf16)
    sums_ref[0, 0:1, :] = jnp.sum(dmod, axis=0, keepdims=True)
    sums_ref[0, 1:2, :] = jnp.sum(dmod * norm, axis=0, keepdims=True)


def value_kernel(bits, units_ref, rhs_ref, send_ref, own_ref):
    product(units_ref, 1 - bits[0], rhs_ref[...], send_ref)
    product(units_ref, bits[0], rhs_ref[...], own_ref)


def fold_kernel(bits, *refs, plans):
    count = len(plans)
    for i, (kind, bit, rows) in enumerate(plans):
        own_ref, got_ref, send_ref, keep_ref = refs[2 * i], refs[2 * i + 1], refs[2 * count + 2 * i], refs[2 * count + 2 * i + 1]
        mine = bits[bit]
        if kind in ("outer", "inner"):
            for j in range(2):
                away = 2 * (1 - mine) + j if kind == "outer" else 2 * j + 1 - mine
                own = 2 * mine + j if kind == "outer" else 2 * j + mine
                send_ref[j] = (own_ref[away].astype(f32) + got_ref[away].astype(f32)).astype(bf16)
                keep_ref[j] = own_ref[own].astype(f32) + got_ref[own].astype(f32)
        elif kind == "unit":
            send_ref[...] = (own_ref[1 - mine] + got_ref[1 - mine].astype(f32)).astype(bf16)
            keep_ref[...] = own_ref[mine] + got_ref[mine].astype(f32)
        else:
            total = own_ref[...] + got_ref[...].astype(f32)
            for j in range(total.shape[0] // (2 * rows)):
                first = total[2 * j * rows : (2 * j + 1) * rows]
                second = total[(2 * j + 1) * rows : (2 * j + 2) * rows]
                place = slice(j * rows, (j + 1) * rows)
                send_ref[place] = jnp.where(mine == 1, first, second).astype(bf16)
                keep_ref[place] = jnp.where(mine == 1, second, first)


def last_kernel(*refs):
    count = len(refs) // 3
    for i in range(count):
        refs[2 * count + i][...] = refs[2 * i][...] + refs[2 * i + 1][...].astype(f32)


class Chain:
    def __init__(self):
        self.last = None

    def __call__(
        self, kernel, grid, in_specs, out_specs, out_shape, args, scalars=None, scratch=(), name=None
    ):
        ahead = 0 if scalars is None else 1
        body = kernel
        token = ()
        if self.last is not None:
            token = (self.last,)
            in_specs = [pl.BlockSpec(memory_space=pl.ANY)] + list(in_specs)

            def body(*refs):
                kernel(*refs[:ahead], *refs[ahead + 1 :])

        spec = pltpu.PrefetchScalarGridSpec(
            num_scalar_prefetch=ahead,
            grid=grid,
            in_specs=in_specs,
            out_specs=out_specs,
            scratch_shapes=scratch,
        )
        outs = pl.pallas_call(
            body,
            grid_spec=spec,
            out_shape=out_shape,
            compiler_params=pltpu.CompilerParams(vmem_limit_bytes=VMEM),
            cost_estimate=pl.CostEstimate(flops=1, bytes_accessed=1, transcendentals=0),
            name=name,
        )(*(() if scalars is None else (scalars,)), *token, *args)
        self.last = outs[-1]
        return outs


def shape(dims, dtype):
    return jax.ShapeDtypeStruct(dims, dtype)


def fixed(dims):
    return pl.BlockSpec(dims, lambda *_: (0,) * len(dims), pipeline_mode=pl.Buffered(1))


def rows_of(dims, axis=0):
    return pl.BlockSpec(dims, lambda b, *_: tuple(b if i == axis else 0 for i in range(len(dims))))


def whole(dims):
    return rows_of(dims, None)


class Reducer:
    def __init__(self, n_dp, n_mod, call):
        self.n_dp, self.n_mod, self.call = n_dp, n_mod, call
        self.position = lax.axis_index("dp")
        steps = range(n_dp.bit_length() - 1)
        dp_bits = [lax.shift_right_logical(self.position, step) & 1 for step in steps]
        self.bits = jnp.stack([dp_bits[0], lax.axis_index("mod")] + dp_bits[1:]).astype(jnp.int32)

    def swap(self, arr, bit):
        if bit == "mod":
            return lax.ppermute(arr, "mod", [(i, i ^ 1) for i in range(self.n_mod)])
        return lax.ppermute(arr, "dp", [(i, i ^ (1 << bit)) for i in range(self.n_dp)])

    def bit_of(self, bit):
        return 1 if bit == "mod" else bit + 1 if bit else 0

    def stream(self, sent, own, mod_first, pair_rows=None):
        return Stream(self, sent, own, mod_first, pair_rows)

    def fold(self, streams, name):
        plans, args, outs = [], [], []
        for stream in streams:
            plan, part_shape = stream.plan()
            plans.append(plan)
            args += [stream.own, stream.got]
            outs += [shape(part_shape, bf16), shape(part_shape, f32)]
        results = self.call(
            functools.partial(fold_kernel, plans=plans),
            (1,),
            [whole(arg.shape) for arg in args],
            [whole(out.shape) for out in outs],
            outs,
            args,
            scalars=self.bits,
            name=name + "_fold",
        )
        for i, stream in enumerate(streams):
            stream.step(results[2 * i], results[2 * i + 1])

    def last(self, streams, name):
        args = [arr for stream in streams for arr in (stream.own, stream.got)]
        outs = [shape(stream.own.shape, f32) for stream in streams]
        return self.call(
            last_kernel,
            (1,),
            [whole(arg.shape) for arg in args],
            [whole(out.shape) for out in outs],
            outs,
            args,
            name=name + "_last",
        )


class Stream:
    def __init__(self, reducer, sent, own, mod_first, pair_rows):
        self.r, self.own, self.pair_rows, self.mod_first = reducer, own, pair_rows, mod_first
        self.steps = ["mod", 1] if mod_first else [1, "mod"]
        self.steps += list(range(2, reducer.n_dp.bit_length() - 1))
        self.at = 0
        self.got = reducer.swap(sent, 0)

    def plan(self):
        bit = self.r.bit_of(self.steps[self.at])
        dims = self.own.shape
        if self.at == 0:
            return ("outer" if self.mod_first else "inner", bit, 0), (2,) + dims[1:]
        if self.at == 1:
            return ("unit", bit, 0), dims[1:]
        return ("rows", bit, self.pair_rows or dims[0] // 2), (dims[0] // 2, dims[1])

    def step(self, sent, own):
        self.own = own
        self.got = self.r.swap(sent, self.steps[self.at])
        self.at += 1


def silu_grad(v):
    sigmoid = jax.nn.sigmoid(v)
    return sigmoid * (1.0 + v * (1.0 - sigmoid))


def pair_order(own, other, mod):
    return jnp.where(mod == 0, jnp.stack([own, other]), jnp.stack([other, own]))


def body(
    n_dp, n_mod, tokens, cond, segments, coords, w_ada, w_qkv, q_gain, k_gain, w_out, w_gate, w_up,
    w_down, cotangent,
):
    _, count, width = tokens.shape
    slots_n = cond.shape[1]
    half = w_ada.shape[1]
    ff = w_gate.shape[1]
    blocks = count // TB
    n_dev = n_dp * n_mod
    call = Chain()
    reducer = Reducer(n_dp, n_mod, call)
    mod_index = lax.axis_index("mod")
    x = tokens[0]
    cot = cotangent[0]
    slots = segments[0, ::TB]
    coord = coords[0]
    cos_table, sin_table = (jnp.asarray(t) for t in rope_tables(width))
    gather, spread = (jnp.asarray(t) for t in head_tables(width))
    perm = jnp.asarray(unit_permutation(width, n_dp, n_mod))
    gains = jnp.stack([jnp.tile(q_gain, HEADS), jnp.tile(k_gain, HEADS)])

    cond_both = pair_order(cond[0], reducer.swap(cond[0], "mod"), mod_index)
    activated = jax.nn.silu(cond_both).astype(bf16).reshape(-1, width)
    mod_half = jnp.dot(activated, w_ada, preferred_element_type=f32).astype(bf16)
    mod_half = mod_half.reshape(n_mod, slots_n, half)
    own_half = lax.dynamic_index_in_dim(mod_half, mod_index, 0, keepdims=False)
    other_half = lax.dynamic_index_in_dim(mod_half, 1 - mod_index, 0, keepdims=False)
    pair = pair_order(own_half, reducer.swap(other_half, "mod"), mod_index)
    modulation = jnp.concatenate([pair[0], pair[1]], axis=1).astype(f32)

    token_f32 = shape((count, width), f32)
    token_bf16 = shape((count, width), bf16)
    units = shape((8, width // 8, count), bf16)
    units_spec = rows_of((8, width // 8, TB), 2)
    token_spec = rows_of((TB, width))
    mod_spec = fixed((slots_n, 6 * width))
    square = fixed((width, width))
    table_specs = [fixed(cos_table.shape), fixed(sin_table.shape), fixed((2, width)), fixed(gather.shape), fixed(spread.shape)]
    tables = (cos_table, sin_table, gains, gather, spread)
    lane_rows = shape((128, count), f32)
    macs = count * width * width

    attn_units, raw, inverse, query, key, value, key_t = call(
        project_kernel,
        (blocks,),
        [token_spec, mod_spec, fixed((width, 3 * width)), rows_of((2, TB), 1)] + table_specs + [square],
        [units_spec, rows_of((TB, 2 * width)), rows_of((TB, 256))] + [token_spec] * 3 + [rows_of((width, TB), 1)],
        [units, shape((count, 2 * width), f32), shape((count, 256), f32)] + [token_bf16] * 3
        + [shape((width, count), bf16)],
        (x, modulation, w_qkv, coord) + tables + (perm,),
        scalars=slots,
        name="project",
    )
    attended, lse, attn, mid, ffn_in, grad_ffn, out_units, ffn_units = call(
        attend_kernel,
        (blocks,),
        [token_spec, token_spec, mod_spec, token_spec] + [fixed((count, width))] * 2 + [square, square],
        [token_spec, rows_of((128, TB), 1)] + [token_spec] * 4 + [units_spec] * 2,
        [token_f32, lane_rows, token_f32, token_f32, token_bf16, token_bf16, units, units],
        (x, cot, modulation, query, key, value, w_out, perm),
        scalars=slots,
        scratch=[pltpu.VMEM((TB, 128), f32)],
        name="attend",
    )

    rows_ff = ff // n_dev
    chunk = 768
    piece = chunk // 8
    half_units = lambda rows, columns: shape((4, rows, columns), bf16)
    square_send = [fixed((4, width // 8, width))] * 2
    square_shapes = [half_units(width // 8, width)] * 2
    gate_send, gate_own, up_send, up_own, down_send, down_own, ffn, grad_mod_ffn = call(
        functools.partial(ffn_kernel, n_mod=n_mod, rows_ff=rows_ff),
        (ff // chunk,),
        [fixed((count, width))] * 2 + [fixed(units.shape)]
        + [rows_of((width, chunk), 1)] * 2 + [rows_of((chunk, width))],
        [rows_of((4, width // 8, chunk), 2)] * 4
        + [rows_of((4, 1, piece, width), 1)] * 2 + [fixed((count, width))] * 2,
        [half_units(width // 8, ff)] * 4
        + [shape((4, ff // chunk, piece, width), bf16)] * 2 + [token_f32] * 2,
        (ffn_in, grad_ffn, ffn_units, w_gate, w_up, w_down),
        scalars=reducer.bits,
        scratch=[pltpu.VMEM((8, piece, count), bf16)],
        name="ffn",
    )
    gate = reducer.stream(gate_send, gate_own, True)
    up = reducer.stream(up_send, up_own, False)
    down = reducer.stream(
        down_send.reshape(4, ff // 8, width), down_own.reshape(4, ff // 8, width), True, rows_ff
    )

    slots_core = jnp.concatenate([slots, reducer.bits[:1]])
    output, grad_mid, grad_attended, dot_term, sums_b, out_send, out_own = call(
        middle_kernel,
        (blocks,),
        [token_spec] * 6 + [units_spec, mod_spec, square, fixed(gather.shape)],
        [token_spec] * 3 + [rows_of((128, TB), 1), rows_of((1, 4, width))] + square_send,
        [token_bf16, token_f32, token_bf16, lane_rows, shape((blocks, 4, width), f32)] + square_shapes,
        (mid, ffn, grad_mod_ffn, cot, attn, attended, out_units, modulation, w_out, gather),
        scalars=slots_core,
        scratch=[pltpu.VMEM((width, width), f32)],
        name="middle",
    )
    out = reducer.stream(out_send, out_own, False)
    reducer.fold([gate], "gate")
    reducer.fold([up], "up")
    reducer.fold([down], "down")
    reducer.fold([out], "out")

    grad_query_t, grad_key, grad_value = call(
        attend_back_kernel,
        (HEADS,),
        [fixed((count, width))] * 4 + [fixed((128, count))] * 2 + [fixed((width, count))],
        [fixed((width, count))] + [fixed((count, width))] * 2,
        [shape((width, count), f32), token_f32, token_bf16],
        (query, key, value, grad_attended, lse, dot_term, key_t),
        scratch=[pltpu.VMEM((count, width), f32)],
        scalars=slots,
        name="attend_back",
    )
    v_send, v_own = call(
        value_kernel,
        (1,),
        [whole(units.shape), whole((count, width))],
        [whole((4, width // 8, width))] * 2,
        square_shapes,
        (attn_units, grad_value),
        scalars=reducer.bits,
        name="value",
    )
    v_part = reducer.stream(v_send, v_own, True)
    reducer.fold([gate, up], "gate_up")
    reducer.fold([out, v_part], "out_v")
    reducer.fold([down], "down")
    grad_tokens, sums_a, gain_sums, q_send, q_own, k_send, k_own = call(
        project_back_kernel,
        (blocks,),
        [rows_of((width, TB), 1), token_spec, token_spec, rows_of((TB, 2 * width)), rows_of((TB, 256))]
        + [token_spec] * 4
        + [units_spec, mod_spec, fixed((width, 3 * width)), rows_of((2, TB), 1)]
        + table_specs,
        [token_spec, rows_of((1, 2, width)), fixed((2, width))] + square_send * 2,
        [token_bf16, shape((blocks, 2, width), f32), shape((2, width), f32)] + square_shapes * 2,
        (grad_query_t, grad_key, grad_value, raw, inverse, query, key, x, grad_mid, attn_units, modulation,
         w_qkv, coord)
        + tables,
        scalars=slots_core,
        scratch=[pltpu.VMEM((width, width), f32)] * 2,
        name="project_back",
    )
    q_part = reducer.stream(q_send, q_own, False)
    k_part = reducer.stream(k_send, k_own, True)
    reducer.fold([gate, up], "gate_up")
    reducer.fold([down, out, v_part], "down_out_v")
    reducer.fold([q_part, k_part], "q_k")
    for _ in range(n_dp.bit_length() - 4):
        reducer.fold([gate, up, down, out], "early")
        reducer.fold([v_part], "v")
        reducer.fold([q_part, k_part], "q_k")
    summed_gate, summed_up, summed_down, summed_out = reducer.last([gate, up, down, out], "early")
    reducer.fold([v_part, q_part, k_part], "v_q_k")
    reducer.fold([q_part, k_part], "q_k")
    summed = reducer.last([q_part, k_part, v_part], "q_k_v")
    summed_qkv = jnp.concatenate(summed, axis=1)

    sums = jnp.concatenate([sums_a, sums_b], axis=1).reshape(blocks, 6 * width)
    in_slot = slots[None, :, None] == jnp.arange(slots_n)[:, None, None]
    grad_modulation = jnp.sum(jnp.where(in_slot, sums[None], 0.0), axis=1).astype(bf16)
    halves = grad_modulation.reshape(slots_n, n_mod, half)
    own_half = lax.dynamic_index_in_dim(halves, mod_index, 1, keepdims=False)
    other_half = lax.dynamic_index_in_dim(halves, 1 - mod_index, 1, keepdims=False)
    grad_mod_flat = pair_order(own_half, reducer.swap(other_half, "mod"), mod_index).reshape(-1, half)
    rows_ada = width // n_dp
    gathered = jnp.concatenate([activated, grad_mod_flat], axis=1)
    for bit in range(n_dp.bit_length() - 1):
        other = reducer.swap(gathered, bit)
        second = (lax.shift_right_logical(reducer.position, bit) & 1) == 1
        gathered = jnp.where(
            second, jnp.concatenate([other, gathered]), jnp.concatenate([gathered, other])
        )
    own_activated = lax.dynamic_slice_in_dim(
        gathered[:, :width], reducer.position * rows_ada, rows_ada, axis=1
    )
    grad_w_ada = jnp.einsum("nd,nc->dc", own_activated, gathered[:, width:], preferred_element_type=f32)
    grad_activated = jnp.einsum("nc,dc->nd", grad_mod_flat, w_ada, preferred_element_type=f32)
    grad_activated = grad_activated.reshape(n_mod, slots_n, width)
    own_part = lax.dynamic_index_in_dim(grad_activated, mod_index, 0, keepdims=False)
    other_part = lax.dynamic_index_in_dim(grad_activated, 1 - mod_index, 0, keepdims=False)
    grad_own = own_part + reducer.swap(other_part.astype(bf16), "mod").astype(f32)
    grad_cond = grad_own[None] * silu_grad(cond)

    gain_grads = jnp.sum(gain_sums.reshape(2, HEADS, HD), axis=1)
    for bit in [0, "mod"] + list(range(1, n_dp.bit_length() - 1)):
        gain_grads = gain_grads + reducer.swap(gain_grads, bit)
    return (
        output[None],
        grad_tokens[None],
        grad_cond,
        grad_w_ada,
        summed_qkv,
        gain_grads[0],
        gain_grads[1],
        summed_out,
        summed_gate,
        summed_up,
        summed_down,
    )


def solution(mesh):
    rows = ("dp", "mod")
    in_specs = (
        P(rows, None, None),
        P(rows, None, None),
        P(rows, None),
        P(rows, None, None),
        P(None, "mod"),
        P(),
        P(),
        P(),
        P(),
        P(),
        P(),
        P(),
        P(rows, None, None),
    )
    out_specs = (
        P(rows, None, None),
        P(rows, None, None),
        P(rows, None, None),
        P("dp", "mod"),
        P(rows, None),
        P(),
        P(),
        P(rows, None),
        P(rows, None),
        P(rows, None),
        P(rows, None),
    )
    return jax.shard_map(
        functools.partial(body, mesh.shape["dp"], mesh.shape["mod"]),
        mesh=mesh,
        in_specs=in_specs,
        out_specs=out_specs,
        check_vma=False,
    )
```

```python
import functools

import jax
import jax.numpy as jnp
import numpy as np
from jax import lax
from jax.experimental import pallas as pl
from jax.experimental.pallas import tpu as pltpu
from jax.sharding import PartitionSpec as P

HEADS = 16
HD = 72
GRID = 32
EPS = 1e-06
ROPE_BASE = 10000.0
TB = 256
WIN = 256
SCORE_SCALE = float(HD**-0.5)
SCORE_LOG2 = float(np.log2(np.e) * HD**-0.5)
VMEM = 60 * 2**20
f32 = jnp.float32
bf16 = jnp.bfloat16


def nn(a, b):
    return lax.dot_general(a, b, (((1,), (0,)), ((), ())), preferred_element_type=f32)


def nt(a, b):
    return lax.dot_general(a, b, (((1,), (1,)), ((), ())), preferred_element_type=f32)


def tn(a, b):
    return lax.dot_general(a, b, (((0,), (0,)), ((), ())), preferred_element_type=f32)


def split3(v):
    hi = v.astype(bf16).astype(f32)
    mid = (v - hi).astype(bf16).astype(f32)
    return hi, mid, v - hi - mid


def np_split3(v):
    v = v.astype(np.float32)
    hi = v.astype(jnp.bfloat16).astype(np.float32)
    mid = (v - hi).astype(jnp.bfloat16).astype(np.float32)
    return [part.astype(jnp.bfloat16) for part in (hi, mid, v - hi - mid)]


@functools.lru_cache(None)
def rope_tables(width):
    quarter = HD // 4
    freqs = ROPE_BASE ** (-np.arange(quarter, dtype=np.float64) / quarter)
    lane = np.arange(width) % HD
    group = lane // quarter
    angle = np.arange(GRID)[:, None] * freqs[lane % quarter][None, :]
    cosine, sine = np.cos(angle), np.sin(angle)
    sine = np.where((group % 2 == 0)[None, :], -sine, sine)
    uses_col = (group >= 2)[None, :]
    tables = []
    for table in (cosine, sine):
        whole = np.concatenate(
            [np.where(uses_col, 0.0, table), np.where(uses_col, table, 0.0)], axis=0
        )
        tables.append(np.concatenate(np_split3(whole), axis=0))
    return tables


@functools.lru_cache(None)
def head_tables(width):
    head = np.arange(width) // HD
    gather = np.zeros((width, 128), np.float32)
    for copy in range(3):
        gather[np.arange(width), copy * HEADS + head] = 1.0
    return gather.astype(jnp.bfloat16), gather.T.astype(jnp.bfloat16)


def unit_of(index, n_mod):
    mod = index % n_mod
    dp = index // n_mod
    return (dp % 2) * 2 * n_mod + mod * 2 + (dp // 2) % 2, dp // 4


def reversed_bits(value, size):
    result = 0
    for bit in range(size.bit_length() - 1):
        result = 2 * result + (value >> bit) % 2
    return result


@functools.lru_cache(None)
def unit_permutation(width, n_dp, n_mod):
    rows = width // (n_dp * n_mod)
    matrix = np.zeros((width, width), np.float32)
    for index in range(n_dp * n_mod):
        unit, rest = unit_of(index, n_mod)
        start = unit * (width // 8) + reversed_bits(rest, n_dp // 4) * rows
        matrix[start + np.arange(rows), index * rows + np.arange(rows)] = 1.0
    return matrix.astype(jnp.bfloat16)


def normed(v):
    centred = v - jnp.mean(v, axis=-1, keepdims=True)
    inverse = lax.rsqrt(jnp.mean(centred * centred, axis=-1, keepdims=True) + EPS)
    return centred * inverse, inverse


def norm_back(grad, scale_part, norm, inverse):
    e = grad * (1.0 + scale_part)
    return inverse * (
        e - jnp.mean(e, axis=-1, keepdims=True) - norm * jnp.mean(e * norm, axis=-1, keepdims=True)
    )


def part(mod_ref, slot, index, width):
    return mod_ref[pl.ds(slot, 1), index * width : (index + 1) * width]


def angles(coords_ref, cos_ref, sin_ref):
    value = lax.broadcasted_iota(jnp.int32, (GRID, 1), 0)
    hot = [(value == coords_ref[i : i + 1, :]).astype(f32) for i in range(2)]
    hot = jnp.concatenate(hot * 3, axis=0).astype(bf16)
    return tn(hot, cos_ref[...]), tn(hot, sin_ref[...])


def partner(v):
    width = v.shape[1]
    quarter = HD // 4
    lane = lax.broadcasted_iota(jnp.int32, (1, width), 1)
    leads = (lane // quarter) % 2 == 0
    return jnp.where(leads, pltpu.roll(v, width - quarter, 1), pltpu.roll(v, quarter, 1))


def head_sum(v, gather_ref):
    hi = v.astype(bf16)
    low = (v - hi.astype(f32)).astype(bf16)
    return nn(hi, gather_ref[...]) + nn(low, gather_ref[...])


def head_spread(v, spread_ref):
    hi, mid, low = split3(v)
    lane = lax.broadcasted_iota(jnp.int32, (1, 128), 1)
    chosen = jnp.where(lane < HEADS, hi, jnp.where(lane < 2 * HEADS, mid, low))
    return nn(chosen.astype(bf16), spread_ref[...])


def window(head, width):
    start = jnp.minimum((head * HD) // 128, width // 128 - WIN // 128) * 128
    return pl.multiple_of(start, 128), head * HD - start


def head_lanes(offset):
    lane = lax.broadcasted_iota(jnp.int32, (1, WIN), 1)
    return (lane >= offset) & (lane < offset + HD)


def product(units_ref, half, rhs, out_ref):
    _, rows, tokens = units_ref.shape
    units = units_ref[pl.ds(4 * half, 4)].reshape(4 * rows, tokens)
    out_ref[...] = nn(units, rhs).astype(bf16).reshape(out_ref.shape)


def halves_out(acc_ref, core, send_ref, own_ref):
    rows = acc_ref.shape[0] // 2
    for half, out_ref in ((1 - core, send_ref), (core, own_ref)):
        start = pl.multiple_of(half * rows, rows)
        out_ref[...] = acc_ref[pl.ds(start, rows)].astype(bf16).reshape(out_ref.shape)


def project_kernel(
    slots, x_ref, mod_ref, w_ref, coords_ref, cos_ref, sin_ref, gain_ref, gather_ref, spread_ref,
    perm_ref, units_ref, raw_ref, inv_ref, q_ref, k_ref, v_ref, kt_ref,
):
    width = x_ref.shape[1]
    slot = slots[pl.program_id(0)]
    norm, _ = normed(x_ref[...].astype(f32))
    low = (norm * (1.0 + part(mod_ref, slot, 1, width)) + part(mod_ref, slot, 0, width)).astype(bf16)
    units_ref[...] = nt(perm_ref[...], low).astype(bf16).reshape(units_ref.shape)
    cosine, sine = angles(coords_ref, cos_ref, sin_ref)
    for index, out_ref in enumerate((q_ref, k_ref)):
        raw = nn(low, w_ref[:, index * width : (index + 1) * width])
        raw_ref[:, index * width : (index + 1) * width] = raw
        inverse = lax.rsqrt(head_sum(raw * raw, gather_ref) * (1.0 / HD) + EPS)
        inv_ref[:, index * 128 : (index + 1) * 128] = inverse
        scaled = raw * head_spread(inverse, spread_ref) * gain_ref[index : index + 1, :]
        turned = scaled * cosine + partner(scaled) * sine
        out_ref[...] = turned.astype(bf16)
        if index == 1:
            kt_ref[...] = turned.T.astype(bf16)
    v_ref[...] = nn(low, w_ref[:, 2 * width :]).astype(bf16)


def attend_kernel(
    slots, x_ref, cot_ref, mod_ref, q_ref, k_ref, v_ref, w_out_ref, perm_ref,
    o_ref, lse_ref, attn_ref, mid_ref, low_ref, gf_ref, att_units_ref, ffn_units_ref, lse_acc,
):
    block = pl.program_id(0)
    width = x_ref.shape[1]
    tokens = k_ref.shape[0]
    lane128 = lax.broadcasted_iota(jnp.int32, (1, 128), 1)
    lane = lax.broadcasted_iota(jnp.int32, (1, WIN), 1)
    o_ref[...] = jnp.zeros_like(o_ref)
    lse_acc[...] = jnp.zeros_like(lse_acc)

    def run(rows):
        def head(h, carry):
            start, offset = window(h, width)
            inside = head_lanes(offset)
            columns = pl.ds(start, WIN)
            query = jnp.where(inside, q_ref[:, columns], 0)
            value = jnp.where(inside, v_ref[rows, columns], 1)
            weight = jnp.exp2(nt(query, k_ref[rows, columns]) * SCORE_LOG2).astype(bf16)
            summed = nn(weight, value)
            free = jnp.where(offset > 0, 0, WIN - 1)
            total = jnp.sum(jnp.where(lane == free, summed, 0.0), axis=1, keepdims=True)
            o_ref[:, columns] += jnp.where(inside, summed * (1.0 / total), 0.0)
            lse_acc[...] += jnp.where(lane128 == h, jnp.log2(total), 0.0)
            return carry

        lax.fori_loop(0, HEADS, head, 0, unroll=2)

    whole = slots[tokens // TB - 1] == slots[0]

    @pl.when(whole)
    def _():
        run(slice(None))

    @pl.when(jnp.logical_not(whole))
    def _():
        run(pl.ds(pl.multiple_of(block * TB, TB), TB))

    lse_ref[...] = lse_acc[...].T
    slot = slots[block]
    attended = o_ref[...].astype(bf16)
    att_units_ref[...] = nt(perm_ref[...], attended).astype(bf16).reshape(att_units_ref.shape)
    attn = nn(attended, w_out_ref[...])
    attn_ref[...] = attn
    mid = x_ref[...].astype(f32) + part(mod_ref, slot, 2, width) * attn
    mid_ref[...] = mid
    norm, _ = normed(mid)
    low = (norm * (1.0 + part(mod_ref, slot, 4, width)) + part(mod_ref, slot, 3, width)).astype(bf16)
    low_ref[...] = low
    ffn_units_ref[...] = nt(perm_ref[...], low).astype(bf16).reshape(ffn_units_ref.shape)
    gf_ref[...] = (cot_ref[...].astype(f32) * part(mod_ref, slot, 5, width)).astype(bf16)


def ffn_kernel(
    bits, x_ref, gf_ref, units_ref, wg_ref, wu_ref, wd_ref,
    gate_send_ref, gate_own_ref, up_send_ref, up_own_ref, down_send_ref, down_own_ref, ffn_ref, dmod_ref,
    turned_ref, *, n_mod, rows_ff,
):
    core = bits[0]
    gate = nn(x_ref[...], wg_ref[...])
    up = nn(x_ref[...], wu_ref[...])
    grad_hidden = nt(gf_ref[...], wd_ref[...])
    sigmoid = 1.0 / (1.0 + jnp.exp(-gate))
    silu = gate * sigmoid
    hidden = (silu * up).astype(bf16)
    turned = hidden.T
    for index in range(turned.shape[0] // rows_ff):
        unit, rest = unit_of(index, n_mod)
        turned_ref[unit, rest * rows_ff : (rest + 1) * rows_ff] = turned[
            index * rows_ff : (index + 1) * rows_ff
        ]
    dg = (grad_hidden * up * (sigmoid * (1.0 + gate * (1.0 - sigmoid)))).astype(bf16)
    du = (grad_hidden * silu).astype(bf16)

    @pl.when(pl.program_id(0) == 0)
    def _():
        ffn_ref[...] = jnp.zeros_like(ffn_ref)
        dmod_ref[...] = jnp.zeros_like(dmod_ref)

    ffn_ref[...] += nn(hidden, wd_ref[...])
    dmod_ref[...] += nt(dg, wg_ref[...]) + nt(du, wu_ref[...])
    product(units_ref, 1 - core, dg, gate_send_ref)
    product(units_ref, 1 - core, du, up_send_ref)
    product(turned_ref, 1 - core, gf_ref[...], down_send_ref)
    product(units_ref, core, dg, gate_own_ref)
    product(units_ref, core, du, up_own_ref)
    product(turned_ref, core, gf_ref[...], down_own_ref)


def middle_kernel(
    slots, mid_ref, ffn_ref, dmod_ref, cot_ref, attn_ref, o_ref, units_ref, mod_ref, w_out_ref, gather_ref,
    out_ref, grad_mid_ref, do_ref, dot_ref, sums_ref, send_ref, own_ref, acc_ref,
):
    width = mid_ref.shape[1]
    block = pl.program_id(0)
    slot = slots[block]
    incoming = cot_ref[...].astype(f32)
    mid = mid_ref[...]
    out_ref[...] = (mid + part(mod_ref, slot, 5, width) * ffn_ref[...]).astype(bf16)
    norm, inverse = normed(mid)
    dmod = dmod_ref[...]
    grad_mid = incoming + norm_back(dmod, part(mod_ref, slot, 4, width), norm, inverse)
    grad_mid_ref[...] = grad_mid
    ga = (grad_mid * part(mod_ref, slot, 2, width)).astype(bf16)
    grow = nn(units_ref[...].reshape(width, TB), ga)

    @pl.when(block == 0)
    def _():
        acc_ref[...] = grow

    @pl.when(block > 0)
    def _():
        acc_ref[...] += grow

    @pl.when(block == pl.num_programs(0) - 1)
    def _():
        halves_out(acc_ref, slots[pl.num_programs(0)], send_ref, own_ref)

    do = nt(ga, w_out_ref[...]).astype(bf16)
    do_ref[...] = do
    dot_ref[...] = head_sum(do.astype(f32) * o_ref[...], gather_ref).T

    @pl.when(block == 0)
    def _():
        sums_ref[...] = jnp.zeros_like(sums_ref)

    for index, term in enumerate((grad_mid * attn_ref[...], dmod, dmod * norm, incoming * ffn_ref[...])):
        columns = slice(index * width, (index + 1) * width)
        sums_ref[pl.ds(slot, 1), columns] += jnp.sum(term, axis=0, keepdims=True)


def attend_back_kernel(
    slots, q_ref, k_ref, v_ref, do_ref, lse_ref, dot_ref, kt_ref, dqt_ref, dk_ref, dv_low_ref, dv_ref
):
    h = pl.program_id(0)
    tokens, width = q_ref.shape

    @pl.when(h == 0)
    def _():
        dqt_ref[...] = jnp.zeros_like(dqt_ref)
        dk_ref[...] = jnp.zeros_like(dk_ref)
        dv_ref[...] = jnp.zeros_like(dv_ref)

    start, offset = window(h, width)
    inside = head_lanes(offset)
    columns = pl.ds(start, WIN)
    first_row = pl.multiple_of((h * HD) // 16 * 16, 16)
    row = lax.broadcasted_iota(jnp.int32, (HD + 8, 1), 0) + first_row
    own_rows = (row >= h * HD) & (row < h * HD + HD)

    def step(rows):
        query = q_ref[rows, columns]
        grad_out = do_ref[rows, columns]
        key = jnp.where(inside, k_ref[rows, columns], 0)
        value = jnp.where(inside, v_ref[rows, columns], 0)
        probs = jnp.exp2(nt(key, query) * SCORE_LOG2 - lse_ref[pl.ds(h, 1), rows])
        scores = (probs * (nt(value, grad_out) - dot_ref[pl.ds(h, 1), rows])).astype(bf16)
        dv_ref[rows, columns] += jnp.where(inside, nn(probs.astype(bf16), grad_out), 0.0)
        dk_ref[rows, columns] += jnp.where(inside, nn(scores, query) * SCORE_SCALE, 0.0)
        turned = nn(kt_ref[pl.ds(first_row, HD + 8), rows], scores) * SCORE_SCALE
        dqt_ref[pl.ds(first_row, HD + 8), rows] += jnp.where(own_rows, turned, 0.0)

    whole = slots[tokens // TB - 1] == slots[0]

    @pl.when(whole)
    def _():
        step(slice(None))

    @pl.when(jnp.logical_not(whole))
    def _():
        def block(i, carry):
            step(pl.ds(pl.multiple_of(i * TB, TB), TB))
            return carry

        lax.fori_loop(0, tokens // TB, block, 0)

    @pl.when(h == HEADS - 1)
    def _():
        dv_low_ref[...] = dv_ref[...].astype(bf16)


def project_back_kernel(
    slots, dqt_ref, dk_ref, dv_ref, raw_ref, inv_ref, q_ref, k_ref, x_ref, grad_mid_ref, units_ref, mod_ref,
    w_ref, coords_ref, cos_ref, sin_ref, gain_ref, gather_ref, spread_ref, other_sums_ref,
    grad_x_ref, gains_ref, grad_own_ref, grad_other_ref, q_send_ref, q_own_ref, k_send_ref, k_own_ref,
    accq_ref, acck_ref, sums_ref,
):
    width = x_ref.shape[1]
    block = pl.program_id(0)
    last_block = pl.num_programs(0) - 1
    slot = slots[block]

    @pl.when(block == 0)
    def _():
        gains_ref[...] = jnp.zeros_like(gains_ref)
        accq_ref[...] = jnp.zeros_like(accq_ref)
        acck_ref[...] = jnp.zeros_like(acck_ref)

    dmod = nt(dv_ref[...], w_ref[:, 2 * width :])

    cosine, sine = angles(coords_ref, cos_ref, sin_ref)
    for index, (low_ref, acc_ref) in enumerate(((q_ref, accq_ref), (k_ref, acck_ref))):
        grad = dqt_ref[...].T if index == 0 else dk_ref[...]
        raw = raw_ref[:, index * width : (index + 1) * width]
        inverse = head_spread(inv_ref[:, index * 128 : (index + 1) * 128], spread_ref)
        mean = head_sum(grad * low_ref[...].astype(f32), gather_ref) * (1.0 / HD)
        norm = raw * inverse
        back = grad * cosine - partner(grad) * sine
        gains_ref[index : index + 1, :] += jnp.sum(back * norm, axis=0, keepdims=True)
        grad_raw = (
            inverse * (back * gain_ref[index : index + 1, :] - norm * head_spread(mean, spread_ref))
        ).astype(bf16)
        acc_ref[...] += nn(units_ref[...].reshape(width, TB), grad_raw)
        dmod = dmod + nt(grad_raw, w_ref[:, index * width : (index + 1) * width])

    @pl.when(block == pl.num_programs(0) - 1)
    def _():
        halves_out(accq_ref, slots[pl.num_programs(0)], q_send_ref, q_own_ref)
        halves_out(acck_ref, slots[pl.num_programs(0)], k_send_ref, k_own_ref)

    norm, inverse = normed(x_ref[...].astype(f32))
    grad_x = grad_mid_ref[...] + norm_back(dmod, part(mod_ref, slot, 1, width), norm, inverse)
    grad_x_ref[...] = grad_x.astype(bf16)

    @pl.when(block == 0)
    def _():
        sums_ref[...] = jnp.zeros_like(sums_ref)

    for index, term in enumerate((dmod, dmod * norm)):
        columns = slice(index * width, (index + 1) * width)
        sums_ref[pl.ds(slot, 1), columns] += jnp.sum(term, axis=0, keepdims=True)

    @pl.when(block == last_block)
    def _():
        mod = slots[last_block + 2]
        count = sums_ref.shape[0]
        mine = jnp.concatenate([sums_ref[...]] * 2, axis=0)
        rest = jnp.concatenate([other_sums_ref[...]] * 2, axis=0)
        row = lax.broadcasted_iota(jnp.int32, (2 * count, 1), 0) // count
        attn_part = jnp.where(row == mod, jnp.concatenate([mine, rest[:, :width]], axis=1), 0.0)
        ffn_part = jnp.where(row == mod, rest[:, width:], 0.0)
        grad_own_ref[...] = jnp.where(mod == 0, attn_part, ffn_part).astype(bf16)
        grad_other_ref[...] = jnp.where(mod == 0, ffn_part, attn_part).astype(bf16)


def value_kernel(bits, units_ref, rhs_ref, send_ref, own_ref):
    product(units_ref, 1 - bits[0], rhs_ref[...], send_ref)
    product(units_ref, bits[0], rhs_ref[...], own_ref)


def split_step(bits, ins, outs, *, lead, at, bit, pair_rows):
    own_ref, got_ref = ins
    send_ref, keep_ref = outs
    mine = bits[bit]

    def total(*index):
        return own_ref[index].astype(f32) + got_ref[index].astype(f32)

    if at is None:
        for j in range(max(lead, 1)):
            index = (j,) if lead else ()
            value = total(*index) if lead else own_ref[...].astype(f32) + got_ref[...].astype(f32)
            rows = pair_rows or value.shape[0] // 2
            for p in range(value.shape[0] // (2 * rows)):
                first = value[2 * p * rows : (2 * p + 1) * rows]
                second = value[(2 * p + 1) * rows : (2 * p + 2) * rows]
                place = index + (slice(p * rows, (p + 1) * rows),)
                send_ref[place] = jnp.where(mine == 1, first, second).astype(bf16)
                keep_ref[place] = jnp.where(mine == 1, second, first)
        return
    for j in range(lead // 2):
        place = (j,) if lead > 2 else (Ellipsis,)
        away = 1 - mine if lead == 2 else 2 * (1 - mine) + j if at == 0 else 2 * j + 1 - mine
        own = mine if lead == 2 else 2 * mine + j if at == 0 else 2 * j + mine
        send_ref[place] = total(away).astype(bf16)
        keep_ref[place] = total(own)


def sum_step(bits, ins, outs):
    outs[0][...] = ins[0][...] + ins[1][...]


def pair_step(bits, ins, outs):
    own_ref, got_ref, activated_ref = ins
    width = activated_ref.shape[1]
    outs[0][:, :width] = activated_ref[...]
    outs[0][:, width:] = (own_ref[...].astype(f32) + got_ref[...].astype(f32)).astype(bf16)


def joined(ins):
    return jnp.concatenate([ref[...].astype(f32) for ref in ins], axis=0).astype(bf16)


def join_step(bits, ins, outs):
    outs[0][...] = joined(ins)


def last_step(bits, ins, outs):
    outs[0][...] = ins[0][...] + ins[1][...].astype(f32)


def ada_step(bits, ins, outs, *, width):
    rows = outs[0].shape[0]
    every = joined(ins)
    position = bits[0] + sum(bits[1 + k] * 2**k for k in range(1, (width // rows).bit_length() - 1))
    feature = lax.broadcasted_iota(jnp.int32, (width, 128), 0)
    place = lax.broadcasted_iota(jnp.int32, (width, 128), 1)
    chosen = (feature == position * rows + place) & (place < rows)
    own = nn(every[:, :width], chosen.astype(f32).astype(bf16)).astype(bf16)
    outs[0][...] = tn(own, every[:, width:])[:rows]


def step_kernel(bits, *refs, plans):
    n_in = sum(plan[1] for plan in plans)
    ins, outs = refs[:n_in], refs[n_in:]
    for function, takes, gives in plans:
        function(bits, ins[:takes], outs[:gives])
        ins, outs = ins[takes:], outs[gives:]


class Chain:
    def __init__(self):
        self.last = None

    def __call__(
        self, kernel, grid, in_specs, out_specs, out_shape, args, scalars=None, scratch=(), name=None, aliases=None
    ):
        ahead = 0 if scalars is None else 1
        body = kernel
        token = ()
        if self.last is not None:
            token = (self.last,)
            in_specs = [pl.BlockSpec(memory_space=pl.ANY)] + list(in_specs)

            def body(*refs):
                kernel(*refs[:ahead], *refs[ahead + 1 :])

        spec = pltpu.PrefetchScalarGridSpec(
            num_scalar_prefetch=ahead,
            grid=grid,
            in_specs=in_specs,
            out_specs=out_specs,
            scratch_shapes=scratch,
        )
        outs = pl.pallas_call(
            body,
            grid_spec=spec,
            input_output_aliases=aliases or {},
            out_shape=out_shape,
            compiler_params=pltpu.CompilerParams(vmem_limit_bytes=VMEM),
            cost_estimate=pl.CostEstimate(flops=1, bytes_accessed=1, transcendentals=0),
            name=name,
        )(*(() if scalars is None else (scalars,)), *token, *args)
        self.last = outs[0]
        return outs


def shape(dims, dtype):
    return jax.ShapeDtypeStruct(dims, dtype)


def fixed(dims):
    return pl.BlockSpec(dims, lambda *_: (0,) * len(dims), pipeline_mode=pl.Buffered(1))


def rows_of(dims, axis=0):
    return pl.BlockSpec(dims, lambda b, *_: tuple(b if i == axis else 0 for i in range(len(dims))))


def whole(dims):
    return rows_of(dims, None)


def column_parts(dims, steps):
    return rows_of(dims[:-1] + (dims[-1] // steps,), len(dims) - 1)


class Reducer:
    def __init__(self, n_dp, n_mod, call):
        self.n_dp, self.n_mod, self.call = n_dp, n_mod, call
        self.position = lax.axis_index("dp")
        steps = range(n_dp.bit_length() - 1)
        dp_bits = [lax.shift_right_logical(self.position, step) & 1 for step in steps]
        self.bits = jnp.stack([dp_bits[0], lax.axis_index("mod")] + dp_bits[1:]).astype(jnp.int32)

    def swap(self, arr, bit):
        if bit == "mod":
            return lax.ppermute(arr, "mod", [(i, i ^ 1) for i in range(self.n_mod)])
        return lax.ppermute(arr, "dp", [(i, i ^ (1 << bit)) for i in range(self.n_dp)])

    def bit_of(self, bit):
        return 1 if bit == "mod" else bit + 1 if bit else 0

    def fold(self, streams, name, last=False):
        plans, args, outs = [], [], []
        for stream in streams:
            function, shapes = stream.last_plan() if last else stream.plan()
            inputs = stream.inputs()
            plans.append((function, len(inputs), len(shapes)))
            args += inputs
            outs += shapes
        steps = 3 if not last and len(streams) == 1 and args[0].ndim == 3 and args[0].shape[-1] % 384 == 0 else 1
        results = self.call(
            functools.partial(step_kernel, plans=plans),
            (steps,),
            [column_parts(arg.shape, steps) for arg in args],
            [column_parts(out.shape, steps) for out in outs],
            outs,
            args,
            scalars=self.bits,
            name=name,
        )
        results = list(results)
        if last:
            return results
        for stream, plan in zip(streams, plans):
            stream.step(results[: plan[2]])
            results = results[plan[2] :]

    def pass_on(self, arrays):
        anywhere = [pl.BlockSpec(memory_space=pl.ANY)] * len(arrays)
        return self.call(
            lambda *refs: None,
            (1,),
            anywhere,
            anywhere,
            [shape(arr.shape, arr.dtype) for arr in arrays],
            arrays,
            name="pass_on",
            aliases={i + 1: i for i in range(len(arrays))},
        )


class Stream:
    def __init__(self, reducer, sent, own, first, pair_rows=None):
        self.r, self.own, self.pair_rows = reducer, own, pair_rows
        order = ["mod", 1, 2]
        self.steps = order[first:] + order[:first] + list(range(3, reducer.n_dp.bit_length() - 1))
        self.lead = ["mod", 1]
        self.got = reducer.swap(sent, 0)

    def inputs(self):
        return [self.own, self.got]

    def plan(self):
        bit = self.steps[0]
        dims = self.own.shape
        at = self.lead.index(bit) if bit in self.lead else None
        function = functools.partial(
            split_step, lead=dims[0] if self.lead else 0, at=at, bit=self.r.bit_of(bit), pair_rows=self.pair_rows
        )
        if at is None:
            dims = dims[:-2] + (dims[-2] // 2, dims[-1])
        else:
            dims = dims[1:] if len(self.lead) == 1 else (2,) + dims[1:]
        return function, [shape(dims, bf16), shape(dims, f32)]

    def step(self, results):
        bit = self.steps.pop(0)
        if bit in self.lead:
            self.lead.remove(bit)
        sent, self.own = results
        self.got = self.r.swap(sent, bit)

    def last_plan(self):
        return last_step, [shape(self.own.shape, f32)]


class Total:
    def __init__(self, reducer, own):
        self.r, self.own = reducer, own
        self.steps = ["mod"] + list(range(1, reducer.n_dp.bit_length() - 1))
        self.got = reducer.swap(own, 0)

    def inputs(self):
        return [self.own, self.got]

    def plan(self):
        return sum_step, [shape(self.own.shape, f32)]

    def step(self, results):
        (self.own,) = results
        self.got = self.r.swap(self.own, self.steps.pop(0))

    def last_plan(self):
        return self.plan()


class Gather:
    def __init__(self, reducer, sent, own, activated):
        self.r, self.own, self.activated = reducer, own, activated
        self.steps = list(range(reducer.n_dp.bit_length() - 2, -1, -1))
        self.got = reducer.swap(sent, "mod")
        self.pair = None

    def inputs(self):
        return [self.own, self.got] + ([self.activated] if self.pair is None else [])

    def plan(self):
        rows, columns = self.own.shape
        if self.pair is None:
            return pair_step, [shape((rows, columns + self.activated.shape[1]), bf16)]
        return join_step, [shape((2 * rows, columns), bf16)]

    def step(self, results):
        (self.own,) = results
        if self.pair is None:
            self.pair = self.own
        self.got = self.r.swap(self.own, self.steps.pop(0))

    def last_plan(self):
        width = self.activated.shape[1]
        function = functools.partial(ada_step, width=width)
        return function, [shape((width // self.r.n_dp, self.own.shape[1] - width), f32)]


def silu_grad(v):
    sigmoid = jax.nn.sigmoid(v)
    return sigmoid * (1.0 + v * (1.0 - sigmoid))


def pair_order(own, other, mod):
    return jnp.where(mod == 0, jnp.stack([own, other]), jnp.stack([other, own]))


def body(
    n_dp, n_mod, tokens, cond, segments, coords, w_ada, w_qkv, q_gain, k_gain, w_out, w_gate, w_up,
    w_down, cotangent,
):
    _, count, width = tokens.shape
    slots_n = cond.shape[1]
    half = w_ada.shape[1]
    ff = w_gate.shape[1]
    blocks = count // TB
    n_dev = n_dp * n_mod
    call = Chain()
    reducer = Reducer(n_dp, n_mod, call)
    mod_index = lax.axis_index("mod")
    x = tokens[0]
    cot = cotangent[0]
    slots = segments[0, ::TB]
    coord = coords[0]
    cos_table, sin_table = (jnp.asarray(t) for t in rope_tables(width))
    gather, spread = (jnp.asarray(t) for t in head_tables(width))
    perm = jnp.asarray(unit_permutation(width, n_dp, n_mod))
    gains = jnp.stack([jnp.tile(q_gain, HEADS), jnp.tile(k_gain, HEADS)])

    cond_both = pair_order(cond[0], reducer.swap(cond[0], "mod"), mod_index)
    activated = jax.nn.silu(cond_both).astype(bf16).reshape(-1, width)
    mod_half = jnp.dot(activated, w_ada, preferred_element_type=f32).astype(bf16)
    mod_half = mod_half.reshape(n_mod, slots_n, half)
    own_half = lax.dynamic_index_in_dim(mod_half, mod_index, 0, keepdims=False)
    other_half = lax.dynamic_index_in_dim(mod_half, 1 - mod_index, 0, keepdims=False)
    pair = pair_order(own_half, reducer.swap(other_half, "mod"), mod_index)
    modulation = jnp.concatenate([pair[0], pair[1]], axis=1).astype(f32)

    token_f32 = shape((count, width), f32)
    token_bf16 = shape((count, width), bf16)
    units = shape((8, width // 8, count), bf16)
    units_spec = rows_of((8, width // 8, TB), 2)
    token_spec = rows_of((TB, width))
    mod_spec = fixed((slots_n, 6 * width))
    square = fixed((width, width))
    table_specs = [fixed(cos_table.shape), fixed(sin_table.shape), fixed((2, width)), fixed(gather.shape), fixed(spread.shape)]
    tables = (cos_table, sin_table, gains, gather, spread)
    lane_rows = shape((128, count), f32)
    macs = count * width * width

    attn_units, raw, inverse, query, key, value, key_t = call(
        project_kernel,
        (blocks,),
        [token_spec, mod_spec, fixed((width, 3 * width)), rows_of((2, TB), 1)] + table_specs + [square],
        [units_spec, rows_of((TB, 2 * width)), rows_of((TB, 256))] + [token_spec] * 3 + [rows_of((width, TB), 1)],
        [units, shape((count, 2 * width), f32), shape((count, 256), f32)] + [token_bf16] * 3
        + [shape((width, count), bf16)],
        (x, modulation, w_qkv, coord) + tables + (perm,),
        scalars=slots,
        name="project",
    )
    attended, lse, attn, mid, ffn_in, grad_ffn, out_units, ffn_units = call(
        attend_kernel,
        (blocks,),
        [token_spec, token_spec, mod_spec, token_spec] + [fixed((count, width))] * 2 + [square, square],
        [token_spec, rows_of((128, TB), 1)] + [token_spec] * 4 + [units_spec] * 2,
        [token_f32, lane_rows, token_f32, token_f32, token_bf16, token_bf16, units, units],
        (x, cot, modulation, query, key, value, w_out, perm),
        scalars=slots,
        scratch=[pltpu.VMEM((TB, 128), f32)],
        name="attend",
    )

    rows_ff = ff // n_dev
    chunk = 768
    piece = chunk // 8
    half_units = lambda rows, columns: shape((4, rows, columns), bf16)
    square_send = [fixed((4, width // 8, width))] * 2
    square_shapes = [half_units(width // 8, width)] * 2
    gate_send, gate_own, up_send, up_own, down_send, down_own, ffn, grad_mod_ffn = call(
        functools.partial(ffn_kernel, n_mod=n_mod, rows_ff=rows_ff),
        (ff // chunk,),
        [fixed((count, width))] * 2 + [fixed(units.shape)]
        + [rows_of((width, chunk), 1)] * 2 + [rows_of((chunk, width))],
        [rows_of((4, width // 8, chunk), 2)] * 4
        + [rows_of((4, 1, piece, width), 1)] * 2 + [fixed((count, width))] * 2,
        [half_units(width // 8, ff)] * 4
        + [shape((4, ff // chunk, piece, width), bf16)] * 2 + [token_f32] * 2,
        (ffn_in, grad_ffn, ffn_units, w_gate, w_up, w_down),
        scalars=reducer.bits,
        scratch=[pltpu.VMEM((8, piece, count), bf16)],
        name="ffn",
    )
    gate = Stream(reducer, gate_send, gate_own, 0)
    up = Stream(reducer, up_send, up_own, 1)
    down = Stream(
        reducer, down_send.reshape(4, ff // 8, width), down_own.reshape(4, ff // 8, width), 2, rows_ff
    )

    slots_core = jnp.concatenate([slots, reducer.bits[:2]])
    output, grad_mid, grad_attended, dot_term, sums_b, out_send, out_own = call(
        middle_kernel,
        (blocks,),
        [token_spec] * 6 + [units_spec, mod_spec, square, fixed(gather.shape)],
        [token_spec] * 3 + [rows_of((128, TB), 1), fixed((slots_n, 4 * width))] + square_send,
        [token_bf16, token_f32, token_bf16, lane_rows, shape((slots_n, 4 * width), f32)] + square_shapes,
        (mid, ffn, grad_mod_ffn, cot, attn, attended, out_units, modulation, w_out, gather),
        scalars=slots_core,
        scratch=[pltpu.VMEM((width, width), f32)],
        name="middle",
    )
    out = Stream(reducer, out_send, out_own, 1)
    reducer.fold([gate], "gate")
    reducer.fold([up], "up")
    reducer.fold([down], "down")
    reducer.fold([out], "out")

    grad_query_t, grad_key, grad_value = call(
        attend_back_kernel,
        (HEADS,),
        [fixed((count, width))] * 4 + [fixed((128, count))] * 2 + [fixed((width, count))],
        [fixed((width, count))] + [fixed((count, width))] * 2,
        [shape((width, count), f32), token_f32, token_bf16],
        (query, key, value, grad_attended, lse, dot_term, key_t),
        scratch=[pltpu.VMEM((count, width), f32)],
        scalars=slots,
        name="attend_back",
    )
    reducer.fold([gate], "gate")
    reducer.fold([up], "up")
    reducer.fold([down], "down")
    reducer.fold([out], "out")
    v_send, v_own = call(
        value_kernel,
        (1,),
        [whole(units.shape), whole((count, width))],
        [whole((4, width // 8, width))] * 2,
        square_shapes,
        (attn_units, grad_value),
        scalars=reducer.bits,
        name="value",
    )
    v_part = Stream(reducer, v_send, v_own, 2)
    grad_tokens, gain_sums, mod_own, mod_other, q_send, q_own, k_send, k_own = call(
        project_back_kernel,
        (blocks,),
        [rows_of((width, TB), 1), token_spec, token_spec, rows_of((TB, 2 * width)), rows_of((TB, 256))]
        + [token_spec] * 4
        + [units_spec, mod_spec, fixed((width, 3 * width)), rows_of((2, TB), 1)]
        + table_specs + [fixed((slots_n, 4 * width))],
        [token_spec, fixed((2, width))] + [fixed((2 * slots_n, half))] * 2 + square_send * 2,
        [token_bf16, shape((2, width), f32)] + [shape((2 * slots_n, half), bf16)] * 2 + square_shapes * 2,
        (grad_query_t, grad_key, grad_value, raw, inverse, query, key, x, grad_mid, attn_units, modulation,
         w_qkv, coord)
        + tables + (sums_b,),
        scalars=slots_core,
        scratch=[pltpu.VMEM((width, width), f32)] * 2 + [pltpu.VMEM((slots_n, 2 * width), f32)],
        name="project_back",
    )
    early = [gate, up, down, out]
    arrived = [stream.got for stream in early + [v_part]]
    *arrived, q_send, k_send, mod_other, gain_sums = reducer.pass_on(
        arrived + [q_send, k_send, mod_other, gain_sums]
    )
    for stream, got in zip(early + [v_part], arrived):
        stream.got = got
    q_part = Stream(reducer, q_send, q_own, 1)
    k_part = Stream(reducer, k_send, k_own, 0)
    gains_total = Total(reducer, gain_sums)
    every_mod = Gather(reducer, mod_other, mod_own, activated)
    late = [q_part, k_part, gains_total, every_mod]
    reducer.fold([v_part], "v")
    reducer.fold(early, "early")
    reducer.fold(late, "late")
    for _ in range(n_dp.bit_length() - 4):
        reducer.fold(early, "early")
        reducer.fold([v_part] + late, "late")
    summed_gate, summed_up, summed_down, summed_out = reducer.fold(early, "early", last=True)
    reducer.fold([v_part] + late, "late")
    reducer.fold([v_part] + late, "late")
    *summed, gain_sums, grad_w_ada = reducer.fold([v_part] + late, "late", last=True)
    summed_qkv = jnp.concatenate([summed[1], summed[2], summed[0]], axis=1)

    grad_activated = jnp.einsum("nc,dc->nd", every_mod.pair[:, width:], w_ada, preferred_element_type=f32)
    grad_activated = grad_activated.reshape(n_mod, slots_n, width)
    own_part = lax.dynamic_index_in_dim(grad_activated, mod_index, 0, keepdims=False)
    other_part = lax.dynamic_index_in_dim(grad_activated, 1 - mod_index, 0, keepdims=False)
    grad_own = own_part + reducer.swap(other_part.astype(bf16), "mod").astype(f32)
    grad_cond = grad_own[None] * silu_grad(cond)
    gain_grads = jnp.sum(gain_sums.reshape(2, HEADS, HD), axis=1)
    return (
        output[None],
        grad_tokens[None],
        grad_cond,
        grad_w_ada,
        summed_qkv,
        gain_grads[0],
        gain_grads[1],
        summed_out,
        summed_gate,
        summed_up,
        summed_down,
    )


def solution(mesh):
    rows = ("dp", "mod")
    in_specs = (
        P(rows, None, None),
        P(rows, None, None),
        P(rows, None),
        P(rows, None, None),
        P(None, "mod"),
        P(),
        P(),
        P(),
        P(),
        P(),
        P(),
        P(),
        P(rows, None, None),
    )
    out_specs = (
        P(rows, None, None),
        P(rows, None, None),
        P(rows, None, None),
        P("dp", "mod"),
        P(rows, None),
        P(),
        P(),
        P(rows, None),
        P(rows, None),
        P(rows, None),
        P(rows, None),
    )
    return jax.shard_map(
        functools.partial(body, mesh.shape["dp"], mesh.shape["mod"]),
        mesh=mesh,
        in_specs=in_specs,
        out_specs=out_specs,
        check_vma=False,
    )
```

```python
import functools

import jax
import jax.numpy as jnp
import numpy as np
from jax import lax
from jax.experimental import pallas as pl
from jax.experimental.pallas import tpu as pltpu
from jax.sharding import PartitionSpec as P

HEADS = 16
HD = 72
GRID = 32
EPS = 1e-06
ROPE_BASE = 10000.0
TB = 256
WIN = 256
SCORE_SCALE = float(HD**-0.5)
SCORE_LOG2 = float(np.log2(np.e) * HD**-0.5)
VMEM = 60 * 2**20
f32 = jnp.float32
bf16 = jnp.bfloat16


def nn(a, b):
    return lax.dot_general(a, b, (((1,), (0,)), ((), ())), preferred_element_type=f32)


def nt(a, b):
    return lax.dot_general(a, b, (((1,), (1,)), ((), ())), preferred_element_type=f32)


def tn(a, b):
    return lax.dot_general(a, b, (((0,), (0,)), ((), ())), preferred_element_type=f32)


def split3(v):
    hi = v.astype(bf16).astype(f32)
    mid = (v - hi).astype(bf16).astype(f32)
    return hi, mid, v - hi - mid


def np_split3(v):
    v = v.astype(np.float32)
    hi = v.astype(jnp.bfloat16).astype(np.float32)
    mid = (v - hi).astype(jnp.bfloat16).astype(np.float32)
    return [part.astype(jnp.bfloat16) for part in (hi, mid, v - hi - mid)]


@functools.lru_cache(None)
def rope_tables(width):
    quarter = HD // 4
    freqs = ROPE_BASE ** (-np.arange(quarter, dtype=np.float64) / quarter)
    lane = np.arange(width) % HD
    group = lane // quarter
    angle = np.arange(GRID)[:, None] * freqs[lane % quarter][None, :]
    cosine, sine = np.cos(angle), np.sin(angle)
    sine = np.where((group % 2 == 0)[None, :], -sine, sine)
    uses_col = (group >= 2)[None, :]
    tables = []
    for table in (cosine, sine):
        whole = np.concatenate(
            [np.where(uses_col, 0.0, table), np.where(uses_col, table, 0.0)], axis=0
        )
        tables.append(np.concatenate(np_split3(whole), axis=0))
    return tables


@functools.lru_cache(None)
def head_tables(width):
    head = np.arange(width) // HD
    gather = np.zeros((width, 128), np.float32)
    for copy in range(3):
        gather[np.arange(width), copy * HEADS + head] = 1.0
    fold = np.zeros((width, 128), np.float32)
    fold[np.arange(width), np.arange(width) % HD] = 1.0
    return gather.astype(jnp.bfloat16), gather.T.astype(jnp.bfloat16), fold.astype(jnp.bfloat16)


def unit_of(index, n_mod):
    mod = index % n_mod
    dp = index // n_mod
    return (dp % 2) * 2 * n_mod + mod * 2 + (dp // 2) % 2, dp // 4


def reversed_bits(value, size):
    result = 0
    for bit in range(size.bit_length() - 1):
        result = 2 * result + (value >> bit) % 2
    return result


@functools.lru_cache(None)
def unit_permutation(width, n_dp, n_mod):
    rows = width // (n_dp * n_mod)
    matrix = np.zeros((width, width), np.float32)
    for index in range(n_dp * n_mod):
        unit, rest = unit_of(index, n_mod)
        start = unit * (width // 8) + reversed_bits(rest, n_dp // 4) * rows
        matrix[start + np.arange(rows), index * rows + np.arange(rows)] = 1.0
    return matrix.astype(jnp.bfloat16)


def normed(v):
    centred = v - jnp.mean(v, axis=-1, keepdims=True)
    inverse = lax.rsqrt(jnp.mean(centred * centred, axis=-1, keepdims=True) + EPS)
    return centred * inverse, inverse


def norm_back(grad, scale_part, norm, inverse):
    e = grad * (1.0 + scale_part)
    return inverse * (
        e - jnp.mean(e, axis=-1, keepdims=True) - norm * jnp.mean(e * norm, axis=-1, keepdims=True)
    )


def part(mod_ref, slot, index, width):
    return mod_ref[pl.ds(slot, 1), index * width : (index + 1) * width]


def angles(coords_ref, cos_ref, sin_ref):
    value = lax.broadcasted_iota(jnp.int32, (GRID, 1), 0)
    hot = [(value == coords_ref[i : i + 1, :]).astype(f32) for i in range(2)]
    hot = jnp.concatenate(hot * 3, axis=0).astype(bf16)
    return tn(hot, cos_ref[...]), tn(hot, sin_ref[...])


def partner(v):
    width = v.shape[1]
    quarter = HD // 4
    lane = lax.broadcasted_iota(jnp.int32, (1, width), 1)
    leads = (lane // quarter) % 2 == 0
    return jnp.where(leads, pltpu.roll(v, width - quarter, 1), pltpu.roll(v, quarter, 1))


def head_sum(v, gather_ref):
    hi = v.astype(bf16)
    low = (v - hi.astype(f32)).astype(bf16)
    return nn(hi, gather_ref[...]) + nn(low, gather_ref[...])


def head_spread(v, spread_ref):
    hi, mid, low = split3(v)
    lane = lax.broadcasted_iota(jnp.int32, (1, 128), 1)
    chosen = jnp.where(lane < HEADS, hi, jnp.where(lane < 2 * HEADS, mid, low))
    return nn(chosen.astype(bf16), spread_ref[...])


def window(head, width):
    start = jnp.minimum((head * HD) // 128, width // 128 - WIN // 128) * 128
    return pl.multiple_of(start, 128), head * HD - start


def head_lanes(offset):
    lane = lax.broadcasted_iota(jnp.int32, (1, WIN), 1)
    return (lane >= offset) & (lane < offset + HD)


def product(units_ref, half, rhs, out_ref):
    _, rows, tokens = units_ref.shape
    units = units_ref[pl.ds(4 * half, 4)].reshape(4 * rows, tokens)
    out_ref[...] = nn(units, rhs).astype(bf16).reshape(out_ref.shape)


def halves_out(acc_ref, core, send_ref, own_ref):
    rows = acc_ref.shape[0] // 2
    for half, out_ref in ((1 - core, send_ref), (core, own_ref)):
        start = pl.multiple_of(half * rows, rows)
        out_ref[...] = acc_ref[pl.ds(start, rows)].astype(bf16).reshape(out_ref.shape)


def project_kernel(
    slots, x_ref, mod_ref, w_ref, coords_ref, cos_ref, sin_ref, gain_ref, gather_ref, spread_ref,
    perm_ref, units_ref, raw_ref, inv_ref, q_ref, k_ref, v_ref, kt_ref,
):
    width = x_ref.shape[1]
    slot = slots[pl.program_id(0)]
    norm, _ = normed(x_ref[...].astype(f32))
    low = (norm * (1.0 + part(mod_ref, slot, 1, width)) + part(mod_ref, slot, 0, width)).astype(bf16)
    units_ref[...] = nt(perm_ref[...], low).astype(bf16).reshape(units_ref.shape)
    cosine, sine = angles(coords_ref, cos_ref, sin_ref)
    for index, out_ref in enumerate((q_ref, k_ref)):
        raw = nn(low, w_ref[:, index * width : (index + 1) * width])
        raw_ref[:, index * width : (index + 1) * width] = raw
        inverse = lax.rsqrt(head_sum(raw * raw, gather_ref) * (1.0 / HD) + EPS)
        inv_ref[:, index * 128 : (index + 1) * 128] = inverse
        scaled = raw * head_spread(inverse, spread_ref) * gain_ref[index : index + 1, :]
        turned = scaled * cosine + partner(scaled) * sine
        out_ref[...] = turned.astype(bf16)
        if index == 1:
            kt_ref[...] = turned.T.astype(bf16)
    v_ref[...] = nn(low, w_ref[:, 2 * width :]).astype(bf16)


def attend_kernel(
    slots, x_ref, cot_ref, mod_ref, q_ref, k_ref, v_ref, w_out_ref, perm_ref,
    o_ref, lse_ref, attn_ref, mid_ref, low_ref, gf_ref, att_units_ref, ffn_units_ref, lse_acc,
):
    block = pl.program_id(0)
    width = x_ref.shape[1]
    tokens = k_ref.shape[0]
    lane128 = lax.broadcasted_iota(jnp.int32, (1, 128), 1)
    lane = lax.broadcasted_iota(jnp.int32, (1, WIN), 1)
    o_ref[...] = jnp.zeros_like(o_ref)
    lse_acc[...] = jnp.zeros_like(lse_acc)

    def run(rows):
        def head(h, carry):
            start, offset = window(h, width)
            inside = head_lanes(offset)
            columns = pl.ds(start, WIN)
            query = jnp.where(inside, q_ref[:, columns], 0)
            value = jnp.where(inside, v_ref[rows, columns], 1)
            weight = jnp.exp2(nt(query, k_ref[rows, columns]) * SCORE_LOG2).astype(bf16)
            summed = nn(weight, value)
            free = jnp.where(offset > 0, 0, WIN - 1)
            total = jnp.sum(jnp.where(lane == free, summed, 0.0), axis=1, keepdims=True)
            o_ref[:, columns] += jnp.where(inside, summed * (1.0 / total), 0.0)
            lse_acc[...] += jnp.where(lane128 == h, jnp.log2(total), 0.0)
            return carry

        lax.fori_loop(0, HEADS, head, 0, unroll=2)

    whole = slots[tokens // TB - 1] == slots[0]

    @pl.when(whole)
    def _():
        run(slice(None))

    @pl.when(jnp.logical_not(whole))
    def _():
        run(pl.ds(pl.multiple_of(block * TB, TB), TB))

    lse_ref[...] = lse_acc[...].T
    slot = slots[block]
    attended = o_ref[...].astype(bf16)
    att_units_ref[...] = nt(perm_ref[...], attended).astype(bf16).reshape(att_units_ref.shape)
    attn = nn(attended, w_out_ref[...])
    attn_ref[...] = attn
    mid = x_ref[...].astype(f32) + part(mod_ref, slot, 2, width) * attn
    mid_ref[...] = mid
    norm, _ = normed(mid)
    low = (norm * (1.0 + part(mod_ref, slot, 4, width)) + part(mod_ref, slot, 3, width)).astype(bf16)
    low_ref[...] = low
    ffn_units_ref[...] = nt(perm_ref[...], low).astype(bf16).reshape(ffn_units_ref.shape)
    gf_ref[...] = (cot_ref[...].astype(f32) * part(mod_ref, slot, 5, width)).astype(bf16)


def ffn_kernel(
    bits, x_ref, gf_ref, units_ref, wg_ref, wu_ref, wd_ref,
    gate_send_ref, gate_own_ref, up_send_ref, up_own_ref, down_send_ref, down_own_ref, ffn_ref, dmod_ref,
    turned_ref, *, n_mod, rows_ff,
):
    core = bits[0]
    gate = nn(x_ref[...], wg_ref[...])
    up = nn(x_ref[...], wu_ref[...])
    grad_hidden = nt(gf_ref[...], wd_ref[...])
    sigmoid = 1.0 / (1.0 + jnp.exp(-gate))
    silu = gate * sigmoid
    hidden = (silu * up).astype(bf16)
    turned = hidden.T
    for index in range(turned.shape[0] // rows_ff):
        unit, rest = unit_of(index, n_mod)
        turned_ref[unit, rest * rows_ff : (rest + 1) * rows_ff] = turned[
            index * rows_ff : (index + 1) * rows_ff
        ]
    dg = (grad_hidden * up * (sigmoid * (1.0 + gate * (1.0 - sigmoid)))).astype(bf16)
    du = (grad_hidden * silu).astype(bf16)

    @pl.when(pl.program_id(0) == 0)
    def _():
        ffn_ref[...] = jnp.zeros_like(ffn_ref)
        dmod_ref[...] = jnp.zeros_like(dmod_ref)

    ffn_ref[...] += nn(hidden, wd_ref[...])
    dmod_ref[...] += nt(dg, wg_ref[...]) + nt(du, wu_ref[...])
    product(units_ref, 1 - core, dg, gate_send_ref)
    product(units_ref, 1 - core, du, up_send_ref)
    product(turned_ref, 1 - core, gf_ref[...], down_send_ref)
    product(units_ref, core, dg, gate_own_ref)
    product(units_ref, core, du, up_own_ref)
    product(turned_ref, core, gf_ref[...], down_own_ref)


def middle_kernel(
    slots, mid_ref, ffn_ref, dmod_ref, cot_ref, attn_ref, o_ref, units_ref, mod_ref, w_out_ref, gather_ref,
    out_ref, grad_mid_ref, do_ref, dot_ref, sums_ref, send_ref, own_ref, acc_ref,
):
    width = mid_ref.shape[1]
    block = pl.program_id(0)
    slot = slots[block]
    incoming = cot_ref[...].astype(f32)
    mid = mid_ref[...]
    out_ref[...] = (mid + part(mod_ref, slot, 5, width) * ffn_ref[...]).astype(bf16)
    norm, inverse = normed(mid)
    dmod = dmod_ref[...]
    grad_mid = incoming + norm_back(dmod, part(mod_ref, slot, 4, width), norm, inverse)
    grad_mid_ref[...] = grad_mid
    ga = (grad_mid * part(mod_ref, slot, 2, width)).astype(bf16)
    grow = nn(units_ref[...].reshape(width, TB), ga)

    @pl.when(block == 0)
    def _():
        acc_ref[...] = grow

    @pl.when(block > 0)
    def _():
        acc_ref[...] += grow

    @pl.when(block == pl.num_programs(0) - 1)
    def _():
        halves_out(acc_ref, slots[pl.num_programs(0)], send_ref, own_ref)

    do = nt(ga, w_out_ref[...]).astype(bf16)
    do_ref[...] = do
    dot_ref[...] = head_sum(do.astype(f32) * o_ref[...], gather_ref).T

    @pl.when(block == 0)
    def _():
        sums_ref[...] = jnp.zeros_like(sums_ref)

    for index, term in enumerate((grad_mid * attn_ref[...], dmod, dmod * norm, incoming * ffn_ref[...])):
        columns = slice(index * width, (index + 1) * width)
        sums_ref[pl.ds(slot, 1), columns] += jnp.sum(term, axis=0, keepdims=True)


def attend_back_kernel(
    slots, q_ref, k_ref, v_ref, do_ref, lse_ref, dot_ref, kt_ref, dqt_ref, dk_ref, dv_low_ref, dv_ref,
    *, first, base, base_row,
):
    h = pl.program_id(0) + first
    tokens, width = q_ref.shape

    @pl.when(pl.program_id(0) == 0)
    def _():
        dqt_ref[...] = jnp.zeros_like(dqt_ref)
        dk_ref[...] = jnp.zeros_like(dk_ref)
        dv_ref[...] = jnp.zeros_like(dv_ref)

    start, offset = window(h, kt_ref.shape[0])
    inside = head_lanes(offset)
    columns = pl.ds(start, WIN)
    out_columns = pl.ds(pl.multiple_of(start - base, 128), WIN)
    first_row = pl.multiple_of((h * HD) // 16 * 16, 16)
    out_rows = pl.ds(pl.multiple_of(first_row - base_row, 16), HD + 8)
    row = lax.broadcasted_iota(jnp.int32, (HD + 8, 1), 0) + first_row
    own_rows = (row >= h * HD) & (row < h * HD + HD)

    def step(rows):
        query = q_ref[rows, columns]
        grad_out = do_ref[rows, columns]
        key = jnp.where(inside, k_ref[rows, columns], 0)
        value = jnp.where(inside, v_ref[rows, columns], 0)
        probs = jnp.exp2(nt(key, query) * SCORE_LOG2 - lse_ref[pl.ds(h, 1), rows])
        scores = (probs * (nt(value, grad_out) - dot_ref[pl.ds(h, 1), rows])).astype(bf16)
        dv_ref[rows, out_columns] += jnp.where(inside, nn(probs.astype(bf16), grad_out), 0.0)
        dk_ref[rows, out_columns] += jnp.where(inside, nn(scores, query) * SCORE_SCALE, 0.0)
        turned = nn(kt_ref[pl.ds(first_row, HD + 8), rows], scores) * SCORE_SCALE
        dqt_ref[out_rows, rows] += jnp.where(own_rows, turned, 0.0)

    whole = slots[tokens // TB - 1] == slots[0]

    @pl.when(whole)
    def _():
        step(slice(None))

    @pl.when(jnp.logical_not(whole))
    def _():
        def block(i, carry):
            step(pl.ds(pl.multiple_of(i * TB, TB), TB))
            return carry

        lax.fori_loop(0, tokens // TB, block, 0)

    @pl.when(pl.program_id(0) == pl.num_programs(0) - 1)
    def _():
        dv_low_ref[...] = dv_ref[...].astype(bf16)


def head_span(first, end, width):
    begin = lambda head: min(head * HD // 128, width // 128 - WIN // 128) * 128
    return begin(first), begin(end - 1) + WIN, first * HD // 16 * 16, (end - 1) * HD // 16 * 16 + HD + 8


def join_spans(low, high, begin, axis):
    size = low.shape[axis] - begin
    cut = lambda arr, start, stop: lax.slice_in_dim(arr, start, stop, axis=axis)
    middle = cut(low, begin, begin + size) + cut(high, 0, size)
    return jnp.concatenate([cut(low, 0, begin), middle, cut(high, size, high.shape[axis])], axis=axis)


def project_back_kernel(
    bits, dqt0_ref, dqt1_ref, dk0_ref, dk1_ref, raw_ref, inv_ref, q_ref, k_ref, units_ref,
    coords_ref, cos_ref, sin_ref, gain_ref, gather_ref, spread_ref, fold_ref,
    gq_ref, gk_ref, gains_low_ref, q_send_ref, q_own_ref, k_send_ref, k_own_ref, accq_ref, acck_ref, gains_ref,
    *, base, base_row,
):
    width = q_ref.shape[1]
    block = pl.program_id(0)

    @pl.when(block == 0)
    def _():
        gains_ref[...] = jnp.zeros_like(gains_ref)
        accq_ref[...] = jnp.zeros_like(accq_ref)
        acck_ref[...] = jnp.zeros_like(acck_ref)

    cosine, sine = angles(coords_ref, cos_ref, sin_ref)
    parts = ((q_ref, gq_ref, accq_ref), (k_ref, gk_ref, acck_ref))
    for index, (low_ref, out_ref, acc_ref) in enumerate(parts):
        if index == 0:
            grad = join_spans(dqt0_ref[...], dqt1_ref[...], base_row, 0).T
        else:
            grad = join_spans(dk0_ref[...], dk1_ref[...], base, 1)
        raw = raw_ref[:, index * width : (index + 1) * width]
        inverse = head_spread(inv_ref[:, index * 128 : (index + 1) * 128], spread_ref)
        mean = head_sum(grad * low_ref[...].astype(f32), gather_ref) * (1.0 / HD)
        norm = raw * inverse
        back = grad * cosine - partner(grad) * sine
        gains_ref[index : index + 1, :] += jnp.sum(back * norm, axis=0, keepdims=True)
        grad_raw = (
            inverse * (back * gain_ref[index : index + 1, :] - norm * head_spread(mean, spread_ref))
        ).astype(bf16)
        out_ref[...] = grad_raw
        acc_ref[...] += nn(units_ref[...].reshape(width, TB), grad_raw)

    @pl.when(block == pl.num_programs(0) - 1)
    def _():
        halves_out(accq_ref, bits[0], q_send_ref, q_own_ref)
        halves_out(acck_ref, bits[0], k_send_ref, k_own_ref)
        terms = split3(gains_ref[...])
        sums = sum(nn(term.astype(bf16), fold_ref[...]) for term in terms)
        high = sums.astype(bf16).astype(f32)
        row = lax.broadcasted_iota(jnp.int32, (8, 1), 0)
        mine = 4 * bits[1]
        placed = jnp.zeros((8, 128), f32)
        for index, term in enumerate((high[0:1], (sums - high)[0:1], high[1:2], (sums - high)[1:2])):
            placed = jnp.where(row == mine + index, term, placed)
        gains_low_ref[...] = placed.astype(bf16)


def input_back_kernel(
    slots, gq_ref, gk_ref, dv0_ref, dv1_ref, x_ref, grad_mid_ref, mod_ref, w_ref, other_sums_ref, gains_ref,
    grad_x_ref, grad_own_ref, grad_other_ref, sums_ref, *, base,
):
    width = x_ref.shape[1]
    block = pl.program_id(0)
    slot = slots[block]
    last_block = pl.num_programs(0) - 1
    dmod = nt(gq_ref[...], w_ref[:, :width]) + nt(gk_ref[...], w_ref[:, width : 2 * width])
    dmod = dmod + nt(join_spans(dv0_ref[...], dv1_ref[...], base, 1), w_ref[:, 2 * width :])
    norm, inverse = normed(x_ref[...].astype(f32))
    grad_x = grad_mid_ref[...] + norm_back(dmod, part(mod_ref, slot, 1, width), norm, inverse)
    grad_x_ref[...] = grad_x.astype(bf16)

    @pl.when(block == 0)
    def _():
        sums_ref[...] = jnp.zeros_like(sums_ref)

    for index, term in enumerate((dmod, dmod * norm)):
        columns = slice(index * width, (index + 1) * width)
        sums_ref[pl.ds(slot, 1), columns] += jnp.sum(term, axis=0, keepdims=True)

    @pl.when(block == last_block)
    def _():
        mod = slots[last_block + 2]
        count = sums_ref.shape[0]
        half = 3 * width
        mine = jnp.concatenate([sums_ref[...]] * 2, axis=0)
        rest = jnp.concatenate([other_sums_ref[...]] * 2, axis=0)
        row = lax.broadcasted_iota(jnp.int32, (2 * count, 1), 0) // count
        attn_part = jnp.where(row == mod, jnp.concatenate([mine, rest[:, :width]], axis=1), 0.0)
        ffn_part = jnp.where(row == mod, rest[:, width:], 0.0)
        grad_own_ref[:, :half] = jnp.where(mod == 0, attn_part, ffn_part).astype(bf16)
        grad_other_ref[:, :half] = jnp.where(mod == 0, ffn_part, attn_part).astype(bf16)
        grad_own_ref[:, half:] = gains_ref[...]
        grad_other_ref[:, half:] = gains_ref[...]


def value_kernel(bits, units_ref, dv0_ref, dv1_ref, send_ref, own_ref, *, base):
    rhs = join_spans(dv0_ref[...], dv1_ref[...], base, 1)
    product(units_ref, 1 - bits[0], rhs, send_ref)
    product(units_ref, bits[0], rhs, own_ref)


def split_step(bits, ins, outs, *, lead, at, bit, pair_rows):
    own_ref, got_ref = ins
    send_ref, keep_ref = outs
    mine = bits[bit]

    def total(*index):
        return own_ref[index].astype(f32) + got_ref[index].astype(f32)

    if at is None:
        for j in range(max(lead, 1)):
            index = (j,) if lead else ()
            value = total(*index) if lead else own_ref[...].astype(f32) + got_ref[...].astype(f32)
            rows = pair_rows or value.shape[0] // 2
            for p in range(value.shape[0] // (2 * rows)):
                first = value[2 * p * rows : (2 * p + 1) * rows]
                second = value[(2 * p + 1) * rows : (2 * p + 2) * rows]
                place = index + (slice(p * rows, (p + 1) * rows),)
                send_ref[place] = jnp.where(mine == 1, first, second).astype(bf16)
                keep_ref[place] = jnp.where(mine == 1, second, first).astype(keep_ref.dtype)
        return
    for j in range(lead // 2):
        place = (j,) if lead > 2 else (Ellipsis,)
        away = 1 - mine if lead == 2 else 2 * (1 - mine) + j if at == 0 else 2 * j + 1 - mine
        own = mine if lead == 2 else 2 * mine + j if at == 0 else 2 * j + mine
        send_ref[place] = total(away).astype(bf16)
        keep_ref[place] = total(own).astype(keep_ref.dtype)


def merge_step(bits, ins, outs, *, bit):
    send_ref, keep_ref = outs
    start = 0
    for own_ref, got_ref in zip(ins[::2], ins[1::2]):
        value = own_ref[...].astype(f32) + got_ref[...].astype(f32)
        rows = value.shape[0] // 2
        place = slice(start, start + value.shape[1])
        first, second = value[:rows], value[rows:]
        send_ref[:, place] = jnp.where(bits[bit] == 1, first, second).astype(bf16)
        keep_ref[:, place] = jnp.where(bits[bit] == 1, second, first)
        start += value.shape[1]


def pair_step(bits, ins, outs):
    own_ref, got_ref, activated_ref = ins
    width = activated_ref.shape[1]
    outs[0][:, :width] = activated_ref[...]
    outs[0][:, width:] = (own_ref[...].astype(f32) + got_ref[...].astype(f32)).astype(bf16)


def joined(ins):
    return jnp.concatenate([ref[...].astype(f32) for ref in ins], axis=0).astype(bf16)


def join_step(bits, ins, outs):
    outs[0][...] = joined(ins)


def last_step(bits, ins, outs):
    outs[0][...] = ins[0][...] + ins[1][...].astype(f32)


def ada_step(bits, ins, outs, *, width):
    rows = outs[0].shape[0]
    every = joined(ins)
    position = bits[0] + sum(bits[1 + k] * 2**k for k in range(1, (width // rows).bit_length() - 1))
    feature = lax.broadcasted_iota(jnp.int32, (width, 128), 0)
    place = lax.broadcasted_iota(jnp.int32, (width, 128), 1)
    chosen = (feature == position * rows + place) & (place < rows)
    own = nn(every[:, :width], chosen.astype(f32).astype(bf16)).astype(bf16)
    half = outs[0].shape[1]
    outs[0][...] = tn(own, every[:, width : width + half])[:rows]
    terms = every[:, width + half :].astype(f32)
    kind = lax.broadcasted_iota(jnp.int32, (terms.shape[0], 1), 0) // 2 % 2
    for index in range(2):
        outs[1][index : index + 1, :] = jnp.sum(jnp.where(kind == index, terms, 0.0), axis=0, keepdims=True)


def step_kernel(bits, *refs, plans):
    n_in = sum(plan[1] for plan in plans)
    ins, outs = refs[:n_in], refs[n_in:]
    for function, takes, gives in plans:
        function(bits, ins[:takes], outs[:gives])
        ins, outs = ins[takes:], outs[gives:]


class Chain:
    def __init__(self):
        self.last = None

    def __call__(
        self, kernel, grid, in_specs, out_specs, out_shape, args, scalars=None, scratch=(), name=None, aliases=None
    ):
        ahead = 0 if scalars is None else 1
        body = kernel
        token = ()
        if self.last is not None:
            token = (self.last,)
            in_specs = [pl.BlockSpec(memory_space=pl.ANY)] + list(in_specs)

            def body(*refs):
                kernel(*refs[:ahead], *refs[ahead + 1 :])

        spec = pltpu.PrefetchScalarGridSpec(
            num_scalar_prefetch=ahead,
            grid=grid,
            in_specs=in_specs,
            out_specs=out_specs,
            scratch_shapes=scratch,
        )
        outs = pl.pallas_call(
            body,
            grid_spec=spec,
            input_output_aliases=aliases or {},
            out_shape=out_shape,
            compiler_params=pltpu.CompilerParams(vmem_limit_bytes=VMEM),
            cost_estimate=pl.CostEstimate(flops=1, bytes_accessed=1, transcendentals=0),
            name=name,
        )(*(() if scalars is None else (scalars,)), *token, *args)
        self.last = outs[0]
        return outs


def shape(dims, dtype):
    return jax.ShapeDtypeStruct(dims, dtype)


def fixed(dims):
    return pl.BlockSpec(dims, lambda *_: (0,) * len(dims), pipeline_mode=pl.Buffered(1))


def rows_of(dims, axis=0):
    return pl.BlockSpec(dims, lambda b, *_: tuple(b if i == axis else 0 for i in range(len(dims))))


def whole(dims):
    return rows_of(dims, None)


def column_parts(dims, steps):
    return rows_of(dims[:-1] + (dims[-1] // steps,), len(dims) - 1)


class Reducer:
    def __init__(self, n_dp, n_mod, call):
        self.n_dp, self.n_mod, self.call = n_dp, n_mod, call
        self.position = lax.axis_index("dp")
        steps = range(n_dp.bit_length() - 1)
        dp_bits = [lax.shift_right_logical(self.position, step) & 1 for step in steps]
        self.bits = jnp.stack([dp_bits[0], lax.axis_index("mod")] + dp_bits[1:]).astype(jnp.int32)

    def swap(self, arr, bit):
        if bit == "mod":
            return lax.ppermute(arr, "mod", [(i, i ^ 1) for i in range(self.n_mod)])
        return lax.ppermute(arr, "dp", [(i, i ^ (1 << bit)) for i in range(self.n_dp)])

    def bit_of(self, bit):
        return 1 if bit == "mod" else bit + 1 if bit else 0

    def fold(self, streams, name, last=False):
        plans, args, outs = [], [], []
        for stream in streams:
            function, shapes = stream.last_plan() if last else stream.plan()
            inputs = stream.inputs()
            plans.append((function, len(inputs), len(shapes)))
            args += inputs
            outs += shapes
        size = sum(arg.size for arg in args)
        split = all(isinstance(stream, Stream) and stream.own.shape[-1] % 384 == 0 for stream in streams)
        steps = 3 if split and size > 2**20 else 1
        results = self.call(
            functools.partial(step_kernel, plans=plans),
            (steps,),
            [column_parts(arg.shape, steps) for arg in args],
            [column_parts(out.shape, steps) for out in outs],
            outs,
            args,
            scalars=self.bits,
            name=name,
        )
        results = list(results)
        if last:
            return results
        for stream, plan in zip(streams, plans):
            stream.step(results[: plan[2]])
            results = results[plan[2] :]

    def pass_on(self, arrays):
        anywhere = [pl.BlockSpec(memory_space=pl.ANY)] * len(arrays)
        return self.call(
            lambda *refs: None,
            (1,),
            anywhere,
            anywhere,
            [shape(arr.shape, arr.dtype) for arr in arrays],
            arrays,
            name="pass_on",
            aliases={i + 1: i for i in range(len(arrays))},
        )


class Stream:
    def __init__(self, reducer, sent, own, first, pair_rows=None):
        self.r, self.own, self.pair_rows = reducer, own, pair_rows
        order = ["mod", 1, 2]
        self.steps = order[first:] + order[:first] + list(range(3, reducer.n_dp.bit_length() - 1))
        self.lead = ["mod", 1]
        self.got = reducer.swap(sent, 0)

    def inputs(self):
        return [self.own, self.got]

    def plan(self):
        bit = self.steps[0]
        dims = self.own.shape
        at = self.lead.index(bit) if bit in self.lead else None
        function = functools.partial(
            split_step, lead=dims[0] if self.lead else 0, at=at, bit=self.r.bit_of(bit), pair_rows=self.pair_rows
        )
        if at is None:
            dims = dims[:-2] + (dims[-2] // 2, dims[-1])
        else:
            dims = dims[1:] if len(self.lead) == 1 else (2,) + dims[1:]
        return function, [shape(dims, bf16), shape(dims, bf16 if len(self.lead) == 2 else f32)]

    def step(self, results):
        bit = self.steps.pop(0)
        if bit in self.lead:
            self.lead.remove(bit)
        sent, self.own = results
        self.got = self.r.swap(sent, bit)

    def last_plan(self):
        return last_step, [shape(self.own.shape, f32)]


class Merged:
    def __init__(self, streams):
        self.streams, self.r, self.bit = streams, streams[0].r, streams[0].steps[0]
        self.own = None

    def inputs(self):
        if self.own is not None:
            return [self.own, self.got]
        return [arr for stream in self.streams for arr in (stream.own, stream.got)]

    def plan(self):
        columns = sum(stream.own.shape[1] for stream in self.streams)
        dims = (self.streams[0].own.shape[0] // 2, columns)
        function = functools.partial(merge_step, bit=self.r.bit_of(self.bit))
        return function, [shape(dims, bf16), shape(dims, f32)]

    def step(self, results):
        sent, self.own = results
        self.got = self.r.swap(sent, self.bit)

    def last_plan(self):
        return last_step, [shape(self.own.shape, f32)]


class Gather:
    def __init__(self, reducer, sent, own, activated):
        self.r, self.own, self.activated = reducer, own, activated
        self.steps = list(range(reducer.n_dp.bit_length() - 2, -1, -1))
        self.got = reducer.swap(sent, "mod")
        self.pair = None

    def inputs(self):
        return [self.own, self.got] + ([self.activated] if self.pair is None else [])

    def plan(self):
        rows, columns = self.own.shape
        if self.pair is None:
            return pair_step, [shape((rows, columns + self.activated.shape[1]), bf16)]
        return join_step, [shape((2 * rows, columns), bf16)]

    def step(self, results):
        (self.own,) = results
        if self.pair is None:
            self.pair = self.own
        self.got = self.r.swap(self.own, self.steps.pop(0))

    def last_plan(self):
        width = self.activated.shape[1]
        function = functools.partial(ada_step, width=width)
        dims = (width // self.r.n_dp, self.own.shape[1] - width - 128)
        return function, [shape(dims, f32), shape((2, 128), f32)]


def silu_grad(v):
    sigmoid = jax.nn.sigmoid(v)
    return sigmoid * (1.0 + v * (1.0 - sigmoid))


def pair_order(own, other, mod):
    return jnp.where(mod == 0, jnp.stack([own, other]), jnp.stack([other, own]))


def body(
    n_dp, n_mod, tokens, cond, segments, coords, w_ada, w_qkv, q_gain, k_gain, w_out, w_gate, w_up,
    w_down, cotangent,
):
    _, count, width = tokens.shape
    slots_n = cond.shape[1]
    half = w_ada.shape[1]
    ff = w_gate.shape[1]
    blocks = count // TB
    n_dev = n_dp * n_mod
    call = Chain()
    reducer = Reducer(n_dp, n_mod, call)
    mod_index = lax.axis_index("mod")
    x = tokens[0]
    cot = cotangent[0]
    slots = segments[0, ::TB]
    coord = coords[0]
    cos_table, sin_table = (jnp.asarray(t) for t in rope_tables(width))
    gather, spread, head_fold = (jnp.asarray(t) for t in head_tables(width))
    perm = jnp.asarray(unit_permutation(width, n_dp, n_mod))
    gains = jnp.stack([jnp.tile(q_gain, HEADS), jnp.tile(k_gain, HEADS)])

    cond_both = pair_order(cond[0], reducer.swap(cond[0], "mod"), mod_index)
    activated = jax.nn.silu(cond_both).astype(bf16).reshape(-1, width)
    mod_half = jnp.dot(activated, w_ada, preferred_element_type=f32).astype(bf16)
    mod_half = mod_half.reshape(n_mod, slots_n, half)
    own_half = lax.dynamic_index_in_dim(mod_half, mod_index, 0, keepdims=False)
    other_half = lax.dynamic_index_in_dim(mod_half, 1 - mod_index, 0, keepdims=False)
    pair = pair_order(own_half, reducer.swap(other_half, "mod"), mod_index)
    modulation = jnp.concatenate([pair[0], pair[1]], axis=1).astype(f32)

    token_f32 = shape((count, width), f32)
    token_bf16 = shape((count, width), bf16)
    units = shape((8, width // 8, count), bf16)
    units_spec = rows_of((8, width // 8, TB), 2)
    token_spec = rows_of((TB, width))
    mod_spec = fixed((slots_n, 6 * width))
    square = fixed((width, width))
    table_specs = [fixed(cos_table.shape), fixed(sin_table.shape), fixed((2, width)), fixed(gather.shape), fixed(spread.shape)]
    tables = (cos_table, sin_table, gains, gather, spread)
    lane_rows = shape((128, count), f32)
    macs = count * width * width

    attn_units, raw, inverse, query, key, value, key_t = call(
        project_kernel,
        (blocks,),
        [token_spec, mod_spec, fixed((width, 3 * width)), rows_of((2, TB), 1)] + table_specs + [square],
        [units_spec, rows_of((TB, 2 * width)), rows_of((TB, 256))] + [token_spec] * 3 + [rows_of((width, TB), 1)],
        [units, shape((count, 2 * width), f32), shape((count, 256), f32)] + [token_bf16] * 3
        + [shape((width, count), bf16)],
        (x, modulation, w_qkv, coord) + tables + (perm,),
        scalars=slots,
        name="project",
    )
    attended, lse, attn, mid, ffn_in, grad_ffn, out_units, ffn_units = call(
        attend_kernel,
        (blocks,),
        [token_spec, token_spec, mod_spec, token_spec] + [fixed((count, width))] * 2 + [square, square],
        [token_spec, rows_of((128, TB), 1)] + [token_spec] * 4 + [units_spec] * 2,
        [token_f32, lane_rows, token_f32, token_f32, token_bf16, token_bf16, units, units],
        (x, cot, modulation, query, key, value, w_out, perm),
        scalars=slots,
        scratch=[pltpu.VMEM((TB, 128), f32)],
        name="attend",
    )

    rows_ff = ff // n_dev
    chunk = 768
    piece = chunk // 8
    half_units = lambda rows, columns: shape((4, rows, columns), bf16)
    square_send = [fixed((4, width // 8, width))] * 2
    square_shapes = [half_units(width // 8, width)] * 2
    gate_send, gate_own, up_send, up_own, down_send, down_own, ffn, grad_mod_ffn = call(
        functools.partial(ffn_kernel, n_mod=n_mod, rows_ff=rows_ff),
        (ff // chunk,),
        [fixed((count, width))] * 2 + [fixed(units.shape)]
        + [rows_of((width, chunk), 1)] * 2 + [rows_of((chunk, width))],
        [rows_of((4, width // 8, chunk), 2)] * 4
        + [rows_of((4, 1, piece, width), 1)] * 2 + [fixed((count, width))] * 2,
        [half_units(width // 8, ff)] * 4
        + [shape((4, ff // chunk, piece, width), bf16)] * 2 + [token_f32] * 2,
        (ffn_in, grad_ffn, ffn_units, w_gate, w_up, w_down),
        scalars=reducer.bits,
        scratch=[pltpu.VMEM((8, piece, count), bf16)],
        name="ffn",
    )
    gate = Stream(reducer, gate_send, gate_own, 0)
    up = Stream(reducer, up_send, up_own, 1)
    down = Stream(
        reducer, down_send.reshape(4, ff // 8, width), down_own.reshape(4, ff // 8, width), 2, rows_ff
    )

    slots_core = jnp.concatenate([slots, reducer.bits[:2]])
    output, grad_mid, grad_attended, dot_term, sums_b, out_send, out_own = call(
        middle_kernel,
        (blocks,),
        [token_spec] * 6 + [units_spec, mod_spec, square, fixed(gather.shape)],
        [token_spec] * 3 + [rows_of((128, TB), 1), fixed((slots_n, 4 * width))] + square_send,
        [token_bf16, token_f32, token_bf16, lane_rows, shape((slots_n, 4 * width), f32)] + square_shapes,
        (mid, ffn, grad_mod_ffn, cot, attn, attended, out_units, modulation, w_out, gather),
        scalars=slots_core,
        scratch=[pltpu.VMEM((width, width), f32)],
        name="middle",
    )
    out = Stream(reducer, out_send, out_own, 1)
    early = [gate, up, down, out]
    reducer.fold(early, "early")

    def attend_back(first, end, name):
        begin, stop, begin_row, stop_row = head_span(first, end, width)
        columns, rows = stop - begin, stop_row - begin_row
        used = fixed((count, stop))
        return call(
            functools.partial(attend_back_kernel, first=first, base=begin, base_row=begin_row),
            (end - first,),
            [used] * 4 + [fixed((128, count))] * 2 + [fixed((width, count))],
            [fixed((rows, count))] + [fixed((count, columns))] * 2,
            [shape((rows, count), f32), shape((count, columns), f32), shape((count, columns), bf16)],
            (query, key, value, grad_attended, lse, dot_term, key_t),
            scratch=[pltpu.VMEM((count, columns), f32)],
            scalars=slots,
            name=name,
        )

    cut = HEADS // 2 + 1
    dqt0, dk0, dv0 = attend_back(0, cut, "attend_back_0")
    reducer.fold(early, "early")
    dqt1, dk1, dv1 = attend_back(cut, HEADS, "attend_back_1")
    reducer.fold(early, "early")
    base, _, base_row, _ = head_span(cut, HEADS, width)
    v_send, v_own = call(
        functools.partial(value_kernel, base=base),
        (1,),
        [whole(units.shape), whole(dv0.shape), whole(dv1.shape)],
        [whole((4, width // 8, width))] * 2,
        square_shapes,
        (attn_units, dv0, dv1),
        scalars=reducer.bits,
        name="value",
    )
    v_part = Stream(reducer, v_send, v_own, 2)
    grad_q, grad_k, gains_low, q_send, q_own, k_send, k_own = call(
        functools.partial(project_back_kernel, base=base, base_row=base_row),
        (blocks,),
        [rows_of((dqt0.shape[0], TB), 1), rows_of((dqt1.shape[0], TB), 1)]
        + [rows_of((TB, dk0.shape[1])), rows_of((TB, dk1.shape[1]))]
        + [rows_of((TB, 2 * width)), rows_of((TB, 256)), token_spec, token_spec, units_spec, rows_of((2, TB), 1)]
        + table_specs + [fixed(head_fold.shape)],
        [token_spec] * 2 + [fixed((8, 128))] + square_send * 2,
        [token_bf16] * 2 + [shape((8, 128), bf16)] + square_shapes * 2,
        (dqt0, dqt1, dk0, dk1, raw, inverse, query, key, attn_units, coord) + tables + (head_fold,),
        scalars=reducer.bits,
        scratch=[pltpu.VMEM((width, width), f32)] * 2 + [pltpu.VMEM((2, width), f32)],
        name="project_back",
    )
    waiting = early + [v_part]
    *arrived, q_send, k_send = reducer.pass_on([stream.got for stream in waiting] + [q_send, k_send])
    for stream, got in zip(waiting, arrived):
        stream.got = got
    q_part = Stream(reducer, q_send, q_own, 1)
    k_part = Stream(reducer, k_send, k_own, 0)
    late = [q_part, k_part, v_part]
    extra = n_dp.bit_length() - 5
    reducer.fold([v_part], "v")
    for _ in range(extra):
        reducer.fold(early, "early")
    early = [Merged([gate, up, out]), down]
    reducer.fold(early, "early")
    reducer.fold([q_part, k_part], "late")
    grad_tokens, mod_own, mod_other = call(
        functools.partial(input_back_kernel, base=base),
        (blocks,),
        [token_spec] * 2 + [rows_of((TB, dv0.shape[1])), rows_of((TB, dv1.shape[1]))] + [token_spec] * 2
        + [mod_spec, fixed((width, 3 * width)), fixed((slots_n, 4 * width)), fixed((8, 128))],
        [token_spec] + [fixed((2 * slots_n, half + 128))] * 2,
        [token_bf16] + [shape((2 * slots_n, half + 128), bf16)] * 2,
        (grad_q, grad_k, dv0, dv1, x, grad_mid, modulation, w_qkv, sums_b, gains_low),
        scalars=slots_core,
        scratch=[pltpu.VMEM((slots_n, 2 * width), f32)],
        name="input_back",
    )
    every_mod = Gather(reducer, mod_other, mod_own, activated)
    reducer.fold(late, "late")
    reducer.fold([every_mod], "pair")
    summed_early, summed_down = reducer.fold(early, "early_last", last=True)
    for _ in range(1 + extra):
        reducer.fold(late + [every_mod], "late")
    late = [Merged(late)]
    reducer.fold(late + [every_mod], "late")
    while every_mod.steps:
        reducer.fold([every_mod], "every")
    summed_qkv, grad_w_ada, gain_grads = reducer.fold(late + [every_mod], "late_last", last=True)
    summed_gate, summed_up = summed_early[:, :ff], summed_early[:, ff : 2 * ff]
    summed_out = summed_early[:, 2 * ff :]

    grad_activated = jnp.einsum("nc,dc->nd", every_mod.pair[:, width : width + half], w_ada, preferred_element_type=f32)
    grad_activated = grad_activated.reshape(n_mod, slots_n, width)
    own_part = lax.dynamic_index_in_dim(grad_activated, mod_index, 0, keepdims=False)
    other_part = lax.dynamic_index_in_dim(grad_activated, 1 - mod_index, 0, keepdims=False)
    grad_own = own_part + reducer.swap(other_part.astype(bf16), "mod").astype(f32)
    grad_cond = grad_own[None] * silu_grad(cond)
    return (
        output[None],
        grad_tokens[None],
        grad_cond,
        grad_w_ada,
        summed_qkv,
        gain_grads[0, :HD],
        gain_grads[1, :HD],
        summed_out,
        summed_gate,
        summed_up,
        summed_down,
    )


def solution(mesh):
    rows = ("dp", "mod")
    in_specs = (
        P(rows, None, None),
        P(rows, None, None),
        P(rows, None),
        P(rows, None, None),
        P(None, "mod"),
        P(),
        P(),
        P(),
        P(),
        P(),
        P(),
        P(),
        P(rows, None, None),
    )
    out_specs = (
        P(rows, None, None),
        P(rows, None, None),
        P(rows, None, None),
        P("dp", "mod"),
        P(rows, None),
        P(),
        P(),
        P(rows, None),
        P(rows, None),
        P(rows, None),
        P(rows, None),
    )
    return jax.shard_map(
        functools.partial(body, mesh.shape["dp"], mesh.shape["mod"]),
        mesh=mesh,
        in_specs=in_specs,
        out_specs=out_specs,
        check_vma=False,
    )
```

```python
import functools

import jax
import jax.numpy as jnp
import numpy as np
from jax import lax
from jax.experimental import pallas as pl
from jax.experimental.pallas import tpu as pltpu
from jax.sharding import PartitionSpec as P

HEADS = 16
HD = 72
GRID = 32
EPS = 1e-06
ROPE_BASE = 10000.0
SEG = 256
TB = 512
WIN = 256
TOGETHER = 4
SCORE_SCALE = float(HD**-0.5)
SCORE_LOG2 = float(np.log2(np.e) * HD**-0.5)
VMEM = 60 * 2**20
f32 = jnp.float32
bf16 = jnp.bfloat16


def nn(a, b):
    return lax.dot_general(a, b, (((1,), (0,)), ((), ())), preferred_element_type=f32)


def nt(a, b):
    return lax.dot_general(a, b, (((1,), (1,)), ((), ())), preferred_element_type=f32)


def tn(a, b):
    return lax.dot_general(a, b, (((0,), (0,)), ((), ())), preferred_element_type=f32)


def split3(v):
    hi = v.astype(bf16).astype(f32)
    mid = (v - hi).astype(bf16).astype(f32)
    return hi, mid, v - hi - mid


def np_split3(v):
    v = v.astype(np.float32)
    hi = v.astype(jnp.bfloat16).astype(np.float32)
    mid = (v - hi).astype(jnp.bfloat16).astype(np.float32)
    return [part.astype(jnp.bfloat16) for part in (hi, mid, v - hi - mid)]


@functools.lru_cache(None)
def rope_tables(width):
    quarter = HD // 4
    freqs = ROPE_BASE ** (-np.arange(quarter, dtype=np.float64) / quarter)
    lane = np.arange(width) % HD
    group = lane // quarter
    angle = np.arange(GRID)[:, None] * freqs[lane % quarter][None, :]
    cosine, sine = np.cos(angle), np.sin(angle)
    sine = np.where((group % 2 == 0)[None, :], -sine, sine)
    uses_col = (group >= 2)[None, :]
    tables = []
    for table in (cosine, sine):
        whole = np.concatenate(
            [np.where(uses_col, 0.0, table), np.where(uses_col, table, 0.0)], axis=0
        )
        tables.append(np.concatenate(np_split3(whole), axis=0))
    return tables


@functools.lru_cache(None)
def head_tables(width):
    head = np.arange(width) // HD
    gather = np.zeros((width, 128), np.float32)
    for copy in range(3):
        gather[np.arange(width), copy * HEADS + head] = 1.0
    fold = np.zeros((width, 128), np.float32)
    fold[np.arange(width), np.arange(width) % HD] = 1.0
    return gather.astype(jnp.bfloat16), gather.T.astype(jnp.bfloat16), fold.astype(jnp.bfloat16)


def unit_of(index, n_mod):
    mod = index % n_mod
    dp = index // n_mod
    return (dp % 2) * 2 * n_mod + mod * 2 + (dp // 2) % 2, dp // 4


def reversed_bits(value, size):
    result = 0
    for bit in range(size.bit_length() - 1):
        result = 2 * result + (value >> bit) % 2
    return result


@functools.lru_cache(None)
def unit_permutation(width, n_dp, n_mod):
    rows = width // (n_dp * n_mod)
    matrix = np.zeros((width, width), np.float32)
    for index in range(n_dp * n_mod):
        unit, rest = unit_of(index, n_mod)
        start = unit * (width // 8) + reversed_bits(rest, n_dp // 4) * rows
        matrix[start + np.arange(rows), index * rows + np.arange(rows)] = 1.0
    return matrix.astype(jnp.bfloat16)


def normed(v):
    centred = v - jnp.mean(v, axis=-1, keepdims=True)
    inverse = lax.rsqrt(jnp.mean(centred * centred, axis=-1, keepdims=True) + EPS)
    return centred * inverse, inverse


def norm_back(e, norm, inverse):
    return inverse * (
        e - jnp.mean(e, axis=-1, keepdims=True) - norm * jnp.mean(e * norm, axis=-1, keepdims=True)
    )


def part(mod_ref, slot, index, width):
    return mod_ref[pl.ds(slot, 1), index * width : (index + 1) * width]


def slots_here(slots, rows):
    return [slots[pl.program_id(0) * (rows // SEG) + i] for i in range(rows // SEG)]


def by_slot(function, here, *values):
    done = [
        function(slot, *(value[i * SEG : (i + 1) * SEG] for value in values)) for i, slot in enumerate(here)
    ]
    return jnp.concatenate(done, axis=0)


def angles(coords_ref, cos_ref, sin_ref):
    value = lax.broadcasted_iota(jnp.int32, (GRID, 1), 0)
    hot = [(value == coords_ref[i : i + 1, :]).astype(f32) for i in range(2)]
    hot = jnp.concatenate(hot * 3, axis=0).astype(bf16)
    return tn(hot, cos_ref[...]), tn(hot, sin_ref[...])


def partner(v):
    width = v.shape[1]
    quarter = HD // 4
    lane = lax.broadcasted_iota(jnp.int32, (1, width), 1)
    leads = (lane // quarter) % 2 == 0
    return jnp.where(leads, pltpu.roll(v, width - quarter, 1), pltpu.roll(v, quarter, 1))


def head_sum(v, gather_ref):
    hi = v.astype(bf16)
    low = (v - hi.astype(f32)).astype(bf16)
    return nn(hi, gather_ref[...]) + nn(low, gather_ref[...])


def head_spread(v, spread_ref):
    hi, mid, low = split3(v)
    lane = lax.broadcasted_iota(jnp.int32, (1, 128), 1)
    chosen = jnp.where(lane < HEADS, hi, jnp.where(lane < 2 * HEADS, mid, low))
    return nn(chosen.astype(bf16), spread_ref[...])


def window(head, width):
    start = jnp.minimum((head * HD) // 128, width // 128 - WIN // 128) * 128
    return pl.multiple_of(start, 128), head * HD - start


def head_lanes(offset):
    lane = lax.broadcasted_iota(jnp.int32, (1, WIN), 1)
    return (lane >= offset) & (lane < offset + HD)


def product(units_ref, half, rhs, out_ref):
    _, rows, tokens = units_ref.shape
    units = units_ref[pl.ds(4 * half, 4)].reshape(4 * rows, tokens)
    out_ref[...] = nn(units, rhs).astype(bf16).reshape(out_ref.shape)


def halves_out(acc_ref, core, send_ref, own_ref):
    rows = acc_ref.shape[0] // 2
    for half, out_ref in ((1 - core, send_ref), (core, own_ref)):
        start = pl.multiple_of(half * rows, rows)
        out_ref[...] = acc_ref[pl.ds(start, rows)].astype(bf16).reshape(out_ref.shape)


def add_by_slot(sums_ref, here, index, term):
    width = term.shape[1]
    for i, slot in enumerate(here):
        rows = term[i * SEG : (i + 1) * SEG]
        sums_ref[pl.ds(slot, 1), index * width : (index + 1) * width] += jnp.sum(rows, axis=0, keepdims=True)


def project_kernel(
    slots, x_ref, mod_ref, w_ref, coords_ref, cos_ref, sin_ref, gain_ref, gather_ref, spread_ref,
    perm_ref, units_ref, raw_ref, inv_ref, q_ref, k_ref, v_ref, kt_ref,
):
    width = x_ref.shape[1]
    norm, _ = normed(x_ref[...].astype(f32))

    def modulate(slot, rows):
        return (rows * (1.0 + part(mod_ref, slot, 1, width)) + part(mod_ref, slot, 0, width)).astype(bf16)

    low = by_slot(modulate, slots_here(slots, x_ref.shape[0]), norm)
    units_ref[...] = nt(perm_ref[...], low).astype(bf16).reshape(units_ref.shape)
    cosine, sine = angles(coords_ref, cos_ref, sin_ref)
    for index, out_ref in enumerate((q_ref, k_ref)):
        raw = nn(low, w_ref[:, index * width : (index + 1) * width])
        raw_ref[:, index * width : (index + 1) * width] = raw
        inverse = lax.rsqrt(head_sum(raw * raw, gather_ref) * (1.0 / HD) + EPS)
        inv_ref[:, index * 128 : (index + 1) * 128] = inverse
        scaled = raw * head_spread(inverse, spread_ref) * gain_ref[index : index + 1, :]
        turned = scaled * cosine + partner(scaled) * sine
        out_ref[...] = turned.astype(bf16)
        if index == 1:
            kt_ref[...] = turned.T.astype(bf16)
    v_ref[...] = nn(low, w_ref[:, 2 * width :]).astype(bf16)


def attend_kernel(slots, q_ref, k_ref, v_ref, o_ref, lse_ref):
    step = pl.program_id(0)
    tokens, width = q_ref.shape
    lane128 = lax.broadcasted_iota(jnp.int32, (1, 128), 1)
    lane = lax.broadcasted_iota(jnp.int32, (1, WIN), 1)

    @pl.when(step == 0)
    def _():
        o_ref[...] = jnp.zeros_like(o_ref)
        lse_ref[...] = jnp.zeros_like(lse_ref)

    def head(h, rows):
        start, offset = window(h, width)
        inside = head_lanes(offset)
        columns = pl.ds(start, WIN)
        query = jnp.where(inside, q_ref[rows, columns], 0)
        value = jnp.where(inside, v_ref[rows, columns], 1)
        weight = jnp.exp2(nt(query, k_ref[rows, columns]) * SCORE_LOG2).astype(bf16)
        summed = nn(weight, value)
        free = jnp.where(offset > 0, 0, WIN - 1)
        total = jnp.sum(jnp.where(lane == free, summed, 0.0), axis=1, keepdims=True)
        o_ref[rows, columns] += jnp.where(inside, summed * (1.0 / total), 0.0)
        lse_ref[rows, :] += jnp.where(lane128 == h, jnp.log2(total), 0.0)

    whole = slots[tokens // SEG - 1] == slots[0]

    @pl.when(whole)
    def _():
        for i in range(TOGETHER):
            head(step * TOGETHER + i, slice(None))

    @pl.when(jnp.logical_not(whole))
    def _():
        for i in range(TOGETHER):
            for b in range(tokens // SEG):
                head(step * TOGETHER + i, slice(b * SEG, (b + 1) * SEG))


def mix_kernel(
    slots, x_ref, cot_ref, mod_ref, o_ref, lse_ref, w_out_ref, perm_ref,
    lse_out_ref, attn_ref, mid_ref, low_ref, gf_ref, att_units_ref, ffn_units_ref,
):
    width = x_ref.shape[1]
    here = slots_here(slots, x_ref.shape[0])
    lse_out_ref[...] = lse_ref[...].T
    attended = o_ref[...].astype(bf16)
    att_units_ref[...] = nt(perm_ref[...], attended).astype(bf16).reshape(att_units_ref.shape)
    attn = nn(attended, w_out_ref[...])
    attn_ref[...] = attn
    mid = by_slot(
        lambda slot, x, rows: x.astype(f32) + part(mod_ref, slot, 2, width) * rows, here, x_ref[...], attn
    )
    mid_ref[...] = mid
    norm, _ = normed(mid)

    def modulate(slot, rows):
        return (rows * (1.0 + part(mod_ref, slot, 4, width)) + part(mod_ref, slot, 3, width)).astype(bf16)

    low = by_slot(modulate, here, norm)
    low_ref[...] = low
    ffn_units_ref[...] = nt(perm_ref[...], low).astype(bf16).reshape(ffn_units_ref.shape)
    gf_ref[...] = by_slot(
        lambda slot, rows: (rows.astype(f32) * part(mod_ref, slot, 5, width)).astype(bf16), here, cot_ref[...]
    )


def ffn_kernel(
    bits, x_ref, gf_hbm, units_hbm, wg_ref, wu_ref, wd_ref,
    gate_send_ref, gate_own_ref, up_send_ref, up_own_ref, down_send_ref, down_own_ref, ffn_hbm, dmod_hbm,
    turned_ref, gf_ref, units_ref, ffn_ref, dmod_ref, sems, *, n_mod, rows_ff,
):
    core = bits[0]
    first = pl.program_id(0) == 0
    last = pl.program_id(0) == pl.num_programs(0) - 1
    load_gf = pltpu.make_async_copy(gf_hbm, gf_ref, sems.at[0])
    load_units = pltpu.make_async_copy(units_hbm, units_ref, sems.at[1])
    store_ffn = pltpu.make_async_copy(ffn_ref, ffn_hbm, sems.at[2])
    store_dmod = pltpu.make_async_copy(dmod_ref, dmod_hbm, sems.at[3])

    @pl.when(first)
    def _():
        load_gf.start()
        load_units.start()
        ffn_ref[...] = jnp.zeros_like(ffn_ref)
        dmod_ref[...] = jnp.zeros_like(dmod_ref)

    gate = nn(x_ref[...], wg_ref[...])
    up = nn(x_ref[...], wu_ref[...])

    @pl.when(first)
    def _():
        load_gf.wait()
        load_units.wait()

    grad_hidden = nt(gf_ref[...], wd_ref[...])
    sigmoid = 1.0 / (1.0 + jnp.exp(-gate))
    silu = gate * sigmoid
    hidden = (silu * up).astype(bf16)
    turned = hidden.T
    for index in range(turned.shape[0] // rows_ff):
        unit, rest = unit_of(index, n_mod)
        turned_ref[unit, rest * rows_ff : (rest + 1) * rows_ff] = turned[
            index * rows_ff : (index + 1) * rows_ff
        ]
    dg = (grad_hidden * up * (sigmoid * (1.0 + gate * (1.0 - sigmoid)))).astype(bf16)
    du = (grad_hidden * silu).astype(bf16)

    ffn_ref[...] += nn(hidden, wd_ref[...])
    dmod_ref[...] += nt(dg, wg_ref[...]) + nt(du, wu_ref[...])

    @pl.when(last)
    def _():
        store_ffn.start()
        store_dmod.start()

    product(units_ref, 1 - core, dg, gate_send_ref)
    product(units_ref, 1 - core, du, up_send_ref)
    product(turned_ref, 1 - core, gf_ref[...], down_send_ref)
    product(units_ref, core, dg, gate_own_ref)
    product(units_ref, core, du, up_own_ref)
    product(turned_ref, core, gf_ref[...], down_own_ref)

    @pl.when(last)
    def _():
        store_ffn.wait()
        store_dmod.wait()


def middle_kernel(
    slots, mid_ref, ffn_ref, dmod_ref, cot_ref, attn_ref, o_ref, units_ref, mod_ref, w_out_ref, gather_ref,
    out_ref, grad_mid_ref, do_ref, dot_ref, sums_ref, send_ref, own_ref, acc_ref,
):
    width = mid_ref.shape[1]
    block = pl.program_id(0)
    here = slots_here(slots, mid_ref.shape[0])
    segments = pl.num_programs(0) * len(here)
    incoming = cot_ref[...].astype(f32)
    mid = mid_ref[...]
    out_ref[...] = by_slot(
        lambda slot, rows, ffn: (rows + part(mod_ref, slot, 5, width) * ffn).astype(bf16), here, mid, ffn_ref[...]
    )
    norm, inverse = normed(mid)
    dmod = dmod_ref[...]
    scaled = by_slot(lambda slot, rows: rows * (1.0 + part(mod_ref, slot, 4, width)), here, dmod)
    grad_mid = incoming + norm_back(scaled, norm, inverse)
    grad_mid_ref[...] = grad_mid
    ga = by_slot(lambda slot, rows: (rows * part(mod_ref, slot, 2, width)).astype(bf16), here, grad_mid)
    grow = nn(units_ref[...].reshape(width, -1), ga)

    @pl.when(block == 0)
    def _():
        acc_ref[...] = grow

    @pl.when(block > 0)
    def _():
        acc_ref[...] += grow

    @pl.when(block == pl.num_programs(0) - 1)
    def _():
        halves_out(acc_ref, slots[segments], send_ref, own_ref)

    do = nt(ga, w_out_ref[...]).astype(bf16)
    do_ref[...] = do
    dot_ref[...] = head_sum(do.astype(f32) * o_ref[...], gather_ref).T

    @pl.when(block == 0)
    def _():
        sums_ref[...] = jnp.zeros_like(sums_ref)

    for index, term in enumerate((grad_mid * attn_ref[...], dmod, dmod * norm, incoming * ffn_ref[...])):
        add_by_slot(sums_ref, here, index, term)


def attend_back_kernel(
    slots, q_ref, k_ref, v_ref, do_ref, lse_ref, dot_ref, kt_ref, dqt_ref, dk_ref, dv_low_ref, dv_ref,
    *, first, base, base_row,
):
    tokens = q_ref.shape[0]

    @pl.when(pl.program_id(0) == 0)
    def _():
        dqt_ref[...] = jnp.zeros_like(dqt_ref)
        dk_ref[...] = jnp.zeros_like(dk_ref)
        dv_ref[...] = jnp.zeros_like(dv_ref)

    def head(h, rows):
        start, offset = window(h, kt_ref.shape[0])
        inside = head_lanes(offset)
        columns = pl.ds(start, WIN)
        out_columns = pl.ds(pl.multiple_of(start - base, 128), WIN)
        first_row = pl.multiple_of((h * HD) // 16 * 16, 16)
        out_rows = pl.ds(pl.multiple_of(first_row - base_row, 16), HD + 8)
        row = lax.broadcasted_iota(jnp.int32, (HD + 8, 1), 0) + first_row
        own_rows = (row >= h * HD) & (row < h * HD + HD)
        query = q_ref[rows, columns]
        grad_out = do_ref[rows, columns]
        key = jnp.where(inside, k_ref[rows, columns], 0)
        value = jnp.where(inside, v_ref[rows, columns], 0)
        probs = jnp.exp2(nt(key, query) * SCORE_LOG2 - lse_ref[pl.ds(h, 1), rows])
        scores = (probs * (nt(value, grad_out) - dot_ref[pl.ds(h, 1), rows])).astype(bf16)
        dv_ref[rows, out_columns] += jnp.where(inside, nn(probs.astype(bf16), grad_out), 0.0)
        dk_ref[rows, out_columns] += jnp.where(inside, nn(scores, query) * SCORE_SCALE, 0.0)
        turned = nn(kt_ref[pl.ds(first_row, HD + 8), rows], scores) * SCORE_SCALE
        dqt_ref[out_rows, rows] += jnp.where(own_rows, turned, 0.0)

    whole = slots[tokens // SEG - 1] == slots[0]
    begin = first + pl.program_id(0) * TOGETHER

    @pl.when(whole)
    def _():
        for i in range(TOGETHER):
            head(begin + i, slice(None))

    @pl.when(jnp.logical_not(whole))
    def _():
        for i in range(TOGETHER):
            for b in range(tokens // SEG):
                head(begin + i, slice(b * SEG, (b + 1) * SEG))

    @pl.when(pl.program_id(0) == pl.num_programs(0) - 1)
    def _():
        dv_low_ref[...] = dv_ref[...].astype(bf16)


def head_span(first, end, width):
    begin = lambda head: min(head * HD // 128, width // 128 - WIN // 128) * 128
    return begin(first), begin(end - 1) + WIN, first * HD // 16 * 16, (end - 1) * HD // 16 * 16 + HD + 8


def join_spans(low, high, begin, axis):
    size = low.shape[axis] - begin
    if size == 0:
        return jnp.concatenate([low, high], axis=axis)
    cut = lambda arr, start, stop: lax.slice_in_dim(arr, start, stop, axis=axis)
    middle = cut(low, begin, begin + size) + cut(high, 0, size)
    return jnp.concatenate([cut(low, 0, begin), middle, cut(high, size, high.shape[axis])], axis=axis)


def project_back_kernel(
    bits, dqt0_ref, dqt1_ref, dk0_ref, dk1_ref, raw_ref, inv_ref, q_ref, k_ref, units_ref,
    coords_ref, cos_ref, sin_ref, gain_ref, gather_ref, spread_ref, fold_ref,
    gq_ref, gk_ref, gains_low_ref, q_send_ref, q_own_ref, k_send_ref, k_own_ref, accq_ref, acck_ref, gains_ref,
    *, base, base_row,
):
    width = q_ref.shape[1]
    block = pl.program_id(0)

    @pl.when(block == 0)
    def _():
        gains_ref[...] = jnp.zeros_like(gains_ref)
        accq_ref[...] = jnp.zeros_like(accq_ref)
        acck_ref[...] = jnp.zeros_like(acck_ref)

    cosine, sine = angles(coords_ref, cos_ref, sin_ref)
    parts = ((q_ref, gq_ref, accq_ref), (k_ref, gk_ref, acck_ref))
    for index, (low_ref, out_ref, acc_ref) in enumerate(parts):
        if index == 0:
            grad = join_spans(dqt0_ref[...], dqt1_ref[...], base_row, 0).T
        else:
            grad = join_spans(dk0_ref[...], dk1_ref[...], base, 1)
        raw = raw_ref[:, index * width : (index + 1) * width]
        inverse = head_spread(inv_ref[:, index * 128 : (index + 1) * 128], spread_ref)
        mean = head_sum(grad * low_ref[...].astype(f32), gather_ref) * (1.0 / HD)
        norm = raw * inverse
        back = grad * cosine - partner(grad) * sine
        gains_ref[index : index + 1, :] += jnp.sum(back * norm, axis=0, keepdims=True)
        grad_raw = (
            inverse * (back * gain_ref[index : index + 1, :] - norm * head_spread(mean, spread_ref))
        ).astype(bf16)
        out_ref[...] = grad_raw
        acc_ref[...] += nn(units_ref[...].reshape(width, -1), grad_raw)

    @pl.when(block == pl.num_programs(0) - 1)
    def _():
        halves_out(accq_ref, bits[0], q_send_ref, q_own_ref)
        halves_out(acck_ref, bits[0], k_send_ref, k_own_ref)
        terms = split3(gains_ref[...])
        sums = sum(nn(term.astype(bf16), fold_ref[...]) for term in terms)
        high = sums.astype(bf16).astype(f32)
        row = lax.broadcasted_iota(jnp.int32, (8, 1), 0)
        mine = 4 * bits[1]
        placed = jnp.zeros((8, 128), f32)
        for index, term in enumerate((high[0:1], (sums - high)[0:1], high[1:2], (sums - high)[1:2])):
            placed = jnp.where(row == mine + index, term, placed)
        gains_low_ref[...] = placed.astype(bf16)


def input_back_kernel(
    slots, gq_ref, gk_ref, dv0_ref, dv1_ref, x_ref, grad_mid_ref, mod_ref, w_ref, other_sums_ref, gains_ref,
    grad_x_ref, grad_own_ref, grad_other_ref, sums_ref, *, base,
):
    width = x_ref.shape[1]
    block = pl.program_id(0)
    here = slots_here(slots, x_ref.shape[0])
    last_block = pl.num_programs(0) - 1
    segments = pl.num_programs(0) * len(here)
    dmod = nt(gq_ref[...], w_ref[:, :width]) + nt(gk_ref[...], w_ref[:, width : 2 * width])
    dmod = dmod + nt(join_spans(dv0_ref[...], dv1_ref[...], base, 1), w_ref[:, 2 * width :])
    norm, inverse = normed(x_ref[...].astype(f32))
    scaled = by_slot(lambda slot, rows: rows * (1.0 + part(mod_ref, slot, 1, width)), here, dmod)
    grad_x = grad_mid_ref[...] + norm_back(scaled, norm, inverse)
    grad_x_ref[...] = grad_x.astype(bf16)

    @pl.when(block == 0)
    def _():
        sums_ref[...] = jnp.zeros_like(sums_ref)

    for index, term in enumerate((dmod, dmod * norm)):
        add_by_slot(sums_ref, here, index, term)

    @pl.when(block == last_block)
    def _():
        mod = slots[segments + 1]
        count = sums_ref.shape[0]
        half = 3 * width
        mine = jnp.concatenate([sums_ref[...]] * 2, axis=0)
        rest = jnp.concatenate([other_sums_ref[...]] * 2, axis=0)
        row = lax.broadcasted_iota(jnp.int32, (2 * count, 1), 0) // count
        attn_part = jnp.where(row == mod, jnp.concatenate([mine, rest[:, :width]], axis=1), 0.0)
        ffn_part = jnp.where(row == mod, rest[:, width:], 0.0)
        grad_own_ref[:, :half] = jnp.where(mod == 0, attn_part, ffn_part).astype(bf16)
        grad_other_ref[:, :half] = jnp.where(mod == 0, ffn_part, attn_part).astype(bf16)
        grad_own_ref[:, half:] = gains_ref[...]
        grad_other_ref[:, half:] = gains_ref[...]


def value_kernel(bits, units_ref, dv0_ref, dv1_ref, send_ref, own_ref, *, base):
    rhs = join_spans(dv0_ref[...], dv1_ref[...], base, 1)
    product(units_ref, 1 - bits[0], rhs, send_ref)
    product(units_ref, bits[0], rhs, own_ref)


def split_step(bits, ins, outs, *, lead, at, bit, pair_rows, cuts):
    send_ref, keep_ref = outs
    mine = bits[bit]
    start = 0
    for own_ref, got_ref, cut in zip(ins[::2], ins[1::2], cuts):
        columns, target = slice(None), slice(None)
        if cut:
            columns, target = slice(*cut), slice(start, start + cut[1] - cut[0])
            start = target.stop

        def total(*index):
            place = index + (slice(None), columns)
            return own_ref[place].astype(f32) + got_ref[place].astype(f32)

        if at is None:
            for j in range(max(lead, 1)):
                index = (j,) if lead else ()
                value = total(*index)
                rows = pair_rows or value.shape[0] // 2
                for p in range(value.shape[0] // (2 * rows)):
                    first = value[2 * p * rows : (2 * p + 1) * rows]
                    second = value[(2 * p + 1) * rows : (2 * p + 2) * rows]
                    place = index + (slice(p * rows, (p + 1) * rows), target)
                    send_ref[place] = jnp.where(mine == 1, first, second).astype(bf16)
                    keep_ref[place] = jnp.where(mine == 1, second, first).astype(keep_ref.dtype)
            continue
        for j in range(lead // 2):
            place = ((j,) if lead > 2 else ()) + (slice(None), target)
            away = 1 - mine if lead == 2 else 2 * (1 - mine) + j if at == 0 else 2 * j + 1 - mine
            own = mine if lead == 2 else 2 * mine + j if at == 0 else 2 * j + mine
            send_ref[place] = total(away).astype(bf16)
            keep_ref[place] = total(own).astype(keep_ref.dtype)


def merge_step(bits, ins, outs, *, bit, parts):
    send_ref, keep_ref = outs
    start = 0
    for own_ref, got_ref, pieces in zip(ins[::2], ins[1::2], parts):
        value = own_ref[...].astype(f32) + got_ref[...].astype(f32)
        rows, columns = value.shape[0] // 2, value.shape[1]
        first, second = value[:rows], value[rows:]
        sent = jnp.where(bits[bit] == 1, first, second).astype(bf16)
        kept = jnp.where(bits[bit] == 1, second, first)
        for i in range(pieces):
            place = slice(start, start + columns)
            if pieces > 1:
                send_ref[:, place] = jnp.zeros_like(send_ref[:, place])
                keep_ref[:, place] = jnp.zeros_like(keep_ref[:, place])
            taken = slice(i * rows // pieces, (i + 1) * rows // pieces)
            send_ref[: rows // pieces, place] = sent[taken]
            keep_ref[: rows // pieces, place] = kept[taken]
            start += columns


def apart_step(bits, ins, outs, *, places):
    own_ref, got_ref = ins
    for out, at, start, stop, rows in places:
        value = own_ref[:, start:stop] + got_ref[:, start:stop].astype(f32)
        if rows is None:
            outs[out][:, at : at + stop - start] = value
        else:
            count = rows[1] - rows[0]
            outs[out][rows[0] : rows[1], :] = value[:count]


def pair_step(bits, ins, outs):
    own_ref, got_ref, activated_ref = ins
    width = activated_ref.shape[1]
    outs[0][:, :width] = activated_ref[...]
    outs[0][:, width:] = (own_ref[...].astype(f32) + got_ref[...].astype(f32)).astype(bf16)


def joined(ins):
    return jnp.concatenate([ref[...].astype(f32) for ref in ins], axis=0).astype(bf16)


def join_step(bits, ins, outs):
    outs[0][...] = joined(ins)


def last_step(bits, ins, outs):
    outs[0][...] = ins[0][...] + ins[1][...].astype(f32)


def ada_step(bits, ins, outs, *, width):
    rows = outs[0].shape[0]
    every = joined(ins)
    position = bits[0] + sum(bits[1 + k] * 2**k for k in range(1, (width // rows).bit_length() - 1))
    feature = lax.broadcasted_iota(jnp.int32, (width, 128), 0)
    place = lax.broadcasted_iota(jnp.int32, (width, 128), 1)
    chosen = (feature == position * rows + place) & (place < rows)
    own = nn(every[:, :width], chosen.astype(f32).astype(bf16)).astype(bf16)
    half = outs[0].shape[1]
    outs[0][...] = tn(own, every[:, width : width + half])[:rows]
    terms = every[:, width + half :].astype(f32)
    kind = lax.broadcasted_iota(jnp.int32, (terms.shape[0], 1), 0) // 2 % 2
    for index in range(2):
        outs[1][index : index + 1, :] = jnp.sum(jnp.where(kind == index, terms, 0.0), axis=0, keepdims=True)


def step_kernel(bits, *refs, plans):
    n_in = sum(plan[1] for plan in plans)
    ins, outs = refs[:n_in], refs[n_in:]
    for function, takes, gives in plans:
        function(bits, ins[:takes], outs[:gives])
        ins, outs = ins[takes:], outs[gives:]


class Chain:
    def __init__(self):
        self.last = None

    def __call__(
        self, kernel, grid, in_specs, out_specs, out_shape, args, scalars=None, scratch=(), name=None, aliases=None
    ):
        ahead = 0 if scalars is None else 1
        body = kernel
        token = ()
        if self.last is not None:
            token = (self.last,)
            in_specs = [pl.BlockSpec(memory_space=pl.ANY)] + list(in_specs)

            def body(*refs):
                kernel(*refs[:ahead], *refs[ahead + 1 :])

        spec = pltpu.PrefetchScalarGridSpec(
            num_scalar_prefetch=ahead,
            grid=grid,
            in_specs=in_specs,
            out_specs=out_specs,
            scratch_shapes=scratch,
        )
        outs = pl.pallas_call(
            body,
            grid_spec=spec,
            input_output_aliases=aliases or {},
            out_shape=out_shape,
            compiler_params=pltpu.CompilerParams(vmem_limit_bytes=VMEM),
            cost_estimate=pl.CostEstimate(flops=1, bytes_accessed=1, transcendentals=0),
            name=name,
        )(*(() if scalars is None else (scalars,)), *token, *args)
        self.last = outs[0]
        return outs


def shape(dims, dtype):
    return jax.ShapeDtypeStruct(dims, dtype)


def fixed(dims):
    return pl.BlockSpec(dims, lambda *_: (0,) * len(dims), pipeline_mode=pl.Buffered(1))


def rows_of(dims, axis=0):
    return pl.BlockSpec(dims, lambda b, *_: tuple(b if i == axis else 0 for i in range(len(dims))))


def whole(dims):
    return rows_of(dims, None)


def column_parts(dims, steps):
    return rows_of(dims[:-1] + (dims[-1] // steps,), len(dims) - 1)


class Reducer:
    def __init__(self, n_dp, n_mod, call):
        self.n_dp, self.n_mod, self.call = n_dp, n_mod, call
        self.position = lax.axis_index("dp")
        steps = range(n_dp.bit_length() - 1)
        dp_bits = [lax.shift_right_logical(self.position, step) & 1 for step in steps]
        self.bits = jnp.stack([dp_bits[0], lax.axis_index("mod")] + dp_bits[1:]).astype(jnp.int32)

    def swap(self, arr, bit):
        if bit == "mod":
            return lax.ppermute(arr, "mod", [(i, i ^ 1) for i in range(self.n_mod)])
        return lax.ppermute(arr, "dp", [(i, i ^ (1 << bit)) for i in range(self.n_dp)])

    def bit_of(self, bit):
        return 1 if bit == "mod" else bit + 1 if bit else 0

    def fold(self, streams, name, last=False):
        plans, args, outs = [], [], []
        for stream in streams:
            function, shapes = stream.last_plan() if last else stream.plan()
            inputs = stream.inputs()
            plans.append((function, len(inputs), len(shapes)))
            args += inputs
            outs += shapes
        size = sum(arg.size for arg in args)
        split = all(
            isinstance(stream, Stream) and stream.side is None and stream.own.shape[-1] % 384 == 0
            for stream in streams
        )
        steps = 3 if split and size > 2**20 else 1
        results = self.call(
            functools.partial(step_kernel, plans=plans),
            (steps,),
            [column_parts(arg.shape, steps) for arg in args],
            [column_parts(out.shape, steps) for out in outs],
            outs,
            args,
            scalars=self.bits,
            name=name,
        )
        results = list(results)
        if last:
            return results
        for stream, plan in zip(streams, plans):
            stream.step(results[: plan[2]])
            results = results[plan[2] :]

    def pass_on(self, arrays):
        anywhere = [pl.BlockSpec(memory_space=pl.ANY)] * len(arrays)
        return self.call(
            lambda *refs: None,
            (1,),
            anywhere,
            anywhere,
            [shape(arr.shape, arr.dtype) for arr in arrays],
            arrays,
            name="pass_on",
            aliases={i + 1: i for i in range(len(arrays))},
        )


class Stream:
    def __init__(self, reducer, sent, own, first, pair_rows=None):
        self.r, self.own, self.pair_rows = reducer, own, pair_rows
        order = ["mod", 1, 2]
        self.steps = order[first:] + order[:first] + list(range(3, reducer.n_dp.bit_length() - 1))
        self.lead = ["mod", 1]
        self.side = None
        self.got = reducer.swap(sent, 0)

    def inputs(self):
        return [self.own, self.got] + ([self.side[0].own, self.side[0].got] if self.side else [])

    def plan(self):
        bit = self.steps[0]
        dims = self.own.shape
        at = self.lead.index(bit) if bit in self.lead else None
        cuts = [None]
        if self.side is not None:
            cuts = [(0, dims[-1]), self.side[1]]
            dims = dims[:-1] + (dims[-1] + self.side[1][1] - self.side[1][0],)
        function = functools.partial(
            split_step, lead=dims[0] if self.lead else 0, at=at, bit=self.r.bit_of(bit), pair_rows=self.pair_rows,
            cuts=cuts,
        )
        if at is None:
            dims = dims[:-2] + (dims[-2] // 2, dims[-1])
        else:
            dims = dims[1:] if len(self.lead) == 1 else (2,) + dims[1:]
        return function, [shape(dims, bf16), shape(dims, bf16 if len(self.lead) == 2 else f32)]

    def step(self, results):
        bit = self.steps.pop(0)
        if bit in self.lead:
            self.lead.remove(bit)
        self.side = None
        sent, self.own = results
        self.got = self.r.swap(sent, bit)

    def join(self, stream, cut):
        self.side = (stream, cut)


class Merged:
    def __init__(self, streams):
        self.streams, self.r, self.bit = streams, streams[0].r, streams[0].steps[0]
        self.own = self.places = self.shapes = None

    def inputs(self):
        if self.own is not None:
            return [self.own, self.got]
        return [arr for stream in self.streams for arr in (stream.own, stream.got)]

    def plan(self):
        parts = [3 if stream.pair_rows else 1 for stream in self.streams]
        columns = sum(pieces * stream.own.shape[1] for pieces, stream in zip(parts, self.streams))
        dims = (self.streams[0].own.shape[0] // 2, columns)
        function = functools.partial(merge_step, bit=self.r.bit_of(self.bit), parts=parts)
        return function, [shape(dims, bf16), shape(dims, f32)]

    def step(self, results):
        sent, self.own = results
        self.got = self.r.swap(sent, self.bit)

    def last_plan(self):
        if self.places is None:
            return last_step, [shape(self.own.shape, f32)]
        return functools.partial(apart_step, places=self.places), self.shapes


class Gather:
    def __init__(self, reducer, sent, own, activated):
        self.r, self.own, self.activated = reducer, own, activated
        self.steps = list(range(reducer.n_dp.bit_length() - 2, -1, -1))
        self.got = reducer.swap(sent, "mod")
        self.pair = None

    def inputs(self):
        return [self.own, self.got] + ([self.activated] if self.pair is None else [])

    def plan(self):
        rows, columns = self.own.shape
        if self.pair is None:
            return pair_step, [shape((rows, columns + self.activated.shape[1]), bf16)]
        return join_step, [shape((2 * rows, columns), bf16)]

    def step(self, results):
        (self.own,) = results
        if self.pair is None:
            self.pair = self.own
        self.got = self.r.swap(self.own, self.steps.pop(0))

    def last_plan(self):
        width = self.activated.shape[1]
        function = functools.partial(ada_step, width=width)
        dims = (width // self.r.n_dp, self.own.shape[1] - width - 128)
        return function, [shape(dims, f32), shape((2, 128), f32)]


def silu_grad(v):
    sigmoid = jax.nn.sigmoid(v)
    return sigmoid * (1.0 + v * (1.0 - sigmoid))


def pair_order(own, other, mod):
    return jnp.where(mod == 0, jnp.stack([own, other]), jnp.stack([other, own]))


def body(
    n_dp, n_mod, tokens, cond, segments, coords, w_ada, w_qkv, q_gain, k_gain, w_out, w_gate, w_up,
    w_down, cotangent,
):
    _, count, width = tokens.shape
    slots_n = cond.shape[1]
    half = w_ada.shape[1]
    ff = w_gate.shape[1]
    blocks = count // TB
    n_dev = n_dp * n_mod
    call = Chain()
    reducer = Reducer(n_dp, n_mod, call)
    mod_index = lax.axis_index("mod")
    x = tokens[0]
    cot = cotangent[0]
    slots = segments[0, ::SEG]
    coord = coords[0]
    cos_table, sin_table = (jnp.asarray(t) for t in rope_tables(width))
    gather, spread, head_fold = (jnp.asarray(t) for t in head_tables(width))
    perm = jnp.asarray(unit_permutation(width, n_dp, n_mod))
    gains = jnp.stack([jnp.tile(q_gain, HEADS), jnp.tile(k_gain, HEADS)])

    cond_both = pair_order(cond[0], reducer.swap(cond[0], "mod"), mod_index)
    activated = jax.nn.silu(cond_both).astype(bf16).reshape(-1, width)
    mod_half = jnp.dot(activated, w_ada, preferred_element_type=f32).astype(bf16)
    mod_half = mod_half.reshape(n_mod, slots_n, half)
    own_half = lax.dynamic_index_in_dim(mod_half, mod_index, 0, keepdims=False)
    other_half = lax.dynamic_index_in_dim(mod_half, 1 - mod_index, 0, keepdims=False)
    pair = pair_order(own_half, reducer.swap(other_half, "mod"), mod_index)
    modulation = jnp.concatenate([pair[0], pair[1]], axis=1).astype(f32)

    token_f32 = shape((count, width), f32)
    token_bf16 = shape((count, width), bf16)
    units = shape((8, width // 8, count), bf16)
    units_spec = rows_of((8, width // 8, TB), 2)
    token_spec = rows_of((TB, width))
    mod_spec = fixed((slots_n, 6 * width))
    square = fixed((width, width))
    table_specs = [fixed(cos_table.shape), fixed(sin_table.shape), fixed((2, width)), fixed(gather.shape), fixed(spread.shape)]
    tables = (cos_table, sin_table, gains, gather, spread)
    lane_rows = shape((128, count), f32)
    macs = count * width * width

    attn_units, raw, inverse, query, key, value, key_t = call(
        project_kernel,
        (blocks,),
        [token_spec, mod_spec, fixed((width, 3 * width)), rows_of((2, TB), 1)] + table_specs + [square],
        [units_spec, rows_of((TB, 2 * width)), rows_of((TB, 256))] + [token_spec] * 3 + [rows_of((width, TB), 1)],
        [units, shape((count, 2 * width), f32), shape((count, 256), f32)] + [token_bf16] * 3
        + [shape((width, count), bf16)],
        (x, modulation, w_qkv, coord) + tables + (perm,),
        scalars=slots,
        name="project",
    )
    attended, lse_columns = call(
        attend_kernel,
        (HEADS // TOGETHER,),
        [fixed((count, width))] * 3,
        [fixed((count, width)), fixed((count, 128))],
        [token_f32, shape((count, 128), f32)],
        (query, key, value),
        scalars=slots,
        name="attend",
    )
    lse, attn, mid, ffn_in, grad_ffn, out_units, ffn_units = call(
        mix_kernel,
        (blocks,),
        [token_spec, token_spec, mod_spec, token_spec, rows_of((TB, 128)), square, square],
        [rows_of((128, TB), 1)] + [token_spec] * 4 + [units_spec] * 2,
        [lane_rows, token_f32, token_f32, token_bf16, token_bf16, units, units],
        (x, cot, modulation, attended, lse_columns, w_out, perm),
        scalars=slots,
        name="mix",
    )

    anywhere = pl.BlockSpec(memory_space=pl.ANY)
    rows_ff = ff // n_dev
    chunk = 768
    piece = chunk // 8
    half_units = lambda rows, columns: shape((4, rows, columns), bf16)
    square_send = [fixed((4, width // 8, width))] * 2
    square_shapes = [half_units(width // 8, width)] * 2
    gate_send, gate_own, up_send, up_own, down_send, down_own, ffn, grad_mod_ffn = call(
        functools.partial(ffn_kernel, n_mod=n_mod, rows_ff=rows_ff),
        (ff // chunk,),
        [fixed((count, width)), anywhere, anywhere]
        + [rows_of((width, chunk), 1)] * 2 + [rows_of((chunk, width))],
        [rows_of((4, width // 8, chunk), 2)] * 4
        + [rows_of((4, 1, piece, width), 1)] * 2 + [anywhere] * 2,
        [half_units(width // 8, ff)] * 4
        + [shape((4, ff // chunk, piece, width), bf16)] * 2 + [token_f32] * 2,
        (ffn_in, grad_ffn, ffn_units, w_gate, w_up, w_down),
        scalars=reducer.bits,
        scratch=[
            pltpu.VMEM((8, piece, count), bf16),
            pltpu.VMEM((count, width), bf16),
            pltpu.VMEM(units.shape, bf16),
            pltpu.VMEM((count, width), f32),
            pltpu.VMEM((count, width), f32),
            pltpu.SemaphoreType.DMA((4,)),
        ],
        name="ffn",
    )
    gate = Stream(reducer, gate_send, gate_own, 0)
    up = Stream(reducer, up_send, up_own, 1)
    down = Stream(
        reducer, down_send.reshape(4, ff // 8, width), down_own.reshape(4, ff // 8, width), 2, rows_ff
    )

    slots_core = jnp.concatenate([slots, reducer.bits[:2]])
    seg_spec = rows_of((SEG, width))
    output, grad_mid, grad_attended, dot_term, sums_b, out_send, out_own = call(
        middle_kernel,
        (count // SEG,),
        [seg_spec] * 6 + [rows_of((8, width // 8, SEG), 2), mod_spec, square, fixed(gather.shape)],
        [seg_spec] * 3 + [rows_of((128, SEG), 1), fixed((slots_n, 4 * width))] + square_send,
        [token_bf16, token_f32, token_bf16, lane_rows, shape((slots_n, 4 * width), f32)] + square_shapes,
        (mid, ffn, grad_mod_ffn, cot, attn, attended, out_units, modulation, w_out, gather),
        scalars=slots_core,
        scratch=[pltpu.VMEM((width, width), f32)],
        name="middle",
    )
    out = Stream(reducer, out_send, out_own, 1)
    early = [gate, up, down]
    middle_cut = width // 256 * 128 + 128
    gate.join(out, (0, middle_cut))
    up.join(out, (middle_cut, width))
    reducer.fold(early, "early")

    def attend_back(first, end, name):
        begin, stop, begin_row, stop_row = head_span(first, end, width)
        columns, rows = stop - begin, stop_row - begin_row
        used = fixed((count, stop))
        return call(
            functools.partial(attend_back_kernel, first=first, base=begin, base_row=begin_row),
            ((end - first) // TOGETHER,),
            [used] * 4 + [fixed((128, count))] * 2 + [fixed((width, count))],
            [fixed((rows, count))] + [fixed((count, columns))] * 2,
            [shape((rows, count), f32), shape((count, columns), f32), shape((count, columns), bf16)],
            (query, key, value, grad_attended, lse, dot_term, key_t),
            scratch=[pltpu.VMEM((count, columns), f32)],
            scalars=slots,
            name=name,
        )

    cut = 3 * HEADS // 4
    dqt0, dk0, dv0 = attend_back(0, cut, "attend_back_0")
    reducer.fold(early, "early")
    dqt1, dk1, dv1 = attend_back(cut, HEADS, "attend_back_1")
    base, _, base_row, _ = head_span(cut, HEADS, width)
    v_send, v_own = call(
        functools.partial(value_kernel, base=base),
        (1,),
        [whole(units.shape), whole(dv0.shape), whole(dv1.shape)],
        [whole((4, width // 8, width))] * 2,
        square_shapes,
        (attn_units, dv0, dv1),
        scalars=reducer.bits,
        name="value",
    )
    v_part = Stream(reducer, v_send, v_own, 2)
    reducer.fold(early, "early")
    grad_q, grad_k, gains_low, q_send, q_own, k_send, k_own = call(
        functools.partial(project_back_kernel, base=base, base_row=base_row),
        (count // SEG,),
        [rows_of((dqt0.shape[0], SEG), 1), rows_of((dqt1.shape[0], SEG), 1)]
        + [rows_of((SEG, dk0.shape[1])), rows_of((SEG, dk1.shape[1]))]
        + [rows_of((SEG, 2 * width)), rows_of((SEG, 256)), seg_spec, seg_spec, rows_of((8, width // 8, SEG), 2), rows_of((2, SEG), 1)]
        + table_specs + [fixed(head_fold.shape)],
        [seg_spec] * 2 + [fixed((8, 128))] + square_send * 2,
        [token_bf16] * 2 + [shape((8, 128), bf16)] + square_shapes * 2,
        (dqt0, dqt1, dk0, dk1, raw, inverse, query, key, attn_units, coord) + tables + (head_fold,),
        scalars=reducer.bits,
        scratch=[pltpu.VMEM((width, width), f32)] * 2 + [pltpu.VMEM((2, width), f32)],
        name="project_back",
    )
    waiting = early + [v_part]
    *arrived, q_send, k_send = reducer.pass_on([stream.got for stream in waiting] + [q_send, k_send])
    for stream, got in zip(waiting, arrived):
        stream.got = got
    q_part = Stream(reducer, q_send, q_own, 1)
    k_part = Stream(reducer, k_send, k_own, 0)
    late = [q_part, k_part, v_part]
    extra = n_dp.bit_length() - 5
    reducer.fold([v_part], "v")
    for _ in range(extra):
        reducer.fold(early, "early")
    rows_d = width // n_dev
    merged = Merged([gate, up, down])
    third = rows_ff // 3
    gate_end = ff + middle_cut
    up_end = gate_end + ff + width - middle_cut
    merged.places = [
        (0, 0, 0, ff, None),
        (2, 0, ff, gate_end, None),
        (1, 0, gate_end, gate_end + ff, None),
        (2, middle_cut, gate_end + ff, up_end, None),
    ] + [
        (3, 0, up_end + i * width, up_end + (i + 1) * width, (i * third, (i + 1) * third)) for i in range(3)
    ]
    merged.shapes = [shape((rows_d, ff), f32)] * 2 + [shape((rows_d, width), f32), shape((rows_ff, width), f32)]
    early = [merged]
    reducer.fold(early, "early")
    reducer.fold([q_part, k_part], "late")
    grad_tokens, mod_own, mod_other = call(
        functools.partial(input_back_kernel, base=base),
        (blocks,),
        [token_spec] * 2 + [rows_of((TB, dv0.shape[1])), rows_of((TB, dv1.shape[1]))] + [token_spec] * 2
        + [mod_spec, fixed((width, 3 * width)), fixed((slots_n, 4 * width)), fixed((8, 128))],
        [token_spec] + [fixed((2 * slots_n, half + 128))] * 2,
        [token_bf16] + [shape((2 * slots_n, half + 128), bf16)] * 2,
        (grad_q, grad_k, dv0, dv1, x, grad_mid, modulation, w_qkv, sums_b, gains_low),
        scalars=slots_core,
        scratch=[pltpu.VMEM((slots_n, 2 * width), f32)],
        name="input_back",
    )
    every_mod = Gather(reducer, mod_other, mod_own, activated)
    reducer.fold([every_mod], "pair")
    reducer.fold(late, "late")
    reducer.fold([every_mod], "every")
    summed_gate, summed_up, summed_out, summed_down = reducer.fold(early, "early_last", last=True)
    for _ in range(1 + extra):
        reducer.fold(late + [every_mod], "late")
    late = [Merged(late)]
    reducer.fold(late + [every_mod], "late")
    summed_qkv, grad_w_ada, gain_grads = reducer.fold(late + [every_mod], "late_last", last=True)
    grad_activated = jnp.einsum("nc,dc->nd", every_mod.pair[:, width : width + half], w_ada, preferred_element_type=f32)
    grad_activated = grad_activated.reshape(n_mod, slots_n, width)
    own_part = lax.dynamic_index_in_dim(grad_activated, mod_index, 0, keepdims=False)
    other_part = lax.dynamic_index_in_dim(grad_activated, 1 - mod_index, 0, keepdims=False)
    grad_own = own_part + reducer.swap(other_part.astype(bf16), "mod").astype(f32)
    grad_cond = grad_own[None] * silu_grad(cond)
    return (
        output[None],
        grad_tokens[None],
        grad_cond,
        grad_w_ada,
        summed_qkv,
        gain_grads[0, :HD],
        gain_grads[1, :HD],
        summed_out,
        summed_gate,
        summed_up,
        summed_down,
    )


def solution(mesh):
    rows = ("dp", "mod")
    in_specs = (
        P(rows, None, None),
        P(rows, None, None),
        P(rows, None),
        P(rows, None, None),
        P(None, "mod"),
        P(),
        P(),
        P(),
        P(),
        P(),
        P(),
        P(),
        P(rows, None, None),
    )
    out_specs = (
        P(rows, None, None),
        P(rows, None, None),
        P(rows, None, None),
        P("dp", "mod"),
        P(rows, None),
        P(),
        P(),
        P(rows, None),
        P(rows, None),
        P(rows, None),
        P(rows, None),
    )
    return jax.shard_map(
        functools.partial(body, mesh.shape["dp"], mesh.shape["mod"]),
        mesh=mesh,
        in_specs=in_specs,
        out_specs=out_specs,
        check_vma=False,
    )
```

```python
import functools

import jax
import jax.numpy as jnp
import numpy as np
from jax import lax
from jax.experimental import pallas as pl
from jax.experimental.pallas import tpu as pltpu
from jax.sharding import PartitionSpec as P

HEADS = 16
HD = 72
GRID = 32
EPS = 1e-06
ROPE_BASE = 10000.0
SEG = 256
TB = 512
WIN = 256
TOGETHER = 4
SCORE_SCALE = float(HD**-0.5)
SCORE_LOG2 = float(np.log2(np.e) * HD**-0.5)
VMEM = 60 * 2**20
f32 = jnp.float32
bf16 = jnp.bfloat16


def nn(a, b):
    return lax.dot_general(a, b, (((1,), (0,)), ((), ())), preferred_element_type=f32)


def nt(a, b):
    return lax.dot_general(a, b, (((1,), (1,)), ((), ())), preferred_element_type=f32)


def tn(a, b):
    return lax.dot_general(a, b, (((0,), (0,)), ((), ())), preferred_element_type=f32)


def split3(v):
    hi = v.astype(bf16).astype(f32)
    mid = (v - hi).astype(bf16).astype(f32)
    return hi, mid, v - hi - mid


def np_split3(v):
    v = v.astype(np.float32)
    hi = v.astype(jnp.bfloat16).astype(np.float32)
    mid = (v - hi).astype(jnp.bfloat16).astype(np.float32)
    return [part.astype(jnp.bfloat16) for part in (hi, mid, v - hi - mid)]


@functools.lru_cache(None)
def rope_tables(width):
    quarter = HD // 4
    freqs = ROPE_BASE ** (-np.arange(quarter, dtype=np.float64) / quarter)
    lane = np.arange(width) % HD
    group = lane // quarter
    angle = np.arange(GRID)[:, None] * freqs[lane % quarter][None, :]
    cosine, sine = np.cos(angle), np.sin(angle)
    sine = np.where((group % 2 == 0)[None, :], -sine, sine)
    uses_col = (group >= 2)[None, :]
    tables = []
    for table in (cosine, sine):
        whole = np.concatenate(
            [np.where(uses_col, 0.0, table), np.where(uses_col, table, 0.0)], axis=0
        )
        tables.append(np.concatenate(np_split3(whole), axis=0))
    return tables


@functools.lru_cache(None)
def head_tables(width):
    head = np.arange(width) // HD
    gather = np.zeros((width, 128), np.float32)
    for copy in range(3):
        gather[np.arange(width), copy * HEADS + head] = 1.0
    fold = np.zeros((width, 128), np.float32)
    fold[np.arange(width), np.arange(width) % HD] = 1.0
    return gather.astype(jnp.bfloat16), gather.T.astype(jnp.bfloat16), fold.astype(jnp.bfloat16)


def unit_of(index, n_mod):
    mod = index % n_mod
    dp = index // n_mod
    return (dp % 2) * 2 * n_mod + mod * 2 + (dp // 2) % 2, dp // 4


def reversed_bits(value, size):
    result = 0
    for bit in range(size.bit_length() - 1):
        result = 2 * result + (value >> bit) % 2
    return result


@functools.lru_cache(None)
def unit_permutation(width, n_dp, n_mod):
    rows = width // (n_dp * n_mod)
    matrix = np.zeros((width, width), np.float32)
    for index in range(n_dp * n_mod):
        unit, rest = unit_of(index, n_mod)
        start = unit * (width // 8) + reversed_bits(rest, n_dp // 4) * rows
        matrix[start + np.arange(rows), index * rows + np.arange(rows)] = 1.0
    return matrix.astype(jnp.bfloat16)


def normed(v):
    centred = v - jnp.mean(v, axis=-1, keepdims=True)
    inverse = lax.rsqrt(jnp.mean(centred * centred, axis=-1, keepdims=True) + EPS)
    return centred * inverse, inverse


def norm_back(e, norm, inverse):
    return inverse * (
        e - jnp.mean(e, axis=-1, keepdims=True) - norm * jnp.mean(e * norm, axis=-1, keepdims=True)
    )


def part(mod_ref, slot, index, width):
    return mod_ref[pl.ds(slot, 1), index * width : (index + 1) * width]


def slots_here(slots, rows):
    return [slots[pl.program_id(0) * (rows // SEG) + i] for i in range(rows // SEG)]


def by_slot(function, here, *values):
    done = [
        function(slot, *(value[i * SEG : (i + 1) * SEG] for value in values)) for i, slot in enumerate(here)
    ]
    return jnp.concatenate(done, axis=0)


def angles(coords_ref, cos_ref, sin_ref):
    value = lax.broadcasted_iota(jnp.int32, (GRID, 1), 0)
    hot = [(value == coords_ref[i : i + 1, :]).astype(f32) for i in range(2)]
    hot = jnp.concatenate(hot * 3, axis=0).astype(bf16)
    return tn(hot, cos_ref[...]), tn(hot, sin_ref[...])


def partner(v):
    width = v.shape[1]
    quarter = HD // 4
    lane = lax.broadcasted_iota(jnp.int32, (1, width), 1)
    leads = (lane // quarter) % 2 == 0
    return jnp.where(leads, pltpu.roll(v, width - quarter, 1), pltpu.roll(v, quarter, 1))


def head_sum(v, gather_ref):
    hi = v.astype(bf16)
    low = (v - hi.astype(f32)).astype(bf16)
    return nn(hi, gather_ref[...]) + nn(low, gather_ref[...])


def head_spread(v, spread_ref):
    hi, mid, low = split3(v)
    lane = lax.broadcasted_iota(jnp.int32, (1, 128), 1)
    chosen = jnp.where(lane < HEADS, hi, jnp.where(lane < 2 * HEADS, mid, low))
    return nn(chosen.astype(bf16), spread_ref[...])


def window(head, width):
    start = jnp.minimum((head * HD) // 128, width // 128 - WIN // 128) * 128
    return pl.multiple_of(start, 128), head * HD - start


def head_lanes(offset):
    lane = lax.broadcasted_iota(jnp.int32, (1, WIN), 1)
    return (lane >= offset) & (lane < offset + HD)


def product(units_ref, half, rhs, out_ref):
    _, rows, tokens = units_ref.shape
    units = units_ref[pl.ds(4 * half, 4)].reshape(4 * rows, tokens)
    out_ref[...] = nn(units, rhs).astype(bf16).reshape(out_ref.shape)


def halves_out(acc_ref, core, send_ref, own_ref):
    rows = acc_ref.shape[0] // 2
    for half, out_ref in ((1 - core, send_ref), (core, own_ref)):
        start = pl.multiple_of(half * rows, rows)
        out_ref[...] = acc_ref[pl.ds(start, rows)].astype(bf16).reshape(out_ref.shape)


def column_loads(source, target, sems, parts):
    columns = source.shape[1] // parts
    spans = [pl.ds(i * columns, columns) for i in range(parts)]
    return [pltpu.make_async_copy(source.at[:, span], target.at[:, span], sems.at[i]) for i, span in enumerate(spans)]


def wait_if(condition, copy):
    @pl.when(condition)
    def _():
        copy.wait()


def add_by_slot(sums_ref, here, index, term):
    width = term.shape[1]
    for i, slot in enumerate(here):
        rows = term[i * SEG : (i + 1) * SEG]
        sums_ref[pl.ds(slot, 1), index * width : (index + 1) * width] += jnp.sum(rows, axis=0, keepdims=True)


def project_kernel(
    slots, x_ref, mod_ref, w_hbm, coords_ref, cos_ref, sin_ref, gain_ref, gather_ref, spread_ref,
    perm_hbm, units_ref, raw_ref, inv_ref, q_ref, k_ref, v_ref, kt_ref, w_ref, perm_ref, sems,
):
    width = x_ref.shape[1]
    first = pl.program_id(0) == 0
    loads = column_loads(w_hbm, w_ref, sems, 3)
    load_perm = pltpu.make_async_copy(perm_hbm, perm_ref, sems.at[3])

    @pl.when(first)
    def _():
        for load in loads:
            load.start()
        load_perm.start()

    norm, _ = normed(x_ref[...].astype(f32))

    def modulate(slot, rows):
        return (rows * (1.0 + part(mod_ref, slot, 1, width)) + part(mod_ref, slot, 0, width)).astype(bf16)

    low = by_slot(modulate, slots_here(slots, x_ref.shape[0]), norm)
    cosine, sine = angles(coords_ref, cos_ref, sin_ref)
    for index, out_ref in enumerate((q_ref, k_ref)):
        wait_if(first, loads[index])
        raw = nn(low, w_ref[:, index * width : (index + 1) * width])
        raw_ref[:, index * width : (index + 1) * width] = raw
        inverse = lax.rsqrt(head_sum(raw * raw, gather_ref) * (1.0 / HD) + EPS)
        inv_ref[:, index * 128 : (index + 1) * 128] = inverse
        scaled = raw * head_spread(inverse, spread_ref) * gain_ref[index : index + 1, :]
        turned = scaled * cosine + partner(scaled) * sine
        out_ref[...] = turned.astype(bf16)
        if index == 1:
            kt_ref[...] = turned.T.astype(bf16)
    wait_if(first, loads[2])
    v_ref[...] = nn(low, w_ref[:, 2 * width :]).astype(bf16)
    wait_if(first, load_perm)
    units_ref[...] = nt(perm_ref[...], low).astype(bf16).reshape(units_ref.shape)


def attend_kernel(slots, q_ref, k_ref, v_ref, o_ref, lse_ref):
    step = pl.program_id(0)
    tokens, width = q_ref.shape
    lane128 = lax.broadcasted_iota(jnp.int32, (1, 128), 1)
    lane = lax.broadcasted_iota(jnp.int32, (1, WIN), 1)

    @pl.when(step == 0)
    def _():
        o_ref[...] = jnp.zeros_like(o_ref)
        lse_ref[...] = jnp.zeros_like(lse_ref)

    def head(h, rows):
        start, offset = window(h, width)
        inside = head_lanes(offset)
        columns = pl.ds(start, WIN)
        query = jnp.where(inside, q_ref[rows, columns], 0)
        value = jnp.where(inside, v_ref[rows, columns], 1)
        weight = jnp.exp2(nt(query, k_ref[rows, columns]) * SCORE_LOG2).astype(bf16)
        summed = nn(weight, value)
        free = jnp.where(offset > 0, 0, WIN - 1)
        total = jnp.sum(jnp.where(lane == free, summed, 0.0), axis=1, keepdims=True)
        o_ref[rows, columns] += jnp.where(inside, summed * (1.0 / total), 0.0)
        lse_ref[rows, :] += jnp.where(lane128 == h, jnp.log2(total), 0.0)

    whole = slots[tokens // SEG - 1] == slots[0]

    @pl.when(whole)
    def _():
        for i in range(TOGETHER):
            head(step * TOGETHER + i, slice(None))

    @pl.when(jnp.logical_not(whole))
    def _():
        for i in range(TOGETHER):
            for b in range(tokens // SEG):
                head(step * TOGETHER + i, slice(b * SEG, (b + 1) * SEG))


def mix_kernel(
    slots, x_ref, cot_ref, mod_ref, o_ref, lse_ref, w_out_ref, perm_ref,
    attended_ref, lse_out_ref, attn_ref, mid_ref, low_ref, gf_ref, att_units_ref, ffn_units_ref,
):
    width = x_ref.shape[1]
    here = slots_here(slots, x_ref.shape[0])
    lse_out_ref[...] = lse_ref[...].T
    attended = o_ref[...].astype(bf16)
    attended_ref[...] = attended
    att_units_ref[...] = nt(perm_ref[...], attended).astype(bf16).reshape(att_units_ref.shape)
    attn = nn(attended, w_out_ref[...])
    attn_ref[...] = attn.astype(bf16)
    mid = by_slot(
        lambda slot, x, rows: x.astype(f32) + part(mod_ref, slot, 2, width) * rows, here, x_ref[...], attn
    )
    mid_ref[...] = mid
    norm, _ = normed(mid)

    def modulate(slot, rows):
        return (rows * (1.0 + part(mod_ref, slot, 4, width)) + part(mod_ref, slot, 3, width)).astype(bf16)

    low = by_slot(modulate, here, norm)
    low_ref[...] = low
    ffn_units_ref[...] = nt(perm_ref[...], low).astype(bf16).reshape(ffn_units_ref.shape)
    gf_ref[...] = by_slot(
        lambda slot, rows: (rows.astype(f32) * part(mod_ref, slot, 5, width)).astype(bf16), here, cot_ref[...]
    )


def ffn_kernel(
    bits, x_ref, gf_hbm, units_hbm, wg_ref, wu_ref, wd_ref,
    gate_send_ref, gate_own_ref, up_send_ref, up_own_ref, down_send_ref, down_own_ref, ffn_hbm, dmod_hbm,
    turned_ref, gf_ref, units_ref, ffn_ref, dmod_ref, sems, *, n_mod, rows_ff,
):
    core = bits[0]
    first = pl.program_id(0) == 0
    last = pl.program_id(0) == pl.num_programs(0) - 1
    load_gf = pltpu.make_async_copy(gf_hbm, gf_ref, sems.at[0])
    load_units = pltpu.make_async_copy(units_hbm, units_ref, sems.at[1])
    store_ffn = pltpu.make_async_copy(ffn_ref, ffn_hbm, sems.at[2])
    store_dmod = pltpu.make_async_copy(dmod_ref, dmod_hbm, sems.at[3])

    @pl.when(first)
    def _():
        load_gf.start()
        load_units.start()
        ffn_ref[...] = jnp.zeros_like(ffn_ref)
        dmod_ref[...] = jnp.zeros_like(dmod_ref)

    gate = nn(x_ref[...], wg_ref[...])
    up = nn(x_ref[...], wu_ref[...])

    @pl.when(first)
    def _():
        load_gf.wait()
        load_units.wait()

    grad_hidden = nt(gf_ref[...], wd_ref[...])
    sigmoid = 1.0 / (1.0 + jnp.exp(-gate))
    silu = gate * sigmoid
    hidden = (silu * up).astype(bf16)
    turned = hidden.T
    for index in range(turned.shape[0] // rows_ff):
        unit, rest = unit_of(index, n_mod)
        turned_ref[unit, rest * rows_ff : (rest + 1) * rows_ff] = turned[
            index * rows_ff : (index + 1) * rows_ff
        ]
    dg = (grad_hidden * up * (sigmoid * (1.0 + gate * (1.0 - sigmoid)))).astype(bf16)
    du = (grad_hidden * silu).astype(bf16)

    ffn_ref[...] += nn(hidden, wd_ref[...])
    dmod_ref[...] += nt(dg, wg_ref[...]) + nt(du, wu_ref[...])

    @pl.when(last)
    def _():
        store_ffn.start()
        store_dmod.start()

    product(units_ref, 1 - core, dg, gate_send_ref)
    product(units_ref, 1 - core, du, up_send_ref)
    product(turned_ref, 1 - core, gf_ref[...], down_send_ref)
    product(units_ref, core, dg, gate_own_ref)
    product(units_ref, core, du, up_own_ref)
    product(turned_ref, core, gf_ref[...], down_own_ref)

    @pl.when(last)
    def _():
        store_ffn.wait()
        store_dmod.wait()


def middle_kernel(
    slots, mid_ref, ffn_ref, dmod_ref, cot_ref, attn_ref, o_ref, units_ref, mod_ref, w_out_ref, gather_ref,
    out_ref, grad_mid_ref, do_ref, dot_ref, sums_ref, send_ref, own_ref, acc_ref,
):
    width = mid_ref.shape[1]
    block = pl.program_id(0)
    here = slots_here(slots, mid_ref.shape[0])
    segments = pl.num_programs(0) * len(here)
    incoming = cot_ref[...].astype(f32)
    mid = mid_ref[...]
    out_ref[...] = by_slot(
        lambda slot, rows, ffn: (rows + part(mod_ref, slot, 5, width) * ffn).astype(bf16), here, mid, ffn_ref[...]
    )
    norm, inverse = normed(mid)
    dmod = dmod_ref[...]
    scaled = by_slot(lambda slot, rows: rows * (1.0 + part(mod_ref, slot, 4, width)), here, dmod)
    grad_mid = incoming + norm_back(scaled, norm, inverse)
    grad_mid_ref[...] = grad_mid
    ga = by_slot(lambda slot, rows: (rows * part(mod_ref, slot, 2, width)).astype(bf16), here, grad_mid)
    grow = nn(units_ref[...].reshape(width, -1), ga)

    @pl.when(block == 0)
    def _():
        acc_ref[...] = grow

    @pl.when(block > 0)
    def _():
        acc_ref[...] += grow

    @pl.when(block == pl.num_programs(0) - 1)
    def _():
        halves_out(acc_ref, slots[segments], send_ref, own_ref)

    do = nt(ga, w_out_ref[...]).astype(bf16)
    do_ref[...] = do
    dot_ref[...] = head_sum(do.astype(f32) * o_ref[...].astype(f32), gather_ref).T

    @pl.when(block == 0)
    def _():
        sums_ref[...] = jnp.zeros_like(sums_ref)

    for index, term in enumerate((grad_mid * attn_ref[...].astype(f32), dmod, dmod * norm, incoming * ffn_ref[...])):
        add_by_slot(sums_ref, here, index, term)


def attend_back_kernel(
    slots, q_ref, k_ref, v_ref, do_ref, lse_ref, dot_ref, kt_ref, dqt_ref, dk_ref, dv_low_ref, dv_ref,
    *, first, base, base_row, width,
):
    tokens = q_ref.shape[0]

    @pl.when(pl.program_id(0) == 0)
    def _():
        dqt_ref[...] = jnp.zeros_like(dqt_ref)
        dk_ref[...] = jnp.zeros_like(dk_ref)
        dv_ref[...] = jnp.zeros_like(dv_ref)

    def head(h, rows):
        start, offset = window(h, width)
        inside = head_lanes(offset)
        columns = pl.ds(pl.multiple_of(start - base, 128), WIN)
        first_row = pl.multiple_of((h * HD) // 16 * 16, 16)
        own_place = pl.ds(pl.multiple_of(first_row - base_row, 16), HD + 8)
        row = lax.broadcasted_iota(jnp.int32, (HD + 8, 1), 0) + first_row
        own_rows = (row >= h * HD) & (row < h * HD + HD)
        query = q_ref[rows, columns]
        grad_out = do_ref[rows, columns]
        key = jnp.where(inside, k_ref[rows, columns], 0)
        value = jnp.where(inside, v_ref[rows, columns], 0)
        probs = jnp.exp2(nt(key, query) * SCORE_LOG2 - lse_ref[pl.ds(h, 1), rows])
        scores = (probs * (nt(value, grad_out) - dot_ref[pl.ds(h, 1), rows])).astype(bf16)
        dv_ref[rows, columns] += jnp.where(inside, nn(probs.astype(bf16), grad_out), 0.0)
        dk_ref[rows, columns] += jnp.where(inside, nn(scores, query) * SCORE_SCALE, 0.0)
        turned = nn(kt_ref[own_place, rows], scores) * SCORE_SCALE
        dqt_ref[own_place, rows] += jnp.where(own_rows, turned, 0.0)

    whole = slots[tokens // SEG - 1] == slots[0]
    begin = first + pl.program_id(0) * TOGETHER

    @pl.when(whole)
    def _():
        for i in range(TOGETHER):
            head(begin + i, slice(None))

    @pl.when(jnp.logical_not(whole))
    def _():
        for i in range(TOGETHER):
            for b in range(tokens // SEG):
                head(begin + i, slice(b * SEG, (b + 1) * SEG))

    @pl.when(pl.program_id(0) == pl.num_programs(0) - 1)
    def _():
        dv_low_ref[...] = dv_ref[...].astype(bf16)


def head_span(first, end, width):
    begin = lambda head: min(head * HD // 128, width // 128 - WIN // 128) * 128
    return begin(first), begin(end - 1) + WIN, first * HD // 16 * 16, (end - 1) * HD // 16 * 16 + HD + 8


def join_spans(low, high, begin, axis):
    size = low.shape[axis] - begin
    if size == 0:
        return jnp.concatenate([low, high], axis=axis)
    cut = lambda arr, start, stop: lax.slice_in_dim(arr, start, stop, axis=axis)
    middle = cut(low, begin, begin + size) + cut(high, 0, size)
    return jnp.concatenate([cut(low, 0, begin), middle, cut(high, size, high.shape[axis])], axis=axis)


def project_back_kernel(
    bits, dqt0_ref, dqt1_ref, dk0_ref, dk1_ref, raw_ref, inv_ref, q_ref, k_ref, units_ref,
    coords_ref, cos_ref, sin_ref, gain_ref, gather_ref, spread_ref, fold_ref,
    gq_ref, gk_ref, gains_low_ref, q_send_ref, q_own_ref, k_send_ref, k_own_ref, accq_ref, acck_ref, gains_ref,
    *, base, base_row,
):
    width = q_ref.shape[1]
    block = pl.program_id(0)

    @pl.when(block == 0)
    def _():
        gains_ref[...] = jnp.zeros_like(gains_ref)
        accq_ref[...] = jnp.zeros_like(accq_ref)
        acck_ref[...] = jnp.zeros_like(acck_ref)

    cosine, sine = angles(coords_ref, cos_ref, sin_ref)
    parts = ((q_ref, gq_ref, accq_ref), (k_ref, gk_ref, acck_ref))
    for index, (low_ref, out_ref, acc_ref) in enumerate(parts):
        if index == 0:
            grad = join_spans(dqt0_ref[...], dqt1_ref[...], base_row, 0).T
        else:
            grad = join_spans(dk0_ref[...], dk1_ref[...], base, 1)
        raw = raw_ref[:, index * width : (index + 1) * width]
        inverse = head_spread(inv_ref[:, index * 128 : (index + 1) * 128], spread_ref)
        mean = head_sum(grad * low_ref[...].astype(f32), gather_ref) * (1.0 / HD)
        norm = raw * inverse
        back = grad * cosine - partner(grad) * sine
        gains_ref[index : index + 1, :] += jnp.sum(back * norm, axis=0, keepdims=True)
        grad_raw = (
            inverse * (back * gain_ref[index : index + 1, :] - norm * head_spread(mean, spread_ref))
        ).astype(bf16)
        out_ref[...] = grad_raw
        acc_ref[...] += nn(units_ref[...].reshape(width, -1), grad_raw)

    @pl.when(block == pl.num_programs(0) - 1)
    def _():
        halves_out(accq_ref, bits[0], q_send_ref, q_own_ref)
        halves_out(acck_ref, bits[0], k_send_ref, k_own_ref)
        terms = split3(gains_ref[...])
        sums = sum(nn(term.astype(bf16), fold_ref[...]) for term in terms)
        high = sums.astype(bf16).astype(f32)
        row = lax.broadcasted_iota(jnp.int32, (8, 1), 0)
        mine = 4 * bits[1]
        placed = jnp.zeros((8, 128), f32)
        for index, term in enumerate((high[0:1], (sums - high)[0:1], high[1:2], (sums - high)[1:2])):
            placed = jnp.where(row == mine + index, term, placed)
        gains_low_ref[...] = placed.astype(bf16)


def input_back_kernel(
    slots, gq_ref, gk_ref, dv0_ref, dv1_ref, x_ref, grad_mid_ref, mod_ref, w_hbm, other_sums_ref, gains_ref,
    sums_in_ref, before_hbm, grad_x_ref, grad_own_ref, grad_other_ref, sums_ref, w_ref, sems, *, base, start, segments,
):
    width = x_ref.shape[1]
    block = pl.program_id(0)
    here = [slots[start + block]]
    last_block = pl.num_programs(0) - 1
    loads = column_loads(w_hbm, w_ref, sems, 3)

    @pl.when(block == 0)
    def _():
        for load in reversed(loads):
            load.start()

    wait_if(block == 0, loads[2])
    dmod = nt(join_spans(dv0_ref[...], dv1_ref[...], base, 1), w_ref[:, 2 * width :])
    for index, grad_ref in ((1, gk_ref), (0, gq_ref)):
        wait_if(block == 0, loads[index])
        dmod = dmod + nt(grad_ref[...], w_ref[:, index * width : (index + 1) * width])

    norm, inverse = normed(x_ref[...].astype(f32))
    scaled = by_slot(lambda slot, rows: rows * (1.0 + part(mod_ref, slot, 1, width)), here, dmod)
    grad_x = grad_mid_ref[...] + norm_back(scaled, norm, inverse)
    grad_x_ref[...] = grad_x.astype(bf16)

    @pl.when(block == 0)
    def _():
        sums_ref[...] = sums_in_ref[...]

    for index, term in enumerate((dmod, dmod * norm)):
        add_by_slot(sums_ref, here, index, term)

    @pl.when(block == last_block)
    def _():
        mod = slots[segments + 1]
        count = sums_ref.shape[0]
        half = 3 * width
        mine = jnp.concatenate([sums_ref[...]] * 2, axis=0)
        rest = jnp.concatenate([other_sums_ref[...]] * 2, axis=0)
        row = lax.broadcasted_iota(jnp.int32, (2 * count, 1), 0) // count
        attn_part = jnp.where(row == mod, jnp.concatenate([mine, rest[:, :width]], axis=1), 0.0)
        ffn_part = jnp.where(row == mod, rest[:, width:], 0.0)
        grad_own_ref[:, :half] = jnp.where(mod == 0, attn_part, ffn_part).astype(bf16)
        grad_other_ref[:, :half] = jnp.where(mod == 0, ffn_part, attn_part).astype(bf16)
        grad_own_ref[:, half:] = gains_ref[...]
        grad_other_ref[:, half:] = gains_ref[...]


def value_kernel(bits, units_ref, dv0_ref, dv1_ref, send_ref, own_ref, *, base):
    rhs = join_spans(dv0_ref[...], dv1_ref[...], base, 1)
    product(units_ref, 1 - bits[0], rhs, send_ref)
    product(units_ref, bits[0], rhs, own_ref)


def split_step(bits, ins, outs, *, lead, at, bit, pair_rows, cuts):
    send_ref, keep_ref = outs
    mine = bits[bit]
    start = 0
    for own_ref, got_ref, cut in zip(ins[::2], ins[1::2], cuts):
        columns, target = slice(None), slice(None)
        if cut:
            columns, target = slice(*cut), slice(start, start + cut[1] - cut[0])
            start = target.stop

        def total(*index):
            place = index + (slice(None), columns)
            return own_ref[place].astype(f32) + got_ref[place].astype(f32)

        if at is None:
            for j in range(max(lead, 1)):
                index = (j,) if lead else ()
                value = total(*index)
                rows = pair_rows or value.shape[0] // 2
                for p in range(value.shape[0] // (2 * rows)):
                    first = value[2 * p * rows : (2 * p + 1) * rows]
                    second = value[(2 * p + 1) * rows : (2 * p + 2) * rows]
                    place = index + (slice(p * rows, (p + 1) * rows), target)
                    send_ref[place] = jnp.where(mine == 1, first, second).astype(bf16)
                    keep_ref[place] = jnp.where(mine == 1, second, first).astype(keep_ref.dtype)
            continue
        for j in range(lead // 2):
            place = ((j,) if lead > 2 else ()) + (slice(None), target)
            away = 1 - mine if lead == 2 else 2 * (1 - mine) + j if at == 0 else 2 * j + 1 - mine
            own = mine if lead == 2 else 2 * mine + j if at == 0 else 2 * j + mine
            send_ref[place] = total(away).astype(bf16)
            keep_ref[place] = total(own).astype(keep_ref.dtype)


def merge_step(bits, ins, outs, *, bit, parts):
    send_ref, keep_ref = outs
    start = 0
    for own_ref, got_ref, pieces in zip(ins[::2], ins[1::2], parts):
        value = own_ref[...].astype(f32) + got_ref[...].astype(f32)
        rows, columns = value.shape[0] // 2, value.shape[1]
        first, second = value[:rows], value[rows:]
        sent = jnp.where(bits[bit] == 1, first, second).astype(bf16)
        kept = jnp.where(bits[bit] == 1, second, first)
        for i in range(pieces):
            place = slice(start, start + columns)
            if pieces > 1:
                send_ref[:, place] = jnp.zeros_like(send_ref[:, place])
                keep_ref[:, place] = jnp.zeros_like(keep_ref[:, place])
            taken = slice(i * rows // pieces, (i + 1) * rows // pieces)
            send_ref[: rows // pieces, place] = sent[taken]
            keep_ref[: rows // pieces, place] = kept[taken]
            start += columns


def apart_step(bits, ins, outs, *, places):
    own_ref, got_ref = ins
    for out, at, start, stop, rows in places:
        value = own_ref[:, start:stop] + got_ref[:, start:stop].astype(f32)
        if rows is None:
            outs[out][:, at : at + stop - start] = value
        else:
            count = rows[1] - rows[0]
            outs[out][rows[0] : rows[1], :] = value[:count]


def pair_step(bits, ins, outs):
    own_ref, got_ref, activated_ref = ins
    width = activated_ref.shape[1]
    outs[0][:, :width] = activated_ref[...]
    outs[0][:, width:] = (own_ref[...].astype(f32) + got_ref[...].astype(f32)).astype(bf16)


def joined(ins):
    return jnp.concatenate([ref[...].astype(f32) for ref in ins], axis=0).astype(bf16)


def join_step(bits, ins, outs):
    outs[0][...] = joined(ins)


def last_step(bits, ins, outs):
    outs[0][...] = ins[0][...] + ins[1][...].astype(f32)


def ada_step(bits, ins, outs, *, width):
    rows = outs[0].shape[0]
    every = joined(ins)
    position = bits[0] + sum(bits[1 + k] * 2**k for k in range(1, (width // rows).bit_length() - 1))
    feature = lax.broadcasted_iota(jnp.int32, (width, 128), 0)
    place = lax.broadcasted_iota(jnp.int32, (width, 128), 1)
    chosen = (feature == position * rows + place) & (place < rows)
    own = nn(every[:, :width], chosen.astype(f32).astype(bf16)).astype(bf16)
    half = outs[0].shape[1]
    outs[0][...] = tn(own, every[:, width : width + half])[:rows]
    terms = every[:, width + half :].astype(f32)
    kind = lax.broadcasted_iota(jnp.int32, (terms.shape[0], 1), 0) // 2 % 2
    for index in range(2):
        outs[1][index : index + 1, :] = jnp.sum(jnp.where(kind == index, terms, 0.0), axis=0, keepdims=True)


def step_kernel(bits, *refs, plans):
    n_in = sum(plan[1] for plan in plans)
    ins, outs = refs[:n_in], refs[n_in:]
    for function, takes, gives in plans:
        function(bits, ins[:takes], outs[:gives])
        ins, outs = ins[takes:], outs[gives:]


class Chain:
    def __init__(self):
        self.last = None

    def __call__(
        self, kernel, grid, in_specs, out_specs, out_shape, args, scalars=None, scratch=(), name=None, aliases=None
    ):
        ahead = 0 if scalars is None else 1
        body = kernel
        token = ()
        if self.last is not None:
            token = (self.last,)
            in_specs = [pl.BlockSpec(memory_space=pl.ANY)] + list(in_specs)

            def body(*refs):
                kernel(*refs[:ahead], *refs[ahead + 1 :])

        spec = pltpu.PrefetchScalarGridSpec(
            num_scalar_prefetch=ahead,
            grid=grid,
            in_specs=in_specs,
            out_specs=out_specs,
            scratch_shapes=scratch,
        )
        outs = pl.pallas_call(
            body,
            grid_spec=spec,
            input_output_aliases=aliases or {},
            out_shape=out_shape,
            compiler_params=pltpu.CompilerParams(vmem_limit_bytes=VMEM),
            cost_estimate=pl.CostEstimate(flops=1, bytes_accessed=1, transcendentals=0),
            name=name,
        )(*(() if scalars is None else (scalars,)), *token, *args)
        self.last = outs[0]
        return outs


def shape(dims, dtype):
    return jax.ShapeDtypeStruct(dims, dtype)


def fixed(dims):
    return pl.BlockSpec(dims, lambda *_: (0,) * len(dims), pipeline_mode=pl.Buffered(1))


def rows_of(dims, axis=0):
    return pl.BlockSpec(dims, lambda b, *_: tuple(b if i == axis else 0 for i in range(len(dims))))


def whole(dims):
    return rows_of(dims, None)


def column_parts(dims, steps):
    return rows_of(dims[:-1] + (dims[-1] // steps,), len(dims) - 1)


class Reducer:
    def __init__(self, n_dp, n_mod, call):
        self.n_dp, self.n_mod, self.call = n_dp, n_mod, call
        self.position = lax.axis_index("dp")
        steps = range(n_dp.bit_length() - 1)
        dp_bits = [lax.shift_right_logical(self.position, step) & 1 for step in steps]
        self.bits = jnp.stack([dp_bits[0], lax.axis_index("mod")] + dp_bits[1:]).astype(jnp.int32)

    def swap(self, arr, bit):
        if bit == "mod":
            return lax.ppermute(arr, "mod", [(i, i ^ 1) for i in range(self.n_mod)])
        return lax.ppermute(arr, "dp", [(i, i ^ (1 << bit)) for i in range(self.n_dp)])

    def bit_of(self, bit):
        return 1 if bit == "mod" else bit + 1 if bit else 0

    def fold(self, streams, name, last=False):
        plans, args, outs = [], [], []
        for stream in streams:
            function, shapes = stream.last_plan() if last else stream.plan()
            inputs = stream.inputs()
            plans.append((function, len(inputs), len(shapes)))
            args += inputs
            outs += shapes
        size = sum(arg.size for arg in args)
        split = all(
            isinstance(stream, Stream) and stream.side is None and stream.own.shape[-1] % 384 == 0
            for stream in streams
        )
        steps = 3 if split and size > 2**20 else 1
        results = self.call(
            functools.partial(step_kernel, plans=plans),
            (steps,),
            [column_parts(arg.shape, steps) for arg in args],
            [column_parts(out.shape, steps) for out in outs],
            outs,
            args,
            scalars=self.bits,
            name=name,
        )
        results = list(results)
        if last:
            return results
        for stream, plan in zip(streams, plans):
            stream.step(results[: plan[2]])
            results = results[plan[2] :]

    def pass_on(self, arrays):
        anywhere = [pl.BlockSpec(memory_space=pl.ANY)] * len(arrays)
        return self.call(
            lambda *refs: None,
            (1,),
            anywhere,
            anywhere,
            [shape(arr.shape, arr.dtype) for arr in arrays],
            arrays,
            name="pass_on",
            aliases={i + 1: i for i in range(len(arrays))},
        )


class Stream:
    def __init__(self, reducer, sent, own, first, pair_rows=None):
        self.r, self.own, self.pair_rows = reducer, own, pair_rows
        order = ["mod", 1, 2]
        self.steps = order[first:] + order[:first] + list(range(3, reducer.n_dp.bit_length() - 1))
        self.lead = ["mod", 1]
        self.side = None
        self.got = reducer.swap(sent, 0)

    def inputs(self):
        return [self.own, self.got] + ([self.side[0].own, self.side[0].got] if self.side else [])

    def plan(self):
        bit = self.steps[0]
        dims = self.own.shape
        at = self.lead.index(bit) if bit in self.lead else None
        cuts = [None]
        if self.side is not None:
            cuts = [(0, dims[-1]), self.side[1]]
            dims = dims[:-1] + (dims[-1] + self.side[1][1] - self.side[1][0],)
        function = functools.partial(
            split_step, lead=dims[0] if self.lead else 0, at=at, bit=self.r.bit_of(bit), pair_rows=self.pair_rows,
            cuts=cuts,
        )
        if at is None:
            dims = dims[:-2] + (dims[-2] // 2, dims[-1])
        else:
            dims = dims[1:] if len(self.lead) == 1 else (2,) + dims[1:]
        return function, [shape(dims, bf16), shape(dims, bf16 if len(self.lead) == 2 else f32)]

    def step(self, results):
        bit = self.steps.pop(0)
        if bit in self.lead:
            self.lead.remove(bit)
        self.side = None
        sent, self.own = results
        self.got = self.r.swap(sent, bit)

    def join(self, stream, cut):
        self.side = (stream, cut)


class Merged:
    def __init__(self, streams):
        self.streams, self.r, self.bit = streams, streams[0].r, streams[0].steps[0]
        self.own = self.places = self.shapes = None

    def inputs(self):
        if self.own is not None:
            return [self.own, self.got]
        return [arr for stream in self.streams for arr in (stream.own, stream.got)]

    def plan(self):
        parts = [3 if stream.pair_rows else 1 for stream in self.streams]
        columns = sum(pieces * stream.own.shape[1] for pieces, stream in zip(parts, self.streams))
        dims = (self.streams[0].own.shape[0] // 2, columns)
        function = functools.partial(merge_step, bit=self.r.bit_of(self.bit), parts=parts)
        return function, [shape(dims, bf16), shape(dims, f32)]

    def step(self, results):
        sent, self.own = results
        self.got = self.r.swap(sent, self.bit)

    def last_plan(self):
        if self.places is None:
            return last_step, [shape(self.own.shape, f32)]
        return functools.partial(apart_step, places=self.places), self.shapes


class Gather:
    def __init__(self, reducer, sent, own, activated):
        self.r, self.own, self.activated = reducer, own, activated
        self.steps = list(range(reducer.n_dp.bit_length() - 2, -1, -1))
        self.got = reducer.swap(sent, "mod")
        self.pair = None

    def inputs(self):
        return [self.own, self.got] + ([self.activated] if self.pair is None else [])

    def plan(self):
        rows, columns = self.own.shape
        if self.pair is None:
            return pair_step, [shape((rows, columns + self.activated.shape[1]), bf16)]
        return join_step, [shape((2 * rows, columns), bf16)]

    def step(self, results):
        (self.own,) = results
        if self.pair is None:
            self.pair = self.own
        self.got = self.r.swap(self.own, self.steps.pop(0))

    def last_plan(self):
        width = self.activated.shape[1]
        function = functools.partial(ada_step, width=width)
        dims = (width // self.r.n_dp, self.own.shape[1] - width - 128)
        return function, [shape(dims, f32), shape((2, 128), f32)]


def silu_grad(v):
    sigmoid = jax.nn.sigmoid(v)
    return sigmoid * (1.0 + v * (1.0 - sigmoid))


def pair_order(own, other, mod):
    return jnp.where(mod == 0, jnp.stack([own, other]), jnp.stack([other, own]))


def body(
    n_dp, n_mod, tokens, cond, segments, coords, w_ada, w_qkv, q_gain, k_gain, w_out, w_gate, w_up,
    w_down, cotangent,
):
    _, count, width = tokens.shape
    slots_n = cond.shape[1]
    half = w_ada.shape[1]
    ff = w_gate.shape[1]
    blocks = count // TB
    n_dev = n_dp * n_mod
    call = Chain()
    reducer = Reducer(n_dp, n_mod, call)
    mod_index = lax.axis_index("mod")
    x = tokens[0]
    cot = cotangent[0]
    slots = segments[0, ::SEG]
    coord = coords[0]
    cos_table, sin_table = (jnp.asarray(t) for t in rope_tables(width))
    gather, spread, head_fold = (jnp.asarray(t) for t in head_tables(width))
    perm = jnp.asarray(unit_permutation(width, n_dp, n_mod))
    gains = jnp.stack([jnp.tile(q_gain, HEADS), jnp.tile(k_gain, HEADS)])

    cond_both = pair_order(cond[0], reducer.swap(cond[0], "mod"), mod_index)
    activated = jax.nn.silu(cond_both).astype(bf16).reshape(-1, width)
    mod_half = jnp.dot(activated, w_ada, preferred_element_type=f32).astype(bf16)
    mod_half = mod_half.reshape(n_mod, slots_n, half)
    own_half = lax.dynamic_index_in_dim(mod_half, mod_index, 0, keepdims=False)
    other_half = lax.dynamic_index_in_dim(mod_half, 1 - mod_index, 0, keepdims=False)
    pair = pair_order(own_half, reducer.swap(other_half, "mod"), mod_index)
    modulation = jnp.concatenate([pair[0], pair[1]], axis=1).astype(f32)

    anywhere = pl.BlockSpec(memory_space=pl.ANY)
    token_f32 = shape((count, width), f32)
    token_bf16 = shape((count, width), bf16)
    units = shape((8, width // 8, count), bf16)
    units_spec = rows_of((8, width // 8, TB), 2)
    token_spec = rows_of((TB, width))
    mod_spec = fixed((slots_n, 6 * width))
    square = fixed((width, width))
    table_specs = [fixed(cos_table.shape), fixed(sin_table.shape), fixed((2, width)), fixed(gather.shape), fixed(spread.shape)]
    tables = (cos_table, sin_table, gains, gather, spread)
    lane_rows = shape((128, count), f32)
    macs = count * width * width

    attn_units, raw, inverse, query, key, value, key_t = call(
        project_kernel,
        (blocks,),
        [token_spec, mod_spec, anywhere, rows_of((2, TB), 1)] + table_specs + [anywhere],
        [units_spec, rows_of((TB, 2 * width)), rows_of((TB, 256))] + [token_spec] * 3 + [rows_of((width, TB), 1)],
        [units, shape((count, 2 * width), f32), shape((count, 256), f32)] + [token_bf16] * 3
        + [shape((width, count), bf16)],
        (x, modulation, w_qkv, coord) + tables + (perm,),
        scalars=slots,
        scratch=[
            pltpu.VMEM((width, 3 * width), bf16),
            pltpu.VMEM((width, width), bf16),
            pltpu.SemaphoreType.DMA((4,)),
        ],
        name="project",
    )
    attended, lse_columns = call(
        attend_kernel,
        (HEADS // TOGETHER,),
        [fixed((count, width))] * 3,
        [fixed((count, width)), fixed((count, 128))],
        [token_f32, shape((count, 128), f32)],
        (query, key, value),
        scalars=slots,
        name="attend",
    )
    attended, lse, attn, mid, ffn_in, grad_ffn, out_units, ffn_units = call(
        mix_kernel,
        (blocks,),
        [token_spec, token_spec, mod_spec, token_spec, rows_of((TB, 128)), square, square],
        [token_spec, rows_of((128, TB), 1)] + [token_spec] * 4 + [units_spec] * 2,
        [token_bf16, lane_rows, token_bf16, token_f32, token_bf16, token_bf16, units, units],
        (x, cot, modulation, attended, lse_columns, w_out, perm),
        scalars=slots,
        name="mix",
    )

    rows_ff = ff // n_dev
    chunk = 768
    piece = chunk // 8
    half_units = lambda rows, columns: shape((4, rows, columns), bf16)
    square_send = [fixed((4, width // 8, width))] * 2
    square_shapes = [half_units(width // 8, width)] * 2
    gate_send, gate_own, up_send, up_own, down_send, down_own, ffn, grad_mod_ffn = call(
        functools.partial(ffn_kernel, n_mod=n_mod, rows_ff=rows_ff),
        (ff // chunk,),
        [fixed((count, width)), anywhere, anywhere]
        + [rows_of((width, chunk), 1)] * 2 + [rows_of((chunk, width))],
        [rows_of((4, width // 8, chunk), 2)] * 4
        + [rows_of((4, 1, piece, width), 1)] * 2 + [anywhere] * 2,
        [half_units(width // 8, ff)] * 4
        + [shape((4, ff // chunk, piece, width), bf16)] * 2 + [token_f32] * 2,
        (ffn_in, grad_ffn, ffn_units, w_gate, w_up, w_down),
        scalars=reducer.bits,
        scratch=[
            pltpu.VMEM((8, piece, count), bf16),
            pltpu.VMEM((count, width), bf16),
            pltpu.VMEM(units.shape, bf16),
            pltpu.VMEM((count, width), f32),
            pltpu.VMEM((count, width), f32),
            pltpu.SemaphoreType.DMA((4,)),
        ],
        name="ffn",
    )
    gate = Stream(reducer, gate_send, gate_own, 0)
    up = Stream(reducer, up_send, up_own, 1)
    down = Stream(
        reducer, down_send.reshape(4, ff // 8, width), down_own.reshape(4, ff // 8, width), 2, rows_ff
    )

    slots_core = jnp.concatenate([slots, reducer.bits[:2]])
    seg_spec = rows_of((SEG, width))
    output, grad_mid, grad_attended, dot_term, sums_b, out_send, out_own = call(
        middle_kernel,
        (count // SEG,),
        [seg_spec] * 6 + [rows_of((8, width // 8, SEG), 2), mod_spec, square, fixed(gather.shape)],
        [seg_spec] * 3 + [rows_of((128, SEG), 1), fixed((slots_n, 4 * width))] + square_send,
        [token_bf16, token_f32, token_bf16, lane_rows, shape((slots_n, 4 * width), f32)] + square_shapes,
        (mid, ffn, grad_mod_ffn, cot, attn, attended, out_units, modulation, w_out, gather),
        scalars=slots_core,
        scratch=[pltpu.VMEM((width, width), f32)],
        name="middle",
    )
    out = Stream(reducer, out_send, out_own, 1)
    early = [gate, up, down]
    middle_cut = width // 256 * 128 + 128
    gate.join(out, (0, middle_cut))
    up.join(out, (middle_cut, width))
    reducer.fold(early, "early")

    def attend_back(first, end, name):
        begin, stop, begin_row, stop_row = head_span(first, end, width)
        columns, rows = stop - begin, stop_row - begin_row
        used = pl.BlockSpec((count, columns), lambda *_: (0, begin // columns), pipeline_mode=pl.Buffered(1))
        used_rows = pl.BlockSpec((rows, count), lambda *_: (begin_row // rows, 0), pipeline_mode=pl.Buffered(1))
        return call(
            functools.partial(attend_back_kernel, first=first, base=begin, base_row=begin_row, width=width),
            ((end - first) // TOGETHER,),
            [used] * 4 + [fixed((128, count))] * 2 + [used_rows],
            [fixed((rows, count))] + [fixed((count, columns))] * 2,
            [shape((rows, count), f32), shape((count, columns), f32), shape((count, columns), bf16)],
            (query, key, value, grad_attended, lse, dot_term, key_t),
            scratch=[pltpu.VMEM((count, columns), f32)],
            scalars=slots,
            name=name,
        )

    cut = 3 * HEADS // 4
    dqt0, dk0, dv0 = attend_back(0, cut, "attend_back_0")
    reducer.fold(early, "early")
    dqt1, dk1, dv1 = attend_back(cut, HEADS, "attend_back_1")
    base, _, base_row, _ = head_span(cut, HEADS, width)
    v_send, v_own = call(
        functools.partial(value_kernel, base=base),
        (1,),
        [whole(units.shape), whole(dv0.shape), whole(dv1.shape)],
        [whole((4, width // 8, width))] * 2,
        square_shapes,
        (attn_units, dv0, dv1),
        scalars=reducer.bits,
        name="value",
    )
    v_part = Stream(reducer, v_send, v_own, 2)
    reducer.fold(early, "early")
    grad_q, grad_k, gains_low, q_send, q_own, k_send, k_own = call(
        functools.partial(project_back_kernel, base=base, base_row=base_row),
        (count // SEG,),
        [rows_of((dqt0.shape[0], SEG), 1), rows_of((dqt1.shape[0], SEG), 1)]
        + [rows_of((SEG, dk0.shape[1])), rows_of((SEG, dk1.shape[1]))]
        + [rows_of((SEG, 2 * width)), rows_of((SEG, 256)), seg_spec, seg_spec, rows_of((8, width // 8, SEG), 2), rows_of((2, SEG), 1)]
        + table_specs + [fixed(head_fold.shape)],
        [seg_spec] * 2 + [fixed((8, 128))] + square_send * 2,
        [token_bf16] * 2 + [shape((8, 128), bf16)] + square_shapes * 2,
        (dqt0, dqt1, dk0, dk1, raw, inverse, query, key, attn_units, coord) + tables + (head_fold,),
        scalars=reducer.bits,
        scratch=[pltpu.VMEM((width, width), f32)] * 2 + [pltpu.VMEM((2, width), f32)],
        name="project_back",
    )
    waiting = early + [v_part]
    *arrived, q_send, k_send = reducer.pass_on([stream.got for stream in waiting] + [q_send, k_send])
    for stream, got in zip(waiting, arrived):
        stream.got = got
    q_part = Stream(reducer, q_send, q_own, 1)
    k_part = Stream(reducer, k_send, k_own, 0)
    late = [q_part, k_part, v_part]
    extra = n_dp.bit_length() - 5
    reducer.fold([v_part], "v")
    reducer.fold([q_part, k_part], "late")
    for _ in range(extra):
        reducer.fold(early, "early")
    rows_d = width // n_dev
    merged = Merged([gate, up, down])
    third = rows_ff // 3
    gate_end = ff + middle_cut
    up_end = gate_end + ff + width - middle_cut
    merged.places = [
        (0, 0, 0, ff, None),
        (2, 0, ff, gate_end, None),
        (1, 0, gate_end, gate_end + ff, None),
        (2, middle_cut, gate_end + ff, up_end, None),
    ] + [
        (3, 0, up_end + i * width, up_end + (i + 1) * width, (i * third, (i + 1) * third)) for i in range(3)
    ]
    merged.shapes = [shape((rows_d, ff), f32)] * 2 + [shape((rows_d, width), f32), shape((rows_ff, width), f32)]
    early = [merged]
    reducer.fold(early, "early")

    def input_back(start, end, sums, before, name):
        def seg(columns):
            return pl.BlockSpec((SEG, columns), lambda b, *_: (start + b, 0))

        outs = call(
            functools.partial(input_back_kernel, base=base, start=start, segments=count // SEG),
            (end - start,),
            [seg(width)] * 2 + [seg(dv0.shape[1]), seg(dv1.shape[1])] + [seg(width)] * 2
            + [mod_spec, anywhere, fixed((slots_n, 4 * width)), fixed((8, 128)), fixed((slots_n, 2 * width)), anywhere],
            [seg(width)] + [fixed((2 * slots_n, half + 128))] * 2 + [fixed((slots_n, 2 * width))],
            [token_bf16] + [shape((2 * slots_n, half + 128), bf16)] * 2 + [shape((slots_n, 2 * width), f32)],
            (grad_q, grad_k, dv0, dv1, x, grad_mid, modulation, w_qkv, sums_b, gains_low, sums, before),
            scalars=slots_core,
            scratch=[pltpu.VMEM((width, 3 * width), bf16), pltpu.SemaphoreType.DMA((3,))],
            name=name,
            aliases={13: 0} if start else None,
        )
        return outs

    half_way = count // SEG // 2
    nothing = jnp.zeros((slots_n, 2 * width), f32)
    grad_tokens, _, _, sums_a = input_back(0, half_way, nothing, x, "input_back_0")
    reducer.fold(late, "late")
    grad_tokens, mod_own, mod_other, _ = input_back(half_way, count // SEG, sums_a, grad_tokens, "input_back_1")
    every_mod = Gather(reducer, mod_other, mod_own, activated)
    reducer.fold(late, "late")
    for _ in range(extra):
        reducer.fold(late, "late")
    reducer.fold([every_mod], "pair")
    summed_gate, summed_up, summed_out, summed_down = reducer.fold(early, "early_last", last=True)
    late = [Merged(late)]
    reducer.fold(late, "late")
    while len(every_mod.steps) > 1:
        reducer.fold([every_mod], "every")
    (summed_qkv,) = reducer.fold(late, "late_last", last=True)
    reducer.fold([every_mod], "every")
    grad_w_ada, gain_grads = reducer.fold([every_mod], "ada", last=True)

    grad_activated = jnp.einsum("nc,dc->nd", every_mod.pair[:, width : width + half], w_ada, preferred_element_type=f32)
    grad_activated = grad_activated.reshape(n_mod, slots_n, width)
    own_part = lax.dynamic_index_in_dim(grad_activated, mod_index, 0, keepdims=False)
    other_part = lax.dynamic_index_in_dim(grad_activated, 1 - mod_index, 0, keepdims=False)
    grad_own = own_part + reducer.swap(other_part.astype(bf16), "mod").astype(f32)
    grad_cond = grad_own[None] * silu_grad(cond)
    return (
        output[None],
        grad_tokens[None],
        grad_cond,
        grad_w_ada,
        summed_qkv,
        gain_grads[0, :HD],
        gain_grads[1, :HD],
        summed_out,
        summed_gate,
        summed_up,
        summed_down,
    )


def solution(mesh):
    rows = ("dp", "mod")
    in_specs = (
        P(rows, None, None),
        P(rows, None, None),
        P(rows, None),
        P(rows, None, None),
        P(None, "mod"),
        P(),
        P(),
        P(),
        P(),
        P(),
        P(),
        P(),
        P(rows, None, None),
    )
    out_specs = (
        P(rows, None, None),
        P(rows, None, None),
        P(rows, None, None),
        P("dp", "mod"),
        P(rows, None),
        P(),
        P(),
        P(rows, None),
        P(rows, None),
        P(rows, None),
        P(rows, None),
    )
    return jax.shard_map(
        functools.partial(body, mesh.shape["dp"], mesh.shape["mod"]),
        mesh=mesh,
        in_specs=in_specs,
        out_specs=out_specs,
        check_vma=False,
    )
```

```python
import functools

import jax
import jax.numpy as jnp
import numpy as np
from jax import lax
from jax.experimental import pallas as pl
from jax.experimental.pallas import tpu as pltpu
from jax.sharding import PartitionSpec as P

HEADS = 16
HD = 72
GRID = 32
EPS = 1e-06
ROPE_BASE = 10000.0
SEG = 256
TB = 512
WIN = 256
TOGETHER = 4
SCORE_SCALE = float(HD**-0.5)
SCORE_LOG2 = float(np.log2(np.e) * HD**-0.5)
VMEM = 60 * 2**20
f32 = jnp.float32
bf16 = jnp.bfloat16


def nn(a, b):
    return lax.dot_general(a, b, (((1,), (0,)), ((), ())), preferred_element_type=f32)


def nt(a, b):
    return lax.dot_general(a, b, (((1,), (1,)), ((), ())), preferred_element_type=f32)


def tn(a, b):
    return lax.dot_general(a, b, (((0,), (0,)), ((), ())), preferred_element_type=f32)


def split3(v):
    hi = v.astype(bf16).astype(f32)
    mid = (v - hi).astype(bf16).astype(f32)
    return hi, mid, v - hi - mid


def np_split3(v):
    v = v.astype(np.float32)
    hi = v.astype(jnp.bfloat16).astype(np.float32)
    mid = (v - hi).astype(jnp.bfloat16).astype(np.float32)
    return [part.astype(jnp.bfloat16) for part in (hi, mid, v - hi - mid)]


@functools.lru_cache(None)
def rope_tables(width):
    quarter = HD // 4
    freqs = ROPE_BASE ** (-np.arange(quarter, dtype=np.float64) / quarter)
    lane = np.arange(width) % HD
    group = lane // quarter
    angle = np.arange(GRID)[:, None] * freqs[lane % quarter][None, :]
    cosine, sine = np.cos(angle), np.sin(angle)
    sine = np.where((group % 2 == 0)[None, :], -sine, sine)
    uses_col = (group >= 2)[None, :]
    tables = []
    for table in (cosine, sine):
        whole = np.concatenate(
            [np.where(uses_col, 0.0, table), np.where(uses_col, table, 0.0)], axis=0
        )
        tables.append(np.concatenate(np_split3(whole), axis=0))
    return tables


@functools.lru_cache(None)
def head_tables(width):
    head = np.arange(width) // HD
    gather = np.zeros((width, 128), np.float32)
    for copy in range(3):
        gather[np.arange(width), copy * HEADS + head] = 1.0
    fold = np.zeros((width, 128), np.float32)
    fold[np.arange(width), np.arange(width) % HD] = 1.0
    return gather.astype(jnp.bfloat16), gather.T.astype(jnp.bfloat16), fold.astype(jnp.bfloat16)


def unit_of(index, n_mod):
    mod = index % n_mod
    dp = index // n_mod
    return (dp % 2) * 2 * n_mod + mod * 2 + (dp // 2) % 2, dp // 4


def reversed_bits(value, size):
    result = 0
    for bit in range(size.bit_length() - 1):
        result = 2 * result + (value >> bit) % 2
    return result


@functools.lru_cache(None)
def unit_permutation(width, n_dp, n_mod):
    rows = width // (n_dp * n_mod)
    matrix = np.zeros((width, width), np.float32)
    for index in range(n_dp * n_mod):
        unit, rest = unit_of(index, n_mod)
        start = unit * (width // 8) + reversed_bits(rest, n_dp // 4) * rows
        matrix[start + np.arange(rows), index * rows + np.arange(rows)] = 1.0
    return matrix.astype(jnp.bfloat16)


def normed(v):
    centred = v - jnp.mean(v, axis=-1, keepdims=True)
    inverse = lax.rsqrt(jnp.mean(centred * centred, axis=-1, keepdims=True) + EPS)
    return centred * inverse, inverse


def norm_back(e, norm, inverse):
    return inverse * (
        e - jnp.mean(e, axis=-1, keepdims=True) - norm * jnp.mean(e * norm, axis=-1, keepdims=True)
    )


def part(mod_ref, slot, index, width):
    return mod_ref[pl.ds(slot, 1), index * width : (index + 1) * width]


def slots_here(slots, rows):
    return [slots[pl.program_id(0) * (rows // SEG) + i] for i in range(rows // SEG)]


def by_slot(function, here, *values):
    done = [
        function(slot, *(value[i * SEG : (i + 1) * SEG] for value in values)) for i, slot in enumerate(here)
    ]
    return jnp.concatenate(done, axis=0)


def angles(coords_ref, cos_ref, sin_ref):
    value = lax.broadcasted_iota(jnp.int32, (GRID, 1), 0)
    hot = [(value == coords_ref[i : i + 1, :]).astype(f32) for i in range(2)]
    hot = jnp.concatenate(hot * 3, axis=0).astype(bf16)
    return tn(hot, cos_ref[...]), tn(hot, sin_ref[...])


def partner(v):
    width = v.shape[1]
    quarter = HD // 4
    lane = lax.broadcasted_iota(jnp.int32, (1, width), 1)
    leads = (lane // quarter) % 2 == 0
    return jnp.where(leads, pltpu.roll(v, width - quarter, 1), pltpu.roll(v, quarter, 1))


def head_sum(v, gather_ref):
    hi = v.astype(bf16)
    low = (v - hi.astype(f32)).astype(bf16)
    return nn(hi, gather_ref[...]) + nn(low, gather_ref[...])


def head_spread(v, spread_ref):
    hi, mid, low = split3(v)
    lane = lax.broadcasted_iota(jnp.int32, (1, 128), 1)
    chosen = jnp.where(lane < HEADS, hi, jnp.where(lane < 2 * HEADS, mid, low))
    return nn(chosen.astype(bf16), spread_ref[...])


def window(head, width):
    start = jnp.minimum((head * HD) // 128, width // 128 - WIN // 128) * 128
    return pl.multiple_of(start, 128), head * HD - start


def head_lanes(offset):
    lane = lax.broadcasted_iota(jnp.int32, (1, WIN), 1)
    return (lane >= offset) & (lane < offset + HD)


def product(units_ref, half, rhs, out_ref):
    _, rows, tokens = units_ref.shape
    units = units_ref[pl.ds(4 * half, 4)].reshape(4 * rows, tokens)
    out_ref[...] = nn(units, rhs).astype(bf16).reshape(out_ref.shape)


def halves_out(acc_ref, core, send_ref, own_ref):
    rows = acc_ref.shape[0] // 2
    for half, out_ref in ((1 - core, send_ref), (core, own_ref)):
        start = pl.multiple_of(half * rows, rows)
        out_ref[...] = acc_ref[pl.ds(start, rows)].astype(bf16).reshape(out_ref.shape)


def add_by_slot(sums_ref, here, index, term):
    width = term.shape[1]
    for i, slot in enumerate(here):
        rows = term[i * SEG : (i + 1) * SEG]
        sums_ref[pl.ds(slot, 1), index * width : (index + 1) * width] += jnp.sum(rows, axis=0, keepdims=True)


def project_kernel(
    slots, x_ref, mod_ref, w_ref, coords_ref, cos_ref, sin_ref, gain_ref, gather_ref, spread_ref,
    perm_ref, units_ref, raw_ref, inv_ref, q_ref, k_ref, v_ref, kt_ref,
):
    width = x_ref.shape[1]
    norm, _ = normed(x_ref[...].astype(f32))

    def modulate(slot, rows):
        return (rows * (1.0 + part(mod_ref, slot, 1, width)) + part(mod_ref, slot, 0, width)).astype(bf16)

    low = by_slot(modulate, slots_here(slots, x_ref.shape[0]), norm)
    units_ref[...] = nt(perm_ref[...], low).astype(bf16).reshape(units_ref.shape)
    cosine, sine = angles(coords_ref, cos_ref, sin_ref)
    for index, out_ref in enumerate((q_ref, k_ref)):
        raw = nn(low, w_ref[:, index * width : (index + 1) * width])
        raw_ref[:, index * width : (index + 1) * width] = raw
        inverse = lax.rsqrt(head_sum(raw * raw, gather_ref) * (1.0 / HD) + EPS)
        inv_ref[:, index * 128 : (index + 1) * 128] = inverse
        scaled = raw * head_spread(inverse, spread_ref) * gain_ref[index : index + 1, :]
        turned = scaled * cosine + partner(scaled) * sine
        out_ref[...] = turned.astype(bf16)
        if index == 1:
            kt_ref[...] = turned.T.astype(bf16)
    v_ref[...] = nn(low, w_ref[:, 2 * width :]).astype(bf16)


def attend_kernel(slots, q_ref, k_ref, v_ref, o_ref, lse_ref):
    step = pl.program_id(0)
    tokens, width = q_ref.shape
    lane128 = lax.broadcasted_iota(jnp.int32, (1, 128), 1)
    lane = lax.broadcasted_iota(jnp.int32, (1, WIN), 1)

    @pl.when(step == 0)
    def _():
        o_ref[...] = jnp.zeros_like(o_ref)
        lse_ref[...] = jnp.zeros_like(lse_ref)

    def head(h, rows):
        start, offset = window(h, width)
        inside = head_lanes(offset)
        columns = pl.ds(start, WIN)
        query = jnp.where(inside, q_ref[rows, columns], 0)
        value = jnp.where(inside, v_ref[rows, columns], 1)
        weight = jnp.exp2(nt(query, k_ref[rows, columns]) * SCORE_LOG2).astype(bf16)
        summed = nn(weight, value)
        free = jnp.where(offset > 0, 0, WIN - 1)
        total = jnp.sum(jnp.where(lane == free, summed, 0.0), axis=1, keepdims=True)
        o_ref[rows, columns] += jnp.where(inside, summed * (1.0 / total), 0.0)
        lse_ref[rows, :] += jnp.where(lane128 == h, jnp.log2(total), 0.0)

    whole = slots[tokens // SEG - 1] == slots[0]

    @pl.when(whole)
    def _():
        for i in range(TOGETHER):
            head(step * TOGETHER + i, slice(None))

    @pl.when(jnp.logical_not(whole))
    def _():
        for i in range(TOGETHER):
            for b in range(tokens // SEG):
                head(step * TOGETHER + i, slice(b * SEG, (b + 1) * SEG))


def mix_kernel(
    slots, x_ref, cot_ref, mod_ref, o_ref, lse_ref, w_out_ref, perm_ref,
    attended_ref, lse_out_ref, attn_ref, mid_ref, low_ref, gf_ref, att_units_ref, ffn_units_ref,
):
    width = x_ref.shape[1]
    here = slots_here(slots, x_ref.shape[0])
    lse_out_ref[...] = lse_ref[...].T
    attended = o_ref[...].astype(bf16)
    attended_ref[...] = attended
    att_units_ref[...] = nt(perm_ref[...], attended).astype(bf16).reshape(att_units_ref.shape)
    attn = nn(attended, w_out_ref[...])
    attn_ref[...] = attn.astype(bf16)
    mid = by_slot(
        lambda slot, x, rows: x.astype(f32) + part(mod_ref, slot, 2, width) * rows, here, x_ref[...], attn
    )
    mid_ref[...] = mid
    norm, _ = normed(mid)

    def modulate(slot, rows):
        return (rows * (1.0 + part(mod_ref, slot, 4, width)) + part(mod_ref, slot, 3, width)).astype(bf16)

    low = by_slot(modulate, here, norm)
    low_ref[...] = low
    ffn_units_ref[...] = nt(perm_ref[...], low).astype(bf16).reshape(ffn_units_ref.shape)
    gf_ref[...] = by_slot(
        lambda slot, rows: (rows.astype(f32) * part(mod_ref, slot, 5, width)).astype(bf16), here, cot_ref[...]
    )


def ffn_kernel(
    bits, x_ref, gf_hbm, units_hbm, wg_ref, wu_ref, wd_ref,
    gate_send_ref, gate_own_ref, up_send_ref, up_own_ref, down_send_ref, down_own_ref, ffn_hbm, dmod_hbm,
    turned_ref, gf_ref, units_ref, ffn_ref, dmod_ref, sems, *, n_mod, rows_ff,
):
    core = bits[0]
    first = pl.program_id(0) == 0
    last = pl.program_id(0) == pl.num_programs(0) - 1
    load_gf = pltpu.make_async_copy(gf_hbm, gf_ref, sems.at[0])
    load_units = pltpu.make_async_copy(units_hbm, units_ref, sems.at[1])
    store_ffn = pltpu.make_async_copy(ffn_ref, ffn_hbm, sems.at[2])
    store_dmod = pltpu.make_async_copy(dmod_ref, dmod_hbm, sems.at[3])

    @pl.when(first)
    def _():
        load_gf.start()
        load_units.start()
        ffn_ref[...] = jnp.zeros_like(ffn_ref)
        dmod_ref[...] = jnp.zeros_like(dmod_ref)

    gate = nn(x_ref[...], wg_ref[...])
    up = nn(x_ref[...], wu_ref[...])

    @pl.when(first)
    def _():
        load_gf.wait()
        load_units.wait()

    grad_hidden = nt(gf_ref[...], wd_ref[...])
    sigmoid = 1.0 / (1.0 + jnp.exp(-gate))
    silu = gate * sigmoid
    hidden = (silu * up).astype(bf16)
    turned = hidden.T
    for index in range(turned.shape[0] // rows_ff):
        unit, rest = unit_of(index, n_mod)
        turned_ref[unit, rest * rows_ff : (rest + 1) * rows_ff] = turned[
            index * rows_ff : (index + 1) * rows_ff
        ]
    dg = (grad_hidden * up * (sigmoid * (1.0 + gate * (1.0 - sigmoid)))).astype(bf16)
    du = (grad_hidden * silu).astype(bf16)

    ffn_ref[...] += nn(hidden, wd_ref[...])
    dmod_ref[...] += nt(dg, wg_ref[...]) + nt(du, wu_ref[...])

    @pl.when(last)
    def _():
        store_ffn.start()
        store_dmod.start()

    product(units_ref, 1 - core, dg, gate_send_ref)
    product(units_ref, 1 - core, du, up_send_ref)
    product(turned_ref, 1 - core, gf_ref[...], down_send_ref)
    product(units_ref, core, dg, gate_own_ref)
    product(units_ref, core, du, up_own_ref)
    product(turned_ref, core, gf_ref[...], down_own_ref)

    @pl.when(last)
    def _():
        store_ffn.wait()
        store_dmod.wait()


def middle_kernel(
    slots, mid_ref, ffn_ref, dmod_ref, cot_ref, attn_ref, o_ref, units_ref, mod_ref, w_out_ref, gather_ref,
    out_ref, grad_mid_ref, do_ref, dot_ref, sums_ref, send_ref, own_ref, acc_ref,
):
    width = mid_ref.shape[1]
    block = pl.program_id(0)
    here = slots_here(slots, mid_ref.shape[0])
    segments = pl.num_programs(0) * len(here)
    incoming = cot_ref[...].astype(f32)
    mid = mid_ref[...]
    out_ref[...] = by_slot(
        lambda slot, rows, ffn: (rows + part(mod_ref, slot, 5, width) * ffn).astype(bf16), here, mid, ffn_ref[...]
    )
    norm, inverse = normed(mid)
    dmod = dmod_ref[...]
    scaled = by_slot(lambda slot, rows: rows * (1.0 + part(mod_ref, slot, 4, width)), here, dmod)
    grad_mid = incoming + norm_back(scaled, norm, inverse)
    grad_mid_ref[...] = grad_mid
    ga = by_slot(lambda slot, rows: (rows * part(mod_ref, slot, 2, width)).astype(bf16), here, grad_mid)
    grow = nn(units_ref[...].reshape(width, -1), ga)

    @pl.when(block == 0)
    def _():
        acc_ref[...] = grow

    @pl.when(block > 0)
    def _():
        acc_ref[...] += grow

    @pl.when(block == pl.num_programs(0) - 1)
    def _():
        halves_out(acc_ref, slots[segments], send_ref, own_ref)

    do = nt(ga, w_out_ref[...]).astype(bf16)
    do_ref[...] = do
    dot_ref[...] = head_sum(do.astype(f32) * o_ref[...].astype(f32), gather_ref).T

    @pl.when(block == 0)
    def _():
        sums_ref[...] = jnp.zeros_like(sums_ref)

    for index, term in enumerate((grad_mid * attn_ref[...].astype(f32), dmod, dmod * norm, incoming * ffn_ref[...])):
        add_by_slot(sums_ref, here, index, term)


def attend_back_kernel(
    slots, q_ref, k_ref, v_ref, do_ref, lse_ref, dot_ref, kt_ref, dqt_ref, dk_ref, dv_low_ref, dv_ref,
    *, first, base, base_row, width,
):
    tokens = q_ref.shape[0]

    @pl.when(pl.program_id(0) == 0)
    def _():
        dqt_ref[...] = jnp.zeros_like(dqt_ref)
        dk_ref[...] = jnp.zeros_like(dk_ref)
        dv_ref[...] = jnp.zeros_like(dv_ref)

    def head(h, rows):
        start, offset = window(h, width)
        inside = head_lanes(offset)
        columns = pl.ds(pl.multiple_of(start - base, 128), WIN)
        first_row = pl.multiple_of((h * HD) // 16 * 16, 16)
        own_place = pl.ds(pl.multiple_of(first_row - base_row, 16), HD + 8)
        row = lax.broadcasted_iota(jnp.int32, (HD + 8, 1), 0) + first_row
        own_rows = (row >= h * HD) & (row < h * HD + HD)
        query = q_ref[rows, columns]
        grad_out = do_ref[rows, columns]
        key = jnp.where(inside, k_ref[rows, columns], 0)
        value = jnp.where(inside, v_ref[rows, columns], 0)
        probs = jnp.exp2(nt(key, query) * SCORE_LOG2 - lse_ref[pl.ds(h, 1), rows])
        scores = (probs * (nt(value, grad_out) - dot_ref[pl.ds(h, 1), rows])).astype(bf16)
        dv_ref[rows, columns] += jnp.where(inside, nn(probs.astype(bf16), grad_out), 0.0)
        dk_ref[rows, columns] += jnp.where(inside, nn(scores, query) * SCORE_SCALE, 0.0)
        turned = nn(kt_ref[own_place, rows], scores) * SCORE_SCALE
        dqt_ref[own_place, rows] += jnp.where(own_rows, turned, 0.0)

    whole = slots[tokens // SEG - 1] == slots[0]
    begin = first + pl.program_id(0) * TOGETHER

    @pl.when(whole)
    def _():
        for i in range(TOGETHER):
            head(begin + i, slice(None))

    @pl.when(jnp.logical_not(whole))
    def _():
        for i in range(TOGETHER):
            for b in range(tokens // SEG):
                head(begin + i, slice(b * SEG, (b + 1) * SEG))

    @pl.when(pl.program_id(0) == pl.num_programs(0) - 1)
    def _():
        dv_low_ref[...] = dv_ref[...].astype(bf16)


def head_span(first, end, width):
    begin = lambda head: min(head * HD // 128, width // 128 - WIN // 128) * 128
    return begin(first), begin(end - 1) + WIN, first * HD // 16 * 16, (end - 1) * HD // 16 * 16 + HD + 8


def join_spans(low, high, begin, axis):
    size = low.shape[axis] - begin
    if size == 0:
        return jnp.concatenate([low, high], axis=axis)
    cut = lambda arr, start, stop: lax.slice_in_dim(arr, start, stop, axis=axis)
    middle = cut(low, begin, begin + size) + cut(high, 0, size)
    return jnp.concatenate([cut(low, 0, begin), middle, cut(high, size, high.shape[axis])], axis=axis)


def project_back_kernel(
    bits, dqt0_ref, dqt1_ref, dk0_ref, dk1_ref, raw_ref, inv_ref, q_ref, k_ref, units_ref,
    coords_ref, cos_ref, sin_ref, gain_ref, gather_ref, spread_ref, fold_ref,
    gq_ref, gk_ref, gains_low_ref, q_send_ref, q_own_ref, k_send_ref, k_own_ref, accq_ref, acck_ref, gains_ref,
    *, base, base_row,
):
    width = q_ref.shape[1]
    block = pl.program_id(0)

    @pl.when(block == 0)
    def _():
        gains_ref[...] = jnp.zeros_like(gains_ref)
        accq_ref[...] = jnp.zeros_like(accq_ref)
        acck_ref[...] = jnp.zeros_like(acck_ref)

    cosine, sine = angles(coords_ref, cos_ref, sin_ref)
    parts = ((q_ref, gq_ref, accq_ref), (k_ref, gk_ref, acck_ref))
    for index, (low_ref, out_ref, acc_ref) in enumerate(parts):
        if index == 0:
            grad = join_spans(dqt0_ref[...], dqt1_ref[...], base_row, 0).T
        else:
            grad = join_spans(dk0_ref[...], dk1_ref[...], base, 1)
        raw = raw_ref[:, index * width : (index + 1) * width]
        inverse = head_spread(inv_ref[:, index * 128 : (index + 1) * 128], spread_ref)
        mean = head_sum(grad * low_ref[...].astype(f32), gather_ref) * (1.0 / HD)
        norm = raw * inverse
        back = grad * cosine - partner(grad) * sine
        gains_ref[index : index + 1, :] += jnp.sum(back * norm, axis=0, keepdims=True)
        grad_raw = (
            inverse * (back * gain_ref[index : index + 1, :] - norm * head_spread(mean, spread_ref))
        ).astype(bf16)
        out_ref[...] = grad_raw
        acc_ref[...] += nn(units_ref[...].reshape(width, -1), grad_raw)

    @pl.when(block == pl.num_programs(0) - 1)
    def _():
        halves_out(accq_ref, bits[0], q_send_ref, q_own_ref)
        halves_out(acck_ref, bits[0], k_send_ref, k_own_ref)
        terms = split3(gains_ref[...])
        sums = sum(nn(term.astype(bf16), fold_ref[...]) for term in terms)
        high = sums.astype(bf16).astype(f32)
        row = lax.broadcasted_iota(jnp.int32, (4, 1), 0)
        placed = jnp.zeros((4, 128), f32)
        for index, term in enumerate((high[0:1], (sums - high)[0:1], high[1:2], (sums - high)[1:2])):
            placed = jnp.where(row == index, term, placed)
        gains_low_ref[...] = placed.astype(bf16)


def input_back_kernel(
    slots, gq_ref, gk_ref, dv0_ref, dv1_ref, x_ref, grad_mid_ref, mod_ref, w_ref, other_sums_ref, gains_ref,
    activated_ref, grad_x_ref, rows_ref, sums_ref, *, base,
):
    width = x_ref.shape[1]
    block = pl.program_id(0)
    here = slots_here(slots, x_ref.shape[0])
    dmod = nt(gq_ref[...], w_ref[:, :width]) + nt(gk_ref[...], w_ref[:, width : 2 * width])
    dmod = dmod + nt(join_spans(dv0_ref[...], dv1_ref[...], base, 1), w_ref[:, 2 * width :])
    norm, inverse = normed(x_ref[...].astype(f32))
    scaled = by_slot(lambda slot, rows: rows * (1.0 + part(mod_ref, slot, 1, width)), here, dmod)
    grad_x = grad_mid_ref[...] + norm_back(scaled, norm, inverse)
    grad_x_ref[...] = grad_x.astype(bf16)

    @pl.when(block == 0)
    def _():
        sums_ref[...] = jnp.zeros_like(sums_ref)

    for index, term in enumerate((dmod, dmod * norm)):
        add_by_slot(sums_ref, here, index, term)

    @pl.when(block == pl.num_programs(0) - 1)
    def _():
        rows_ref[:, : 2 * width] = sums_ref[...].astype(bf16)
        rows_ref[:, 2 * width : 6 * width] = other_sums_ref[...].astype(bf16)
        rows_ref[:, 6 * width : 7 * width] = activated_ref[...]
        rows_ref[:, 7 * width :] = gains_ref[...]


def value_kernel(bits, units_ref, dv0_ref, dv1_ref, send_ref, own_ref, *, base):
    rhs = join_spans(dv0_ref[...], dv1_ref[...], base, 1)
    product(units_ref, 1 - bits[0], rhs, send_ref)
    product(units_ref, bits[0], rhs, own_ref)


def split_step(bits, ins, outs, *, lead, at, bit, pair_rows, cuts):
    send_ref, keep_ref = outs
    mine = bits[bit]
    start = 0
    for own_ref, got_ref, cut in zip(ins[::2], ins[1::2], cuts):
        columns, target = slice(None), slice(None)
        if cut:
            columns, target = slice(*cut), slice(start, start + cut[1] - cut[0])
            start = target.stop

        def total(*index):
            place = index + (slice(None), columns)
            return own_ref[place].astype(f32) + got_ref[place].astype(f32)

        if at is None:
            for j in range(max(lead, 1)):
                index = (j,) if lead else ()
                value = total(*index)
                rows = pair_rows or value.shape[0] // 2
                for p in range(value.shape[0] // (2 * rows)):
                    first = value[2 * p * rows : (2 * p + 1) * rows]
                    second = value[(2 * p + 1) * rows : (2 * p + 2) * rows]
                    place = index + (slice(p * rows, (p + 1) * rows), target)
                    send_ref[place] = jnp.where(mine == 1, first, second).astype(bf16)
                    keep_ref[place] = jnp.where(mine == 1, second, first).astype(keep_ref.dtype)
            continue
        for j in range(lead // 2):
            place = ((j,) if lead > 2 else ()) + (slice(None), target)
            away = 1 - mine if lead == 2 else 2 * (1 - mine) + j if at == 0 else 2 * j + 1 - mine
            own = mine if lead == 2 else 2 * mine + j if at == 0 else 2 * j + mine
            send_ref[place] = total(away).astype(bf16)
            keep_ref[place] = total(own).astype(keep_ref.dtype)


def merge_step(bits, ins, outs, *, bit, parts):
    send_ref, keep_ref = outs
    start = 0
    for own_ref, got_ref, pieces in zip(ins[::2], ins[1::2], parts):
        value = own_ref[...].astype(f32) + got_ref[...].astype(f32)
        rows, columns = value.shape[0] // 2, value.shape[1]
        first, second = value[:rows], value[rows:]
        sent = jnp.where(bits[bit] == 1, first, second).astype(bf16)
        kept = jnp.where(bits[bit] == 1, second, first)
        for i in range(pieces):
            place = slice(start, start + columns)
            if pieces > 1:
                send_ref[:, place] = jnp.zeros_like(send_ref[:, place])
                keep_ref[:, place] = jnp.zeros_like(keep_ref[:, place])
            taken = slice(i * rows // pieces, (i + 1) * rows // pieces)
            send_ref[: rows // pieces, place] = sent[taken]
            keep_ref[: rows // pieces, place] = kept[taken]
            start += columns


def apart_step(bits, ins, outs, *, places):
    own_ref, got_ref = ins
    for out, at, start, stop, rows in places:
        value = own_ref[:, start:stop] + got_ref[:, start:stop].astype(f32)
        if rows is None:
            outs[out][:, at : at + stop - start] = value
        else:
            count = rows[1] - rows[0]
            outs[out][rows[0] : rows[1], :] = value[:count]


def last_step(bits, ins, outs):
    outs[0][...] = ins[0][...] + ins[1][...].astype(f32)


def ada_kernel(bits, rows_ref, grad_ref, gains_ref, *, width):
    rows, half = grad_ref.shape
    position = bits[0] + sum(bits[1 + k] * 2**k for k in range(1, (width // rows).bit_length() - 1))
    feature = lax.broadcasted_iota(jnp.int32, (width, 128), 0)
    place = lax.broadcasted_iota(jnp.int32, (width, 128), 1)
    chosen = (feature == position * rows + place) & (place < rows)
    own = nn(rows_ref[:, 6 * width : 7 * width], chosen.astype(f32).astype(bf16)).astype(bf16)
    channels = pl.ds(pl.multiple_of(bits[1] * half, 128), half)
    grad_ref[...] = tn(own, rows_ref[:, channels])[:rows]
    terms = rows_ref[:, 7 * width :].astype(f32)
    kind = lax.broadcasted_iota(jnp.int32, (terms.shape[0], 1), 0) // 2 % 2
    for index in range(2):
        gains_ref[index : index + 1, :] = jnp.sum(jnp.where(kind == index, terms, 0.0), axis=0, keepdims=True)


def step_kernel(bits, *refs, plans, passed):
    n_in = sum(plan[1] for plan in plans)
    ins, outs = refs[:n_in], refs[n_in + passed :]
    for function, takes, gives in plans:
        function(bits, ins[:takes], outs[:gives])
        ins, outs = ins[takes:], outs[gives:]


class Chain:
    def __init__(self):
        self.last = None

    def __call__(
        self, kernel, grid, in_specs, out_specs, out_shape, args, scalars=None, scratch=(), name=None, aliases=None
    ):
        ahead = 0 if scalars is None else 1
        body = kernel
        token = ()
        if self.last is not None:
            token = (self.last,)
            in_specs = [pl.BlockSpec(memory_space=pl.ANY)] + list(in_specs)

            def body(*refs):
                kernel(*refs[:ahead], *refs[ahead + 1 :])

        spec = pltpu.PrefetchScalarGridSpec(
            num_scalar_prefetch=ahead,
            grid=grid,
            in_specs=in_specs,
            out_specs=out_specs,
            scratch_shapes=scratch,
        )
        outs = pl.pallas_call(
            body,
            grid_spec=spec,
            input_output_aliases=aliases or {},
            out_shape=out_shape,
            compiler_params=pltpu.CompilerParams(vmem_limit_bytes=VMEM),
            cost_estimate=pl.CostEstimate(flops=1, bytes_accessed=1, transcendentals=0),
            name=name,
        )(*(() if scalars is None else (scalars,)), *token, *args)
        self.last = outs[0]
        return outs


def shape(dims, dtype):
    return jax.ShapeDtypeStruct(dims, dtype)


def fixed(dims):
    return pl.BlockSpec(dims, lambda *_: (0,) * len(dims), pipeline_mode=pl.Buffered(1))


def rows_of(dims, axis=0):
    return pl.BlockSpec(dims, lambda b, *_: tuple(b if i == axis else 0 for i in range(len(dims))))


def whole(dims):
    return rows_of(dims, None)


def column_parts(dims, steps):
    return rows_of(dims[:-1] + (dims[-1] // steps,), len(dims) - 1)


class Reducer:
    def __init__(self, n_dp, n_mod, call):
        self.n_dp, self.n_mod, self.call = n_dp, n_mod, call
        self.position = lax.axis_index("dp")
        steps = range(n_dp.bit_length() - 1)
        dp_bits = [lax.shift_right_logical(self.position, step) & 1 for step in steps]
        self.bits = jnp.stack([dp_bits[0], lax.axis_index("mod")] + dp_bits[1:]).astype(jnp.int32)

    def swap(self, arr, bit):
        if bit == "mod":
            return lax.ppermute(arr, "mod", [(i, i ^ 1) for i in range(self.n_mod)])
        return lax.ppermute(arr, "dp", [(i, i ^ (1 << bit)) for i in range(self.n_dp)])

    def bit_of(self, bit):
        return 1 if bit == "mod" else bit + 1 if bit else 0

    def fold(self, streams, name, last=False, passed=()):
        plans, args, outs = [], [], []
        for stream in streams:
            function, shapes = stream.last_plan() if last else stream.plan()
            inputs = stream.inputs()
            plans.append((function, len(inputs), len(shapes)))
            args += inputs
            outs += shapes
        size = sum(arg.size for arg in args)
        split = all(
            isinstance(stream, Stream) and stream.side is None and stream.own.shape[-1] % 384 == 0
            for stream in streams
        )
        steps = 3 if split and size > 2**20 else 1
        results = self.call(
            functools.partial(step_kernel, plans=plans, passed=len(passed)),
            (steps,),
            [column_parts(arg.shape, steps) for arg in args] + [pl.BlockSpec(memory_space=pl.ANY)] * len(passed),
            [column_parts(out.shape, steps) for out in outs] + [pl.BlockSpec(memory_space=pl.ANY)] * len(passed),
            outs + [shape(arr.shape, arr.dtype) for arr in passed],
            args + list(passed),
            scalars=self.bits,
            name=name,
            aliases={2 + len(args) + i: len(outs) + i for i in range(len(passed))},
        )
        results = list(results)
        if last:
            return results
        self.passed = results[len(outs) :]
        for stream, plan in zip(streams, plans):
            stream.step(results[: plan[2]])
            results = results[plan[2] :]

    def pass_on(self, arrays):
        anywhere = [pl.BlockSpec(memory_space=pl.ANY)] * len(arrays)
        return self.call(
            lambda *refs: None,
            (1,),
            anywhere,
            anywhere,
            [shape(arr.shape, arr.dtype) for arr in arrays],
            arrays,
            name="pass_on",
            aliases={i + 1: i for i in range(len(arrays))},
        )


class Stream:
    def __init__(self, reducer, sent, own, first, pair_rows=None):
        self.r, self.own, self.pair_rows = reducer, own, pair_rows
        order = ["mod", 1, 2]
        self.steps = order[first:] + order[:first] + list(range(3, reducer.n_dp.bit_length() - 1))
        self.lead = ["mod", 1]
        self.side = None
        self.got = reducer.swap(sent, 0)

    def inputs(self):
        return [self.own, self.got] + ([self.side[0].own, self.side[0].got] if self.side else [])

    def plan(self):
        bit = self.steps[0]
        dims = self.own.shape
        at = self.lead.index(bit) if bit in self.lead else None
        cuts = [None]
        if self.side is not None:
            cuts = [(0, dims[-1]), self.side[1]]
            dims = dims[:-1] + (dims[-1] + self.side[1][1] - self.side[1][0],)
        function = functools.partial(
            split_step, lead=dims[0] if self.lead else 0, at=at, bit=self.r.bit_of(bit), pair_rows=self.pair_rows,
            cuts=cuts,
        )
        if at is None:
            dims = dims[:-2] + (dims[-2] // 2, dims[-1])
        else:
            dims = dims[1:] if len(self.lead) == 1 else (2,) + dims[1:]
        return function, [shape(dims, bf16), shape(dims, bf16 if len(self.lead) == 2 else f32)]

    def step(self, results):
        bit = self.steps.pop(0)
        if bit in self.lead:
            self.lead.remove(bit)
        self.side = None
        sent, self.own = results
        self.got = self.r.swap(sent, bit)

    def join(self, stream, cut):
        self.side = (stream, cut)


class Merged:
    def __init__(self, streams):
        self.streams, self.r, self.bit = streams, streams[0].r, streams[0].steps[0]
        self.own = self.places = self.shapes = None

    def inputs(self):
        if self.own is not None:
            return [self.own, self.got]
        return [arr for stream in self.streams for arr in (stream.own, stream.got)]

    def plan(self):
        parts = [3 if stream.pair_rows else 1 for stream in self.streams]
        columns = sum(pieces * stream.own.shape[1] for pieces, stream in zip(parts, self.streams))
        dims = (self.streams[0].own.shape[0] // 2, columns)
        function = functools.partial(merge_step, bit=self.r.bit_of(self.bit), parts=parts)
        return function, [shape(dims, bf16), shape(dims, f32)]

    def step(self, results):
        sent, self.own = results
        self.got = self.r.swap(sent, self.bit)

    def last_plan(self):
        if self.places is None:
            return last_step, [shape(self.own.shape, f32)]
        return functools.partial(apart_step, places=self.places), self.shapes


def silu_grad(v):
    sigmoid = jax.nn.sigmoid(v)
    return sigmoid * (1.0 + v * (1.0 - sigmoid))


def pair_order(own, other, mod):
    return jnp.where(mod == 0, jnp.stack([own, other]), jnp.stack([other, own]))


def body(
    n_dp, n_mod, tokens, cond, segments, coords, w_ada, w_qkv, q_gain, k_gain, w_out, w_gate, w_up,
    w_down, cotangent,
):
    _, count, width = tokens.shape
    slots_n = cond.shape[1]
    half = w_ada.shape[1]
    ff = w_gate.shape[1]
    blocks = count // TB
    n_dev = n_dp * n_mod
    call = Chain()
    reducer = Reducer(n_dp, n_mod, call)
    mod_index = lax.axis_index("mod")
    x = tokens[0]
    cot = cotangent[0]
    slots = segments[0, ::SEG]
    coord = coords[0]
    cos_table, sin_table = (jnp.asarray(t) for t in rope_tables(width))
    gather, spread, head_fold = (jnp.asarray(t) for t in head_tables(width))
    perm = jnp.asarray(unit_permutation(width, n_dp, n_mod))
    gains = jnp.stack([jnp.tile(q_gain, HEADS), jnp.tile(k_gain, HEADS)])

    cond_both = pair_order(cond[0], reducer.swap(cond[0], "mod"), mod_index)
    activated = jax.nn.silu(cond_both).astype(bf16).reshape(-1, width)
    own_activated = jax.nn.silu(cond[0]).astype(bf16)
    mod_half = jnp.dot(activated, w_ada, preferred_element_type=f32).astype(bf16)
    mod_half = mod_half.reshape(n_mod, slots_n, half)
    own_half = lax.dynamic_index_in_dim(mod_half, mod_index, 0, keepdims=False)
    other_half = lax.dynamic_index_in_dim(mod_half, 1 - mod_index, 0, keepdims=False)
    pair = pair_order(own_half, reducer.swap(other_half, "mod"), mod_index)
    modulation = jnp.concatenate([pair[0], pair[1]], axis=1).astype(f32)

    anywhere = pl.BlockSpec(memory_space=pl.ANY)
    token_f32 = shape((count, width), f32)
    token_bf16 = shape((count, width), bf16)
    units = shape((8, width // 8, count), bf16)
    units_spec = rows_of((8, width // 8, TB), 2)
    token_spec = rows_of((TB, width))
    mod_spec = fixed((slots_n, 6 * width))
    square = fixed((width, width))
    table_specs = [fixed(cos_table.shape), fixed(sin_table.shape), fixed((2, width)), fixed(gather.shape), fixed(spread.shape)]
    tables = (cos_table, sin_table, gains, gather, spread)
    lane_rows = shape((128, count), f32)
    macs = count * width * width

    attn_units, raw, inverse, query, key, value, key_t = call(
        project_kernel,
        (blocks,),
        [token_spec, mod_spec, fixed((width, 3 * width)), rows_of((2, TB), 1)] + table_specs + [square],
        [units_spec, rows_of((TB, 2 * width)), rows_of((TB, 256))] + [token_spec] * 3 + [rows_of((width, TB), 1)],
        [units, shape((count, 2 * width), f32), shape((count, 256), f32)] + [token_bf16] * 3
        + [shape((width, count), bf16)],
        (x, modulation, w_qkv, coord) + tables + (perm,),
        scalars=slots,
        name="project",
    )
    attended, lse_columns = call(
        attend_kernel,
        (HEADS // TOGETHER,),
        [fixed((count, width))] * 3,
        [fixed((count, width)), fixed((count, 128))],
        [token_f32, shape((count, 128), f32)],
        (query, key, value),
        scalars=slots,
        name="attend",
    )
    attended, lse, attn, mid, ffn_in, grad_ffn, out_units, ffn_units = call(
        mix_kernel,
        (blocks,),
        [token_spec, token_spec, mod_spec, token_spec, rows_of((TB, 128)), square, square],
        [token_spec, rows_of((128, TB), 1)] + [token_spec] * 4 + [units_spec] * 2,
        [token_bf16, lane_rows, token_bf16, token_f32, token_bf16, token_bf16, units, units],
        (x, cot, modulation, attended, lse_columns, w_out, perm),
        scalars=slots,
        name="mix",
    )

    rows_ff = ff // n_dev
    chunk = 768
    piece = chunk // 8
    half_units = lambda rows, columns: shape((4, rows, columns), bf16)
    square_send = [fixed((4, width // 8, width))] * 2
    square_shapes = [half_units(width // 8, width)] * 2
    gate_send, gate_own, up_send, up_own, down_send, down_own, ffn, grad_mod_ffn = call(
        functools.partial(ffn_kernel, n_mod=n_mod, rows_ff=rows_ff),
        (ff // chunk,),
        [fixed((count, width)), anywhere, anywhere]
        + [rows_of((width, chunk), 1)] * 2 + [rows_of((chunk, width))],
        [rows_of((4, width // 8, chunk), 2)] * 4
        + [rows_of((4, 1, piece, width), 1)] * 2 + [anywhere] * 2,
        [half_units(width // 8, ff)] * 4
        + [shape((4, ff // chunk, piece, width), bf16)] * 2 + [token_f32] * 2,
        (ffn_in, grad_ffn, ffn_units, w_gate, w_up, w_down),
        scalars=reducer.bits,
        scratch=[
            pltpu.VMEM((8, piece, count), bf16),
            pltpu.VMEM((count, width), bf16),
            pltpu.VMEM(units.shape, bf16),
            pltpu.VMEM((count, width), f32),
            pltpu.VMEM((count, width), f32),
            pltpu.SemaphoreType.DMA((4,)),
        ],
        name="ffn",
    )
    gate = Stream(reducer, gate_send, gate_own, 0)
    up = Stream(reducer, up_send, up_own, 1)
    down = Stream(
        reducer, down_send.reshape(4, ff // 8, width), down_own.reshape(4, ff // 8, width), 2, rows_ff
    )

    slots_core = jnp.concatenate([slots, reducer.bits[:2]])
    seg_spec = rows_of((SEG, width))
    output, grad_mid, grad_attended, dot_term, sums_b, out_send, out_own = call(
        middle_kernel,
        (count // SEG,),
        [seg_spec] * 6 + [rows_of((8, width // 8, SEG), 2), mod_spec, square, fixed(gather.shape)],
        [seg_spec] * 3 + [rows_of((128, SEG), 1), fixed((slots_n, 4 * width))] + square_send,
        [token_bf16, token_f32, token_bf16, lane_rows, shape((slots_n, 4 * width), f32)] + square_shapes,
        (mid, ffn, grad_mod_ffn, cot, attn, attended, out_units, modulation, w_out, gather),
        scalars=slots_core,
        scratch=[pltpu.VMEM((width, width), f32)],
        name="middle",
    )
    out = Stream(reducer, out_send, out_own, 1)
    early = [gate, up, down]
    middle_cut = width // 256 * 128 + 128
    gate.join(out, (0, middle_cut))
    up.join(out, (middle_cut, width))
    reducer.fold(early, "early")

    def attend_back(first, end, name):
        begin, stop, begin_row, stop_row = head_span(first, end, width)
        columns, rows = stop - begin, stop_row - begin_row
        used = pl.BlockSpec((count, columns), lambda *_: (0, begin // columns), pipeline_mode=pl.Buffered(1))
        used_rows = pl.BlockSpec((rows, count), lambda *_: (begin_row // rows, 0), pipeline_mode=pl.Buffered(1))
        return call(
            functools.partial(attend_back_kernel, first=first, base=begin, base_row=begin_row, width=width),
            ((end - first) // TOGETHER,),
            [used] * 4 + [fixed((128, count))] * 2 + [used_rows],
            [fixed((rows, count))] + [fixed((count, columns))] * 2,
            [shape((rows, count), f32), shape((count, columns), f32), shape((count, columns), bf16)],
            (query, key, value, grad_attended, lse, dot_term, key_t),
            scratch=[pltpu.VMEM((count, columns), f32)],
            scalars=slots,
            name=name,
        )

    cut = 3 * HEADS // 4
    dqt0, dk0, dv0 = attend_back(0, cut, "attend_back_0")
    reducer.fold(early, "early")
    dqt1, dk1, dv1 = attend_back(cut, HEADS, "attend_back_1")
    base, _, base_row, _ = head_span(cut, HEADS, width)
    v_send, v_own = call(
        functools.partial(value_kernel, base=base),
        (1,),
        [whole(units.shape), whole(dv0.shape), whole(dv1.shape)],
        [whole((4, width // 8, width))] * 2,
        square_shapes,
        (attn_units, dv0, dv1),
        scalars=reducer.bits,
        name="value",
    )
    v_part = Stream(reducer, v_send, v_own, 2)
    reducer.fold(early, "early")
    grad_q, grad_k, gains_low, q_send, q_own, k_send, k_own = call(
        functools.partial(project_back_kernel, base=base, base_row=base_row),
        (count // SEG,),
        [rows_of((dqt0.shape[0], SEG), 1), rows_of((dqt1.shape[0], SEG), 1)]
        + [rows_of((SEG, dk0.shape[1])), rows_of((SEG, dk1.shape[1]))]
        + [rows_of((SEG, 2 * width)), rows_of((SEG, 256)), seg_spec, seg_spec, rows_of((8, width // 8, SEG), 2), rows_of((2, SEG), 1)]
        + table_specs + [fixed(head_fold.shape)],
        [seg_spec] * 2 + [fixed((4, 128))] + square_send * 2,
        [token_bf16] * 2 + [shape((4, 128), bf16)] + square_shapes * 2,
        (dqt0, dqt1, dk0, dk1, raw, inverse, query, key, attn_units, coord) + tables + (head_fold,),
        scalars=reducer.bits,
        scratch=[pltpu.VMEM((width, width), f32)] * 2 + [pltpu.VMEM((2, width), f32)],
        name="project_back",
    )
    waiting = early + [v_part]
    *arrived, q_send, k_send = reducer.pass_on([stream.got for stream in waiting] + [q_send, k_send])
    for stream, got in zip(waiting, arrived):
        stream.got = got
    q_part = Stream(reducer, q_send, q_own, 1)
    k_part = Stream(reducer, k_send, k_own, 0)
    late = [q_part, k_part, v_part]
    extra = n_dp.bit_length() - 5
    reducer.fold([v_part], "v")
    reducer.fold([q_part, k_part], "late")
    for _ in range(extra):
        reducer.fold(early, "early")
    rows_d = width // n_dev
    merged = Merged([gate, up, down])
    third = rows_ff // 3
    gate_end = ff + middle_cut
    up_end = gate_end + ff + width - middle_cut
    merged.places = [
        (0, 0, 0, ff, None),
        (2, 0, ff, gate_end, None),
        (1, 0, gate_end, gate_end + ff, None),
        (2, middle_cut, gate_end + ff, up_end, None),
    ] + [
        (3, 0, up_end + i * width, up_end + (i + 1) * width, (i * third, (i + 1) * third)) for i in range(3)
    ]
    merged.shapes = [shape((rows_d, ff), f32)] * 2 + [shape((rows_d, width), f32), shape((rows_ff, width), f32)]
    early = [merged]
    reducer.fold(early, "early")

    columns = 7 * width + 128
    grad_tokens, own_rows = call(
        functools.partial(input_back_kernel, base=base),
        (blocks,),
        [token_spec] * 2 + [rows_of((TB, dv0.shape[1])), rows_of((TB, dv1.shape[1]))] + [token_spec] * 2
        + [mod_spec, fixed((width, 3 * width)), fixed((slots_n, 4 * width)), fixed((4, 128)), fixed((slots_n, width))],
        [token_spec, fixed((slots_n, columns))],
        [token_bf16, shape((slots_n, columns), bf16)],
        (grad_q, grad_k, dv0, dv1, x, grad_mid, modulation, w_qkv, sums_b, gains_low, own_activated),
        scalars=slots,
        scratch=[pltpu.VMEM((slots_n, 2 * width), f32)],
        name="input_back",
    )
    reducer.fold(late, "late")
    summed_gate, summed_up, summed_out, summed_down = reducer.fold(early, "early_last", last=True)
    reducer.fold(late, "late", passed=[own_rows])
    (own_rows,) = reducer.passed
    every_row = lax.all_gather(own_rows, ("dp", "mod"), axis=0, tiled=True)
    for _ in range(extra):
        reducer.fold(late, "late")
    late = [Merged(late)]
    reducer.fold(late, "late")
    (summed_qkv,) = reducer.fold(late, "late_last", last=True)
    grad_w_ada, gain_grads = call(
        functools.partial(ada_kernel, width=width),
        (1,),
        [whole(every_row.shape)],
        [whole((width // n_dp, half)), whole((2, 128))],
        [shape((width // n_dp, half), f32), shape((2, 128), f32)],
        (every_row,),
        scalars=reducer.bits,
        name="ada",
    )

    halves = own_rows[:, : 6 * width].reshape(slots_n, n_mod, half)
    own_half = lax.dynamic_index_in_dim(halves, mod_index, 1, keepdims=False)
    other_half = lax.dynamic_index_in_dim(halves, 1 - mod_index, 1, keepdims=False)
    both = pair_order(own_half, reducer.swap(other_half, "mod"), mod_index).reshape(-1, half)
    grad_activated = jnp.einsum("nc,dc->nd", both, w_ada, preferred_element_type=f32)
    grad_activated = grad_activated.reshape(n_mod, slots_n, width)
    own_part = lax.dynamic_index_in_dim(grad_activated, mod_index, 0, keepdims=False)
    other_part = lax.dynamic_index_in_dim(grad_activated, 1 - mod_index, 0, keepdims=False)
    grad_own = own_part + reducer.swap(other_part.astype(bf16), "mod").astype(f32)
    grad_cond = grad_own[None] * silu_grad(cond)
    return (
        output[None],
        grad_tokens[None],
        grad_cond,
        grad_w_ada,
        summed_qkv,
        gain_grads[0, :HD],
        gain_grads[1, :HD],
        summed_out,
        summed_gate,
        summed_up,
        summed_down,
    )


def solution(mesh):
    rows = ("dp", "mod")
    in_specs = (
        P(rows, None, None),
        P(rows, None, None),
        P(rows, None),
        P(rows, None, None),
        P(None, "mod"),
        P(),
        P(),
        P(),
        P(),
        P(),
        P(),
        P(),
        P(rows, None, None),
    )
    out_specs = (
        P(rows, None, None),
        P(rows, None, None),
        P(rows, None, None),
        P("dp", "mod"),
        P(rows, None),
        P(),
        P(),
        P(rows, None),
        P(rows, None),
        P(rows, None),
        P(rows, None),
    )
    return jax.shard_map(
        functools.partial(body, mesh.shape["dp"], mesh.shape["mod"]),
        mesh=mesh,
        in_specs=in_specs,
        out_specs=out_specs,
        check_vma=False,
    )
```

```python
import functools

import jax
import jax.numpy as jnp
import numpy as np
from jax import lax
from jax.experimental import pallas as pl
from jax.experimental.pallas import tpu as pltpu
from jax.sharding import PartitionSpec as P

HEADS = 16
HD = 72
GRID = 32
EPS = 1e-06
ROPE_BASE = 10000.0
SEG = 256
TB = 512
WIN = 256
TOGETHER = 4
SCORE_SCALE = float(HD**-0.5)
SCORE_LOG2 = float(np.log2(np.e) * HD**-0.5)
VMEM = 60 * 2**20
f32 = jnp.float32
bf16 = jnp.bfloat16


def nn(a, b):
    return lax.dot_general(a, b, (((1,), (0,)), ((), ())), preferred_element_type=f32)


def nt(a, b):
    return lax.dot_general(a, b, (((1,), (1,)), ((), ())), preferred_element_type=f32)


def tn(a, b):
    return lax.dot_general(a, b, (((0,), (0,)), ((), ())), preferred_element_type=f32)


def split3(v):
    hi = v.astype(bf16).astype(f32)
    mid = (v - hi).astype(bf16).astype(f32)
    return hi, mid, v - hi - mid


def np_split3(v):
    v = v.astype(np.float32)
    hi = v.astype(jnp.bfloat16).astype(np.float32)
    mid = (v - hi).astype(jnp.bfloat16).astype(np.float32)
    return [part.astype(jnp.bfloat16) for part in (hi, mid, v - hi - mid)]


@functools.lru_cache(None)
def rope_tables(width):
    quarter = HD // 4
    freqs = ROPE_BASE ** (-np.arange(quarter, dtype=np.float64) / quarter)
    lane = np.arange(width) % HD
    group = lane // quarter
    angle = np.arange(GRID)[:, None] * freqs[lane % quarter][None, :]
    cosine, sine = np.cos(angle), np.sin(angle)
    sine = np.where((group % 2 == 0)[None, :], -sine, sine)
    uses_col = (group >= 2)[None, :]
    tables = []
    for table in (cosine, sine):
        whole = np.concatenate(
            [np.where(uses_col, 0.0, table), np.where(uses_col, table, 0.0)], axis=0
        )
        tables.append(np.concatenate(np_split3(whole), axis=0))
    return tables


@functools.lru_cache(None)
def head_tables(width):
    head = np.arange(width) // HD
    gather = np.zeros((width, 128), np.float32)
    for copy in range(3):
        gather[np.arange(width), copy * HEADS + head] = 1.0
    fold = np.zeros((width, 128), np.float32)
    fold[np.arange(width), np.arange(width) % HD] = 1.0
    return gather.astype(jnp.bfloat16), gather.T.astype(jnp.bfloat16), fold.astype(jnp.bfloat16)


def unit_of(index, n_mod):
    mod = index % n_mod
    dp = index // n_mod
    return (dp % 2) * 2 * n_mod + mod * 2 + (dp // 2) % 2, dp // 4


def reversed_bits(value, size):
    result = 0
    for bit in range(size.bit_length() - 1):
        result = 2 * result + (value >> bit) % 2
    return result


@functools.lru_cache(None)
def unit_permutation(width, n_dp, n_mod):
    rows = width // (n_dp * n_mod)
    matrix = np.zeros((width, width), np.float32)
    for index in range(n_dp * n_mod):
        unit, rest = unit_of(index, n_mod)
        start = unit * (width // 8) + reversed_bits(rest, n_dp // 4) * rows
        matrix[start + np.arange(rows), index * rows + np.arange(rows)] = 1.0
    return matrix.astype(jnp.bfloat16)


def normed(v):
    centred = v - jnp.mean(v, axis=-1, keepdims=True)
    inverse = lax.rsqrt(jnp.mean(centred * centred, axis=-1, keepdims=True) + EPS)
    return centred * inverse, inverse


def norm_back(e, norm, inverse):
    return inverse * (
        e - jnp.mean(e, axis=-1, keepdims=True) - norm * jnp.mean(e * norm, axis=-1, keepdims=True)
    )


def part(mod_ref, slot, index, width):
    return mod_ref[pl.ds(slot, 1), index * width : (index + 1) * width]


def slots_here(slots, rows):
    return [slots[pl.program_id(0) * (rows // SEG) + i] for i in range(rows // SEG)]


def by_slot(function, here, *values):
    done = [
        function(slot, *(value[i * SEG : (i + 1) * SEG] for value in values)) for i, slot in enumerate(here)
    ]
    return jnp.concatenate(done, axis=0)


def angles(coords_ref, cos_ref, sin_ref):
    value = lax.broadcasted_iota(jnp.int32, (GRID, 1), 0)
    hot = [(value == coords_ref[i : i + 1, :]).astype(f32) for i in range(2)]
    hot = jnp.concatenate(hot * 3, axis=0).astype(bf16)
    return tn(hot, cos_ref[...]), tn(hot, sin_ref[...])


def partner(v):
    width = v.shape[1]
    quarter = HD // 4
    lane = lax.broadcasted_iota(jnp.int32, (1, width), 1)
    leads = (lane // quarter) % 2 == 0
    return jnp.where(leads, pltpu.roll(v, width - quarter, 1), pltpu.roll(v, quarter, 1))


def head_sum(v, gather_ref):
    hi = v.astype(bf16)
    low = (v - hi.astype(f32)).astype(bf16)
    return nn(hi, gather_ref[...]) + nn(low, gather_ref[...])


def head_spread(v, spread_ref):
    hi, mid, low = split3(v)
    lane = lax.broadcasted_iota(jnp.int32, (1, 128), 1)
    chosen = jnp.where(lane < HEADS, hi, jnp.where(lane < 2 * HEADS, mid, low))
    return nn(chosen.astype(bf16), spread_ref[...])


def window(head, width):
    start = jnp.minimum((head * HD) // 128, width // 128 - WIN // 128) * 128
    return pl.multiple_of(start, 128), head * HD - start


def head_lanes(offset):
    lane = lax.broadcasted_iota(jnp.int32, (1, WIN), 1)
    return (lane >= offset) & (lane < offset + HD)


def product(units_ref, half, rhs, out_ref):
    _, rows, tokens = units_ref.shape
    units = units_ref[pl.ds(4 * half, 4)].reshape(4 * rows, tokens)
    out_ref[...] = nn(units, rhs).astype(bf16).reshape(out_ref.shape)


def halves_out(acc_ref, core, send_ref, own_ref):
    rows = acc_ref.shape[0] // 2
    for half, out_ref in ((1 - core, send_ref), (core, own_ref)):
        start = pl.multiple_of(half * rows, rows)
        out_ref[...] = acc_ref[pl.ds(start, rows)].astype(bf16).reshape(out_ref.shape)


def add_by_slot(sums_ref, here, index, term):
    width = term.shape[1]
    for i, slot in enumerate(here):
        rows = term[i * SEG : (i + 1) * SEG]
        sums_ref[pl.ds(slot, 1), index * width : (index + 1) * width] += jnp.sum(rows, axis=0, keepdims=True)


def project_kernel(
    slots, x_ref, mod_ref, w_ref, coords_ref, cos_ref, sin_ref, gain_ref, gather_ref, spread_ref,
    perm_ref, units_ref, raw_ref, inv_ref, q_ref, k_ref, v_ref, kt_ref,
):
    width = x_ref.shape[1]
    norm, _ = normed(x_ref[...].astype(f32))

    def modulate(slot, rows):
        return (rows * (1.0 + part(mod_ref, slot, 1, width)) + part(mod_ref, slot, 0, width)).astype(bf16)

    low = by_slot(modulate, slots_here(slots, x_ref.shape[0]), norm)
    units_ref[...] = nt(perm_ref[...], low).astype(bf16).reshape(units_ref.shape)
    cosine, sine = angles(coords_ref, cos_ref, sin_ref)
    for index, out_ref in enumerate((q_ref, k_ref)):
        raw = nn(low, w_ref[:, index * width : (index + 1) * width])
        raw_ref[:, index * width : (index + 1) * width] = raw
        inverse = lax.rsqrt(head_sum(raw * raw, gather_ref) * (1.0 / HD) + EPS)
        inv_ref[:, index * 128 : (index + 1) * 128] = inverse
        scaled = raw * head_spread(inverse, spread_ref) * gain_ref[index : index + 1, :]
        turned = scaled * cosine + partner(scaled) * sine
        out_ref[...] = turned.astype(bf16)
        if index == 1:
            kt_ref[...] = turned.T.astype(bf16)
    v_ref[...] = nn(low, w_ref[:, 2 * width :]).astype(bf16)


def attend_kernel(slots, q_ref, k_ref, v_ref, o_ref, lse_ref):
    step = pl.program_id(0)
    tokens, width = q_ref.shape
    lane128 = lax.broadcasted_iota(jnp.int32, (1, 128), 1)
    lane = lax.broadcasted_iota(jnp.int32, (1, WIN), 1)

    @pl.when(step == 0)
    def _():
        o_ref[...] = jnp.zeros_like(o_ref)
        lse_ref[...] = jnp.zeros_like(lse_ref)

    def head(h, rows):
        start, offset = window(h, width)
        inside = head_lanes(offset)
        columns = pl.ds(start, WIN)
        query = jnp.where(inside, q_ref[rows, columns], 0)
        value = jnp.where(inside, v_ref[rows, columns], 1)
        weight = jnp.exp2(nt(query, k_ref[rows, columns]) * SCORE_LOG2).astype(bf16)
        summed = nn(weight, value)
        free = jnp.where(offset > 0, 0, WIN - 1)
        total = jnp.sum(jnp.where(lane == free, summed, 0.0), axis=1, keepdims=True)
        o_ref[rows, columns] += jnp.where(inside, summed * (1.0 / total), 0.0)
        lse_ref[rows, :] += jnp.where(lane128 == h, jnp.log2(total), 0.0)

    whole = slots[tokens // SEG - 1] == slots[0]

    @pl.when(whole)
    def _():
        for i in range(TOGETHER):
            head(step * TOGETHER + i, slice(None))

    @pl.when(jnp.logical_not(whole))
    def _():
        for i in range(TOGETHER):
            for b in range(tokens // SEG):
                head(step * TOGETHER + i, slice(b * SEG, (b + 1) * SEG))


def mix_kernel(
    slots, x_ref, cot_ref, mod_ref, o_ref, lse_ref, w_out_ref, perm_ref,
    attended_ref, lse_out_ref, attn_ref, mid_ref, low_ref, gf_ref, att_units_ref, ffn_units_ref,
):
    width = x_ref.shape[1]
    here = slots_here(slots, x_ref.shape[0])
    lse_out_ref[...] = lse_ref[...].T
    attended = o_ref[...].astype(bf16)
    attended_ref[...] = attended
    att_units_ref[...] = nt(perm_ref[...], attended).astype(bf16).reshape(att_units_ref.shape)
    attn = nn(attended, w_out_ref[...])
    attn_ref[...] = attn.astype(bf16)
    mid = by_slot(
        lambda slot, x, rows: x.astype(f32) + part(mod_ref, slot, 2, width) * rows, here, x_ref[...], attn
    )
    mid_ref[...] = mid
    norm, _ = normed(mid)

    def modulate(slot, rows):
        return (rows * (1.0 + part(mod_ref, slot, 4, width)) + part(mod_ref, slot, 3, width)).astype(bf16)

    low = by_slot(modulate, here, norm)
    low_ref[...] = low
    ffn_units_ref[...] = nt(perm_ref[...], low).astype(bf16).reshape(ffn_units_ref.shape)
    gf_ref[...] = by_slot(
        lambda slot, rows: (rows.astype(f32) * part(mod_ref, slot, 5, width)).astype(bf16), here, cot_ref[...]
    )


def ffn_kernel(
    bits, x_ref, gf_hbm, units_hbm, wg_ref, wu_ref, wd_ref,
    gate_send_ref, gate_own_ref, up_send_ref, up_own_ref, down_send_ref, down_own_ref, ffn_hbm, dmod_hbm,
    turned_ref, gf_ref, units_ref, ffn_ref, dmod_ref, sems, *, n_mod, rows_ff,
):
    core = bits[0]
    first = pl.program_id(0) == 0
    last = pl.program_id(0) == pl.num_programs(0) - 1
    load_gf = pltpu.make_async_copy(gf_hbm, gf_ref, sems.at[0])
    load_units = pltpu.make_async_copy(units_hbm, units_ref, sems.at[1])
    store_ffn = pltpu.make_async_copy(ffn_ref, ffn_hbm, sems.at[2])
    store_dmod = pltpu.make_async_copy(dmod_ref, dmod_hbm, sems.at[3])

    @pl.when(first)
    def _():
        load_gf.start()
        load_units.start()
        ffn_ref[...] = jnp.zeros_like(ffn_ref)
        dmod_ref[...] = jnp.zeros_like(dmod_ref)

    gate = nn(x_ref[...], wg_ref[...])
    up = nn(x_ref[...], wu_ref[...])

    @pl.when(first)
    def _():
        load_gf.wait()
        load_units.wait()

    grad_hidden = nt(gf_ref[...], wd_ref[...])
    sigmoid = 1.0 / (1.0 + jnp.exp(-gate))
    silu = gate * sigmoid
    hidden = (silu * up).astype(bf16)
    turned = hidden.T
    for index in range(turned.shape[0] // rows_ff):
        unit, rest = unit_of(index, n_mod)
        turned_ref[unit, rest * rows_ff : (rest + 1) * rows_ff] = turned[
            index * rows_ff : (index + 1) * rows_ff
        ]
    dg = (grad_hidden * up * (sigmoid * (1.0 + gate * (1.0 - sigmoid)))).astype(bf16)
    du = (grad_hidden * silu).astype(bf16)

    ffn_ref[...] += nn(hidden, wd_ref[...])
    dmod_ref[...] += nt(dg, wg_ref[...]) + nt(du, wu_ref[...])

    @pl.when(last)
    def _():
        store_ffn.start()
        store_dmod.start()

    product(units_ref, 1 - core, dg, gate_send_ref)
    product(units_ref, 1 - core, du, up_send_ref)
    product(turned_ref, 1 - core, gf_ref[...], down_send_ref)
    product(units_ref, core, dg, gate_own_ref)
    product(units_ref, core, du, up_own_ref)
    product(turned_ref, core, gf_ref[...], down_own_ref)

    @pl.when(last)
    def _():
        store_ffn.wait()
        store_dmod.wait()


def middle_kernel(
    slots, mid_ref, ffn_ref, dmod_ref, cot_ref, attn_ref, o_ref, units_ref, mod_ref, w_out_ref, gather_ref,
    out_ref, grad_mid_ref, do_ref, dot_ref, sums_ref, send_ref, own_ref, acc_ref,
):
    width = mid_ref.shape[1]
    block = pl.program_id(0)
    here = slots_here(slots, mid_ref.shape[0])
    segments = pl.num_programs(0) * len(here)
    incoming = cot_ref[...].astype(f32)
    mid = mid_ref[...]
    out_ref[...] = by_slot(
        lambda slot, rows, ffn: (rows + part(mod_ref, slot, 5, width) * ffn).astype(bf16), here, mid, ffn_ref[...]
    )
    norm, inverse = normed(mid)
    dmod = dmod_ref[...]
    scaled = by_slot(lambda slot, rows: rows * (1.0 + part(mod_ref, slot, 4, width)), here, dmod)
    grad_mid = incoming + norm_back(scaled, norm, inverse)
    grad_mid_ref[...] = grad_mid
    ga = by_slot(lambda slot, rows: (rows * part(mod_ref, slot, 2, width)).astype(bf16), here, grad_mid)
    grow = nn(units_ref[...].reshape(width, -1), ga)

    @pl.when(block == 0)
    def _():
        acc_ref[...] = grow

    @pl.when(block > 0)
    def _():
        acc_ref[...] += grow

    @pl.when(block == pl.num_programs(0) - 1)
    def _():
        halves_out(acc_ref, slots[segments], send_ref, own_ref)

    do = nt(ga, w_out_ref[...]).astype(bf16)
    do_ref[...] = do
    dot_ref[...] = head_sum(do.astype(f32) * o_ref[...].astype(f32), gather_ref).T

    @pl.when(block == 0)
    def _():
        sums_ref[...] = jnp.zeros_like(sums_ref)

    for index, term in enumerate((grad_mid * attn_ref[...].astype(f32), dmod, dmod * norm, incoming * ffn_ref[...])):
        add_by_slot(sums_ref, here, index, term)


def attend_back_kernel(
    slots, q_ref, k_ref, v_ref, do_ref, lse_ref, dot_ref, kt_ref, dqt_ref, dk_ref, dv_low_ref, dv_ref,
    *, first, base, base_row, width,
):
    tokens = q_ref.shape[0]

    @pl.when(pl.program_id(0) == 0)
    def _():
        dqt_ref[...] = jnp.zeros_like(dqt_ref)
        dk_ref[...] = jnp.zeros_like(dk_ref)
        dv_ref[...] = jnp.zeros_like(dv_ref)

    def head(h, rows):
        start, offset = window(h, width)
        inside = head_lanes(offset)
        columns = pl.ds(pl.multiple_of(start - base, 128), WIN)
        first_row = pl.multiple_of((h * HD) // 16 * 16, 16)
        own_place = pl.ds(pl.multiple_of(first_row - base_row, 16), HD + 8)
        row = lax.broadcasted_iota(jnp.int32, (HD + 8, 1), 0) + first_row
        own_rows = (row >= h * HD) & (row < h * HD + HD)
        query = q_ref[rows, columns]
        grad_out = do_ref[rows, columns]
        key = jnp.where(inside, k_ref[rows, columns], 0)
        value = jnp.where(inside, v_ref[rows, columns], 0)
        probs = jnp.exp2(nt(key, query) * SCORE_LOG2 - lse_ref[pl.ds(h, 1), rows])
        scores = (probs * (nt(value, grad_out) - dot_ref[pl.ds(h, 1), rows])).astype(bf16)
        dv_ref[rows, columns] += jnp.where(inside, nn(probs.astype(bf16), grad_out), 0.0)
        dk_ref[rows, columns] += jnp.where(inside, nn(scores, query) * SCORE_SCALE, 0.0)
        turned = nn(kt_ref[own_place, rows], scores) * SCORE_SCALE
        dqt_ref[own_place, rows] += jnp.where(own_rows, turned, 0.0)

    whole = slots[tokens // SEG - 1] == slots[0]
    begin = first + pl.program_id(0) * TOGETHER

    @pl.when(whole)
    def _():
        for i in range(TOGETHER):
            head(begin + i, slice(None))

    @pl.when(jnp.logical_not(whole))
    def _():
        for i in range(TOGETHER):
            for b in range(tokens // SEG):
                head(begin + i, slice(b * SEG, (b + 1) * SEG))

    @pl.when(pl.program_id(0) == pl.num_programs(0) - 1)
    def _():
        dv_low_ref[...] = dv_ref[...].astype(bf16)


def head_span(first, end, width):
    begin = lambda head: min(head * HD // 128, width // 128 - WIN // 128) * 128
    return begin(first), begin(end - 1) + WIN, first * HD // 16 * 16, (end - 1) * HD // 16 * 16 + HD + 8


def join_spans(low, high, begin, axis):
    size = low.shape[axis] - begin
    if size == 0:
        return jnp.concatenate([low, high], axis=axis)
    cut = lambda arr, start, stop: lax.slice_in_dim(arr, start, stop, axis=axis)
    middle = cut(low, begin, begin + size) + cut(high, 0, size)
    return jnp.concatenate([cut(low, 0, begin), middle, cut(high, size, high.shape[axis])], axis=axis)


def project_back_kernel(
    bits, dqt0_ref, dqt1_ref, dk0_ref, dk1_ref, raw_ref, inv_ref, q_ref, k_ref, units_ref,
    coords_ref, cos_ref, sin_ref, gain_ref, gather_ref, spread_ref, fold_ref,
    gq_ref, gk_ref, gains_low_ref, q_send_ref, q_own_ref, k_send_ref, k_own_ref, accq_ref, acck_ref, gains_ref,
    *, base, base_row,
):
    width = q_ref.shape[1]
    block = pl.program_id(0)

    @pl.when(block == 0)
    def _():
        gains_ref[...] = jnp.zeros_like(gains_ref)
        accq_ref[...] = jnp.zeros_like(accq_ref)
        acck_ref[...] = jnp.zeros_like(acck_ref)

    cosine, sine = angles(coords_ref, cos_ref, sin_ref)
    parts = ((q_ref, gq_ref, accq_ref), (k_ref, gk_ref, acck_ref))
    for index, (low_ref, out_ref, acc_ref) in enumerate(parts):
        if index == 0:
            grad = join_spans(dqt0_ref[...], dqt1_ref[...], base_row, 0).T
        else:
            grad = join_spans(dk0_ref[...], dk1_ref[...], base, 1)
        raw = raw_ref[:, index * width : (index + 1) * width]
        inverse = head_spread(inv_ref[:, index * 128 : (index + 1) * 128], spread_ref)
        mean = head_sum(grad * low_ref[...].astype(f32), gather_ref) * (1.0 / HD)
        norm = raw * inverse
        back = grad * cosine - partner(grad) * sine
        gains_ref[index : index + 1, :] += jnp.sum(back * norm, axis=0, keepdims=True)
        grad_raw = (
            inverse * (back * gain_ref[index : index + 1, :] - norm * head_spread(mean, spread_ref))
        ).astype(bf16)
        out_ref[...] = grad_raw
        acc_ref[...] += nn(units_ref[...].reshape(width, -1), grad_raw)

    @pl.when(block == pl.num_programs(0) - 1)
    def _():
        halves_out(accq_ref, bits[0], q_send_ref, q_own_ref)
        halves_out(acck_ref, bits[0], k_send_ref, k_own_ref)
        terms = split3(gains_ref[...])
        sums = sum(nn(term.astype(bf16), fold_ref[...]) for term in terms)
        high = sums.astype(bf16).astype(f32)
        row = lax.broadcasted_iota(jnp.int32, (8, 1), 0)
        mine = 4 * bits[1]
        placed = jnp.zeros((8, 128), f32)
        for index, term in enumerate((high[0:1], (sums - high)[0:1], high[1:2], (sums - high)[1:2])):
            placed = jnp.where(row == mine + index, term, placed)
        gains_low_ref[...] = placed.astype(bf16)


def input_back_kernel(
    slots, gq_ref, gk_ref, dv0_ref, dv1_ref, x_ref, grad_mid_ref, mod_ref, w_ref, other_sums_ref, gains_ref,
    grad_x_ref, grad_own_ref, grad_other_ref, sums_ref, *, base,
):
    width = x_ref.shape[1]
    block = pl.program_id(0)
    here = slots_here(slots, x_ref.shape[0])
    last_block = pl.num_programs(0) - 1
    segments = pl.num_programs(0) * len(here)
    dmod = nt(gq_ref[...], w_ref[:, :width]) + nt(gk_ref[...], w_ref[:, width : 2 * width])
    dmod = dmod + nt(join_spans(dv0_ref[...], dv1_ref[...], base, 1), w_ref[:, 2 * width :])
    norm, inverse = normed(x_ref[...].astype(f32))
    scaled = by_slot(lambda slot, rows: rows * (1.0 + part(mod_ref, slot, 1, width)), here, dmod)
    grad_x = grad_mid_ref[...] + norm_back(scaled, norm, inverse)
    grad_x_ref[...] = grad_x.astype(bf16)

    @pl.when(block == 0)
    def _():
        sums_ref[...] = jnp.zeros_like(sums_ref)

    for index, term in enumerate((dmod, dmod * norm)):
        add_by_slot(sums_ref, here, index, term)

    @pl.when(block == last_block)
    def _():
        mod = slots[segments + 1]
        count = sums_ref.shape[0]
        half = 3 * width
        mine = jnp.concatenate([sums_ref[...]] * 2, axis=0)
        rest = jnp.concatenate([other_sums_ref[...]] * 2, axis=0)
        row = lax.broadcasted_iota(jnp.int32, (2 * count, 1), 0) // count
        attn_part = jnp.where(row == mod, jnp.concatenate([mine, rest[:, :width]], axis=1), 0.0)
        ffn_part = jnp.where(row == mod, rest[:, width:], 0.0)
        grad_own_ref[:, :half] = jnp.where(mod == 0, attn_part, ffn_part).astype(bf16)
        grad_other_ref[:, :half] = jnp.where(mod == 0, ffn_part, attn_part).astype(bf16)
        grad_own_ref[:, half:] = gains_ref[...]
        grad_other_ref[:, half:] = gains_ref[...]


def value_kernel(bits, units_ref, dv0_ref, dv1_ref, send_ref, own_ref, *, base):
    rhs = join_spans(dv0_ref[...], dv1_ref[...], base, 1)
    product(units_ref, 1 - bits[0], rhs, send_ref)
    product(units_ref, bits[0], rhs, own_ref)


def split_step(bits, ins, outs, *, lead, at, bit, pair_rows, cuts):
    send_ref, keep_ref = outs
    mine = bits[bit]
    start = 0
    for own_ref, got_ref, cut in zip(ins[::2], ins[1::2], cuts):
        columns, target = slice(None), slice(None)
        if cut:
            columns, target = slice(*cut), slice(start, start + cut[1] - cut[0])
            start = target.stop

        def total(*index):
            place = index + (slice(None), columns)
            return own_ref[place].astype(f32) + got_ref[place].astype(f32)

        if at is None:
            for j in range(max(lead, 1)):
                index = (j,) if lead else ()
                value = total(*index)
                rows = pair_rows or value.shape[0] // 2
                for p in range(value.shape[0] // (2 * rows)):
                    first = value[2 * p * rows : (2 * p + 1) * rows]
                    second = value[(2 * p + 1) * rows : (2 * p + 2) * rows]
                    place = index + (slice(p * rows, (p + 1) * rows), target)
                    send_ref[place] = jnp.where(mine == 1, first, second).astype(bf16)
                    keep_ref[place] = jnp.where(mine == 1, second, first).astype(keep_ref.dtype)
            continue
        for j in range(lead // 2):
            place = ((j,) if lead > 2 else ()) + (slice(None), target)
            away = 1 - mine if lead == 2 else 2 * (1 - mine) + j if at == 0 else 2 * j + 1 - mine
            own = mine if lead == 2 else 2 * mine + j if at == 0 else 2 * j + mine
            send_ref[place] = total(away).astype(bf16)
            keep_ref[place] = total(own).astype(keep_ref.dtype)


def merge_step(bits, ins, outs, *, bit, parts):
    send_ref, keep_ref = outs
    start = 0
    for own_ref, got_ref, pieces in zip(ins[::2], ins[1::2], parts):
        value = own_ref[...].astype(f32) + got_ref[...].astype(f32)
        rows, columns = value.shape[0] // 2, value.shape[1]
        first, second = value[:rows], value[rows:]
        sent = jnp.where(bits[bit] == 1, first, second).astype(bf16)
        kept = jnp.where(bits[bit] == 1, second, first)
        for i in range(pieces):
            place = slice(start, start + columns)
            if pieces > 1:
                send_ref[:, place] = jnp.zeros_like(send_ref[:, place])
                keep_ref[:, place] = jnp.zeros_like(keep_ref[:, place])
            taken = slice(i * rows // pieces, (i + 1) * rows // pieces)
            send_ref[: rows // pieces, place] = sent[taken]
            keep_ref[: rows // pieces, place] = kept[taken]
            start += columns


def apart_step(bits, ins, outs, *, places):
    own_ref, got_ref = ins
    for out, at, start, stop, rows in places:
        value = own_ref[:, start:stop] + got_ref[:, start:stop].astype(f32)
        if rows is None:
            outs[out][:, at : at + stop - start] = value
        else:
            count = rows[1] - rows[0]
            outs[out][rows[0] : rows[1], :] = value[:count]


def pair_step(bits, ins, outs):
    own_ref, got_ref, activated_ref = ins
    width = activated_ref.shape[1]
    outs[0][:, :width] = activated_ref[...]
    outs[0][:, width:] = (own_ref[...].astype(f32) + got_ref[...].astype(f32)).astype(bf16)


def joined(ins):
    return jnp.concatenate([ref[...].astype(f32) for ref in ins], axis=0).astype(bf16)


def join_step(bits, ins, outs):
    outs[0][...] = joined(ins)


def last_step(bits, ins, outs):
    outs[0][...] = ins[0][...] + ins[1][...].astype(f32)


def ada_step(bits, ins, outs, *, width):
    rows = outs[0].shape[0]
    every = joined(ins)
    position = bits[0] + sum(bits[1 + k] * 2**k for k in range(1, (width // rows).bit_length() - 1))
    feature = lax.broadcasted_iota(jnp.int32, (width, 128), 0)
    place = lax.broadcasted_iota(jnp.int32, (width, 128), 1)
    chosen = (feature == position * rows + place) & (place < rows)
    own = nn(every[:, :width], chosen.astype(f32).astype(bf16)).astype(bf16)
    half = outs[0].shape[1]
    outs[0][...] = tn(own, every[:, width : width + half])[:rows]
    terms = every[:, width + half :].astype(f32)
    kind = lax.broadcasted_iota(jnp.int32, (terms.shape[0], 1), 0) // 2 % 2
    for index in range(2):
        outs[1][index : index + 1, :] = jnp.sum(jnp.where(kind == index, terms, 0.0), axis=0, keepdims=True)


def step_kernel(bits, *refs, plans):
    n_in = sum(plan[1] for plan in plans)
    ins, outs = refs[:n_in], refs[n_in:]
    for function, takes, gives in plans:
        function(bits, ins[:takes], outs[:gives])
        ins, outs = ins[takes:], outs[gives:]


class Chain:
    def __init__(self):
        self.last = None

    def __call__(
        self, kernel, grid, in_specs, out_specs, out_shape, args, scalars=None, scratch=(), name=None, aliases=None
    ):
        ahead = 0 if scalars is None else 1
        body = kernel
        token = ()
        if self.last is not None:
            token = (self.last,)
            in_specs = [pl.BlockSpec(memory_space=pl.ANY)] + list(in_specs)

            def body(*refs):
                kernel(*refs[:ahead], *refs[ahead + 1 :])

        spec = pltpu.PrefetchScalarGridSpec(
            num_scalar_prefetch=ahead,
            grid=grid,
            in_specs=in_specs,
            out_specs=out_specs,
            scratch_shapes=scratch,
        )
        outs = pl.pallas_call(
            body,
            grid_spec=spec,
            input_output_aliases=aliases or {},
            out_shape=out_shape,
            compiler_params=pltpu.CompilerParams(vmem_limit_bytes=VMEM),
            cost_estimate=pl.CostEstimate(flops=1, bytes_accessed=1, transcendentals=0),
            name=name,
        )(*(() if scalars is None else (scalars,)), *token, *args)
        self.last = outs[0]
        return outs


def shape(dims, dtype):
    return jax.ShapeDtypeStruct(dims, dtype)


def fixed(dims):
    return pl.BlockSpec(dims, lambda *_: (0,) * len(dims), pipeline_mode=pl.Buffered(1))


def rows_of(dims, axis=0):
    return pl.BlockSpec(dims, lambda b, *_: tuple(b if i == axis else 0 for i in range(len(dims))))


def whole(dims):
    return rows_of(dims, None)


def column_parts(dims, steps):
    return rows_of(dims[:-1] + (dims[-1] // steps,), len(dims) - 1)


class Reducer:
    def __init__(self, n_dp, n_mod, call):
        self.n_dp, self.n_mod, self.call = n_dp, n_mod, call
        self.position = lax.axis_index("dp")
        steps = range(n_dp.bit_length() - 1)
        dp_bits = [lax.shift_right_logical(self.position, step) & 1 for step in steps]
        self.bits = jnp.stack([dp_bits[0], lax.axis_index("mod")] + dp_bits[1:]).astype(jnp.int32)

    def swap(self, arr, bit):
        if bit == "mod":
            return lax.ppermute(arr, "mod", [(i, i ^ 1) for i in range(self.n_mod)])
        return lax.ppermute(arr, "dp", [(i, i ^ (1 << bit)) for i in range(self.n_dp)])

    def bit_of(self, bit):
        return 1 if bit == "mod" else bit + 1 if bit else 0

    def fold(self, streams, name, last=False):
        plans, args, outs = [], [], []
        for stream in streams:
            function, shapes = stream.last_plan() if last else stream.plan()
            inputs = stream.inputs()
            plans.append((function, len(inputs), len(shapes)))
            args += inputs
            outs += shapes
        size = sum(arg.size for arg in args)
        split = all(
            isinstance(stream, Stream) and stream.side is None and stream.own.shape[-1] % 384 == 0
            for stream in streams
        )
        steps = 3 if split and size > 2**20 else 1
        results = self.call(
            functools.partial(step_kernel, plans=plans),
            (steps,),
            [column_parts(arg.shape, steps) for arg in args],
            [column_parts(out.shape, steps) for out in outs],
            outs,
            args,
            scalars=self.bits,
            name=name,
        )
        results = list(results)
        if last:
            return results
        for stream, plan in zip(streams, plans):
            stream.step(results[: plan[2]])
            results = results[plan[2] :]

    def pass_on(self, arrays):
        anywhere = [pl.BlockSpec(memory_space=pl.ANY)] * len(arrays)
        return self.call(
            lambda *refs: None,
            (1,),
            anywhere,
            anywhere,
            [shape(arr.shape, arr.dtype) for arr in arrays],
            arrays,
            name="pass_on",
            aliases={i + 1: i for i in range(len(arrays))},
        )


class Stream:
    def __init__(self, reducer, sent, own, first, pair_rows=None):
        self.r, self.own, self.pair_rows = reducer, own, pair_rows
        order = ["mod", 1, 2]
        self.steps = order[first:] + order[:first] + list(range(3, reducer.n_dp.bit_length() - 1))
        self.lead = ["mod", 1]
        self.side = None
        self.got = reducer.swap(sent, 0)

    def inputs(self):
        return [self.own, self.got] + ([self.side[0].own, self.side[0].got] if self.side else [])

    def plan(self):
        bit = self.steps[0]
        dims = self.own.shape
        at = self.lead.index(bit) if bit in self.lead else None
        cuts = [None]
        if self.side is not None:
            cuts = [(0, dims[-1]), self.side[1]]
            dims = dims[:-1] + (dims[-1] + self.side[1][1] - self.side[1][0],)
        function = functools.partial(
            split_step, lead=dims[0] if self.lead else 0, at=at, bit=self.r.bit_of(bit), pair_rows=self.pair_rows,
            cuts=cuts,
        )
        if at is None:
            dims = dims[:-2] + (dims[-2] // 2, dims[-1])
        else:
            dims = dims[1:] if len(self.lead) == 1 else (2,) + dims[1:]
        return function, [shape(dims, bf16), shape(dims, bf16 if len(self.lead) == 2 else f32)]

    def step(self, results):
        bit = self.steps.pop(0)
        if bit in self.lead:
            self.lead.remove(bit)
        self.side = None
        sent, self.own = results
        self.got = self.r.swap(sent, bit)

    def join(self, stream, cut):
        self.side = (stream, cut)


class Merged:
    def __init__(self, streams):
        self.streams, self.r, self.bit = streams, streams[0].r, streams[0].steps[0]
        self.own = self.places = self.shapes = None

    def inputs(self):
        if self.own is not None:
            return [self.own, self.got]
        return [arr for stream in self.streams for arr in (stream.own, stream.got)]

    def plan(self):
        parts = [3 if stream.pair_rows else 1 for stream in self.streams]
        columns = sum(pieces * stream.own.shape[1] for pieces, stream in zip(parts, self.streams))
        dims = (self.streams[0].own.shape[0] // 2, columns)
        function = functools.partial(merge_step, bit=self.r.bit_of(self.bit), parts=parts)
        return function, [shape(dims, bf16), shape(dims, f32)]

    def step(self, results):
        sent, self.own = results
        self.got = self.r.swap(sent, self.bit)

    def last_plan(self):
        if self.places is None:
            return last_step, [shape(self.own.shape, f32)]
        return functools.partial(apart_step, places=self.places), self.shapes


class Gather:
    def __init__(self, reducer, sent, own, activated):
        self.r, self.own, self.activated = reducer, own, activated
        self.steps = [1] + list(range(reducer.n_dp.bit_length() - 2, 1, -1)) + [0]
        self.got = reducer.swap(sent, "mod")
        self.pair = None

    def inputs(self):
        return [self.own, self.got] + ([self.activated] if self.pair is None else [])

    def plan(self):
        rows, columns = self.own.shape
        if self.pair is None:
            return pair_step, [shape((rows, columns + self.activated.shape[1]), bf16)]
        return join_step, [shape((2 * rows, columns), bf16)]

    def step(self, results):
        (self.own,) = results
        if self.pair is None:
            self.pair = self.own
        self.got = self.r.swap(self.own, self.steps.pop(0))

    def last_plan(self):
        width = self.activated.shape[1]
        function = functools.partial(ada_step, width=width)
        dims = (width // self.r.n_dp, self.own.shape[1] - width - 128)
        return function, [shape(dims, f32), shape((2, 128), f32)]


def silu_grad(v):
    sigmoid = jax.nn.sigmoid(v)
    return sigmoid * (1.0 + v * (1.0 - sigmoid))


def pair_order(own, other, mod):
    return jnp.where(mod == 0, jnp.stack([own, other]), jnp.stack([other, own]))


def body(
    n_dp, n_mod, tokens, cond, segments, coords, w_ada, w_qkv, q_gain, k_gain, w_out, w_gate, w_up,
    w_down, cotangent,
):
    _, count, width = tokens.shape
    slots_n = cond.shape[1]
    half = w_ada.shape[1]
    ff = w_gate.shape[1]
    blocks = count // TB
    n_dev = n_dp * n_mod
    call = Chain()
    reducer = Reducer(n_dp, n_mod, call)
    mod_index = lax.axis_index("mod")
    x = tokens[0]
    cot = cotangent[0]
    slots = segments[0, ::SEG]
    coord = coords[0]
    cos_table, sin_table = (jnp.asarray(t) for t in rope_tables(width))
    gather, spread, head_fold = (jnp.asarray(t) for t in head_tables(width))
    perm = jnp.asarray(unit_permutation(width, n_dp, n_mod))
    gains = jnp.stack([jnp.tile(q_gain, HEADS), jnp.tile(k_gain, HEADS)])

    cond_both = pair_order(cond[0], reducer.swap(cond[0], "mod"), mod_index)
    activated = jax.nn.silu(cond_both).astype(bf16).reshape(-1, width)
    mod_half = jnp.dot(activated, w_ada, preferred_element_type=f32).astype(bf16)
    mod_half = mod_half.reshape(n_mod, slots_n, half)
    own_half = lax.dynamic_index_in_dim(mod_half, mod_index, 0, keepdims=False)
    other_half = lax.dynamic_index_in_dim(mod_half, 1 - mod_index, 0, keepdims=False)
    pair = pair_order(own_half, reducer.swap(other_half, "mod"), mod_index)
    modulation = jnp.concatenate([pair[0], pair[1]], axis=1).astype(f32)

    anywhere = pl.BlockSpec(memory_space=pl.ANY)
    token_f32 = shape((count, width), f32)
    token_bf16 = shape((count, width), bf16)
    units = shape((8, width // 8, count), bf16)
    units_spec = rows_of((8, width // 8, TB), 2)
    token_spec = rows_of((TB, width))
    mod_spec = fixed((slots_n, 6 * width))
    square = fixed((width, width))
    table_specs = [fixed(cos_table.shape), fixed(sin_table.shape), fixed((2, width)), fixed(gather.shape), fixed(spread.shape)]
    tables = (cos_table, sin_table, gains, gather, spread)
    lane_rows = shape((128, count), f32)
    macs = count * width * width

    attn_units, raw, inverse, query, key, value, key_t = call(
        project_kernel,
        (blocks,),
        [token_spec, mod_spec, fixed((width, 3 * width)), rows_of((2, TB), 1)] + table_specs + [square],
        [units_spec, rows_of((TB, 2 * width)), rows_of((TB, 256))] + [token_spec] * 3 + [rows_of((width, TB), 1)],
        [units, shape((count, 2 * width), f32), shape((count, 256), f32)] + [token_bf16] * 3
        + [shape((width, count), bf16)],
        (x, modulation, w_qkv, coord) + tables + (perm,),
        scalars=slots,
        name="project",
    )
    attended, lse_columns = call(
        attend_kernel,
        (HEADS // TOGETHER,),
        [fixed((count, width))] * 3,
        [fixed((count, width)), fixed((count, 128))],
        [token_f32, shape((count, 128), f32)],
        (query, key, value),
        scalars=slots,
        name="attend",
    )
    attended, lse, attn, mid, ffn_in, grad_ffn, out_units, ffn_units = call(
        mix_kernel,
        (blocks,),
        [token_spec, token_spec, mod_spec, token_spec, rows_of((TB, 128)), square, square],
        [token_spec, rows_of((128, TB), 1)] + [token_spec] * 4 + [units_spec] * 2,
        [token_bf16, lane_rows, token_bf16, token_f32, token_bf16, token_bf16, units, units],
        (x, cot, modulation, attended, lse_columns, w_out, perm),
        scalars=slots,
        name="mix",
    )

    rows_ff = ff // n_dev
    chunk = 768
    piece = chunk // 8
    half_units = lambda rows, columns: shape((4, rows, columns), bf16)
    square_send = [fixed((4, width // 8, width))] * 2
    square_shapes = [half_units(width // 8, width)] * 2
    gate_send, gate_own, up_send, up_own, down_send, down_own, ffn, grad_mod_ffn = call(
        functools.partial(ffn_kernel, n_mod=n_mod, rows_ff=rows_ff),
        (ff // chunk,),
        [fixed((count, width)), anywhere, anywhere]
        + [rows_of((width, chunk), 1)] * 2 + [rows_of((chunk, width))],
        [rows_of((4, width // 8, chunk), 2)] * 4
        + [rows_of((4, 1, piece, width), 1)] * 2 + [anywhere] * 2,
        [half_units(width // 8, ff)] * 4
        + [shape((4, ff // chunk, piece, width), bf16)] * 2 + [token_f32] * 2,
        (ffn_in, grad_ffn, ffn_units, w_gate, w_up, w_down),
        scalars=reducer.bits,
        scratch=[
            pltpu.VMEM((8, piece, count), bf16),
            pltpu.VMEM((count, width), bf16),
            pltpu.VMEM(units.shape, bf16),
            pltpu.VMEM((count, width), f32),
            pltpu.VMEM((count, width), f32),
            pltpu.SemaphoreType.DMA((4,)),
        ],
        name="ffn",
    )
    gate = Stream(reducer, gate_send, gate_own, 0)
    up = Stream(reducer, up_send, up_own, 1)
    down = Stream(
        reducer, down_send.reshape(4, ff // 8, width), down_own.reshape(4, ff // 8, width), 2, rows_ff
    )

    slots_core = jnp.concatenate([slots, reducer.bits[:2]])
    seg_spec = rows_of((SEG, width))
    output, grad_mid, grad_attended, dot_term, sums_b, out_send, out_own = call(
        middle_kernel,
        (count // SEG,),
        [seg_spec] * 6 + [rows_of((8, width // 8, SEG), 2), mod_spec, square, fixed(gather.shape)],
        [seg_spec] * 3 + [rows_of((128, SEG), 1), fixed((slots_n, 4 * width))] + square_send,
        [token_bf16, token_f32, token_bf16, lane_rows, shape((slots_n, 4 * width), f32)] + square_shapes,
        (mid, ffn, grad_mod_ffn, cot, attn, attended, out_units, modulation, w_out, gather),
        scalars=slots_core,
        scratch=[pltpu.VMEM((width, width), f32)],
        name="middle",
    )
    out = Stream(reducer, out_send, out_own, 1)
    early = [gate, up, down]
    middle_cut = width // 256 * 128 + 128
    gate.join(out, (0, middle_cut))
    up.join(out, (middle_cut, width))
    reducer.fold(early, "early")

    def attend_back(first, end, name):
        begin, stop, begin_row, stop_row = head_span(first, end, width)
        columns, rows = stop - begin, stop_row - begin_row
        used = pl.BlockSpec((count, columns), lambda *_: (0, begin // columns), pipeline_mode=pl.Buffered(1))
        used_rows = pl.BlockSpec((rows, count), lambda *_: (begin_row // rows, 0), pipeline_mode=pl.Buffered(1))
        return call(
            functools.partial(attend_back_kernel, first=first, base=begin, base_row=begin_row, width=width),
            ((end - first) // TOGETHER,),
            [used] * 4 + [fixed((128, count))] * 2 + [used_rows],
            [fixed((rows, count))] + [fixed((count, columns))] * 2,
            [shape((rows, count), f32), shape((count, columns), f32), shape((count, columns), bf16)],
            (query, key, value, grad_attended, lse, dot_term, key_t),
            scratch=[pltpu.VMEM((count, columns), f32)],
            scalars=slots,
            name=name,
        )

    cut = 3 * HEADS // 4
    dqt0, dk0, dv0 = attend_back(0, cut, "attend_back_0")
    reducer.fold(early, "early")
    dqt1, dk1, dv1 = attend_back(cut, HEADS, "attend_back_1")
    base, _, base_row, _ = head_span(cut, HEADS, width)
    v_send, v_own = call(
        functools.partial(value_kernel, base=base),
        (1,),
        [whole(units.shape), whole(dv0.shape), whole(dv1.shape)],
        [whole((4, width // 8, width))] * 2,
        square_shapes,
        (attn_units, dv0, dv1),
        scalars=reducer.bits,
        name="value",
    )
    v_part = Stream(reducer, v_send, v_own, 2)
    reducer.fold(early, "early")
    grad_q, grad_k, gains_low, q_send, q_own, k_send, k_own = call(
        functools.partial(project_back_kernel, base=base, base_row=base_row),
        (count // SEG,),
        [rows_of((dqt0.shape[0], SEG), 1), rows_of((dqt1.shape[0], SEG), 1)]
        + [rows_of((SEG, dk0.shape[1])), rows_of((SEG, dk1.shape[1]))]
        + [rows_of((SEG, 2 * width)), rows_of((SEG, 256)), seg_spec, seg_spec, rows_of((8, width // 8, SEG), 2), rows_of((2, SEG), 1)]
        + table_specs + [fixed(head_fold.shape)],
        [seg_spec] * 2 + [fixed((8, 128))] + square_send * 2,
        [token_bf16] * 2 + [shape((8, 128), bf16)] + square_shapes * 2,
        (dqt0, dqt1, dk0, dk1, raw, inverse, query, key, attn_units, coord) + tables + (head_fold,),
        scalars=reducer.bits,
        scratch=[pltpu.VMEM((width, width), f32)] * 2 + [pltpu.VMEM((2, width), f32)],
        name="project_back",
    )
    waiting = early + [v_part]
    *arrived, q_send, k_send = reducer.pass_on([stream.got for stream in waiting] + [q_send, k_send])
    for stream, got in zip(waiting, arrived):
        stream.got = got
    q_part = Stream(reducer, q_send, q_own, 1)
    k_part = Stream(reducer, k_send, k_own, 0)
    late = [q_part, k_part, v_part]
    extra = n_dp.bit_length() - 5
    reducer.fold([v_part], "v")
    reducer.fold([q_part, k_part], "late")
    for _ in range(extra):
        reducer.fold(early, "early")
    rows_d = width // n_dev
    merged = Merged([gate, up, down])
    third = rows_ff // 3
    gate_end = ff + middle_cut
    up_end = gate_end + ff + width - middle_cut
    merged.places = [
        (0, 0, 0, ff, None),
        (2, 0, ff, gate_end, None),
        (1, 0, gate_end, gate_end + ff, None),
        (2, middle_cut, gate_end + ff, up_end, None),
    ] + [
        (3, 0, up_end + i * width, up_end + (i + 1) * width, (i * third, (i + 1) * third)) for i in range(3)
    ]
    merged.shapes = [shape((rows_d, ff), f32)] * 2 + [shape((rows_d, width), f32), shape((rows_ff, width), f32)]
    early = [merged]
    reducer.fold(early, "early")

    grad_tokens, mod_own, mod_other = call(
        functools.partial(input_back_kernel, base=base),
        (blocks,),
        [token_spec] * 2 + [rows_of((TB, dv0.shape[1])), rows_of((TB, dv1.shape[1]))] + [token_spec] * 2
        + [mod_spec, fixed((width, 3 * width)), fixed((slots_n, 4 * width)), fixed((8, 128))],
        [token_spec] + [fixed((2 * slots_n, half + 128))] * 2,
        [token_bf16] + [shape((2 * slots_n, half + 128), bf16)] * 2,
        (grad_q, grad_k, dv0, dv1, x, grad_mid, modulation, w_qkv, sums_b, gains_low),
        scalars=slots_core,
        scratch=[pltpu.VMEM((slots_n, 2 * width), f32)],
        name="input_back",
    )
    every_mod = Gather(reducer, mod_other, mod_own, activated)
    reducer.fold([v_part], "v")
    reducer.fold([every_mod], "pair")
    reducer.fold([q_part], "q")
    reducer.fold([every_mod], "every")
    reducer.fold([k_part], "k")
    summed_gate, summed_up, summed_out, summed_down = reducer.fold(early, "early_last", last=True)
    for _ in range(1 + extra):
        reducer.fold(late + [every_mod], "late")
    late = [Merged(late)]
    reducer.fold(late + [every_mod], "late")
    summed_qkv, grad_w_ada, gain_grads = reducer.fold(late + [every_mod], "late_last", last=True)

    grad_activated = jnp.einsum("nc,dc->nd", every_mod.pair[:, width : width + half], w_ada, preferred_element_type=f32)
    grad_activated = grad_activated.reshape(n_mod, slots_n, width)
    own_part = lax.dynamic_index_in_dim(grad_activated, mod_index, 0, keepdims=False)
    other_part = lax.dynamic_index_in_dim(grad_activated, 1 - mod_index, 0, keepdims=False)
    grad_own = own_part + reducer.swap(other_part.astype(bf16), "mod").astype(f32)
    grad_cond = grad_own[None] * silu_grad(cond)
    return (
        output[None],
        grad_tokens[None],
        grad_cond,
        grad_w_ada,
        summed_qkv,
        gain_grads[0, :HD],
        gain_grads[1, :HD],
        summed_out,
        summed_gate,
        summed_up,
        summed_down,
    )


def solution(mesh):
    rows = ("dp", "mod")
    in_specs = (
        P(rows, None, None),
        P(rows, None, None),
        P(rows, None),
        P(rows, None, None),
        P(None, "mod"),
        P(),
        P(),
        P(),
        P(),
        P(),
        P(),
        P(),
        P(rows, None, None),
    )
    out_specs = (
        P(rows, None, None),
        P(rows, None, None),
        P(rows, None, None),
        P("dp", "mod"),
        P(rows, None),
        P(),
        P(),
        P(rows, None),
        P(rows, None),
        P(rows, None),
        P(rows, None),
    )
    return jax.shard_map(
        functools.partial(body, mesh.shape["dp"], mesh.shape["mod"]),
        mesh=mesh,
        in_specs=in_specs,
        out_specs=out_specs,
        check_vma=False,
    )
```

```python
import functools

import jax
import jax.numpy as jnp
import numpy as np
from jax import lax
from jax.experimental import pallas as pl
from jax.experimental.pallas import tpu as pltpu
from jax.sharding import PartitionSpec as P

HEADS = 16
HD = 72
GRID = 32
EPS = 1e-06
ROPE_BASE = 10000.0
SEG = 256
TB = 512
WIN = 256
TOGETHER = 4
CHUNKS = 3
SCORE_SCALE = float(HD**-0.5)
SCORE_LOG2 = float(np.log2(np.e) * HD**-0.5)
VMEM = 60 * 2**20
f32 = jnp.float32
bf16 = jnp.bfloat16


def nn(a, b):
    return lax.dot_general(a, b, (((1,), (0,)), ((), ())), preferred_element_type=f32)


def nt(a, b):
    return lax.dot_general(a, b, (((1,), (1,)), ((), ())), preferred_element_type=f32)


def tn(a, b):
    return lax.dot_general(a, b, (((0,), (0,)), ((), ())), preferred_element_type=f32)


def split3(v):
    hi = v.astype(bf16).astype(f32)
    mid = (v - hi).astype(bf16).astype(f32)
    return hi, mid, v - hi - mid


def np_split3(v):
    v = v.astype(np.float32)
    hi = v.astype(jnp.bfloat16).astype(np.float32)
    mid = (v - hi).astype(jnp.bfloat16).astype(np.float32)
    return [part.astype(jnp.bfloat16) for part in (hi, mid, v - hi - mid)]


@functools.lru_cache(None)
def rope_tables(width):
    quarter = HD // 4
    freqs = ROPE_BASE ** (-np.arange(quarter, dtype=np.float64) / quarter)
    lane = np.arange(width) % HD
    group = lane // quarter
    angle = np.arange(GRID)[:, None] * freqs[lane % quarter][None, :]
    cosine, sine = np.cos(angle), np.sin(angle)
    sine = np.where((group % 2 == 0)[None, :], -sine, sine)
    uses_col = (group >= 2)[None, :]
    tables = []
    for table in (cosine, sine):
        whole = np.concatenate(
            [np.where(uses_col, 0.0, table), np.where(uses_col, table, 0.0)], axis=0
        )
        tables.append(np.concatenate(np_split3(whole), axis=0))
    return tables


@functools.lru_cache(None)
def head_tables(width):
    head = np.arange(width) // HD
    gather = np.zeros((width, 128), np.float32)
    for copy in range(3):
        gather[np.arange(width), copy * HEADS + head] = 1.0
    fold = np.zeros((width, 128), np.float32)
    fold[np.arange(width), np.arange(width) % HD] = 1.0
    return gather.astype(jnp.bfloat16), gather.T.astype(jnp.bfloat16), fold.astype(jnp.bfloat16)


def unit_of(index, n_mod):
    mod = index % n_mod
    dp = index // n_mod
    return (dp % 2) * 2 * n_mod + mod * 2 + (dp // 2) % 2, dp // 4


def reversed_bits(value, size):
    result = 0
    for bit in range(size.bit_length() - 1):
        result = 2 * result + (value >> bit) % 2
    return result


@functools.lru_cache(None)
def unit_permutation(width, n_dp, n_mod):
    rows = width // (n_dp * n_mod)
    matrix = np.zeros((width, width), np.float32)
    for index in range(n_dp * n_mod):
        unit, rest = unit_of(index, n_mod)
        start = unit * (width // 8) + reversed_bits(rest, n_dp // 4) * rows
        matrix[start + np.arange(rows), index * rows + np.arange(rows)] = 1.0
    return matrix.astype(jnp.bfloat16)


def normed(v):
    centred = v - jnp.mean(v, axis=-1, keepdims=True)
    inverse = lax.rsqrt(jnp.mean(centred * centred, axis=-1, keepdims=True) + EPS)
    return centred * inverse, inverse


def norm_back(e, norm, inverse):
    return inverse * (
        e - jnp.mean(e, axis=-1, keepdims=True) - norm * jnp.mean(e * norm, axis=-1, keepdims=True)
    )


def part(mod_ref, slot, index, width):
    return mod_ref[pl.ds(slot, 1), index * width : (index + 1) * width]


def slots_here(slots, rows):
    return [slots[pl.program_id(0) * (rows // SEG) + i] for i in range(rows // SEG)]


def by_slot(function, here, *values):
    done = [
        function(slot, *(value[i * SEG : (i + 1) * SEG] for value in values)) for i, slot in enumerate(here)
    ]
    return jnp.concatenate(done, axis=0)


def angles(coords_ref, cos_ref, sin_ref):
    value = lax.broadcasted_iota(jnp.int32, (GRID, 1), 0)
    hot = [(value == coords_ref[i : i + 1, :]).astype(f32) for i in range(2)]
    hot = jnp.concatenate(hot * 3, axis=0).astype(bf16)
    return tn(hot, cos_ref[...]), tn(hot, sin_ref[...])


def partner(v):
    width = v.shape[1]
    quarter = HD // 4
    lane = lax.broadcasted_iota(jnp.int32, (1, width), 1)
    leads = (lane // quarter) % 2 == 0
    return jnp.where(leads, pltpu.roll(v, width - quarter, 1), pltpu.roll(v, quarter, 1))


def head_sum(v, gather_ref):
    hi = v.astype(bf16)
    low = (v - hi.astype(f32)).astype(bf16)
    return nn(hi, gather_ref[...]) + nn(low, gather_ref[...])


def head_spread(v, spread_ref):
    hi, mid, low = split3(v)
    lane = lax.broadcasted_iota(jnp.int32, (1, 128), 1)
    chosen = jnp.where(lane < HEADS, hi, jnp.where(lane < 2 * HEADS, mid, low))
    return nn(chosen.astype(bf16), spread_ref[...])


def window(head, width):
    start = jnp.minimum((head * HD) // 128, width // 128 - WIN // 128) * 128
    return pl.multiple_of(start, 128), head * HD - start


def head_lanes(offset):
    lane = lax.broadcasted_iota(jnp.int32, (1, WIN), 1)
    return (lane >= offset) & (lane < offset + HD)


def product(units_ref, half, rhs, out_ref):
    _, rows, tokens = units_ref.shape
    units = units_ref[pl.ds(4 * half, 4)].reshape(4 * rows, tokens)
    out_ref[...] = nn(units, rhs).astype(bf16).reshape(out_ref.shape)


def halves_out(acc_ref, core, send_ref, own_ref):
    rows = acc_ref.shape[0] // 2
    for half, out_ref in ((1 - core, send_ref), (core, own_ref)):
        start = pl.multiple_of(half * rows, rows)
        out_ref[...] = acc_ref[pl.ds(start, rows)].astype(bf16).reshape(out_ref.shape)


def add_by_slot(sums_ref, here, index, term):
    width = term.shape[1]
    for i, slot in enumerate(here):
        rows = term[i * SEG : (i + 1) * SEG]
        sums_ref[pl.ds(slot, 1), index * width : (index + 1) * width] += jnp.sum(rows, axis=0, keepdims=True)


def project_kernel(
    slots, x_ref, mod_ref, w_ref, coords_ref, cos_ref, sin_ref, gain_ref, gather_ref, spread_ref,
    perm_ref, units_ref, raw_ref, inv_ref, q_ref, k_ref, v_ref, kt_ref,
):
    width = x_ref.shape[1]
    norm, _ = normed(x_ref[...].astype(f32))

    def modulate(slot, rows):
        return (rows * (1.0 + part(mod_ref, slot, 1, width)) + part(mod_ref, slot, 0, width)).astype(bf16)

    low = by_slot(modulate, slots_here(slots, x_ref.shape[0]), norm)
    units_ref[...] = nt(perm_ref[...], low).astype(bf16).reshape(units_ref.shape)
    cosine, sine = angles(coords_ref, cos_ref, sin_ref)
    for index, out_ref in enumerate((q_ref, k_ref)):
        raw = nn(low, w_ref[:, index * width : (index + 1) * width])
        raw_ref[:, index * width : (index + 1) * width] = raw
        inverse = lax.rsqrt(head_sum(raw * raw, gather_ref) * (1.0 / HD) + EPS)
        inv_ref[:, index * 128 : (index + 1) * 128] = inverse
        scaled = raw * head_spread(inverse, spread_ref) * gain_ref[index : index + 1, :]
        turned = scaled * cosine + partner(scaled) * sine
        out_ref[...] = turned.astype(bf16)
        if index == 1:
            kt_ref[...] = turned.T.astype(bf16)
    v_ref[...] = nn(low, w_ref[:, 2 * width :]).astype(bf16)


def attend_kernel(slots, q_ref, k_ref, v_ref, o_ref, lse_ref):
    step = pl.program_id(0)
    tokens, width = q_ref.shape
    lane128 = lax.broadcasted_iota(jnp.int32, (1, 128), 1)
    lane = lax.broadcasted_iota(jnp.int32, (1, WIN), 1)

    @pl.when(step == 0)
    def _():
        o_ref[...] = jnp.zeros_like(o_ref)
        lse_ref[...] = jnp.zeros_like(lse_ref)

    def head(h, rows):
        start, offset = window(h, width)
        inside = head_lanes(offset)
        columns = pl.ds(start, WIN)
        query = jnp.where(inside, q_ref[rows, columns], 0)
        value = jnp.where(inside, v_ref[rows, columns], 1)
        weight = jnp.exp2(nt(query, k_ref[rows, columns]) * SCORE_LOG2).astype(bf16)
        summed = nn(weight, value)
        free = jnp.where(offset > 0, 0, WIN - 1)
        total = jnp.sum(jnp.where(lane == free, summed, 0.0), axis=1, keepdims=True)
        o_ref[rows, columns] += jnp.where(inside, summed * (1.0 / total), 0.0)
        lse_ref[rows, :] += jnp.where(lane128 == h, jnp.log2(total), 0.0)

    whole = slots[tokens // SEG - 1] == slots[0]

    @pl.when(whole)
    def _():
        for i in range(TOGETHER):
            head(step * TOGETHER + i, slice(None))

    @pl.when(jnp.logical_not(whole))
    def _():
        for i in range(TOGETHER):
            for b in range(tokens // SEG):
                head(step * TOGETHER + i, slice(b * SEG, (b + 1) * SEG))


def mix_kernel(
    slots, x_ref, cot_ref, mod_ref, o_ref, lse_ref, w_out_ref, perm_ref,
    attended_ref, lse_out_ref, attn_ref, mid_ref, low_ref, gf_ref, att_units_ref, ffn_units_ref,
):
    width = x_ref.shape[1]
    here = slots_here(slots, x_ref.shape[0])
    lse_out_ref[...] = lse_ref[...].T
    attended = o_ref[...].astype(bf16)
    attended_ref[...] = attended
    att_units_ref[...] = nt(perm_ref[...], attended).astype(bf16).reshape(att_units_ref.shape)
    attn = nn(attended, w_out_ref[...])
    attn_ref[...] = attn.astype(bf16)
    mid = by_slot(
        lambda slot, x, rows: x.astype(f32) + part(mod_ref, slot, 2, width) * rows, here, x_ref[...], attn
    )
    mid_ref[...] = mid
    norm, _ = normed(mid)

    def modulate(slot, rows):
        return (rows * (1.0 + part(mod_ref, slot, 4, width)) + part(mod_ref, slot, 3, width)).astype(bf16)

    low = by_slot(modulate, here, norm)
    low_ref[...] = low
    ffn_units_ref[...] = nt(perm_ref[...], low).astype(bf16).reshape(ffn_units_ref.shape)
    gf_ref[...] = by_slot(
        lambda slot, rows: (rows.astype(f32) * part(mod_ref, slot, 5, width)).astype(bf16), here, cot_ref[...]
    )


def ffn_kernel(
    bits, x_ref, gf_hbm, units_hbm, wg_ref, wu_ref, wd_ref,
    gate_send_ref, gate_own_ref, up_send_ref, up_own_ref, down_send_ref, down_own_ref, ffn_hbm, dmod_hbm,
    turned_ref, gf_ref, units_ref, ffn_ref, dmod_ref, sems, *, n_mod, rows_ff,
):
    core = bits[0]
    first = pl.program_id(0) == 0
    last = pl.program_id(0) == pl.num_programs(0) - 1
    load_gf = pltpu.make_async_copy(gf_hbm, gf_ref, sems.at[0])
    load_units = pltpu.make_async_copy(units_hbm, units_ref, sems.at[1])
    store_ffn = pltpu.make_async_copy(ffn_ref, ffn_hbm, sems.at[2])
    store_dmod = pltpu.make_async_copy(dmod_ref, dmod_hbm, sems.at[3])

    @pl.when(first)
    def _():
        load_gf.start()
        load_units.start()
        ffn_ref[...] = jnp.zeros_like(ffn_ref)
        dmod_ref[...] = jnp.zeros_like(dmod_ref)

    gate = nn(x_ref[...], wg_ref[...])
    up = nn(x_ref[...], wu_ref[...])

    @pl.when(first)
    def _():
        load_gf.wait()
        load_units.wait()

    grad_hidden = nt(gf_ref[...], wd_ref[...])
    sigmoid = 1.0 / (1.0 + jnp.exp(-gate))
    silu = gate * sigmoid
    hidden = (silu * up).astype(bf16)
    turned = hidden.T
    for index in range(turned.shape[0] // rows_ff):
        unit, rest = unit_of(index, n_mod)
        turned_ref[unit, rest * rows_ff : (rest + 1) * rows_ff] = turned[
            index * rows_ff : (index + 1) * rows_ff
        ]
    dg = (grad_hidden * up * (sigmoid * (1.0 + gate * (1.0 - sigmoid)))).astype(bf16)
    du = (grad_hidden * silu).astype(bf16)

    ffn_ref[...] += nn(hidden, wd_ref[...])
    dmod_ref[...] += nt(dg, wg_ref[...]) + nt(du, wu_ref[...])

    @pl.when(last)
    def _():
        store_ffn.start()
        store_dmod.start()

    product(units_ref, 1 - core, dg, gate_send_ref)
    product(units_ref, 1 - core, du, up_send_ref)
    product(turned_ref, 1 - core, gf_ref[...], down_send_ref)
    product(units_ref, core, dg, gate_own_ref)
    product(units_ref, core, du, up_own_ref)
    product(turned_ref, core, gf_ref[...], down_own_ref)

    @pl.when(last)
    def _():
        store_ffn.wait()
        store_dmod.wait()


def middle_kernel(
    slots, mid_ref, ffn_ref, dmod_ref, cot_ref, attn_ref, o_ref, units_ref, mod_ref, w_out_ref, gather_ref,
    out_ref, grad_mid_ref, do_ref, dot_ref, sums_ref, send_ref, own_ref, acc_ref,
):
    width = mid_ref.shape[1]
    block = pl.program_id(0)
    here = slots_here(slots, mid_ref.shape[0])
    segments = pl.num_programs(0) * len(here)
    incoming = cot_ref[...].astype(f32)
    mid = mid_ref[...]
    out_ref[...] = by_slot(
        lambda slot, rows, ffn: (rows + part(mod_ref, slot, 5, width) * ffn).astype(bf16), here, mid, ffn_ref[...]
    )
    norm, inverse = normed(mid)
    dmod = dmod_ref[...]
    scaled = by_slot(lambda slot, rows: rows * (1.0 + part(mod_ref, slot, 4, width)), here, dmod)
    grad_mid = incoming + norm_back(scaled, norm, inverse)
    grad_mid_ref[...] = grad_mid
    ga = by_slot(lambda slot, rows: (rows * part(mod_ref, slot, 2, width)).astype(bf16), here, grad_mid)
    grow = nn(units_ref[...].reshape(width, -1), ga)

    @pl.when(block == 0)
    def _():
        acc_ref[...] = grow

    @pl.when(block > 0)
    def _():
        acc_ref[...] += grow

    @pl.when(block == pl.num_programs(0) - 1)
    def _():
        halves_out(acc_ref, slots[segments], send_ref, own_ref)

    do = nt(ga, w_out_ref[...]).astype(bf16)
    do_ref[...] = do
    dot_ref[...] = head_sum(do.astype(f32) * o_ref[...].astype(f32), gather_ref).T

    @pl.when(block == 0)
    def _():
        sums_ref[...] = jnp.zeros_like(sums_ref)

    for index, term in enumerate((grad_mid * attn_ref[...].astype(f32), dmod, dmod * norm, incoming * ffn_ref[...])):
        add_by_slot(sums_ref, here, index, term)


def attend_back_kernel(
    slots, q_ref, k_ref, v_ref, do_ref, lse_ref, dot_ref, kt_ref, dqt_ref, dk_ref, dv_low_ref, dv_ref,
    *, first, base, base_row, width,
):
    tokens = q_ref.shape[0]

    @pl.when(pl.program_id(0) == 0)
    def _():
        dqt_ref[...] = jnp.zeros_like(dqt_ref)
        dk_ref[...] = jnp.zeros_like(dk_ref)
        dv_ref[...] = jnp.zeros_like(dv_ref)

    def head(h, rows):
        start, offset = window(h, width)
        inside = head_lanes(offset)
        columns = pl.ds(pl.multiple_of(start - base, 128), WIN)
        first_row = pl.multiple_of((h * HD) // 16 * 16, 16)
        own_place = pl.ds(pl.multiple_of(first_row - base_row, 16), HD + 8)
        row = lax.broadcasted_iota(jnp.int32, (HD + 8, 1), 0) + first_row
        own_rows = (row >= h * HD) & (row < h * HD + HD)
        query = q_ref[rows, columns]
        grad_out = do_ref[rows, columns]
        key = jnp.where(inside, k_ref[rows, columns], 0)
        value = jnp.where(inside, v_ref[rows, columns], 0)
        probs = jnp.exp2(nt(key, query) * SCORE_LOG2 - lse_ref[pl.ds(h, 1), rows])
        scores = (probs * (nt(value, grad_out) - dot_ref[pl.ds(h, 1), rows])).astype(bf16)
        dv_ref[rows, columns] += jnp.where(inside, nn(probs.astype(bf16), grad_out), 0.0)
        dk_ref[rows, columns] += jnp.where(inside, nn(scores, query) * SCORE_SCALE, 0.0)
        turned = nn(kt_ref[own_place, rows], scores) * SCORE_SCALE
        dqt_ref[own_place, rows] += jnp.where(own_rows, turned, 0.0)

    whole = slots[tokens // SEG - 1] == slots[0]
    begin = first + pl.program_id(0) * TOGETHER

    @pl.when(whole)
    def _():
        for i in range(TOGETHER):
            head(begin + i, slice(None))

    @pl.when(jnp.logical_not(whole))
    def _():
        for i in range(TOGETHER):
            for b in range(tokens // SEG):
                head(begin + i, slice(b * SEG, (b + 1) * SEG))

    @pl.when(pl.program_id(0) == pl.num_programs(0) - 1)
    def _():
        dv_low_ref[...] = dv_ref[...].astype(bf16)


def head_span(first, end, width):
    begin = lambda head: min(head * HD // 128, width // 128 - WIN // 128) * 128
    return begin(first), begin(end - 1) + WIN, first * HD // 16 * 16, (end - 1) * HD // 16 * 16 + HD + 8


def join_spans(low, high, begin, axis):
    size = low.shape[axis] - begin
    if size == 0:
        return jnp.concatenate([low, high], axis=axis)
    cut = lambda arr, start, stop: lax.slice_in_dim(arr, start, stop, axis=axis)
    middle = cut(low, begin, begin + size) + cut(high, 0, size)
    return jnp.concatenate([cut(low, 0, begin), middle, cut(high, size, high.shape[axis])], axis=axis)


def project_back_kernel(
    bits, dqt0_ref, dqt1_ref, dk0_ref, dk1_ref, raw_ref, inv_ref, q_ref, k_ref, units_ref,
    coords_ref, cos_ref, sin_ref, gain_ref, gather_ref, spread_ref, fold_ref,
    gq_ref, gk_ref, gains_low_ref, q_send_ref, q_own_ref, k_send_ref, k_own_ref, accq_ref, acck_ref, gains_ref,
    *, base, base_row,
):
    width = q_ref.shape[1]
    block = pl.program_id(0)

    @pl.when(block == 0)
    def _():
        gains_ref[...] = jnp.zeros_like(gains_ref)
        accq_ref[...] = jnp.zeros_like(accq_ref)
        acck_ref[...] = jnp.zeros_like(acck_ref)

    cosine, sine = angles(coords_ref, cos_ref, sin_ref)
    parts = ((q_ref, gq_ref, accq_ref), (k_ref, gk_ref, acck_ref))
    for index, (low_ref, out_ref, acc_ref) in enumerate(parts):
        if index == 0:
            grad = join_spans(dqt0_ref[...], dqt1_ref[...], base_row, 0).T
        else:
            grad = join_spans(dk0_ref[...], dk1_ref[...], base, 1)
        raw = raw_ref[:, index * width : (index + 1) * width]
        inverse = head_spread(inv_ref[:, index * 128 : (index + 1) * 128], spread_ref)
        mean = head_sum(grad * low_ref[...].astype(f32), gather_ref) * (1.0 / HD)
        norm = raw * inverse
        back = grad * cosine - partner(grad) * sine
        gains_ref[index : index + 1, :] += jnp.sum(back * norm, axis=0, keepdims=True)
        grad_raw = (
            inverse * (back * gain_ref[index : index + 1, :] - norm * head_spread(mean, spread_ref))
        ).astype(bf16)
        out_ref[...] = grad_raw
        acc_ref[...] += nn(units_ref[...].reshape(width, -1), grad_raw)

    @pl.when(block == pl.num_programs(0) - 1)
    def _():
        halves_out(accq_ref, bits[0], q_send_ref, q_own_ref)
        halves_out(acck_ref, bits[0], k_send_ref, k_own_ref)
        terms = split3(gains_ref[...])
        sums = sum(nn(term.astype(bf16), fold_ref[...]) for term in terms)
        high = sums.astype(bf16).astype(f32)
        row = lax.broadcasted_iota(jnp.int32, (8, 1), 0)
        mine = 4 * bits[1]
        placed = jnp.zeros((8, 128), f32)
        for index, term in enumerate((high[0:1], (sums - high)[0:1], high[1:2], (sums - high)[1:2])):
            placed = jnp.where(row == mine + index, term, placed)
        gains_low_ref[...] = placed.astype(bf16)


def input_back_kernel(
    slots, gq_ref, gk_ref, dv0_ref, dv1_ref, x_ref, grad_mid_ref, mod_ref, w_ref, other_sums_ref, gains_ref,
    grad_x_ref, grad_own_ref, grad_other_ref, sums_ref, *, base,
):
    width = x_ref.shape[1]
    block = pl.program_id(0)
    here = slots_here(slots, x_ref.shape[0])
    last_block = pl.num_programs(0) - 1
    segments = pl.num_programs(0) * len(here)
    dmod = nt(gq_ref[...], w_ref[:, :width]) + nt(gk_ref[...], w_ref[:, width : 2 * width])
    dmod = dmod + nt(join_spans(dv0_ref[...], dv1_ref[...], base, 1), w_ref[:, 2 * width :])
    norm, inverse = normed(x_ref[...].astype(f32))
    scaled = by_slot(lambda slot, rows: rows * (1.0 + part(mod_ref, slot, 1, width)), here, dmod)
    grad_x = grad_mid_ref[...] + norm_back(scaled, norm, inverse)
    grad_x_ref[...] = grad_x.astype(bf16)

    @pl.when(block == 0)
    def _():
        sums_ref[...] = jnp.zeros_like(sums_ref)

    for index, term in enumerate((dmod, dmod * norm)):
        add_by_slot(sums_ref, here, index, term)

    @pl.when(block == last_block)
    def _():
        mod = slots[segments + 1]
        count = sums_ref.shape[0]
        half = 3 * width
        mine = jnp.concatenate([sums_ref[...]] * 2, axis=0)
        rest = jnp.concatenate([other_sums_ref[...]] * 2, axis=0)
        row = lax.broadcasted_iota(jnp.int32, (2 * count, 1), 0) // count
        attn_part = jnp.where(row == mod, jnp.concatenate([mine, rest[:, :width]], axis=1), 0.0)
        ffn_part = jnp.where(row == mod, rest[:, width:], 0.0)
        grad_own_ref[:, :half] = jnp.where(mod == 0, attn_part, ffn_part).astype(bf16)
        grad_other_ref[:, :half] = jnp.where(mod == 0, ffn_part, attn_part).astype(bf16)
        grad_own_ref[:, half:] = gains_ref[...]
        grad_other_ref[:, half:] = gains_ref[...]


def value_kernel(bits, units_ref, dv0_ref, dv1_ref, send_ref, own_ref, *, base):
    rhs = join_spans(dv0_ref[...], dv1_ref[...], base, 1)
    product(units_ref, 1 - bits[0], rhs, send_ref)
    product(units_ref, bits[0], rhs, own_ref)


def split_step(bits, ins, outs, *, lead, at, bit, pair_rows, cuts):
    send_ref, keep_ref = outs
    mine = bits[bit]
    start = 0
    for own_ref, got_ref, cut in zip(ins[::2], ins[1::2], cuts):
        columns, target = slice(None), slice(None)
        if cut:
            columns, target = slice(*cut), slice(start, start + cut[1] - cut[0])
            start = target.stop

        def total(*index):
            place = index + (slice(None), columns)
            return own_ref[place].astype(f32) + got_ref[place].astype(f32)

        if at is None:
            for j in range(max(lead, 1)):
                index = (j,) if lead else ()
                value = total(*index)
                rows = pair_rows or value.shape[0] // 2
                for p in range(value.shape[0] // (2 * rows)):
                    first = value[2 * p * rows : (2 * p + 1) * rows]
                    second = value[(2 * p + 1) * rows : (2 * p + 2) * rows]
                    place = index + (slice(p * rows, (p + 1) * rows), target)
                    send_ref[place] = jnp.where(mine == 1, first, second).astype(bf16)
                    keep_ref[place] = jnp.where(mine == 1, second, first).astype(keep_ref.dtype)
            continue
        for j in range(lead // 2):
            place = ((j,) if lead > 2 else ()) + (slice(None), target)
            away = 1 - mine if lead == 2 else 2 * (1 - mine) + j if at == 0 else 2 * j + 1 - mine
            own = mine if lead == 2 else 2 * mine + j if at == 0 else 2 * j + mine
            send_ref[place] = total(away).astype(bf16)
            keep_ref[place] = total(own).astype(keep_ref.dtype)


def merge_step(bits, ins, outs, *, bit, parts):
    send_ref, keep_ref = outs
    start = 0
    for own_ref, got_ref, pieces in zip(ins[::2], ins[1::2], parts):
        value = own_ref[...].astype(f32) + got_ref[...].astype(f32)
        rows, columns = value.shape[0] // 2, value.shape[1]
        first, second = value[:rows], value[rows:]
        sent = jnp.where(bits[bit] == 1, first, second).astype(bf16)
        kept = jnp.where(bits[bit] == 1, second, first)
        for i in range(pieces):
            place = slice(start, start + columns)
            if pieces > 1:
                send_ref[:, place] = jnp.zeros_like(send_ref[:, place])
                keep_ref[:, place] = jnp.zeros_like(keep_ref[:, place])
            taken = slice(i * rows // pieces, (i + 1) * rows // pieces)
            send_ref[: rows // pieces, place] = sent[taken]
            keep_ref[: rows // pieces, place] = kept[taken]
            start += columns


def apart_step(bits, ins, outs, *, places):
    own_ref, got_ref = ins
    for out, at, start, stop, rows in places:
        value = own_ref[:, start:stop] + got_ref[:, start:stop].astype(f32)
        if rows is None:
            outs[out][:, at : at + stop - start] = value
        else:
            count = rows[1] - rows[0]
            outs[out][rows[0] : rows[1], :] = value[:count]


def pair_step(bits, ins, outs):
    own_ref, got_ref, activated_ref = ins
    width = activated_ref.shape[1]
    outs[0][:, :width] = activated_ref[...]
    outs[0][:, width:] = (own_ref[...].astype(f32) + got_ref[...].astype(f32)).astype(bf16)


def joined(ins):
    return jnp.concatenate([ref[...].astype(f32) for ref in ins], axis=0).astype(bf16)


def join_step(bits, ins, outs):
    outs[0][...] = joined(ins)


def last_step(bits, ins, outs):
    outs[0][...] = ins[0][...] + ins[1][...].astype(f32)


def ada_step(bits, ins, outs, *, width):
    rows = outs[0].shape[0]
    every = joined(ins)
    position = bits[0] + sum(bits[1 + k] * 2**k for k in range(1, (width // rows).bit_length() - 1))
    feature = lax.broadcasted_iota(jnp.int32, (width, 128), 0)
    place = lax.broadcasted_iota(jnp.int32, (width, 128), 1)
    chosen = (feature == position * rows + place) & (place < rows)
    own = nn(every[:, :width], chosen.astype(f32).astype(bf16)).astype(bf16)
    half = outs[0].shape[1]
    outs[0][...] = tn(own, every[:, width : width + half])[:rows]
    terms = every[:, width + half :].astype(f32)
    kind = lax.broadcasted_iota(jnp.int32, (terms.shape[0], 1), 0) // 2 % 2
    for index in range(2):
        outs[1][index : index + 1, :] = jnp.sum(jnp.where(kind == index, terms, 0.0), axis=0, keepdims=True)


def step_kernel(bits, *refs, plans):
    n_in = sum(plan[1] for plan in plans)
    ins, outs = refs[:n_in], refs[n_in:]
    for function, takes, gives in plans:
        function(bits, ins[:takes], outs[:gives])
        ins, outs = ins[takes:], outs[gives:]


class Chain:
    def __init__(self):
        self.last = None

    def __call__(
        self, kernel, grid, in_specs, out_specs, out_shape, args, scalars=None, scratch=(), name=None, aliases=None
    ):
        ahead = 0 if scalars is None else 1
        body = kernel
        token = ()
        if self.last is not None:
            token = (self.last,)
            in_specs = [pl.BlockSpec(memory_space=pl.ANY)] + list(in_specs)

            def body(*refs):
                kernel(*refs[:ahead], *refs[ahead + 1 :])

        spec = pltpu.PrefetchScalarGridSpec(
            num_scalar_prefetch=ahead,
            grid=grid,
            in_specs=in_specs,
            out_specs=out_specs,
            scratch_shapes=scratch,
        )
        outs = pl.pallas_call(
            body,
            grid_spec=spec,
            input_output_aliases=aliases or {},
            out_shape=out_shape,
            compiler_params=pltpu.CompilerParams(vmem_limit_bytes=VMEM),
            cost_estimate=pl.CostEstimate(flops=1, bytes_accessed=1, transcendentals=0),
            name=name,
        )(*(() if scalars is None else (scalars,)), *token, *args)
        self.last = outs[0]
        return outs


def shape(dims, dtype):
    return jax.ShapeDtypeStruct(dims, dtype)


def fixed(dims):
    return pl.BlockSpec(dims, lambda *_: (0,) * len(dims), pipeline_mode=pl.Buffered(1))


def rows_of(dims, axis=0):
    return pl.BlockSpec(dims, lambda b, *_: tuple(b if i == axis else 0 for i in range(len(dims))))


def whole(dims):
    return rows_of(dims, None)


def column_parts(dims, steps):
    return rows_of(dims[:-1] + (dims[-1] // steps,), len(dims) - 1)


class Reducer:
    def __init__(self, n_dp, n_mod, call):
        self.n_dp, self.n_mod, self.call = n_dp, n_mod, call
        self.position = lax.axis_index("dp")
        steps = range(n_dp.bit_length() - 1)
        dp_bits = [lax.shift_right_logical(self.position, step) & 1 for step in steps]
        self.bits = jnp.stack([dp_bits[0], lax.axis_index("mod")] + dp_bits[1:]).astype(jnp.int32)

    def swap(self, arr, bit):
        if bit == "mod":
            return lax.ppermute(arr, "mod", [(i, i ^ 1) for i in range(self.n_mod)])
        return lax.ppermute(arr, "dp", [(i, i ^ (1 << bit)) for i in range(self.n_dp)])

    def bit_of(self, bit):
        return 1 if bit == "mod" else bit + 1 if bit else 0

    def fold(self, streams, name, last=False):
        plans, args, outs = [], [], []
        for stream in streams:
            function, shapes = stream.last_plan() if last else stream.plan()
            inputs = stream.inputs()
            plans.append((function, len(inputs), len(shapes)))
            args += inputs
            outs += shapes
        size = sum(arg.size for arg in args)
        split = all(
            isinstance(stream, Stream) and stream.own.shape[-1] % (CHUNKS * 128) == 0 for stream in streams
        )
        steps = CHUNKS if split and size > 2**20 else 1
        results = self.call(
            functools.partial(step_kernel, plans=plans),
            (steps,),
            [column_parts(arg.shape, steps) for arg in args],
            [column_parts(out.shape, steps) for out in outs],
            outs,
            args,
            scalars=self.bits,
            name=name,
        )
        results = list(results)
        if last:
            return results
        for stream, plan in zip(streams, plans):
            stream.step(results[: plan[2]])
            results = results[plan[2] :]

    def pass_on(self, arrays):
        anywhere = [pl.BlockSpec(memory_space=pl.ANY)] * len(arrays)
        return self.call(
            lambda *refs: None,
            (1,),
            anywhere,
            anywhere,
            [shape(arr.shape, arr.dtype) for arr in arrays],
            arrays,
            name="pass_on",
            aliases={i + 1: i for i in range(len(arrays))},
        )


class Stream:
    def __init__(self, reducer, sent, own, first, pair_rows=None):
        self.r, self.own, self.pair_rows = reducer, own, pair_rows
        order = ["mod", 1, 2]
        self.steps = order[first:] + order[:first] + list(range(3, reducer.n_dp.bit_length() - 1))
        self.lead = ["mod", 1]
        self.side = None
        self.got = reducer.swap(sent, 0)

    def inputs(self):
        return [self.own, self.got] + ([self.side[0].own, self.side[0].got] if self.side else [])

    def plan(self):
        bit = self.steps[0]
        dims = self.own.shape
        at = self.lead.index(bit) if bit in self.lead else None
        cuts = [None]
        if self.side is not None:
            cut = self.side[1]
            cuts = [(0, dims[-1] // CHUNKS), cut]
            dims = dims[:-1] + (dims[-1] + CHUNKS * (cut[1] - cut[0]),)
        function = functools.partial(
            split_step, lead=dims[0] if self.lead else 0, at=at, bit=self.r.bit_of(bit), pair_rows=self.pair_rows,
            cuts=cuts,
        )
        if at is None:
            dims = dims[:-2] + (dims[-2] // 2, dims[-1])
        else:
            dims = dims[1:] if len(self.lead) == 1 else (2,) + dims[1:]
        return function, [shape(dims, bf16), shape(dims, bf16 if len(self.lead) == 2 else f32)]

    def step(self, results):
        bit = self.steps.pop(0)
        if bit in self.lead:
            self.lead.remove(bit)
        self.side = None
        sent, self.own = results
        self.got = self.r.swap(sent, bit)

    def join(self, stream, cut):
        self.side = (stream, cut)


class Merged:
    def __init__(self, streams):
        self.streams, self.r, self.bit = streams, streams[0].r, streams[0].steps[0]
        self.own = self.places = self.shapes = None

    def inputs(self):
        if self.own is not None:
            return [self.own, self.got]
        return [arr for stream in self.streams for arr in (stream.own, stream.got)]

    def plan(self):
        parts = [3 if stream.pair_rows else 1 for stream in self.streams]
        columns = sum(pieces * stream.own.shape[1] for pieces, stream in zip(parts, self.streams))
        dims = (self.streams[0].own.shape[0] // 2, columns)
        function = functools.partial(merge_step, bit=self.r.bit_of(self.bit), parts=parts)
        return function, [shape(dims, bf16), shape(dims, f32)]

    def step(self, results):
        sent, self.own = results
        self.got = self.r.swap(sent, self.bit)

    def last_plan(self):
        if self.places is None:
            return last_step, [shape(self.own.shape, f32)]
        return functools.partial(apart_step, places=self.places), self.shapes


class Gather:
    def __init__(self, reducer, sent, own, activated):
        self.r, self.own, self.activated = reducer, own, activated
        self.steps = [1] + list(range(reducer.n_dp.bit_length() - 2, 1, -1)) + [0]
        self.got = reducer.swap(sent, "mod")
        self.pair = None

    def inputs(self):
        return [self.own, self.got] + ([self.activated] if self.pair is None else [])

    def plan(self):
        rows, columns = self.own.shape
        if self.pair is None:
            return pair_step, [shape((rows, columns + self.activated.shape[1]), bf16)]
        return join_step, [shape((2 * rows, columns), bf16)]

    def step(self, results):
        (self.own,) = results
        if self.pair is None:
            self.pair = self.own
        self.got = self.r.swap(self.own, self.steps.pop(0))

    def last_plan(self):
        width = self.activated.shape[1]
        function = functools.partial(ada_step, width=width)
        dims = (width // self.r.n_dp, self.own.shape[1] - width - 128)
        return function, [shape(dims, f32), shape((2, 128), f32)]


def silu_grad(v):
    sigmoid = jax.nn.sigmoid(v)
    return sigmoid * (1.0 + v * (1.0 - sigmoid))


def pair_order(own, other, mod):
    return jnp.where(mod == 0, jnp.stack([own, other]), jnp.stack([other, own]))


def body(
    n_dp, n_mod, tokens, cond, segments, coords, w_ada, w_qkv, q_gain, k_gain, w_out, w_gate, w_up,
    w_down, cotangent,
):
    _, count, width = tokens.shape
    slots_n = cond.shape[1]
    half = w_ada.shape[1]
    ff = w_gate.shape[1]
    blocks = count // TB
    n_dev = n_dp * n_mod
    call = Chain()
    reducer = Reducer(n_dp, n_mod, call)
    mod_index = lax.axis_index("mod")
    x = tokens[0]
    cot = cotangent[0]
    slots = segments[0, ::SEG]
    coord = coords[0]
    cos_table, sin_table = (jnp.asarray(t) for t in rope_tables(width))
    gather, spread, head_fold = (jnp.asarray(t) for t in head_tables(width))
    perm = jnp.asarray(unit_permutation(width, n_dp, n_mod))
    gains = jnp.stack([jnp.tile(q_gain, HEADS), jnp.tile(k_gain, HEADS)])

    cond_both = pair_order(cond[0], reducer.swap(cond[0], "mod"), mod_index)
    activated = jax.nn.silu(cond_both).astype(bf16).reshape(-1, width)
    mod_half = jnp.dot(activated, w_ada, preferred_element_type=f32).astype(bf16)
    mod_half = mod_half.reshape(n_mod, slots_n, half)
    own_half = lax.dynamic_index_in_dim(mod_half, mod_index, 0, keepdims=False)
    other_half = lax.dynamic_index_in_dim(mod_half, 1 - mod_index, 0, keepdims=False)
    pair = pair_order(own_half, reducer.swap(other_half, "mod"), mod_index)
    modulation = jnp.concatenate([pair[0], pair[1]], axis=1).astype(f32)

    anywhere = pl.BlockSpec(memory_space=pl.ANY)
    token_f32 = shape((count, width), f32)
    token_bf16 = shape((count, width), bf16)
    units = shape((8, width // 8, count), bf16)
    units_spec = rows_of((8, width // 8, TB), 2)
    token_spec = rows_of((TB, width))
    mod_spec = fixed((slots_n, 6 * width))
    square = fixed((width, width))
    table_specs = [fixed(cos_table.shape), fixed(sin_table.shape), fixed((2, width)), fixed(gather.shape), fixed(spread.shape)]
    tables = (cos_table, sin_table, gains, gather, spread)
    lane_rows = shape((128, count), f32)
    macs = count * width * width

    attn_units, raw, inverse, query, key, value, key_t = call(
        project_kernel,
        (blocks,),
        [token_spec, mod_spec, fixed((width, 3 * width)), rows_of((2, TB), 1)] + table_specs + [square],
        [units_spec, rows_of((TB, 2 * width)), rows_of((TB, 256))] + [token_spec] * 3 + [rows_of((width, TB), 1)],
        [units, shape((count, 2 * width), f32), shape((count, 256), f32)] + [token_bf16] * 3
        + [shape((width, count), bf16)],
        (x, modulation, w_qkv, coord) + tables + (perm,),
        scalars=slots,
        name="project",
    )
    attended, lse_columns = call(
        attend_kernel,
        (HEADS // TOGETHER,),
        [fixed((count, width))] * 3,
        [fixed((count, width)), fixed((count, 128))],
        [token_f32, shape((count, 128), f32)],
        (query, key, value),
        scalars=slots,
        name="attend",
    )
    attended, lse, attn, mid, ffn_in, grad_ffn, out_units, ffn_units = call(
        mix_kernel,
        (blocks,),
        [token_spec, token_spec, mod_spec, token_spec, rows_of((TB, 128)), square, square],
        [token_spec, rows_of((128, TB), 1)] + [token_spec] * 4 + [units_spec] * 2,
        [token_bf16, lane_rows, token_bf16, token_f32, token_bf16, token_bf16, units, units],
        (x, cot, modulation, attended, lse_columns, w_out, perm),
        scalars=slots,
        name="mix",
    )

    rows_ff = ff // n_dev
    chunk = 768
    piece = chunk // 8
    half_units = lambda rows, columns: shape((4, rows, columns), bf16)
    square_send = [fixed((4, width // 8, width))] * 2
    square_shapes = [half_units(width // 8, width)] * 2
    gate_send, gate_own, up_send, up_own, down_send, down_own, ffn, grad_mod_ffn = call(
        functools.partial(ffn_kernel, n_mod=n_mod, rows_ff=rows_ff),
        (ff // chunk,),
        [fixed((count, width)), anywhere, anywhere]
        + [rows_of((width, chunk), 1)] * 2 + [rows_of((chunk, width))],
        [rows_of((4, width // 8, chunk), 2)] * 4
        + [rows_of((4, 1, piece, width), 1)] * 2 + [anywhere] * 2,
        [half_units(width // 8, ff)] * 4
        + [shape((4, ff // chunk, piece, width), bf16)] * 2 + [token_f32] * 2,
        (ffn_in, grad_ffn, ffn_units, w_gate, w_up, w_down),
        scalars=reducer.bits,
        scratch=[
            pltpu.VMEM((8, piece, count), bf16),
            pltpu.VMEM((count, width), bf16),
            pltpu.VMEM(units.shape, bf16),
            pltpu.VMEM((count, width), f32),
            pltpu.VMEM((count, width), f32),
            pltpu.SemaphoreType.DMA((4,)),
        ],
        name="ffn",
    )
    gate = Stream(reducer, gate_send, gate_own, 0)
    up = Stream(reducer, up_send, up_own, 1)
    down = Stream(
        reducer, down_send.reshape(4, ff // 8, width), down_own.reshape(4, ff // 8, width), 2, rows_ff
    )

    slots_core = jnp.concatenate([slots, reducer.bits[:2]])
    seg_spec = rows_of((SEG, width))
    output, grad_mid, grad_attended, dot_term, sums_b, out_send, out_own = call(
        middle_kernel,
        (blocks,),
        [token_spec] * 6 + [units_spec, mod_spec, square, fixed(gather.shape)],
        [token_spec] * 3 + [rows_of((128, TB), 1), fixed((slots_n, 4 * width))] + square_send,
        [token_bf16, token_f32, token_bf16, lane_rows, shape((slots_n, 4 * width), f32)] + square_shapes,
        (mid, ffn, grad_mod_ffn, cot, attn, attended, out_units, modulation, w_out, gather),
        scalars=slots_core,
        scratch=[pltpu.VMEM((width, width), f32)],
        name="middle",
    )
    out = Stream(reducer, out_send, out_own, 1)
    early = [gate, up, down]
    out_chunk = width // CHUNKS
    gate.join(out, (0, 128))
    up.join(out, (128, out_chunk))
    reducer.fold(early, "early")

    def attend_back(first, end, name):
        begin, stop, begin_row, stop_row = head_span(first, end, width)
        columns, rows = stop - begin, stop_row - begin_row
        used = pl.BlockSpec((count, columns), lambda *_: (0, begin // columns), pipeline_mode=pl.Buffered(1))
        used_rows = pl.BlockSpec((rows, count), lambda *_: (begin_row // rows, 0), pipeline_mode=pl.Buffered(1))
        return call(
            functools.partial(attend_back_kernel, first=first, base=begin, base_row=begin_row, width=width),
            ((end - first) // TOGETHER,),
            [used] * 4 + [fixed((128, count))] * 2 + [used_rows],
            [fixed((rows, count))] + [fixed((count, columns))] * 2,
            [shape((rows, count), f32), shape((count, columns), f32), shape((count, columns), bf16)],
            (query, key, value, grad_attended, lse, dot_term, key_t),
            scratch=[pltpu.VMEM((count, columns), f32)],
            scalars=slots,
            name=name,
        )

    cut = 3 * HEADS // 4
    dqt0, dk0, dv0 = attend_back(0, cut, "attend_back_0")
    reducer.fold(early, "early")
    dqt1, dk1, dv1 = attend_back(cut, HEADS, "attend_back_1")
    base, _, base_row, _ = head_span(cut, HEADS, width)
    v_send, v_own = call(
        functools.partial(value_kernel, base=base),
        (1,),
        [whole(units.shape), whole(dv0.shape), whole(dv1.shape)],
        [whole((4, width // 8, width))] * 2,
        square_shapes,
        (attn_units, dv0, dv1),
        scalars=reducer.bits,
        name="value",
    )
    v_part = Stream(reducer, v_send, v_own, 2)
    reducer.fold(early, "early")
    grad_q, grad_k, gains_low, q_send, q_own, k_send, k_own = call(
        functools.partial(project_back_kernel, base=base, base_row=base_row),
        (count // SEG,),
        [rows_of((dqt0.shape[0], SEG), 1), rows_of((dqt1.shape[0], SEG), 1)]
        + [rows_of((SEG, dk0.shape[1])), rows_of((SEG, dk1.shape[1]))]
        + [rows_of((SEG, 2 * width)), rows_of((SEG, 256)), seg_spec, seg_spec, rows_of((8, width // 8, SEG), 2), rows_of((2, SEG), 1)]
        + table_specs + [fixed(head_fold.shape)],
        [seg_spec] * 2 + [fixed((8, 128))] + square_send * 2,
        [token_bf16] * 2 + [shape((8, 128), bf16)] + square_shapes * 2,
        (dqt0, dqt1, dk0, dk1, raw, inverse, query, key, attn_units, coord) + tables + (head_fold,),
        scalars=reducer.bits,
        scratch=[pltpu.VMEM((width, width), f32)] * 2 + [pltpu.VMEM((2, width), f32)],
        name="project_back",
    )
    waiting = early + [v_part]
    *arrived, q_send, k_send = reducer.pass_on([stream.got for stream in waiting] + [q_send, k_send])
    for stream, got in zip(waiting, arrived):
        stream.got = got
    q_part = Stream(reducer, q_send, q_own, 1)
    k_part = Stream(reducer, k_send, k_own, 0)
    late = [q_part, k_part, v_part]
    extra = n_dp.bit_length() - 5
    reducer.fold([v_part], "v")
    reducer.fold([q_part, k_part], "late")
    for _ in range(extra):
        reducer.fold(early, "early")
    rows_d = width // n_dev
    merged = Merged([gate, up, down])
    third = rows_ff // 3
    ff_chunk = ff // CHUNKS
    gate_end = ff + CHUNKS * 128
    up_end = gate_end + ff + width - CHUNKS * 128
    merged.places = [
        (3, 0, up_end + i * width, up_end + (i + 1) * width, (i * third, (i + 1) * third)) for i in range(3)
    ]
    for j in range(CHUNKS):
        at = j * (gate_end // CHUNKS)
        merged.places.append((0, j * ff_chunk, at, at + ff_chunk, None))
        merged.places.append((2, j * out_chunk, at + ff_chunk, at + ff_chunk + 128, None))
        at = gate_end + j * ((up_end - gate_end) // CHUNKS)
        merged.places.append((1, j * ff_chunk, at, at + ff_chunk, None))
        merged.places.append((2, j * out_chunk + 128, at + ff_chunk, at + ff_chunk + out_chunk - 128, None))
    merged.shapes = [shape((rows_d, ff), f32)] * 2 + [shape((rows_d, width), f32), shape((rows_ff, width), f32)]
    early = [merged]
    reducer.fold(early, "early")

    grad_tokens, mod_own, mod_other = call(
        functools.partial(input_back_kernel, base=base),
        (blocks,),
        [token_spec] * 2 + [rows_of((TB, dv0.shape[1])), rows_of((TB, dv1.shape[1]))] + [token_spec] * 2
        + [mod_spec, fixed((width, 3 * width)), fixed((slots_n, 4 * width)), fixed((8, 128))],
        [token_spec] + [fixed((2 * slots_n, half + 128))] * 2,
        [token_bf16] + [shape((2 * slots_n, half + 128), bf16)] * 2,
        (grad_q, grad_k, dv0, dv1, x, grad_mid, modulation, w_qkv, sums_b, gains_low),
        scalars=slots_core,
        scratch=[pltpu.VMEM((slots_n, 2 * width), f32)],
        name="input_back",
    )
    every_mod = Gather(reducer, mod_other, mod_own, activated)
    reducer.fold([v_part], "v")
    reducer.fold([every_mod], "pair")
    reducer.fold([q_part], "q")
    reducer.fold([every_mod], "every")
    reducer.fold([k_part], "k")
    summed_gate, summed_up, summed_out, summed_down = reducer.fold(early, "early_last", last=True)
    for _ in range(1 + extra):
        reducer.fold(late + [every_mod], "late")
    late = [Merged(late)]
    reducer.fold(late + [every_mod], "late")
    summed_qkv, grad_w_ada, gain_grads = reducer.fold(late + [every_mod], "late_last", last=True)

    grad_activated = jnp.einsum("nc,dc->nd", every_mod.pair[:, width : width + half], w_ada, preferred_element_type=f32)
    grad_activated = grad_activated.reshape(n_mod, slots_n, width)
    own_part = lax.dynamic_index_in_dim(grad_activated, mod_index, 0, keepdims=False)
    other_part = lax.dynamic_index_in_dim(grad_activated, 1 - mod_index, 0, keepdims=False)
    grad_own = own_part + reducer.swap(other_part.astype(bf16), "mod").astype(f32)
    grad_cond = grad_own[None] * silu_grad(cond)
    return (
        output[None],
        grad_tokens[None],
        grad_cond,
        grad_w_ada,
        summed_qkv,
        gain_grads[0, :HD],
        gain_grads[1, :HD],
        summed_out,
        summed_gate,
        summed_up,
        summed_down,
    )


def solution(mesh):
    rows = ("dp", "mod")
    in_specs = (
        P(rows, None, None),
        P(rows, None, None),
        P(rows, None),
        P(rows, None, None),
        P(None, "mod"),
        P(),
        P(),
        P(),
        P(),
        P(),
        P(),
        P(),
        P(rows, None, None),
    )
    out_specs = (
        P(rows, None, None),
        P(rows, None, None),
        P(rows, None, None),
        P("dp", "mod"),
        P(rows, None),
        P(),
        P(),
        P(rows, None),
        P(rows, None),
        P(rows, None),
        P(rows, None),
    )
    return jax.shard_map(
        functools.partial(body, mesh.shape["dp"], mesh.shape["mod"]),
        mesh=mesh,
        in_specs=in_specs,
        out_specs=out_specs,
        check_vma=False,
    )
```

```python
import functools

import jax
import jax.numpy as jnp
import numpy as np
from jax import lax
from jax.experimental import pallas as pl
from jax.experimental.pallas import tpu as pltpu
from jax.sharding import PartitionSpec as P

HEADS = 16
HD = 72
GRID = 32
EPS = 1e-06
ROPE_BASE = 10000.0
SEG = 256
TB = 512
WIN = 256
TOGETHER = 4
FIRST = 384
SCORE_SCALE = float(HD**-0.5)
SCORE_LOG2 = float(np.log2(np.e) * HD**-0.5)
VMEM = 60 * 2**20
f32 = jnp.float32
bf16 = jnp.bfloat16


def nn(a, b):
    return lax.dot_general(a, b, (((1,), (0,)), ((), ())), preferred_element_type=f32)


def nt(a, b):
    return lax.dot_general(a, b, (((1,), (1,)), ((), ())), preferred_element_type=f32)


def tn(a, b):
    return lax.dot_general(a, b, (((0,), (0,)), ((), ())), preferred_element_type=f32)


def split3(v):
    hi = v.astype(bf16).astype(f32)
    mid = (v - hi).astype(bf16).astype(f32)
    return hi, mid, v - hi - mid


def np_split3(v):
    v = v.astype(np.float32)
    hi = v.astype(jnp.bfloat16).astype(np.float32)
    mid = (v - hi).astype(jnp.bfloat16).astype(np.float32)
    return [part.astype(jnp.bfloat16) for part in (hi, mid, v - hi - mid)]


@functools.lru_cache(None)
def rope_tables(width):
    quarter = HD // 4
    freqs = ROPE_BASE ** (-np.arange(quarter, dtype=np.float64) / quarter)
    lane = np.arange(width) % HD
    group = lane // quarter
    angle = np.arange(GRID)[:, None] * freqs[lane % quarter][None, :]
    cosine, sine = np.cos(angle), np.sin(angle)
    sine = np.where((group % 2 == 0)[None, :], -sine, sine)
    uses_col = (group >= 2)[None, :]
    tables = []
    for table in (cosine, sine):
        whole = np.concatenate(
            [np.where(uses_col, 0.0, table), np.where(uses_col, table, 0.0)], axis=0
        )
        tables.append(np.concatenate(np_split3(whole), axis=0))
    return tables


@functools.lru_cache(None)
def head_tables(width):
    head = np.arange(width) // HD
    gather = np.zeros((width, 128), np.float32)
    for copy in range(3):
        gather[np.arange(width), copy * HEADS + head] = 1.0
    fold = np.zeros((width, 128), np.float32)
    fold[np.arange(width), np.arange(width) % HD] = 1.0
    return gather.astype(jnp.bfloat16), gather.T.astype(jnp.bfloat16), fold.astype(jnp.bfloat16)


def unit_of(index, n_mod):
    mod = index % n_mod
    dp = index // n_mod
    return (dp % 2) * 2 * n_mod + mod * 2 + (dp // 2) % 2, dp // 4


def reversed_bits(value, size):
    result = 0
    for bit in range(size.bit_length() - 1):
        result = 2 * result + (value >> bit) % 2
    return result


@functools.lru_cache(None)
def unit_permutation(width, n_dp, n_mod):
    rows = width // (n_dp * n_mod)
    matrix = np.zeros((width, width), np.float32)
    for index in range(n_dp * n_mod):
        unit, rest = unit_of(index, n_mod)
        start = unit * (width // 8) + reversed_bits(rest, n_dp // 4) * rows
        matrix[start + np.arange(rows), index * rows + np.arange(rows)] = 1.0
    return matrix.astype(jnp.bfloat16)


def normed(v):
    centred = v - jnp.mean(v, axis=-1, keepdims=True)
    inverse = lax.rsqrt(jnp.mean(centred * centred, axis=-1, keepdims=True) + EPS)
    return centred * inverse, inverse


def norm_back(e, norm, inverse):
    return inverse * (
        e - jnp.mean(e, axis=-1, keepdims=True) - norm * jnp.mean(e * norm, axis=-1, keepdims=True)
    )


def part(mod_ref, slot, index, width):
    return mod_ref[pl.ds(slot, 1), index * width : (index + 1) * width]


def slots_here(slots, rows):
    return [slots[pl.program_id(0) * (rows // SEG) + i] for i in range(rows // SEG)]


def by_slot(function, here, *values):
    done = [
        function(slot, *(value[i * SEG : (i + 1) * SEG] for value in values)) for i, slot in enumerate(here)
    ]
    return jnp.concatenate(done, axis=0)


def angles(coords_ref, cos_ref, sin_ref):
    value = lax.broadcasted_iota(jnp.int32, (GRID, 1), 0)
    hot = [(value == coords_ref[i : i + 1, :]).astype(f32) for i in range(2)]
    hot = jnp.concatenate(hot * 3, axis=0).astype(bf16)
    return tn(hot, cos_ref[...]), tn(hot, sin_ref[...])


def partner(v):
    width = v.shape[1]
    quarter = HD // 4
    lane = lax.broadcasted_iota(jnp.int32, (1, width), 1)
    leads = (lane // quarter) % 2 == 0
    return jnp.where(leads, pltpu.roll(v, width - quarter, 1), pltpu.roll(v, quarter, 1))


def head_sum(v, gather_ref):
    hi = v.astype(bf16)
    low = (v - hi.astype(f32)).astype(bf16)
    return nn(hi, gather_ref[...]) + nn(low, gather_ref[...])


def head_spread(v, spread_ref):
    hi, mid, low = split3(v)
    lane = lax.broadcasted_iota(jnp.int32, (1, 128), 1)
    chosen = jnp.where(lane < HEADS, hi, jnp.where(lane < 2 * HEADS, mid, low))
    return nn(chosen.astype(bf16), spread_ref[...])


def window(head, width):
    start = jnp.minimum((head * HD) // 128, width // 128 - WIN // 128) * 128
    return pl.multiple_of(start, 128), head * HD - start


def head_lanes(offset):
    lane = lax.broadcasted_iota(jnp.int32, (1, WIN), 1)
    return (lane >= offset) & (lane < offset + HD)


def product(units_ref, half, rhs, out_ref):
    _, rows, tokens = units_ref.shape
    units = units_ref[pl.ds(4 * half, 4)].reshape(4 * rows, tokens)
    out_ref[...] = nn(units, rhs).astype(bf16).reshape(out_ref.shape)


def halves_out(acc_ref, core, send_ref, own_ref):
    rows = acc_ref.shape[0] // 2
    for half, out_ref in ((1 - core, send_ref), (core, own_ref)):
        start = pl.multiple_of(half * rows, rows)
        out_ref[...] = acc_ref[pl.ds(start, rows)].astype(bf16).reshape(out_ref.shape)


def add_by_slot(sums_ref, here, index, term):
    width = term.shape[1]
    for i, slot in enumerate(here):
        rows = term[i * SEG : (i + 1) * SEG]
        sums_ref[pl.ds(slot, 1), index * width : (index + 1) * width] += jnp.sum(rows, axis=0, keepdims=True)


def project_kernel(
    slots, x_ref, mod_ref, w_ref, coords_ref, cos_ref, sin_ref, gain_ref, gather_ref, spread_ref,
    perm_ref, units_ref, raw_ref, inv_ref, q_ref, k_ref, v_ref, kt_ref,
):
    width = x_ref.shape[1]
    norm, _ = normed(x_ref[...].astype(f32))

    def modulate(slot, rows):
        return (rows * (1.0 + part(mod_ref, slot, 1, width)) + part(mod_ref, slot, 0, width)).astype(bf16)

    low = by_slot(modulate, slots_here(slots, x_ref.shape[0]), norm)
    units_ref[...] = nt(perm_ref[...], low).astype(bf16).reshape(units_ref.shape)
    cosine, sine = angles(coords_ref, cos_ref, sin_ref)
    for index, out_ref in enumerate((q_ref, k_ref)):
        raw = nn(low, w_ref[:, index * width : (index + 1) * width])
        raw_ref[:, index * width : (index + 1) * width] = raw
        inverse = lax.rsqrt(head_sum(raw * raw, gather_ref) * (1.0 / HD) + EPS)
        inv_ref[:, index * 128 : (index + 1) * 128] = inverse
        scaled = raw * head_spread(inverse, spread_ref) * gain_ref[index : index + 1, :]
        turned = scaled * cosine + partner(scaled) * sine
        out_ref[...] = turned.astype(bf16)
        if index == 1:
            kt_ref[...] = turned.T.astype(bf16)
    v_ref[...] = nn(low, w_ref[:, 2 * width :]).astype(bf16)


def load_parts(sources, targets, sems, base, cut):
    columns = targets[0].shape[1]
    spans = [(0, cut), (cut, columns)] if cut else [(0, columns)]
    loads = [
        [
            pltpu.make_async_copy(
                source.at[:, pl.ds(base + start, stop - start)],
                target.at[:, pl.ds(start, stop - start)],
                sems.at[part, i],
            )
            for i, (source, target) in enumerate(zip(sources, targets))
        ]
        for part, (start, stop) in enumerate(spans)
    ]

    @pl.when(pl.program_id(0) == 0)
    def _():
        for part in loads:
            for load in part:
                load.start()

    for step, part in enumerate(loads):

        @pl.when(pl.program_id(0) == step)
        def _(part=part):
            for load in part:
                load.wait()


def attend_kernel(slots, q_hbm, k_hbm, v_hbm, o_ref, lse_ref, q_ref, k_ref, v_ref, sems):
    step = pl.program_id(0)
    tokens, width = q_ref.shape
    load_parts((q_hbm, k_hbm, v_hbm), (q_ref, k_ref, v_ref), sems, 0, FIRST)
    lane128 = lax.broadcasted_iota(jnp.int32, (1, 128), 1)
    lane = lax.broadcasted_iota(jnp.int32, (1, WIN), 1)

    @pl.when(step == 0)
    def _():
        o_ref[...] = jnp.zeros_like(o_ref)
        lse_ref[...] = jnp.zeros_like(lse_ref)

    def head(h, rows):
        start, offset = window(h, width)
        inside = head_lanes(offset)
        columns = pl.ds(start, WIN)
        query = jnp.where(inside, q_ref[rows, columns], 0)
        value = jnp.where(inside, v_ref[rows, columns], 1)
        weight = jnp.exp2(nt(query, k_ref[rows, columns]) * SCORE_LOG2).astype(bf16)
        summed = nn(weight, value)
        free = jnp.where(offset > 0, 0, WIN - 1)
        total = jnp.sum(jnp.where(lane == free, summed, 0.0), axis=1, keepdims=True)
        o_ref[rows, columns] += jnp.where(inside, summed * (1.0 / total), 0.0)
        lse_ref[rows, :] += jnp.where(lane128 == h, jnp.log2(total), 0.0)

    whole = slots[tokens // SEG - 1] == slots[0]

    @pl.when(whole)
    def _():
        for i in range(TOGETHER):
            head(step * TOGETHER + i, slice(None))

    @pl.when(jnp.logical_not(whole))
    def _():
        for i in range(TOGETHER):
            for b in range(tokens // SEG):
                head(step * TOGETHER + i, slice(b * SEG, (b + 1) * SEG))


def mix_kernel(
    slots, x_ref, cot_ref, mod_ref, o_ref, lse_ref, w_out_ref, perm_ref,
    attended_ref, lse_out_ref, attn_ref, mid_ref, low_ref, gf_ref, att_units_ref, ffn_units_ref,
):
    width = x_ref.shape[1]
    here = slots_here(slots, x_ref.shape[0])
    lse_out_ref[...] = lse_ref[...].T
    attended = o_ref[...].astype(bf16)
    attended_ref[...] = attended
    att_units_ref[...] = nt(perm_ref[...], attended).astype(bf16).reshape(att_units_ref.shape)
    attn = nn(attended, w_out_ref[...])
    attn_ref[...] = attn.astype(bf16)
    mid = by_slot(
        lambda slot, x, rows: x.astype(f32) + part(mod_ref, slot, 2, width) * rows, here, x_ref[...], attn
    )
    mid_ref[...] = mid
    norm, _ = normed(mid)

    def modulate(slot, rows):
        return (rows * (1.0 + part(mod_ref, slot, 4, width)) + part(mod_ref, slot, 3, width)).astype(bf16)

    low = by_slot(modulate, here, norm)
    low_ref[...] = low
    ffn_units_ref[...] = nt(perm_ref[...], low).astype(bf16).reshape(ffn_units_ref.shape)
    gf_ref[...] = by_slot(
        lambda slot, rows: (rows.astype(f32) * part(mod_ref, slot, 5, width)).astype(bf16), here, cot_ref[...]
    )


def ffn_kernel(
    bits, x_ref, gf_hbm, units_hbm, wg_ref, wu_ref, wd_ref,
    gate_send_ref, gate_own_ref, up_send_ref, up_own_ref, down_send_ref, down_own_ref, ffn_hbm, dmod_hbm,
    turned_ref, gf_ref, units_ref, ffn_ref, dmod_ref, sems, *, n_mod, rows_ff,
):
    core = bits[0]
    first = pl.program_id(0) == 0
    last = pl.program_id(0) == pl.num_programs(0) - 1
    load_gf = pltpu.make_async_copy(gf_hbm, gf_ref, sems.at[0])
    load_units = pltpu.make_async_copy(units_hbm, units_ref, sems.at[1])
    store_ffn = pltpu.make_async_copy(ffn_ref, ffn_hbm, sems.at[2])
    store_dmod = pltpu.make_async_copy(dmod_ref, dmod_hbm, sems.at[3])

    @pl.when(first)
    def _():
        load_gf.start()
        load_units.start()
        ffn_ref[...] = jnp.zeros_like(ffn_ref)
        dmod_ref[...] = jnp.zeros_like(dmod_ref)

    gate = nn(x_ref[...], wg_ref[...])
    up = nn(x_ref[...], wu_ref[...])

    @pl.when(first)
    def _():
        load_gf.wait()
        load_units.wait()

    grad_hidden = nt(gf_ref[...], wd_ref[...])
    sigmoid = 1.0 / (1.0 + jnp.exp(-gate))
    silu = gate * sigmoid
    hidden = (silu * up).astype(bf16)
    turned = hidden.T
    for index in range(turned.shape[0] // rows_ff):
        unit, rest = unit_of(index, n_mod)
        turned_ref[unit, rest * rows_ff : (rest + 1) * rows_ff] = turned[
            index * rows_ff : (index + 1) * rows_ff
        ]
    dg = (grad_hidden * up * (sigmoid * (1.0 + gate * (1.0 - sigmoid)))).astype(bf16)
    du = (grad_hidden * silu).astype(bf16)

    ffn_ref[...] += nn(hidden, wd_ref[...])
    dmod_ref[...] += nt(dg, wg_ref[...]) + nt(du, wu_ref[...])

    @pl.when(last)
    def _():
        store_ffn.start()
        store_dmod.start()

    product(units_ref, 1 - core, dg, gate_send_ref)
    product(units_ref, 1 - core, du, up_send_ref)
    product(turned_ref, 1 - core, gf_ref[...], down_send_ref)
    product(units_ref, core, dg, gate_own_ref)
    product(units_ref, core, du, up_own_ref)
    product(turned_ref, core, gf_ref[...], down_own_ref)

    @pl.when(last)
    def _():
        store_ffn.wait()
        store_dmod.wait()


def middle_kernel(
    slots, mid_ref, ffn_ref, dmod_ref, cot_ref, attn_ref, o_ref, units_ref, mod_ref, w_out_ref, gather_ref,
    out_ref, grad_mid_ref, do_ref, dot_ref, sums_ref, send_ref, own_ref, acc_ref,
):
    width = mid_ref.shape[1]
    block = pl.program_id(0)
    here = slots_here(slots, mid_ref.shape[0])
    segments = pl.num_programs(0) * len(here)
    incoming = cot_ref[...].astype(f32)
    mid = mid_ref[...]
    out_ref[...] = by_slot(
        lambda slot, rows, ffn: (rows + part(mod_ref, slot, 5, width) * ffn).astype(bf16), here, mid, ffn_ref[...]
    )
    norm, inverse = normed(mid)
    dmod = dmod_ref[...]
    scaled = by_slot(lambda slot, rows: rows * (1.0 + part(mod_ref, slot, 4, width)), here, dmod)
    grad_mid = incoming + norm_back(scaled, norm, inverse)
    grad_mid_ref[...] = grad_mid
    ga = by_slot(lambda slot, rows: (rows * part(mod_ref, slot, 2, width)).astype(bf16), here, grad_mid)
    grow = nn(units_ref[...].reshape(width, -1), ga)

    @pl.when(block == 0)
    def _():
        acc_ref[...] = grow

    @pl.when(block > 0)
    def _():
        acc_ref[...] += grow

    @pl.when(block == pl.num_programs(0) - 1)
    def _():
        halves_out(acc_ref, slots[segments], send_ref, own_ref)

    do = nt(ga, w_out_ref[...]).astype(bf16)
    do_ref[...] = do
    dot_ref[...] = head_sum(do.astype(f32) * o_ref[...].astype(f32), gather_ref).T

    @pl.when(block == 0)
    def _():
        sums_ref[...] = jnp.zeros_like(sums_ref)

    for index, term in enumerate((grad_mid * attn_ref[...].astype(f32), dmod, dmod * norm, incoming * ffn_ref[...])):
        add_by_slot(sums_ref, here, index, term)


def attend_back_kernel(
    slots, q_hbm, k_hbm, v_hbm, do_hbm, lse_ref, dot_ref, kt_ref, dqt_ref, dk_ref, dv_low_ref, dv_ref,
    q_ref, k_ref, v_ref, do_ref, sems, *, first, base, base_row, width, cut,
):
    tokens = q_ref.shape[0]
    load_parts((q_hbm, k_hbm, v_hbm, do_hbm), (q_ref, k_ref, v_ref, do_ref), sems, base, cut)

    @pl.when(pl.program_id(0) == 0)
    def _():
        dqt_ref[...] = jnp.zeros_like(dqt_ref)
        dk_ref[...] = jnp.zeros_like(dk_ref)
        dv_ref[...] = jnp.zeros_like(dv_ref)

    def head(h, rows):
        start, offset = window(h, width)
        inside = head_lanes(offset)
        columns = pl.ds(pl.multiple_of(start - base, 128), WIN)
        first_row = pl.multiple_of((h * HD) // 16 * 16, 16)
        own_place = pl.ds(pl.multiple_of(first_row - base_row, 16), HD + 8)
        row = lax.broadcasted_iota(jnp.int32, (HD + 8, 1), 0) + first_row
        own_rows = (row >= h * HD) & (row < h * HD + HD)
        query = q_ref[rows, columns]
        grad_out = do_ref[rows, columns]
        key = jnp.where(inside, k_ref[rows, columns], 0)
        value = jnp.where(inside, v_ref[rows, columns], 0)
        probs = jnp.exp2(nt(key, query) * SCORE_LOG2 - lse_ref[pl.ds(h, 1), rows])
        scores = (probs * (nt(value, grad_out) - dot_ref[pl.ds(h, 1), rows])).astype(bf16)
        dv_ref[rows, columns] += jnp.where(inside, nn(probs.astype(bf16), grad_out), 0.0)
        dk_ref[rows, columns] += jnp.where(inside, nn(scores, query) * SCORE_SCALE, 0.0)
        turned = nn(kt_ref[own_place, rows], scores) * SCORE_SCALE
        dqt_ref[own_place, rows] += jnp.where(own_rows, turned, 0.0)

    whole = slots[tokens // SEG - 1] == slots[0]
    begin = first + pl.program_id(0) * TOGETHER

    @pl.when(whole)
    def _():
        for i in range(TOGETHER):
            head(begin + i, slice(None))

    @pl.when(jnp.logical_not(whole))
    def _():
        for i in range(TOGETHER):
            for b in range(tokens // SEG):
                head(begin + i, slice(b * SEG, (b + 1) * SEG))

    @pl.when(pl.program_id(0) == pl.num_programs(0) - 1)
    def _():
        dv_low_ref[...] = dv_ref[...].astype(bf16)


def head_span(first, end, width):
    begin = lambda head: min(head * HD // 128, width // 128 - WIN // 128) * 128
    return begin(first), begin(end - 1) + WIN, first * HD // 16 * 16, (end - 1) * HD // 16 * 16 + HD + 8


def join_spans(low, high, begin, axis):
    size = low.shape[axis] - begin
    if size == 0:
        return jnp.concatenate([low, high], axis=axis)
    cut = lambda arr, start, stop: lax.slice_in_dim(arr, start, stop, axis=axis)
    middle = cut(low, begin, begin + size) + cut(high, 0, size)
    return jnp.concatenate([cut(low, 0, begin), middle, cut(high, size, high.shape[axis])], axis=axis)


def project_back_kernel(
    bits, dqt0_ref, dqt1_ref, dk0_ref, dk1_ref, raw_ref, inv_ref, q_ref, k_ref, units_ref,
    coords_ref, cos_ref, sin_ref, gain_ref, gather_ref, spread_ref, fold_ref,
    gq_ref, gk_ref, gains_low_ref, q_send_ref, q_own_ref, k_send_ref, k_own_ref, accq_ref, acck_ref, gains_ref,
    *, base, base_row,
):
    width = q_ref.shape[1]
    block = pl.program_id(0)

    @pl.when(block == 0)
    def _():
        gains_ref[...] = jnp.zeros_like(gains_ref)
        accq_ref[...] = jnp.zeros_like(accq_ref)
        acck_ref[...] = jnp.zeros_like(acck_ref)

    cosine, sine = angles(coords_ref, cos_ref, sin_ref)
    parts = ((q_ref, gq_ref, accq_ref), (k_ref, gk_ref, acck_ref))
    for index, (low_ref, out_ref, acc_ref) in enumerate(parts):
        if index == 0:
            grad = join_spans(dqt0_ref[...], dqt1_ref[...], base_row, 0).T
        else:
            grad = join_spans(dk0_ref[...], dk1_ref[...], base, 1)
        raw = raw_ref[:, index * width : (index + 1) * width]
        inverse = head_spread(inv_ref[:, index * 128 : (index + 1) * 128], spread_ref)
        mean = head_sum(grad * low_ref[...].astype(f32), gather_ref) * (1.0 / HD)
        norm = raw * inverse
        back = grad * cosine - partner(grad) * sine
        gains_ref[index : index + 1, :] += jnp.sum(back * norm, axis=0, keepdims=True)
        grad_raw = (
            inverse * (back * gain_ref[index : index + 1, :] - norm * head_spread(mean, spread_ref))
        ).astype(bf16)
        out_ref[...] = grad_raw
        acc_ref[...] += nn(units_ref[...].reshape(width, -1), grad_raw)

    @pl.when(block == pl.num_programs(0) - 1)
    def _():
        halves_out(accq_ref, bits[0], q_send_ref, q_own_ref)
        halves_out(acck_ref, bits[0], k_send_ref, k_own_ref)
        terms = split3(gains_ref[...])
        sums = sum(nn(term.astype(bf16), fold_ref[...]) for term in terms)
        high = sums.astype(bf16).astype(f32)
        row = lax.broadcasted_iota(jnp.int32, (8, 1), 0)
        mine = 4 * bits[1]
        placed = jnp.zeros((8, 128), f32)
        for index, term in enumerate((high[0:1], (sums - high)[0:1], high[1:2], (sums - high)[1:2])):
            placed = jnp.where(row == mine + index, term, placed)
        gains_low_ref[...] = placed.astype(bf16)


def input_back_kernel(
    slots, gq_ref, gk_ref, dv0_ref, dv1_ref, x_ref, grad_mid_ref, mod_ref, w_ref, other_sums_ref, gains_ref,
    grad_x_ref, grad_own_ref, grad_other_ref, sums_ref, *, base,
):
    width = x_ref.shape[1]
    block = pl.program_id(0)
    here = slots_here(slots, x_ref.shape[0])
    last_block = pl.num_programs(0) - 1
    segments = pl.num_programs(0) * len(here)
    dmod = nt(gq_ref[...], w_ref[:, :width]) + nt(gk_ref[...], w_ref[:, width : 2 * width])
    dmod = dmod + nt(join_spans(dv0_ref[...], dv1_ref[...], base, 1), w_ref[:, 2 * width :])
    norm, inverse = normed(x_ref[...].astype(f32))
    scaled = by_slot(lambda slot, rows: rows * (1.0 + part(mod_ref, slot, 1, width)), here, dmod)
    grad_x = grad_mid_ref[...] + norm_back(scaled, norm, inverse)
    grad_x_ref[...] = grad_x.astype(bf16)

    @pl.when(block == 0)
    def _():
        sums_ref[...] = jnp.zeros_like(sums_ref)

    for index, term in enumerate((dmod, dmod * norm)):
        add_by_slot(sums_ref, here, index, term)

    @pl.when(block == last_block)
    def _():
        mod = slots[segments + 1]
        count = sums_ref.shape[0]
        half = 3 * width
        mine = jnp.concatenate([sums_ref[...]] * 2, axis=0)
        rest = jnp.concatenate([other_sums_ref[...]] * 2, axis=0)
        row = lax.broadcasted_iota(jnp.int32, (2 * count, 1), 0) // count
        attn_part = jnp.where(row == mod, jnp.concatenate([mine, rest[:, :width]], axis=1), 0.0)
        ffn_part = jnp.where(row == mod, rest[:, width:], 0.0)
        grad_own_ref[:, :half] = jnp.where(mod == 0, attn_part, ffn_part).astype(bf16)
        grad_other_ref[:, :half] = jnp.where(mod == 0, ffn_part, attn_part).astype(bf16)
        grad_own_ref[:, half:] = gains_ref[...]
        grad_other_ref[:, half:] = gains_ref[...]


def value_kernel(bits, units_ref, dv0_ref, dv1_ref, send_ref, own_ref, *, base):
    rhs = join_spans(dv0_ref[...], dv1_ref[...], base, 1)
    product(units_ref, 1 - bits[0], rhs, send_ref)
    product(units_ref, bits[0], rhs, own_ref)


def split_step(bits, ins, outs, *, lead, at, bit, pair_rows, cuts):
    send_ref, keep_ref = outs
    mine = bits[bit]
    start = 0
    for own_ref, got_ref, cut in zip(ins[::2], ins[1::2], cuts):
        columns, target = slice(None), slice(None)
        if cut:
            columns, target = slice(*cut), slice(start, start + cut[1] - cut[0])
            start = target.stop

        def total(*index):
            place = index + (slice(None), columns)
            return own_ref[place].astype(f32) + got_ref[place].astype(f32)

        if at is None:
            for j in range(max(lead, 1)):
                index = (j,) if lead else ()
                value = total(*index)
                rows = pair_rows or value.shape[0] // 2
                for p in range(value.shape[0] // (2 * rows)):
                    first = value[2 * p * rows : (2 * p + 1) * rows]
                    second = value[(2 * p + 1) * rows : (2 * p + 2) * rows]
                    place = index + (slice(p * rows, (p + 1) * rows), target)
                    send_ref[place] = jnp.where(mine == 1, first, second).astype(bf16)
                    keep_ref[place] = jnp.where(mine == 1, second, first).astype(keep_ref.dtype)
            continue
        for j in range(lead // 2):
            place = ((j,) if lead > 2 else ()) + (slice(None), target)
            away = 1 - mine if lead == 2 else 2 * (1 - mine) + j if at == 0 else 2 * j + 1 - mine
            own = mine if lead == 2 else 2 * mine + j if at == 0 else 2 * j + mine
            send_ref[place] = total(away).astype(bf16)
            keep_ref[place] = total(own).astype(keep_ref.dtype)


def merge_step(bits, ins, outs, *, bit, parts):
    send_ref, keep_ref = outs
    start = 0
    for own_ref, got_ref, pieces in zip(ins[::2], ins[1::2], parts):
        value = own_ref[...].astype(f32) + got_ref[...].astype(f32)
        rows, columns = value.shape[0] // 2, value.shape[1]
        first, second = value[:rows], value[rows:]
        sent = jnp.where(bits[bit] == 1, first, second).astype(bf16)
        kept = jnp.where(bits[bit] == 1, second, first)
        for i in range(pieces):
            place = slice(start, start + columns)
            if pieces > 1:
                send_ref[:, place] = jnp.zeros_like(send_ref[:, place])
                keep_ref[:, place] = jnp.zeros_like(keep_ref[:, place])
            taken = slice(i * rows // pieces, (i + 1) * rows // pieces)
            send_ref[: rows // pieces, place] = sent[taken]
            keep_ref[: rows // pieces, place] = kept[taken]
            start += columns


def apart_step(bits, ins, outs, *, places):
    own_ref, got_ref = ins
    for out, at, start, stop, rows in places:
        value = own_ref[:, start:stop] + got_ref[:, start:stop].astype(f32)
        if rows is None:
            outs[out][:, at : at + stop - start] = value
        else:
            count = rows[1] - rows[0]
            outs[out][rows[0] : rows[1], :] = value[:count]


def pair_step(bits, ins, outs):
    own_ref, got_ref, activated_ref = ins
    width = activated_ref.shape[1]
    outs[0][:, :width] = activated_ref[...]
    outs[0][:, width:] = (own_ref[...].astype(f32) + got_ref[...].astype(f32)).astype(bf16)


def joined(ins):
    return jnp.concatenate([ref[...].astype(f32) for ref in ins], axis=0).astype(bf16)


def join_step(bits, ins, outs):
    outs[0][...] = joined(ins)


def last_step(bits, ins, outs):
    outs[0][...] = ins[0][...] + ins[1][...].astype(f32)


def ada_step(bits, ins, outs, *, width):
    rows = outs[0].shape[0]
    every = joined(ins)
    position = bits[0] + sum(bits[1 + k] * 2**k for k in range(1, (width // rows).bit_length() - 1))
    feature = lax.broadcasted_iota(jnp.int32, (width, 128), 0)
    place = lax.broadcasted_iota(jnp.int32, (width, 128), 1)
    chosen = (feature == position * rows + place) & (place < rows)
    own = nn(every[:, :width], chosen.astype(f32).astype(bf16)).astype(bf16)
    half = outs[0].shape[1]
    outs[0][...] = tn(own, every[:, width : width + half])[:rows]
    terms = every[:, width + half :].astype(f32)
    kind = lax.broadcasted_iota(jnp.int32, (terms.shape[0], 1), 0) // 2 % 2
    for index in range(2):
        outs[1][index : index + 1, :] = jnp.sum(jnp.where(kind == index, terms, 0.0), axis=0, keepdims=True)


def step_kernel(bits, *refs, plans):
    n_in = sum(plan[1] for plan in plans)
    ins, outs = refs[:n_in], refs[n_in:]
    for function, takes, gives in plans:
        function(bits, ins[:takes], outs[:gives])
        ins, outs = ins[takes:], outs[gives:]


class Chain:
    def __init__(self):
        self.last = None

    def __call__(
        self, kernel, grid, in_specs, out_specs, out_shape, args, scalars=None, scratch=(), name=None, aliases=None
    ):
        ahead = 0 if scalars is None else 1
        body = kernel
        token = ()
        if self.last is not None:
            token = (self.last,)
            in_specs = [pl.BlockSpec(memory_space=pl.ANY)] + list(in_specs)

            def body(*refs):
                kernel(*refs[:ahead], *refs[ahead + 1 :])

        spec = pltpu.PrefetchScalarGridSpec(
            num_scalar_prefetch=ahead,
            grid=grid,
            in_specs=in_specs,
            out_specs=out_specs,
            scratch_shapes=scratch,
        )
        outs = pl.pallas_call(
            body,
            grid_spec=spec,
            input_output_aliases=aliases or {},
            out_shape=out_shape,
            compiler_params=pltpu.CompilerParams(vmem_limit_bytes=VMEM),
            cost_estimate=pl.CostEstimate(flops=1, bytes_accessed=1, transcendentals=0),
            name=name,
        )(*(() if scalars is None else (scalars,)), *token, *args)
        self.last = outs[0]
        return outs


def shape(dims, dtype):
    return jax.ShapeDtypeStruct(dims, dtype)


def fixed(dims):
    return pl.BlockSpec(dims, lambda *_: (0,) * len(dims), pipeline_mode=pl.Buffered(1))


def rows_of(dims, axis=0):
    return pl.BlockSpec(dims, lambda b, *_: tuple(b if i == axis else 0 for i in range(len(dims))))


def whole(dims):
    return rows_of(dims, None)


def column_parts(dims, steps):
    return rows_of(dims[:-1] + (dims[-1] // steps,), len(dims) - 1)


class Reducer:
    def __init__(self, n_dp, n_mod, call):
        self.n_dp, self.n_mod, self.call = n_dp, n_mod, call
        self.position = lax.axis_index("dp")
        steps = range(n_dp.bit_length() - 1)
        dp_bits = [lax.shift_right_logical(self.position, step) & 1 for step in steps]
        self.bits = jnp.stack([dp_bits[0], lax.axis_index("mod")] + dp_bits[1:]).astype(jnp.int32)

    def swap(self, arr, bit):
        if bit == "mod":
            return lax.ppermute(arr, "mod", [(i, i ^ 1) for i in range(self.n_mod)])
        return lax.ppermute(arr, "dp", [(i, i ^ (1 << bit)) for i in range(self.n_dp)])

    def bit_of(self, bit):
        return 1 if bit == "mod" else bit + 1 if bit else 0

    def fold(self, streams, name, last=False):
        plans, args, outs = [], [], []
        for stream in streams:
            function, shapes = stream.last_plan() if last else stream.plan()
            inputs = stream.inputs()
            plans.append((function, len(inputs), len(shapes)))
            args += inputs
            outs += shapes
        size = sum(arg.size for arg in args)
        split = all(
            isinstance(stream, Stream) and stream.side is None and stream.own.shape[-1] % 384 == 0
            for stream in streams
        )
        steps = 3 if split and size > 2**20 else 1
        results = self.call(
            functools.partial(step_kernel, plans=plans),
            (steps,),
            [column_parts(arg.shape, steps) for arg in args],
            [column_parts(out.shape, steps) for out in outs],
            outs,
            args,
            scalars=self.bits,
            name=name,
        )
        results = list(results)
        if last:
            return results
        for stream, plan in zip(streams, plans):
            stream.step(results[: plan[2]])
            results = results[plan[2] :]

    def pass_on(self, arrays):
        anywhere = [pl.BlockSpec(memory_space=pl.ANY)] * len(arrays)
        return self.call(
            lambda *refs: None,
            (1,),
            anywhere,
            anywhere,
            [shape(arr.shape, arr.dtype) for arr in arrays],
            arrays,
            name="pass_on",
            aliases={i + 1: i for i in range(len(arrays))},
        )


class Stream:
    def __init__(self, reducer, sent, own, first, pair_rows=None):
        self.r, self.own, self.pair_rows = reducer, own, pair_rows
        order = ["mod", 1, 2]
        self.steps = order[first:] + order[:first] + list(range(3, reducer.n_dp.bit_length() - 1))
        self.lead = ["mod", 1]
        self.side = None
        self.got = reducer.swap(sent, 0)

    def inputs(self):
        return [self.own, self.got] + ([self.side[0].own, self.side[0].got] if self.side else [])

    def plan(self):
        bit = self.steps[0]
        dims = self.own.shape
        at = self.lead.index(bit) if bit in self.lead else None
        cuts = [None]
        if self.side is not None:
            cuts = [(0, dims[-1]), self.side[1]]
            dims = dims[:-1] + (dims[-1] + self.side[1][1] - self.side[1][0],)
        function = functools.partial(
            split_step, lead=dims[0] if self.lead else 0, at=at, bit=self.r.bit_of(bit), pair_rows=self.pair_rows,
            cuts=cuts,
        )
        if at is None:
            dims = dims[:-2] + (dims[-2] // 2, dims[-1])
        else:
            dims = dims[1:] if len(self.lead) == 1 else (2,) + dims[1:]
        return function, [shape(dims, bf16), shape(dims, bf16 if len(self.lead) == 2 else f32)]

    def step(self, results):
        bit = self.steps.pop(0)
        if bit in self.lead:
            self.lead.remove(bit)
        self.side = None
        sent, self.own = results
        self.got = self.r.swap(sent, bit)

    def join(self, stream, cut):
        self.side = (stream, cut)


class Merged:
    def __init__(self, streams):
        self.streams, self.r, self.bit = streams, streams[0].r, streams[0].steps[0]
        self.own = self.places = self.shapes = None

    def inputs(self):
        if self.own is not None:
            return [self.own, self.got]
        return [arr for stream in self.streams for arr in (stream.own, stream.got)]

    def plan(self):
        parts = [3 if stream.pair_rows else 1 for stream in self.streams]
        columns = sum(pieces * stream.own.shape[1] for pieces, stream in zip(parts, self.streams))
        dims = (self.streams[0].own.shape[0] // 2, columns)
        function = functools.partial(merge_step, bit=self.r.bit_of(self.bit), parts=parts)
        return function, [shape(dims, bf16), shape(dims, f32)]

    def step(self, results):
        sent, self.own = results
        self.got = self.r.swap(sent, self.bit)

    def last_plan(self):
        if self.places is None:
            return last_step, [shape(self.own.shape, f32)]
        return functools.partial(apart_step, places=self.places), self.shapes


class Gather:
    def __init__(self, reducer, sent, own, activated):
        self.r, self.own, self.activated = reducer, own, activated
        self.steps = [1] + list(range(reducer.n_dp.bit_length() - 2, 1, -1)) + [0]
        self.got = reducer.swap(sent, "mod")
        self.pair = None

    def inputs(self):
        return [self.own, self.got] + ([self.activated] if self.pair is None else [])

    def plan(self):
        rows, columns = self.own.shape
        if self.pair is None:
            return pair_step, [shape((rows, columns + self.activated.shape[1]), bf16)]
        return join_step, [shape((2 * rows, columns), bf16)]

    def step(self, results):
        (self.own,) = results
        if self.pair is None:
            self.pair = self.own
        self.got = self.r.swap(self.own, self.steps.pop(0))

    def last_plan(self):
        width = self.activated.shape[1]
        function = functools.partial(ada_step, width=width)
        dims = (width // self.r.n_dp, self.own.shape[1] - width - 128)
        return function, [shape(dims, f32), shape((2, 128), f32)]


def silu_grad(v):
    sigmoid = jax.nn.sigmoid(v)
    return sigmoid * (1.0 + v * (1.0 - sigmoid))


def pair_order(own, other, mod):
    return jnp.where(mod == 0, jnp.stack([own, other]), jnp.stack([other, own]))


def body(
    n_dp, n_mod, tokens, cond, segments, coords, w_ada, w_qkv, q_gain, k_gain, w_out, w_gate, w_up,
    w_down, cotangent,
):
    _, count, width = tokens.shape
    slots_n = cond.shape[1]
    half = w_ada.shape[1]
    ff = w_gate.shape[1]
    blocks = count // TB
    n_dev = n_dp * n_mod
    call = Chain()
    reducer = Reducer(n_dp, n_mod, call)
    mod_index = lax.axis_index("mod")
    x = tokens[0]
    cot = cotangent[0]
    slots = segments[0, ::SEG]
    coord = coords[0]
    cos_table, sin_table = (jnp.asarray(t) for t in rope_tables(width))
    gather, spread, head_fold = (jnp.asarray(t) for t in head_tables(width))
    perm = jnp.asarray(unit_permutation(width, n_dp, n_mod))
    gains = jnp.stack([jnp.tile(q_gain, HEADS), jnp.tile(k_gain, HEADS)])

    cond_both = pair_order(cond[0], reducer.swap(cond[0], "mod"), mod_index)
    activated = jax.nn.silu(cond_both).astype(bf16).reshape(-1, width)
    mod_half = jnp.dot(activated, w_ada, preferred_element_type=f32).astype(bf16)
    mod_half = mod_half.reshape(n_mod, slots_n, half)
    own_half = lax.dynamic_index_in_dim(mod_half, mod_index, 0, keepdims=False)
    other_half = lax.dynamic_index_in_dim(mod_half, 1 - mod_index, 0, keepdims=False)
    pair = pair_order(own_half, reducer.swap(other_half, "mod"), mod_index)
    modulation = jnp.concatenate([pair[0], pair[1]], axis=1).astype(f32)

    anywhere = pl.BlockSpec(memory_space=pl.ANY)
    token_f32 = shape((count, width), f32)
    token_bf16 = shape((count, width), bf16)
    units = shape((8, width // 8, count), bf16)
    units_spec = rows_of((8, width // 8, TB), 2)
    token_spec = rows_of((TB, width))
    mod_spec = fixed((slots_n, 6 * width))
    square = fixed((width, width))
    table_specs = [fixed(cos_table.shape), fixed(sin_table.shape), fixed((2, width)), fixed(gather.shape), fixed(spread.shape)]
    tables = (cos_table, sin_table, gains, gather, spread)
    lane_rows = shape((128, count), f32)
    macs = count * width * width

    attn_units, raw, inverse, query, key, value, key_t = call(
        project_kernel,
        (blocks,),
        [token_spec, mod_spec, fixed((width, 3 * width)), rows_of((2, TB), 1)] + table_specs + [square],
        [units_spec, rows_of((TB, 2 * width)), rows_of((TB, 256))] + [token_spec] * 3 + [rows_of((width, TB), 1)],
        [units, shape((count, 2 * width), f32), shape((count, 256), f32)] + [token_bf16] * 3
        + [shape((width, count), bf16)],
        (x, modulation, w_qkv, coord) + tables + (perm,),
        scalars=slots,
        name="project",
    )
    attended, lse_columns = call(
        attend_kernel,
        (HEADS // TOGETHER,),
        [anywhere] * 3,
        [fixed((count, width)), fixed((count, 128))],
        [token_f32, shape((count, 128), f32)],
        (query, key, value),
        scalars=slots,
        scratch=[pltpu.VMEM((count, width), bf16)] * 3 + [pltpu.SemaphoreType.DMA((2, 3))],
        name="attend",
    )
    attended, lse, attn, mid, ffn_in, grad_ffn, out_units, ffn_units = call(
        mix_kernel,
        (blocks,),
        [token_spec, token_spec, mod_spec, token_spec, rows_of((TB, 128)), square, square],
        [token_spec, rows_of((128, TB), 1)] + [token_spec] * 4 + [units_spec] * 2,
        [token_bf16, lane_rows, token_bf16, token_f32, token_bf16, token_bf16, units, units],
        (x, cot, modulation, attended, lse_columns, w_out, perm),
        scalars=slots,
        name="mix",
    )

    rows_ff = ff // n_dev
    chunk = 768
    piece = chunk // 8
    half_units = lambda rows, columns: shape((4, rows, columns), bf16)
    square_send = [fixed((4, width // 8, width))] * 2
    square_shapes = [half_units(width // 8, width)] * 2
    gate_send, gate_own, up_send, up_own, down_send, down_own, ffn, grad_mod_ffn = call(
        functools.partial(ffn_kernel, n_mod=n_mod, rows_ff=rows_ff),
        (ff // chunk,),
        [fixed((count, width)), anywhere, anywhere]
        + [rows_of((width, chunk), 1)] * 2 + [rows_of((chunk, width))],
        [rows_of((4, width // 8, chunk), 2)] * 4
        + [rows_of((4, 1, piece, width), 1)] * 2 + [anywhere] * 2,
        [half_units(width // 8, ff)] * 4
        + [shape((4, ff // chunk, piece, width), bf16)] * 2 + [token_f32] * 2,
        (ffn_in, grad_ffn, ffn_units, w_gate, w_up, w_down),
        scalars=reducer.bits,
        scratch=[
            pltpu.VMEM((8, piece, count), bf16),
            pltpu.VMEM((count, width), bf16),
            pltpu.VMEM(units.shape, bf16),
            pltpu.VMEM((count, width), f32),
            pltpu.VMEM((count, width), f32),
            pltpu.SemaphoreType.DMA((4,)),
        ],
        name="ffn",
    )
    gate = Stream(reducer, gate_send, gate_own, 0)
    up = Stream(reducer, up_send, up_own, 1)
    down = Stream(
        reducer, down_send.reshape(4, ff // 8, width), down_own.reshape(4, ff // 8, width), 2, rows_ff
    )

    slots_core = jnp.concatenate([slots, reducer.bits[:2]])
    seg_spec = rows_of((SEG, width))
    output, grad_mid, grad_attended, dot_term, sums_b, out_send, out_own = call(
        middle_kernel,
        (count // SEG,),
        [seg_spec] * 6 + [rows_of((8, width // 8, SEG), 2), mod_spec, square, fixed(gather.shape)],
        [seg_spec] * 3 + [rows_of((128, SEG), 1), fixed((slots_n, 4 * width))] + square_send,
        [token_bf16, token_f32, token_bf16, lane_rows, shape((slots_n, 4 * width), f32)] + square_shapes,
        (mid, ffn, grad_mod_ffn, cot, attn, attended, out_units, modulation, w_out, gather),
        scalars=slots_core,
        scratch=[pltpu.VMEM((width, width), f32)],
        name="middle",
    )
    out = Stream(reducer, out_send, out_own, 1)
    early = [gate, up, down]
    middle_cut = width // 256 * 128 + 128
    gate.join(out, (0, middle_cut))
    up.join(out, (middle_cut, width))
    reducer.fold(early, "early")

    def attend_back(first, end, name):
        begin, stop, begin_row, stop_row = head_span(first, end, width)
        columns, rows = stop - begin, stop_row - begin_row
        used_rows = pl.BlockSpec((rows, count), lambda *_: (begin_row // rows, 0), pipeline_mode=pl.Buffered(1))
        return call(
            functools.partial(attend_back_kernel, first=first, base=begin, base_row=begin_row, width=width,
                              cut=FIRST if first == 0 else 0),
            ((end - first) // TOGETHER,),
            [anywhere] * 4 + [fixed((128, count))] * 2 + [used_rows],
            [fixed((rows, count))] + [fixed((count, columns))] * 2,
            [shape((rows, count), f32), shape((count, columns), f32), shape((count, columns), bf16)],
            (query, key, value, grad_attended, lse, dot_term, key_t),
            scratch=[pltpu.VMEM((count, columns), f32)]
            + [pltpu.VMEM((count, columns), bf16)] * 4 + [pltpu.SemaphoreType.DMA((2, 4))],
            scalars=slots,
            name=name,
        )

    cut = 3 * HEADS // 4
    dqt0, dk0, dv0 = attend_back(0, cut, "attend_back_0")
    reducer.fold(early, "early")
    dqt1, dk1, dv1 = attend_back(cut, HEADS, "attend_back_1")
    base, _, base_row, _ = head_span(cut, HEADS, width)
    v_send, v_own = call(
        functools.partial(value_kernel, base=base),
        (1,),
        [whole(units.shape), whole(dv0.shape), whole(dv1.shape)],
        [whole((4, width // 8, width))] * 2,
        square_shapes,
        (attn_units, dv0, dv1),
        scalars=reducer.bits,
        name="value",
    )
    v_part = Stream(reducer, v_send, v_own, 2)
    reducer.fold(early, "early")
    grad_q, grad_k, gains_low, q_send, q_own, k_send, k_own = call(
        functools.partial(project_back_kernel, base=base, base_row=base_row),
        (count // SEG,),
        [rows_of((dqt0.shape[0], SEG), 1), rows_of((dqt1.shape[0], SEG), 1)]
        + [rows_of((SEG, dk0.shape[1])), rows_of((SEG, dk1.shape[1]))]
        + [rows_of((SEG, 2 * width)), rows_of((SEG, 256)), seg_spec, seg_spec, rows_of((8, width // 8, SEG), 2), rows_of((2, SEG), 1)]
        + table_specs + [fixed(head_fold.shape)],
        [seg_spec] * 2 + [fixed((8, 128))] + square_send * 2,
        [token_bf16] * 2 + [shape((8, 128), bf16)] + square_shapes * 2,
        (dqt0, dqt1, dk0, dk1, raw, inverse, query, key, attn_units, coord) + tables + (head_fold,),
        scalars=reducer.bits,
        scratch=[pltpu.VMEM((width, width), f32)] * 2 + [pltpu.VMEM((2, width), f32)],
        name="project_back",
    )
    waiting = early + [v_part]
    *arrived, q_send, k_send = reducer.pass_on([stream.got for stream in waiting] + [q_send, k_send])
    for stream, got in zip(waiting, arrived):
        stream.got = got
    q_part = Stream(reducer, q_send, q_own, 1)
    k_part = Stream(reducer, k_send, k_own, 0)
    late = [q_part, k_part, v_part]
    extra = n_dp.bit_length() - 5
    reducer.fold([v_part], "v")
    reducer.fold([q_part, k_part], "late")
    for _ in range(extra):
        reducer.fold(early, "early")
    rows_d = width // n_dev
    merged = Merged([gate, up, down])
    third = rows_ff // 3
    gate_end = ff + middle_cut
    up_end = gate_end + ff + width - middle_cut
    merged.places = [
        (0, 0, 0, ff, None),
        (2, 0, ff, gate_end, None),
        (1, 0, gate_end, gate_end + ff, None),
        (2, middle_cut, gate_end + ff, up_end, None),
    ] + [
        (3, 0, up_end + i * width, up_end + (i + 1) * width, (i * third, (i + 1) * third)) for i in range(3)
    ]
    merged.shapes = [shape((rows_d, ff), f32)] * 2 + [shape((rows_d, width), f32), shape((rows_ff, width), f32)]
    early = [merged]
    reducer.fold(early, "early")

    grad_tokens, mod_own, mod_other = call(
        functools.partial(input_back_kernel, base=base),
        (blocks,),
        [token_spec] * 2 + [rows_of((TB, dv0.shape[1])), rows_of((TB, dv1.shape[1]))] + [token_spec] * 2
        + [mod_spec, fixed((width, 3 * width)), fixed((slots_n, 4 * width)), fixed((8, 128))],
        [token_spec] + [fixed((2 * slots_n, half + 128))] * 2,
        [token_bf16] + [shape((2 * slots_n, half + 128), bf16)] * 2,
        (grad_q, grad_k, dv0, dv1, x, grad_mid, modulation, w_qkv, sums_b, gains_low),
        scalars=slots_core,
        scratch=[pltpu.VMEM((slots_n, 2 * width), f32)],
        name="input_back",
    )
    every_mod = Gather(reducer, mod_other, mod_own, activated)
    reducer.fold([v_part], "v")
    reducer.fold([every_mod], "pair")
    reducer.fold([q_part], "q")
    reducer.fold([every_mod], "every")
    reducer.fold([k_part], "k")
    summed_gate, summed_up, summed_out, summed_down = reducer.fold(early, "early_last", last=True)
    for _ in range(1 + extra):
        reducer.fold(late + [every_mod], "late")
    late = [Merged(late)]
    reducer.fold(late + [every_mod], "late")
    summed_qkv, grad_w_ada, gain_grads = reducer.fold(late + [every_mod], "late_last", last=True)

    grad_activated = jnp.einsum("nc,dc->nd", every_mod.pair[:, width : width + half], w_ada, preferred_element_type=f32)
    grad_activated = grad_activated.reshape(n_mod, slots_n, width)
    own_part = lax.dynamic_index_in_dim(grad_activated, mod_index, 0, keepdims=False)
    other_part = lax.dynamic_index_in_dim(grad_activated, 1 - mod_index, 0, keepdims=False)
    grad_own = own_part + reducer.swap(other_part.astype(bf16), "mod").astype(f32)
    grad_cond = grad_own[None] * silu_grad(cond)
    return (
        output[None],
        grad_tokens[None],
        grad_cond,
        grad_w_ada,
        summed_qkv,
        gain_grads[0, :HD],
        gain_grads[1, :HD],
        summed_out,
        summed_gate,
        summed_up,
        summed_down,
    )


def solution(mesh):
    rows = ("dp", "mod")
    in_specs = (
        P(rows, None, None),
        P(rows, None, None),
        P(rows, None),
        P(rows, None, None),
        P(None, "mod"),
        P(),
        P(),
        P(),
        P(),
        P(),
        P(),
        P(),
        P(rows, None, None),
    )
    out_specs = (
        P(rows, None, None),
        P(rows, None, None),
        P(rows, None, None),
        P("dp", "mod"),
        P(rows, None),
        P(),
        P(),
        P(rows, None),
        P(rows, None),
        P(rows, None),
        P(rows, None),
    )
    return jax.shard_map(
        functools.partial(body, mesh.shape["dp"], mesh.shape["mod"]),
        mesh=mesh,
        in_specs=in_specs,
        out_specs=out_specs,
        check_vma=False,
    )
```
